128 devices in a mesh: box: 128 (over z, x, y, core).
Axes of the slice: x: 4, y: 4, z: 4, core: 2. Of those that a mesh axis runs over, the one named last changes fastest.
Arguments:
- source: float32 [512, 32, 1024], P('box'), may hold values from -6 to 6
- conductance: float32 [512, 32, 1024], P('box'), may hold values from 0.3 to 3
- initial: float32 [512, 32, 1024], P('box'), may hold values from -6 to 6
- box_counts: int32 [128], replicated, may hold values from 1 to 3, as said below
Outputs:
- solution_field: float32 [512, 32, 1024], P('box')
- residual: float32 [512, 32, 1024], P('box')
The draws below stay inside these ranges and needn't reach their ends.
Inputs may be any that keep to these rules, and one draw needn't show every extreme that they name: `box_counts`: devices 2q and 2q + 1 together own the 4 boxes of column q of the box grid (the boxes q * 4 to q * 4 + 3).
All inputs are finite; a program needn't handle non-finite values.
Results may differ from the reference program's by a relative error of at most 0.0003.
Values sent between devices are 32-bit elements; how exact they have to be, the bound alone decides.
A program may use at most 128 MiB of HBM per device.

```python
import math
import jax
import jax.numpy as jnp

EDGE = 32
COLUMNS_Y = 4
NU = 2
NU_COARSE = 4
SLOTS = 4
BOXES = 256
SLOT_ROWS = 512


def draw_source(key, part):
    key = jax.random.fold_in(key, 7)
    shape = (SLOT_ROWS, EDGE, EDGE * EDGE)
    return jnp.clip(jax.random.normal(key, shape, jnp.float32), -6.0, 6.0)


def draw_box_counts(key, part):
    key = jax.random.fold_in(key, 11)
    split_key, pick_key = jax.random.split(key)
    column_total = SLOT_ROWS // SLOTS // 2
    firsts = jax.random.randint(split_key, (column_total,), 1, SLOTS, dtype=jnp.int32)
    chosen = jax.random.randint(pick_key, (), 0, column_total, dtype=jnp.int32)
    firsts = jnp.where(jnp.arange(column_total, dtype=jnp.int32) == chosen, SLOTS - 1, firsts)
    paired = jnp.stack([firsts, SLOTS - firsts], axis=1)
    return paired.reshape(column_total * 2).astype(jnp.int32)


def level_of(own_key, shape, pieces, low, high):
    factor_of, own = 1.0, jax.random.fold_in(own_key, 6)
    for dim, blocks in pieces:
        heights = jnp.exp(jax.random.uniform(jax.random.fold_in(own, dim), (blocks,), jnp.float32, low / len(pieces), high / len(pieces)))
        factor_of = factor_of * jnp.repeat(heights, shape[dim] // blocks).reshape([-1 if axis == dim else 1 for axis in range(len(shape))])
    return factor_of


def bell_draw(own_key, dims, deviation, most, cuts=(), kind=jnp.bfloat16):
    values = deviation * jax.random.normal(own_key, dims, jnp.float32)
    if cuts:
        values = values * level_of(own_key, dims, cuts, -0.22, 0.18)
    return jnp.clip(values, -most, most).astype(kind)


def setup_inputs(seed: int = 0) -> dict:
    streams_of = jax.random.split(jax.random.key(seed), 5)
    source = draw_source(jax.random.fold_in(streams_of[4], 71), 0)
    conductance = jnp.clip(jnp.exp(math.log(3.0) - 2.3025851 * jax.random.uniform(streams_of[1], (SLOT_ROWS, EDGE, EDGE * EDGE), jnp.float32) ** level_of(streams_of[1], (SLOT_ROWS, EDGE, EDGE * EDGE), ((0, 128),), -0.2, 0.2)), 0.3, 3.0)
    initial = bell_draw(streams_of[2], (SLOT_ROWS, EDGE, EDGE * EDGE), 1.0, 6.0, ((0, 128),), jnp.float32)
    box_counts = draw_box_counts(jax.random.fold_in(streams_of[4], 71), 0)
    return {"source": source, "conductance": conductance, "initial": initial, "box_counts": box_counts}


OMEGA = 0.8


def owner_rows(box_counts, slot_count, boxes_all):
    counts = box_counts.astype(jnp.int32)
    starts = (jnp.cumsum(counts) - counts).astype(jnp.int32)
    numbers = jnp.arange(boxes_all, dtype=jnp.int32)
    owners = (jnp.sum((starts[None, :] <= numbers[:, None]).astype(jnp.int32), axis=1) - 1).astype(jnp.int32)
    rank_ids = jnp.arange(counts.shape[0], dtype=jnp.int32)
    owner_first = jnp.sum(jnp.where(rank_ids[None, :] == owners[:, None], starts[None, :], 0), axis=1).astype(jnp.int32)
    return (owners * slot_count + numbers - owner_first).astype(jnp.int32)


def to_grid(boxes, box_edge, columns_y, depth_boxes):
    rows_x = boxes.shape[0] // (columns_y * depth_boxes)
    shaped = boxes.reshape(rows_x, columns_y, depth_boxes, box_edge, box_edge, box_edge)
    shaped = shaped.transpose(0, 3, 1, 4, 2, 5)
    return shaped.reshape(rows_x * box_edge, columns_y * box_edge, depth_boxes * box_edge)


def from_grid(grid, box_edge, columns_y, depth_boxes):
    rows_x = grid.shape[0] // box_edge
    shaped = grid.reshape(rows_x, box_edge, columns_y, box_edge, depth_boxes, box_edge)
    shaped = shaped.transpose(0, 2, 4, 1, 3, 5)
    return shaped.reshape(rows_x * columns_y * depth_boxes, box_edge, box_edge * box_edge)


def grid_neighbours(field, keep_edge):
    if keep_edge:
        padded = jnp.pad(field, 1, mode="edge")
    else:
        padded = jnp.pad(field, 1)
    return (padded[:-2, 1:-1, 1:-1], padded[2:, 1:-1, 1:-1], padded[1:-1, :-2, 1:-1],
            padded[1:-1, 2:, 1:-1], padded[1:-1, 1:-1, :-2], padded[1:-1, 1:-1, 2:])


def face_coefficients(coeffs):
    return tuple(0.5 * (coeffs + beside) for beside in grid_neighbours(coeffs, True))


def diagonal_of(faces, scale):
    summed = faces[0]
    for more in faces[1:]:
        summed = summed + more
    return scale * summed


def operate(field, faces, scale):
    besides = grid_neighbours(field, False)
    summed = faces[0] * (field - besides[0])
    for number in range(1, 6):
        summed = summed + faces[number] * (field - besides[number])
    return scale * summed


def relax(field, source, faces, diagonal, scale):
    return field + OMEGA * (source - operate(field, faces, scale)) / diagonal


def restrict(field):
    sx, sy, sz = field.shape
    return field.reshape(sx // 2, 2, sy // 2, 2, sz // 2, 2).sum(axis=(1, 3, 5)) * 0.125


def prolong(field):
    sx, sy, sz = field.shape
    grown = jnp.broadcast_to(field[:, None, :, None, :, None], (sx, 2, sy, 2, sz, 2))
    return grown.reshape(2 * sx, 2 * sy, 2 * sz)


def reference(source, conductance, initial, box_counts):
    slot_rows = owner_rows(box_counts, SLOTS, BOXES)
    fine_source = to_grid(source[slot_rows], EDGE, COLUMNS_Y, SLOTS)
    fine_coeffs = to_grid(conductance[slot_rows], EDGE, COLUMNS_Y, SLOTS)
    solution = to_grid(initial[slot_rows], EDGE, COLUMNS_Y, SLOTS)
    fine_faces = face_coefficients(fine_coeffs)
    fine_diag = diagonal_of(fine_faces, 1.0)
    for sweep_step in range(NU):
        solution = relax(solution, fine_source, fine_faces, fine_diag, 1.0)
    fine_resid = fine_source - operate(solution, fine_faces, 1.0)
    middle_source = restrict(fine_resid)
    middle_coeffs = restrict(fine_coeffs)
    middle_faces = face_coefficients(middle_coeffs)
    middle_diag = diagonal_of(middle_faces, 0.25)
    middle_error = OMEGA * middle_source / middle_diag
    for sweep_step in range(NU - 1):
        middle_error = relax(middle_error, middle_source, middle_faces, middle_diag, 0.25)
    middle_resid = middle_source - operate(middle_error, middle_faces, 0.25)
    coarse_source = restrict(middle_resid)
    coarse_coeffs = restrict(middle_coeffs)
    coarse_faces = face_coefficients(coarse_coeffs)
    coarse_diag = diagonal_of(coarse_faces, 0.0625)
    coarse_error = OMEGA * coarse_source / coarse_diag
    for sweep_step in range(NU_COARSE - 1):
        coarse_error = relax(coarse_error, coarse_source, coarse_faces, coarse_diag, 0.0625)
    middle_error = middle_error + prolong(coarse_error)
    for sweep_step in range(NU):
        middle_error = relax(middle_error, middle_source, middle_faces, middle_diag, 0.25)
    solution = solution + prolong(middle_error)
    for sweep_step in range(NU):
        solution = relax(solution, fine_source, fine_faces, fine_diag, 1.0)
    leftover = fine_source - operate(solution, fine_faces, 1.0)
    empty = jnp.zeros(source.shape, source.dtype)
    solution_field = empty.at[slot_rows].set(from_grid(solution, EDGE, COLUMNS_Y, SLOTS))
    residual = empty.at[slot_rows].set(from_grid(leftover, EDGE, COLUMNS_Y, SLOTS))
    return solution_field, residual
```

```python
import functools

import jax
import jax.numpy as jnp
from jax import lax
from jax.experimental import pallas as pl
from jax.experimental.pallas import tpu as pltpu
from jax.sharding import PartitionSpec as P


RF, PF = 48, 24
R1, P1 = 32, 24
R2 = 24
LANES = 128
FULL = (1, 0), (-1, 0), (0, 1), (0, -1), (1, 1), (1, -1), (-1, 1), (-1, -1)
FAR = (0, 2), (0, -2), (1, 2), (1, -2), (-1, 2), (-1, -2)
F32 = jnp.float32


def lane_ids(rows):
    return lax.broadcasted_iota(jnp.int32, (rows, LANES), 1)


def row_ids(rows):
    return lax.broadcasted_iota(jnp.int32, (rows, LANES), 0)


def turn(value, steps):
    return pltpu.roll(value, steps % LANES, 1)


def transposed(four):
    lanes = lane_ids(four[0].shape[0])
    low = lanes < 64
    even = (lanes // 32) % 2 == 0
    a, b, c, d = four
    e = jnp.where(low, a, turn(c, 64))
    f = jnp.where(low, b, turn(d, 64))
    g = jnp.where(low, turn(a, 64), c)
    h = jnp.where(low, turn(b, 64), d)
    return (
        jnp.where(even, e, turn(f, 32)),
        jnp.where(even, turn(e, -32), f),
        jnp.where(even, g, turn(h, 32)),
        jnp.where(even, turn(g, -32), h),
    )


def coefficients(c, besides, inside):
    total = 3.0 * c
    for beside, within in zip(besides, inside):
        total = total + 0.5 * jnp.where(within, beside, c)
    quarter = 0.4 / total
    faces = [
        jnp.where(within, (c + beside) * quarter, 0.0) for beside, within in zip(besides, inside)
    ]
    return faces, total, quarter


def around(ref, base, count, rows, twist):
    centre = ref[pl.ds(base, count), :]
    return centre, (
        ref[pl.ds(base - rows, count), :],
        ref[pl.ds(base + rows, count), :],
        ref[pl.ds(base - 1, count), :],
        ref[pl.ds(base + 1, count), :],
        turn(centre, twist),
        turn(centre, -twist),
    )


def weighted(faces, base, count, besides):
    parts = [faces[n][pl.ds(base, count), :] * besides[n] for n in range(6)]
    return (parts[0] + parts[1]) + (parts[2] + parts[3]) + (parts[4] + parts[5])


def loop(low, high, width, body):
    assert (high - low) % width == 0

    def step(index, carry):
        first = low + index * width
        stores = [item for m in range(width) for item in body(first + m)]
        for ref, at, value in stores:
            ref[at] = value
        return carry

    if high - low == width:
        step(0, 0)
    else:
        lax.fori_loop(0, (high - low) // width, step, 0)


def at(base, count):
    return pl.ds(base, count), slice(None)


def pair_rows(ref, base, count, rows):
    got = [
        ref[pl.ds(base + offset, count, stride=2), :] for offset in (0, 1, rows, rows + 1)
    ]
    return (got[0] + got[1]) + (got[2] + got[3])


def pair_lanes(value, width):
    first = (lane_ids(value.shape[0]) // width) % 2 == 0
    return 0.125 * (value + jnp.where(first, turn(value, -width), turn(value, width)))


def kernel(
    counts, source, conductance, initial, out_field, out_resid,
    raw_c, raw_u, raw_s, cf, uf, sf, u1, u2, fine, gf, df,
    ya, yb, xa, xb, ka, kb,
    c1, f1, e1, e1b, pe2, mid, w1, g1, d1, r1,
    y1a, y1b, x1a, x1b, k1a, k1b,
    y2a, y2b, x2a, x2b, k2a, k2b,
    y3a, y3b, x3a, x3b, k3a, k3b,
    c2, f2, e2, e2b, deep, g2,
    pe1, stage_f, stage_r, other_f, other_r,
    local_sem, send_sem, recv_sem,
):
    me = lax.axis_index("box")
    a, j = me // 8, me % 8
    half = me % 2
    sibling = me + 1 - 2 * half
    split = counts[me - half]

    across = {da: ((a + da + 16) % 16) * 8 for da in (-1, 0, 1)}
    along = {dj: (j + dj + 8) % 8 for dj in (-2, -1, 0, 1, 2)}

    def device(da, dj):
        return across[da] + along[dj]

    used = []

    def send(src, dst, target):
        number = len(used)
        copy = pltpu.make_async_remote_copy(
            src_ref=src, dst_ref=dst, send_sem=send_sem.at[number], recv_sem=recv_sem.at[number],
            device_id=(target,), device_id_type=pl.DeviceIdType.MESH,
        )
        copy.start()
        used.append(copy)
        return copy

    raws = (raw_c, raw_u, raw_s)
    given = (conductance, initial, source)
    mine = pl.ds(pl.multiple_of(512 * half, 512), 512)
    theirs = pl.ds(pl.multiple_of(512 - 512 * half, 512), 512)
    held = pl.ds(3 * half, 3)
    locals_ = []
    for number in range(3):
        copy = pltpu.make_async_copy(
            given[number].at[pl.ds(0, 3), :, mine], raws[number].at[held], local_sem.at[number]
        )
        copy.start()
        locals_.append(copy)

    barrier = pltpu.get_barrier_semaphore()
    for da, dj in FULL + FAR:
        pl.semaphore_signal(
            barrier, inc=1, device_id=(device(da, dj),), device_id_type=pl.DeviceIdType.MESH
        )
    pl.semaphore_wait(barrier, len(FULL + FAR))

    swaps = [
        send(given[number].at[pl.ds(0, 3), :, theirs], raws[number].at[held], sibling)
        for number in range(3)
    ]
    places = [jnp.where(p < split, p, jnp.clip(3 + p - split, 0, 5)) for p in range(4)]

    def bring(number, ref):
        locals_[number].wait()
        swaps[number].wait_recv()
        raw = raws[number]

        def step(t):
            rows = pl.ds(pl.multiple_of(8 * t, 8), 8)
            out = []
            for q in range(4):
                four = [raw[places[p], rows, 128 * q : 128 * q + 128] for p in range(4)]
                for i, value in enumerate(transposed(four)):
                    out.append((ref, at(pl.multiple_of((4 + 4 * q + i) * RF + 8 + 8 * t, 8), 8), value))
            return out

        loop(0, 4, 2, step)

    bring(0, cf)
    bring(1, uf)
    bring(2, sf)

    trio = ((uf, 3, 0), (cf, 3, 3), (sf, 2, 6))
    corner = ((uf, 1, 1), (uf, 1, 2), (uf, 2, 1), (cf, 1, 1), (cf, 1, 2), (cf, 2, 1), (sf, 1, 1))

    def near_plane(dj, depth):
        return 3 + depth if dj < 0 else 20 - depth

    def far_plane(dj, depth):
        return 19 + depth if dj < 0 else 4 - depth

    def near_row(da, depth):
        return 7 + depth if da < 0 else 40 - depth

    def far_row(da, depth):
        return 39 + depth if da < 0 else 8 - depth

    first = []
    for n, dj in enumerate((-1, 1)):
        for ref, most, first_row in trio:
            for d in range(most):
                ya[n, pl.ds(32 * (first_row + d), 32), :] = ref[pl.ds(near_plane(dj, d + 1) * RF + 8, 32), :]
        first.append(send(ya.at[n], yb.at[n], device(0, dj)))
    for n, da in enumerate((-1, 1)):
        for ref, most, first_row in trio:
            for d in range(most):
                xa[n, pl.ds(16 * (first_row + d), 16), :] = ref[
                    pl.ds(4 * RF + near_row(da, d + 1), 16, stride=RF), :
                ]
        first.append(send(xa.at[n], xb.at[n], device(da, 0)))
    for n, (da, dj) in enumerate(FULL[4:]):
        for k, (ref, dy, dx) in enumerate(corner):
            ka[n, pl.ds(k, 1), :] = ref[pl.ds(near_plane(dj, dy) * RF + near_row(da, dx), 1), :]
        first.append(send(ka.at[n], kb.at[n], device(da, dj)))

    def coarse_c(i):
        total = pair_rows(cf, (4 + 2 * i) * RF + 8, 16, RF)
        return [(c1, at(pl.multiple_of((8 + i) * R1 + 8, 8), 16), pair_lanes(total, 1))]

    loop(0, 8, 8, coarse_c)

    def packed(ref):
        lanes = lane_ids(8) % 4
        total = jnp.zeros((8, LANES), F32)
        for i in range(4):
            value = pair_lanes(pair_rows(ref, (8 + 2 * i) * R1 + 8, 8, R1), 2)
            total = total + jnp.where(lanes == i, value, 0.0)
        return total

    own2 = R2 + 2 * R2 + 8

    def near_plane1(dj, depth):
        return 7 + depth if dj < 0 else 16 - depth

    def far_plane1(dj, depth):
        return 15 + depth if dj < 0 else 8 - depth

    def near_row1(da, depth):
        return 7 + depth if da < 0 else 24 - depth

    def far_row1(da, depth):
        return 23 + depth if da < 0 else 8 - depth

    def strips1(ref, most, wide, ysrc, ydst, xsrc, xdst, ksrc, kdst):
        sent = []
        for n, dj in enumerate((-1, 1)):
            for d in range(most):
                ysrc[n, pl.ds(16 * d, 16), :] = ref[pl.ds(near_plane1(dj, d + 1) * R1 + 8, 16), :]
            sent.append(send(ysrc.at[n], ydst.at[n], device(0, dj)))
        for n, da in enumerate((-1, 1)):
            for d in range(most):
                xsrc[n, pl.ds(8 * d, 8), :] = ref[pl.ds(8 * R1 + near_row1(da, d + 1), 8, stride=R1), :]
            sent.append(send(xsrc.at[n], xdst.at[n], device(da, 0)))
        for n, (da, dj) in enumerate(FULL[4:]):
            row = 8 if da < 0 else 24 - wide
            for d in range(most - 1):
                ksrc[n, pl.ds(wide * d, wide), :] = ref[pl.ds(near_plane1(dj, d + 1) * R1 + row, wide), :]
            sent.append(send(ksrc.at[n], kdst.at[n], device(da, dj)))
        return sent

    def land1(ref, most, wide, ydst, xdst, kdst, sent):
        for copy in sent:
            copy.wait_recv()
        for n, dj in enumerate((-1, 1)):
            for d in range(most):
                ref[pl.ds(far_plane1(dj, d + 1) * R1 + 8, 16), :] = ydst[n, pl.ds(16 * d, 16), :]
        for n, da in enumerate((-1, 1)):
            for d in range(most):
                ref[pl.ds(8 * R1 + far_row1(da, d + 1), 8, stride=R1), :] = xdst[n, pl.ds(8 * d, 8), :]
        for n, (da, dj) in enumerate(FULL[4:]):
            row = 24 if da < 0 else 8 - wide
            for d in range(most - 1):
                ref[pl.ds(far_plane1(dj, d + 1) * R1 + row, wide), :] = kdst[n, pl.ds(wide * d, wide), :]

    def blocks2(ref):
        sent = []
        for da, dj in FULL + FAR:
            row = R2 + R2 * (2 - dj) + 8 * (1 - da)
            sent.append(send(ref.at[pl.ds(own2, 8)], ref.at[pl.ds(row, 8)], device(da, dj)))
        return sent

    c2[pl.ds(own2, 8), :] = packed(c1)
    second = strips1(c1, 6, 8, y1a, y1b, x1a, x1b, k1a, k1b)
    third = blocks2(c2)

    for copy in first:
        copy.wait_recv()
    for n, dj in enumerate((-1, 1)):
        for ref, most, first_row in trio:
            for d in range(most):
                ref[pl.ds(far_plane(dj, d + 1) * RF + 8, 32), :] = yb[n, pl.ds(32 * (first_row + d), 32), :]
    for n, da in enumerate((-1, 1)):
        for ref, most, first_row in trio:
            for d in range(most):
                ref[pl.ds(4 * RF + far_row(da, d + 1), 16, stride=RF), :] = xb[
                    n, pl.ds(16 * (first_row + d), 16), :
                ]
    for n, (da, dj) in enumerate(FULL[4:]):
        for k, (ref, dy, dx) in enumerate(corner):
            ref[pl.ds(far_plane(dj, dy) * RF + far_row(da, dx), 1), :] = kb[n, pl.ds(k, 1), :]

    fine_faces = [fine.at[n] for n in range(6)]

    def fine_coeffs(p):
        base = p * RF + 4
        centre, besides = around(cf, base, 40, RF, 1)
        x = row_ids(40) + (32 * a - 4)
        y = 16 * j + p - 4
        z = lane_ids(40)
        inside = (y != 0, y != 127, x != 0, x != 511, z != 0, z != 127)
        faces, total, quarter = coefficients(centre, besides, inside)
        out = [(fine, (n,) + at(base, 40), faces[n]) for n in range(6)]
        out.append((gf, at(base, 40), 2.0 * quarter * sf[pl.ds(base, 40), :]))
        out.append((df, at(base, 40), 1.25 * total))
        return out

    loop(2, 22, 2, fine_coeffs)

    def sweep(src, dst, faces, right, low, high, width, rows, start, count, twist):
        def step(p):
            base = p * rows + start
            centre, besides = around(src, base, count, rows, twist)
            value = 0.2 * centre + right[pl.ds(base, count), :] + weighted(faces, base, count, besides)
            return [(dst, at(base, count), value)]

        loop(low, high, width, step)

    def leftover(src, dst, faces, right, diag, low, high, width, rows, start, count, twist):
        def step(p):
            base = p * rows + start
            centre, besides = around(src, base, count, rows, twist)
            value = diag[pl.ds(base, count), :] * (
                right[pl.ds(base, count), :] + weighted(faces, base, count, besides) - 0.8 * centre
            )
            return [(dst, at(base, count), value)]

        loop(low, high, width, step)

    sweep(uf, u1, fine_faces, gf, 2, 22, 5, RF, 4, 40, 1)
    sweep(u1, u2, fine_faces, gf, 3, 21, 6, RF, 4, 40, 1)
    leftover(u2, u1, fine_faces, gf, df, 4, 20, 4, RF, 8, 32, 1)

    def coarse_f(i):
        total = pair_rows(u1, (4 + 2 * i) * RF + 8, 16, RF)
        return [(f1, at(pl.multiple_of((8 + i) * R1 + 8, 8), 16), pair_lanes(total, 1))]

    loop(0, 8, 8, coarse_f)
    fourth = strips1(f1, 5, 4, y2a, y2b, x2a, x2b, k2a, k2b)

    fifth = []
    for n, dj in enumerate((-1, 1)):
        for d in range(3):
            y3a[n, pl.ds(32 * d, 32), :] = u2[pl.ds(near_plane(dj, d + 1) * RF + 8, 32), :]
        fifth.append(send(y3a.at[n], y3b.at[n], device(0, dj)))
    for n, da in enumerate((-1, 1)):
        for d in range(3):
            x3a[n, pl.ds(16 * d, 16), :] = u2[pl.ds(4 * RF + near_row(da, d + 1), 16, stride=RF), :]
        fifth.append(send(x3a.at[n], x3b.at[n], device(da, 0)))
    for n, (da, dj) in enumerate(FULL[4:]):
        for k, (ref, dy, dx) in enumerate(corner[:3]):
            k3a[n, pl.ds(k, 1), :] = u2[pl.ds(near_plane(dj, dy) * RF + near_row(da, dx), 1), :]
        fifth.append(send(k3a.at[n], k3b.at[n], device(da, dj)))

    land1(c1, 6, 8, y1b, x1b, k1b, second)
    mid_faces = [mid.at[n] for n in range(6)]

    def mid_coeffs(p):
        base = p * R1
        centre, besides = around(c1, base, 32, R1, 2)
        x = row_ids(32) + (16 * a - 8)
        y = 8 * j + p - 8
        z = lane_ids(32)
        inside = (y != 0, y != 63, x != 0, x != 255, z >= 2, z < 126)
        faces, total, quarter = coefficients(centre, besides, inside)
        out = [(mid, (n,) + at(base, 32), faces[n]) for n in range(6)]
        out.append((w1, at(base, 32), 8.0 * quarter))
        out.append((d1, at(base, 32), 0.3125 * total))
        return out

    loop(3, 21, 3, mid_coeffs)

    for copy in third:
        copy.wait_recv()

    def around2(ref):
        lanes = lane_ids(5 * R2) % 4
        centre = ref[R2 : 6 * R2, :]
        return centre, (
            jnp.where(lanes == 0, turn(ref[0 : 5 * R2, :], -3), turn(centre, 1)),
            jnp.where(lanes == 3, turn(ref[2 * R2 : 7 * R2, :], 3), turn(centre, -1)),
            ref[pl.ds(R2 - 1, 5 * R2), :],
            ref[pl.ds(R2 + 1, 5 * R2), :],
            turn(centre, 4),
            turn(centre, -4),
        )

    rows2, lanes2 = row_ids(5 * R2), lane_ids(5 * R2)
    x = rows2 % R2 + (8 * a - 8)
    y = 4 * (rows2 // R2) + lanes2 % 4 + (4 * j - 8)
    inside2 = (y != 0, y != 31, x != 0, x != 127, lanes2 >= 4, lanes2 < 124)
    centre, besides = around2(c2)
    faces, total, quarter = coefficients(centre, besides, inside2)
    for n in range(6):
        deep[n] = faces[n]
    deep[6] = 32.0 * quarter

    land1(f1, 5, 4, y2b, x2b, k2b, fourth)

    def guess(p):
        base = p * R1
        return [(g1, at(base, 32), w1[pl.ds(base, 32), :] * f1[pl.ds(base, 32), :])]

    loop(3, 21, 9, guess)
    sweep(g1, e1, mid_faces, g1, 4, 20, 8, R1, 4, 24, 2)
    leftover(e1, r1, mid_faces, g1, d1, 8, 16, 8, R1, 8, 16, 2)
    f2[pl.ds(own2, 8), :] = packed(r1)
    sixth = blocks2(f2)
    for copy in sixth:
        copy.wait_recv()

    g2[...] = deep[6] * f2[R2 : 6 * R2, :]
    e2[R2 : 6 * R2, :] = g2[...]
    for src, dst in ((e2, e2b), (e2b, e2), (e2, e2b)):
        centre, besides = around2(src)
        parts = [deep[n] * besides[n] for n in range(6)]
        dst[R2 : 6 * R2, :] = (
            (0.2 * centre + g2[...]) + (parts[0] + parts[1]) + (parts[2] + parts[3]) + (parts[4] + parts[5])
        )

    lanes16 = lane_ids(16) % 4
    hops = ((1, 2), (-1, 2), (1, -2), (-1, -2))
    for number in range(8):
        block, i = (number + 6) // 4, (number + 6) % 4
        value = jnp.where(lanes16 == i, e2b[pl.ds(R2 + R2 * block + 4, 16), :], 0.0)
        value = value + turn(value, hops[i][0])
        value = value + turn(value, hops[i][1])
        pe2[pl.ds(32 * number, 16, stride=2), :] = value
        pe2[pl.ds(32 * number + 1, 16, stride=2), :] = value

    def corrected1(p):
        value = e1[pl.ds(p * R1 + 4, 24), :] + pe2[pl.ds((p // 2 - 2) * 32 + 4, 24), :]
        return [(e1, at(p * R1 + 4, 24), value)]

    loop(4, 20, 8, corrected1)
    sweep(e1, e1b, mid_faces, g1, 5, 19, 7, R1, 4, 24, 2)
    sweep(e1b, e1, mid_faces, g1, 6, 18, 6, R1, 4, 24, 2)

    def grown(i):
        value = e1[pl.ds((i + 6) * R1 + 4, 24), :]
        return [(pe1, (pl.ds(RF * i + odd, 24, stride=2), slice(None)), value) for odd in (0, 1)]

    loop(0, 12, 6, grown)
    for copy in fifth:
        copy.wait_recv()
    for n, dj in enumerate((-1, 1)):
        for d in range(3):
            u2[pl.ds(far_plane(dj, d + 1) * RF + 8, 32), :] = y3b[n, pl.ds(32 * d, 32), :]
    for n, da in enumerate((-1, 1)):
        for d in range(3):
            u2[pl.ds(4 * RF + far_row(da, d + 1), 16, stride=RF), :] = x3b[n, pl.ds(16 * d, 16), :]
    for n, (da, dj) in enumerate(FULL[4:]):
        for k, (ref, dy, dx) in enumerate(corner[:3]):
            u2[pl.ds(far_plane(dj, dy) * RF + far_row(da, dx), 1), :] = k3b[n, pl.ds(k, 1), :]

    def corrected0(p):
        base = p * RF + 4
        return [(u2, at(base, 40), u2[pl.ds(base, 40), :] + pe1[pl.ds((p // 2) * RF + 4, 40), :])]

    loop(1, 23, 2, corrected0)
    sweep(u2, u1, fine_faces, gf, 2, 22, 5, RF, 4, 40, 1)
    sweep(u1, u2, fine_faces, gf, 3, 21, 6, RF, 4, 40, 1)
    leftover(u2, u1, fine_faces, gf, df, 4, 20, 4, RF, 8, 32, 1)

    last = []
    for ref, stage, other in ((u2, stage_f, other_f), (u1, stage_r, other_r)):

        def step(t):
            rows = pl.ds(pl.multiple_of(8 * t, 8), 8)
            out = []
            for q in range(4):
                four = [
                    ref[pl.ds(pl.multiple_of((4 + 4 * q + i) * RF + 8 + 8 * t, 8), 8), :]
                    for i in range(4)
                ]
                for p, value in enumerate(transposed(four)):
                    out.append((stage, (p, rows, slice(128 * q, 128 * q + 128)), value))
            return out

        loop(0, 4, 2, step)
        last.append(send(stage.at[pl.ds(1 - half, 3)], other, sibling))

    own = jnp.where(half == 0, split, 4 - split)
    for number, (stage, other, out) in enumerate(
        ((stage_f, other_f, out_field), (stage_r, other_r, out_resid))
    ):
        for s in range(4):
            p = jnp.clip(s + half * split, 0, 3)
            out[s, :, mine] = jnp.where(s < own, stage[p], 0.0)
        last[number].wait_recv()
        for s in range(4):
            p = jnp.clip(s + half * (split - 1), 0, 2)
            out[s, :, theirs] = jnp.where(s < own, other[p], 0.0)

    for copy in used:
        copy.wait_send()


def vmem(*shape):
    return pltpu.VMEM(shape, F32)


def body(source, conductance, initial, box_counts):
    fine_field = vmem(PF * RF, LANES)
    mid_field = vmem(P1 * R1, LANES)
    deep_field = vmem(7 * R2, LANES)
    scratch = [vmem(6, 32, 512)] * 3
    scratch += [fine_field] * 5 + [vmem(6, PF * RF, LANES)] + [fine_field] * 2
    scratch += [vmem(2, 256, LANES)] * 2 + [vmem(2, 128, LANES)] * 2 + [vmem(4, 8, LANES)] * 2
    scratch += [mid_field] * 4 + [vmem(8 * 32, LANES), vmem(6, P1 * R1, LANES)] + [mid_field] * 4
    scratch += [vmem(2, 96, LANES)] * 2 + [vmem(2, 48, LANES)] * 2 + [vmem(4, 40, LANES)] * 2
    scratch += [vmem(2, 80, LANES)] * 2 + [vmem(2, 40, LANES)] * 2 + [vmem(4, 16, LANES)] * 2
    scratch += [vmem(2, 96, LANES)] * 2 + [vmem(2, 48, LANES)] * 2 + [vmem(4, 8, LANES)] * 2
    scratch += [deep_field] * 4 + [vmem(7, 5 * R2, LANES), vmem(5 * R2, LANES)]
    scratch += [vmem(12 * RF, LANES)] + [vmem(4, 32, 512)] * 2 + [vmem(3, 32, 512)] * 2
    messages = 3 + 8 + 8 + 14 + 8 + 8 + 14 + 2
    scratch += [pltpu.SemaphoreType.DMA((3,))] + [pltpu.SemaphoreType.DMA((messages,))] * 2
    shape = jax.ShapeDtypeStruct(source.shape, source.dtype)
    return pl.pallas_call(
        kernel,
        out_shape=(shape, shape),
        in_specs=[pl.BlockSpec(memory_space=pltpu.SMEM)] + [pl.BlockSpec(memory_space=pl.ANY)] * 3,
        out_specs=(pl.BlockSpec(memory_space=pltpu.VMEM),) * 2,
        scratch_shapes=scratch,
        compiler_params=pltpu.CompilerParams(
            collective_id=0, has_side_effects=True, vmem_limit_bytes=60 * 2**20
        ),
        cost_estimate=pl.CostEstimate(flops=3 * 10**7, bytes_accessed=3 * 10**6, transcendentals=0),
    )(box_counts, source, conductance, initial)


def solution(mesh):
    return jax.shard_map(
        body,
        mesh=mesh,
        in_specs=(P("box", None, None), P("box", None, None), P("box", None, None), P()),
        out_specs=(P("box", None, None), P("box", None, None)),
        check_vma=False,
    )
```

```python
import functools

import jax
import jax.numpy as jnp
from jax import lax
from jax.experimental import pallas as pl
from jax.experimental.pallas import tpu as pltpu
from jax.sharding import PartitionSpec as P


RF, PF = 48, 24
R1, P1 = 32, 24
R2 = 24
LANES = 128
FULL = (1, 0), (-1, 0), (0, 1), (0, -1), (1, 1), (1, -1), (-1, 1), (-1, -1)
FAR = (0, 2), (0, -2), (1, 2), (1, -2), (-1, 2), (-1, -2)
F32 = jnp.float32


def lane_ids(rows):
    return lax.broadcasted_iota(jnp.int32, (rows, LANES), 1)


def row_ids(rows):
    return lax.broadcasted_iota(jnp.int32, (rows, LANES), 0)


def turn(value, steps):
    return pltpu.roll(value, steps % LANES, 1)


def transposed(four):
    lanes = lane_ids(four[0].shape[0])
    low = lanes < 64
    even = (lanes // 32) % 2 == 0
    a, b, c, d = four
    e = jnp.where(low, a, turn(c, 64))
    f = jnp.where(low, b, turn(d, 64))
    g = jnp.where(low, turn(a, 64), c)
    h = jnp.where(low, turn(b, 64), d)
    return (
        jnp.where(even, e, turn(f, 32)),
        jnp.where(even, turn(e, -32), f),
        jnp.where(even, g, turn(h, 32)),
        jnp.where(even, turn(g, -32), h),
    )


def coefficients(c, besides, inside):
    total = 3.0 * c
    for beside, within in zip(besides, inside):
        total = total + 0.5 * jnp.where(within, beside, c)
    quarter = 0.4 / total
    faces = [
        jnp.where(within, (c + beside) * quarter, 0.0) for beside, within in zip(besides, inside)
    ]
    return faces, total, quarter


def around(ref, base, count, rows, twist):
    centre = ref[pl.ds(base, count), :]
    return centre, (
        ref[pl.ds(base - rows, count), :],
        ref[pl.ds(base + rows, count), :],
        ref[pl.ds(base - 1, count), :],
        ref[pl.ds(base + 1, count), :],
        turn(centre, twist),
        turn(centre, -twist),
    )


def weighted(faces, base, count, besides):
    parts = [faces[n][pl.ds(base, count), :] * besides[n] for n in range(6)]
    return (parts[0] + parts[1]) + (parts[2] + parts[3]) + (parts[4] + parts[5])


def loop(low, high, width, body):
    assert (high - low) % width == 0

    def step(index, carry):
        first = low + index * width
        stores = [item for m in range(width) for item in body(first + m)]
        for ref, at, value in stores:
            ref[at] = value
        return carry

    if high - low == width:
        step(0, 0)
    else:
        lax.fori_loop(0, (high - low) // width, step, 0)


def at(base, count):
    return pl.ds(base, count), slice(None)


def pair_rows(ref, base, count, rows):
    got = [
        ref[pl.ds(base + offset, count, stride=2), :] for offset in (0, 1, rows, rows + 1)
    ]
    return (got[0] + got[1]) + (got[2] + got[3])


def pair_lanes(value, width):
    first = (lane_ids(value.shape[0]) // width) % 2 == 0
    return 0.125 * (value + jnp.where(first, turn(value, -width), turn(value, width)))


def kernel(
    counts, source, conductance, initial, out_field, out_resid,
    owners, raw_c, raw_u, raw_s, cf, uf, sf, u1, u2, fine, gf, df,
    c1, f1, e1, e1b, pe2, mid, w1, g1, d1, r1, c2, f2, e2, e2b, deep, g2, pe1,
    stage_f, stage_r, other_f, other_r, *rest,
):
    post, local_sem, send_sem, recv_sem = rest[:-3], rest[-3], rest[-2], rest[-1]
    me = lax.axis_index("box")
    a, j = me // 8, me % 8
    half = me % 2
    sibling = me + 1 - 2 * half
    across = {da: ((a + da + 16) % 16) * 8 for da in (-1, 0, 1)}
    along = {dj: (j + dj + 8) % 8 for dj in (-2, -1, 0, 1, 2)}

    def device(da, dj):
        return across[da] + along[dj]

    used = []

    def send(src, dst, target):
        number = len(used)
        copy = pltpu.make_async_remote_copy(
            src_ref=src, dst_ref=dst, send_sem=send_sem.at[number], recv_sem=recv_sem.at[number],
            device_id=(target,), device_id_type=pl.DeviceIdType.MESH,
        )
        copy.start()
        used.append(copy)
        return copy

    raws = (raw_c, raw_u, raw_s)
    given = (conductance, initial, source)
    mine = pl.ds(pl.multiple_of(512 * half, 512), 512)
    theirs = pl.ds(pl.multiple_of(512 - 512 * half, 512), 512)
    held = pl.ds(3 * half, 3)
    locals_ = [pltpu.make_async_copy(counts, owners, local_sem.at[3])]
    for number in range(3):
        locals_.append(
            pltpu.make_async_copy(
                given[number].at[pl.ds(0, 3), :, mine], raws[number].at[held], local_sem.at[number]
            )
        )
    for copy in locals_:
        copy.start()

    barrier = pltpu.get_barrier_semaphore()
    for da, dj in FULL + FAR:
        pl.semaphore_signal(
            barrier, inc=1, device_id=(device(da, dj),), device_id_type=pl.DeviceIdType.MESH
        )
    pl.semaphore_wait(barrier, len(FULL + FAR))

    swaps = [
        send(given[number].at[pl.ds(0, 3), :, theirs], raws[number].at[held], sibling)
        for number in range(3)
    ]
    locals_[0].wait()
    split = owners[me - half]
    places = [jnp.where(p < split, p, jnp.clip(3 + p - split, 0, 5)) for p in range(4)]

    def bring(number, ref):
        locals_[1 + number].wait()
        swaps[number].wait_recv()
        raw = raws[number]

        def step(t):
            rows = pl.ds(pl.multiple_of(8 * t, 8), 8)
            out = []
            for q in range(4):
                four = [raw[places[p], rows, 128 * q : 128 * q + 128] for p in range(4)]
                for i, value in enumerate(transposed(four)):
                    out.append((ref, at(pl.multiple_of((4 + 4 * q + i) * RF + 8 + 8 * t, 8), 8), value))
            return out

        loop(0, 4, 2, step)

    ROWS = (RF, R1)
    OWN = ((4, 16, 8, 32), (8, 8, 8, 16))

    def near(first, count, side, depth):
        return first - 1 + depth if side < 0 else first + count - depth

    def far(first, count, side, depth):
        return first + count - 1 + depth if side < 0 else first - depth

    def pieces(strips, corners, da, dj, pick):
        out = []
        if da == 0:
            for ref, level, depths in strips:
                plane, planes, row, rows = OWN[level]
                for d in depths:
                    out.append((ref, pick(plane, planes, dj, d) * ROWS[level] + row, rows, 1))
        elif dj == 0:
            for ref, level, depths in strips:
                plane, planes, row, rows = OWN[level]
                for d in depths:
                    out.append(
                        (ref, plane * ROWS[level] + pick(row, rows, da, d), planes, ROWS[level])
                    )
        else:
            for ref, level, depth, low, count in corners:
                plane, planes, row, rows = OWN[level]
                ends = [pick(row, rows, da, d) for d in (low, low + count - 1)]
                out.append((ref, pick(plane, planes, dj, depth) * ROWS[level] + min(ends), count, 1))
        return out

    def slab(ref, first, count, stride):
        return (pl.ds(first, count, stride=stride) if stride > 1 else pl.ds(first, count)), slice(None)

    spare = list(post)

    def exchange(strips, corners):
        boxes = [(spare.pop(0), spare.pop(0)) for _ in range(3)]
        started = []
        for number, (da, dj) in enumerate(FULL):
            kind = 2 if da and dj else 1 if da else 0
            slot = number % 2 if number < 4 else number - 4
            out, got = boxes[kind]
            offset = 0
            for ref, first, count, stride in pieces(strips, corners, da, dj, near):
                out[slot, pl.ds(offset, count), :] = ref[slab(ref, first, count, stride)]
                offset += count
            started.append((send(out.at[slot], got.at[slot], device(da, dj)), got, slot, da, dj))

        def land():
            for copy, got, slot, da, dj in started:
                copy.wait_recv()
                offset = 0
                for ref, first, count, stride in pieces(strips, corners, da, dj, far):
                    ref[slab(ref, first, count, stride)] = got[slot, pl.ds(offset, count), :]
                    offset += count

        return land

    def fine_corner(ref, depth):
        return [(ref, 0, d, 1, depth - d) for d in range(1, depth)]

    bring(0, cf)
    land_c = exchange(((cf, 0, (1, 2, 3)),), fine_corner(cf, 3))

    def coarse_c(i):
        total = pair_rows(cf, (4 + 2 * i) * RF + 8, 16, RF)
        return [(c1, at(pl.multiple_of((8 + i) * R1 + 8, 8), 16), pair_lanes(total, 1))]

    loop(0, 8, 8, coarse_c)

    def packed(ref):
        lanes = lane_ids(8) % 4
        total = jnp.zeros((8, LANES), F32)
        for i in range(4):
            value = pair_lanes(pair_rows(ref, (8 + 2 * i) * R1 + 8, 8, R1), 2)
            total = total + jnp.where(lanes == i, value, 0.0)
        return total

    own2 = R2 + 2 * R2 + 8

    def blocks2(ref):
        sent = []
        for da, dj in FAR + FULL:
            row = R2 + R2 * (2 - dj) + 8 * (1 - da)
            sent.append(send(ref.at[pl.ds(own2, 8)], ref.at[pl.ds(row, 8)], device(da, dj)))
        return sent

    bring(1, uf)
    bring(2, sf)
    land_u = exchange(
        ((uf, 0, (1, 2, 3)), (sf, 0, (1, 2))), fine_corner(uf, 3) + fine_corner(sf, 2)
    )
    c2[pl.ds(own2, 8), :] = packed(c1)
    land_c1 = exchange(((c1, 1, (1, 2, 3, 4, 5, 6)),), [(c1, 1, d, 1, 6 - d) for d in range(1, 6)])
    third = blocks2(c2)

    land_c()
    fine_faces = [fine.at[n] for n in range(6)]

    def fine_coeffs(p):
        base = p * RF + 4
        centre, besides = around(cf, base, 40, RF, 1)
        x = row_ids(40) + (32 * a - 4)
        y = 16 * j + p - 4
        z = lane_ids(40)
        inside = (y != 0, y != 127, x != 0, x != 511, z != 0, z != 127)
        faces, total, quarter = coefficients(centre, besides, inside)
        out = [(fine, (n,) + at(base, 40), faces[n]) for n in range(6)]
        out.append((gf, at(base, 40), 2.0 * quarter))
        out.append((df, at(base, 40), 1.25 * total))
        return out

    loop(2, 22, 2, fine_coeffs)
    land_u()

    def fine_right(p):
        base = p * RF + 4
        return [(gf, at(base, 40), gf[pl.ds(base, 40), :] * sf[pl.ds(base, 40), :])]

    loop(2, 22, 4, fine_right)

    def sweep(src, dst, faces, right, low, high, width, rows, start, count, twist):
        def step(p):
            base = p * rows + start
            centre, besides = around(src, base, count, rows, twist)
            value = 0.2 * centre + right[pl.ds(base, count), :] + weighted(faces, base, count, besides)
            return [(dst, at(base, count), value)]

        loop(low, high, width, step)

    def leftover(src, dst, faces, right, diag, low, high, width, rows, start, count, twist):
        def step(p):
            base = p * rows + start
            centre, besides = around(src, base, count, rows, twist)
            value = diag[pl.ds(base, count), :] * (
                right[pl.ds(base, count), :] + weighted(faces, base, count, besides) - 0.8 * centre
            )
            return [(dst, at(base, count), value)]

        loop(low, high, width, step)

    sweep(uf, u1, fine_faces, gf, 2, 22, 5, RF, 4, 40, 1)
    sweep(u1, u2, fine_faces, gf, 3, 21, 6, RF, 4, 40, 1)
    leftover(u2, u1, fine_faces, gf, df, 4, 20, 4, RF, 8, 32, 1)

    def coarse_f(i):
        total = pair_rows(u1, (4 + 2 * i) * RF + 8, 16, RF)
        return [(f1, at(pl.multiple_of((8 + i) * R1 + 8, 8), 16), pair_lanes(total, 1))]

    loop(0, 8, 8, coarse_f)
    land_f = exchange(((f1, 1, (1, 2)),), [(f1, 1, 1, 1, 1)])
    land_rest = exchange(
        ((f1, 1, (3, 4, 5)), (u2, 0, (1, 2, 3))),
        [(f1, 1, 1, 2, 3), (f1, 1, 2, 1, 3), (f1, 1, 3, 1, 2), (f1, 1, 4, 1, 1)] + fine_corner(u2, 3),
    )

    land_c1()
    mid_faces = [mid.at[n] for n in range(6)]

    def mid_coeffs(p):
        base = p * R1
        centre, besides = around(c1, base, 32, R1, 2)
        x = row_ids(32) + (16 * a - 8)
        y = 8 * j + p - 8
        z = lane_ids(32)
        inside = (y != 0, y != 63, x != 0, x != 255, z >= 2, z < 126)
        faces, total, quarter = coefficients(centre, besides, inside)
        out = [(mid, (n,) + at(base, 32), faces[n]) for n in range(6)]
        out.append((w1, at(base, 32), 8.0 * quarter))
        out.append((d1, at(base, 32), 0.3125 * total))
        return out

    loop(3, 21, 3, mid_coeffs)

    for copy in third:
        copy.wait_recv()

    def around2(ref):
        lanes = lane_ids(5 * R2) % 4
        centre = ref[R2 : 6 * R2, :]
        return centre, (
            jnp.where(lanes == 0, turn(ref[0 : 5 * R2, :], -3), turn(centre, 1)),
            jnp.where(lanes == 3, turn(ref[2 * R2 : 7 * R2, :], 3), turn(centre, -1)),
            ref[pl.ds(R2 - 1, 5 * R2), :],
            ref[pl.ds(R2 + 1, 5 * R2), :],
            turn(centre, 4),
            turn(centre, -4),
        )

    rows2, lanes2 = row_ids(5 * R2), lane_ids(5 * R2)
    x = rows2 % R2 + (8 * a - 8)
    y = 4 * (rows2 // R2) + lanes2 % 4 + (4 * j - 8)
    inside2 = (y != 0, y != 31, x != 0, x != 127, lanes2 >= 4, lanes2 < 124)
    centre, besides = around2(c2)
    faces, total, quarter = coefficients(centre, besides, inside2)
    for n in range(6):
        deep[n] = faces[n]
    deep[6] = 32.0 * quarter

    def guess(p):
        base = p * R1
        return [(g1, at(base, 32), w1[pl.ds(base, 32), :] * f1[pl.ds(base, 32), :])]

    land_f()
    loop(6, 18, 12, guess)
    sweep(g1, e1, mid_faces, g1, 7, 17, 10, R1, 4, 24, 2)
    leftover(e1, r1, mid_faces, g1, d1, 8, 16, 8, R1, 8, 16, 2)
    f2[pl.ds(own2, 8), :] = packed(r1)
    sixth = blocks2(f2)

    land_rest()
    loop(3, 21, 9, guess)
    sweep(g1, e1, mid_faces, g1, 4, 20, 8, R1, 4, 24, 2)

    for copy in sixth:
        copy.wait_recv()
    g2[...] = deep[6] * f2[R2 : 6 * R2, :]
    e2[R2 : 6 * R2, :] = g2[...]
    for src, dst in ((e2, e2b), (e2b, e2), (e2, e2b)):
        centre, besides = around2(src)
        parts = [deep[n] * besides[n] for n in range(6)]
        dst[R2 : 6 * R2, :] = (
            (0.2 * centre + g2[...]) + (parts[0] + parts[1]) + (parts[2] + parts[3]) + (parts[4] + parts[5])
        )

    lanes16 = lane_ids(16) % 4
    hops = ((1, 2), (-1, 2), (1, -2), (-1, -2))
    for number in range(8):
        block, i = (number + 6) // 4, (number + 6) % 4
        value = jnp.where(lanes16 == i, e2b[pl.ds(R2 + R2 * block + 4, 16), :], 0.0)
        value = value + turn(value, hops[i][0])
        value = value + turn(value, hops[i][1])
        pe2[pl.ds(32 * number, 16, stride=2), :] = value
        pe2[pl.ds(32 * number + 1, 16, stride=2), :] = value

    def corrected1(p):
        value = e1[pl.ds(p * R1 + 4, 24), :] + pe2[pl.ds((p // 2 - 2) * 32 + 4, 24), :]
        return [(e1, at(p * R1 + 4, 24), value)]

    loop(4, 20, 8, corrected1)
    sweep(e1, e1b, mid_faces, g1, 5, 19, 7, R1, 4, 24, 2)
    sweep(e1b, e1, mid_faces, g1, 6, 18, 6, R1, 4, 24, 2)

    def grown(i):
        value = e1[pl.ds((i + 6) * R1 + 4, 24), :]
        return [(pe1, (pl.ds(RF * i + odd, 24, stride=2), slice(None)), value) for odd in (0, 1)]

    loop(0, 12, 6, grown)

    def corrected0(p):
        base = p * RF + 4
        return [(u2, at(base, 40), u2[pl.ds(base, 40), :] + pe1[pl.ds((p // 2) * RF + 4, 40), :])]

    loop(1, 23, 2, corrected0)
    sweep(u2, u1, fine_faces, gf, 2, 22, 5, RF, 4, 40, 1)
    sweep(u1, u2, fine_faces, gf, 3, 21, 6, RF, 4, 40, 1)

    def give(ref, stage, other):
        def step(t):
            rows = pl.ds(pl.multiple_of(8 * t, 8), 8)
            out = []
            for q in range(4):
                four = [
                    ref[pl.ds(pl.multiple_of((4 + 4 * q + i) * RF + 8 + 8 * t, 8), 8), :]
                    for i in range(4)
                ]
                for p, value in enumerate(transposed(four)):
                    out.append((stage, (p, rows, slice(128 * q, 128 * q + 128)), value))
            return out

        loop(0, 4, 2, step)
        return send(stage.at[pl.ds(1 - half, 3)], other, sibling)

    own = jnp.where(half == 0, split, 4 - split)

    def keep(stage, out):
        for s in range(4):
            out[s, :, mine] = jnp.where(s < own, stage[jnp.clip(s + half * split, 0, 3)], 0.0)

    def take(copy, other, out):
        copy.wait_recv()
        for s in range(4):
            out[s, :, theirs] = jnp.where(s < own, other[jnp.clip(s + half * (split - 1), 0, 2)], 0.0)

    last_f = give(u2, stage_f, other_f)
    leftover(u2, u1, fine_faces, gf, df, 4, 20, 4, RF, 8, 32, 1)
    last_r = give(u1, stage_r, other_r)
    keep(stage_f, out_field)
    take(last_f, other_f, out_field)
    keep(stage_r, out_resid)
    take(last_r, other_r, out_resid)
    for copy in used:
        copy.wait_send()


def vmem(*shape):
    return pltpu.VMEM(shape, F32)


def body(source, conductance, initial, box_counts):
    fine_field = vmem(PF * RF, LANES)
    mid_field = vmem(P1 * R1, LANES)
    deep_field = vmem(7 * R2, LANES)
    scratch = [pltpu.SMEM(box_counts.shape, jnp.int32)] + [vmem(6, 32, 512)] * 3
    scratch += [fine_field] * 5 + [vmem(6, PF * RF, LANES)] + [fine_field] * 2
    scratch += [mid_field] * 4 + [vmem(8 * 32, LANES), vmem(6, P1 * R1, LANES)] + [mid_field] * 4
    scratch += [deep_field] * 4 + [vmem(7, 5 * R2, LANES), vmem(5 * R2, LANES), vmem(12 * RF, LANES)]
    scratch += [vmem(4, 32, 512)] * 2 + [vmem(3, 32, 512)] * 2
    for big, middle, small in ((96, 48, 8), (160, 80, 8), (96, 48, 16), (32, 16, 8), (144, 72, 16)):
        for count, rows in ((2, big), (2, middle), (4, small)):
            scratch += [vmem(count, rows, LANES)] * 2
    messages = 3 + 5 * 8 + 2 * 14 + 2
    scratch += [pltpu.SemaphoreType.DMA((4,))] + [pltpu.SemaphoreType.DMA((messages,))] * 2
    hbm = pl.BlockSpec(memory_space=pltpu.HBM)
    shape = jax.ShapeDtypeStruct(source.shape, source.dtype)
    return pl.pallas_call(
        kernel,
        out_shape=(shape, shape),
        in_specs=[hbm] * 4,
        out_specs=(pl.BlockSpec(memory_space=pltpu.VMEM),) * 2,
        scratch_shapes=scratch,
        compiler_params=pltpu.CompilerParams(
            collective_id=0, has_side_effects=True, vmem_limit_bytes=40 * 2**20
        ),
        cost_estimate=pl.CostEstimate(flops=3 * 10**7, bytes_accessed=3 * 10**6, transcendentals=0),
    )(*[pltpu.with_memory_space_constraint(x, pltpu.HBM) for x in (box_counts, source, conductance, initial)])


def solution(mesh):
    return jax.shard_map(
        body,
        mesh=mesh,
        in_specs=(P("box", None, None), P("box", None, None), P("box", None, None), P()),
        out_specs=(P("box", None, None), P("box", None, None)),
        check_vma=False,
    )
```

```python
import functools

import jax
import jax.numpy as jnp
from jax import lax
from jax.experimental import pallas as pl
from jax.experimental.pallas import tpu as pltpu
from jax.sharding import PartitionSpec as P


RF, PF = 48, 24
R1, P1 = 32, 24
R2 = 24
LANES = 128
FULL = (1, 0), (-1, 0), (0, 1), (0, -1), (1, 1), (1, -1), (-1, 1), (-1, -1)
FAR = (0, 2), (0, -2), (1, 2), (1, -2), (-1, 2), (-1, -2)
F32 = jnp.float32


def lane_ids(rows):
    return lax.broadcasted_iota(jnp.int32, (rows, LANES), 1)


def row_ids(rows):
    return lax.broadcasted_iota(jnp.int32, (rows, LANES), 0)


def turn(value, steps):
    return pltpu.roll(value, steps % LANES, 1)


def transposed(four):
    lanes = lane_ids(four[0].shape[0])
    low = lanes < 64
    even = (lanes // 32) % 2 == 0
    a, b, c, d = four
    e = jnp.where(low, a, turn(c, 64))
    f = jnp.where(low, b, turn(d, 64))
    g = jnp.where(low, turn(a, 64), c)
    h = jnp.where(low, turn(b, 64), d)
    return (
        jnp.where(even, e, turn(f, 32)),
        jnp.where(even, turn(e, -32), f),
        jnp.where(even, g, turn(h, 32)),
        jnp.where(even, turn(g, -32), h),
    )


def coefficients(c, besides, inside):
    around_ = [
        beside if within is None else jnp.where(within, beside, c)
        for beside, within in zip(besides, inside)
    ]
    total = 3.0 * c + 0.5 * (
        (around_[0] + around_[1]) + (around_[2] + around_[3]) + (around_[4] + around_[5])
    )
    quarter = 0.4 / total
    faces = [
        (c + beside) * quarter if within is None else jnp.where(within, (c + beside) * quarter, 0.0)
        for beside, within in zip(besides, inside)
    ]
    return faces, total, quarter


def around(ref, base, count, rows, twist):
    centre = ref[pl.ds(base, count), :]
    return centre, (
        ref[pl.ds(base - rows, count), :],
        ref[pl.ds(base + rows, count), :],
        ref[pl.ds(base - 1, count), :],
        ref[pl.ds(base + 1, count), :],
        turn(centre, twist),
        turn(centre, -twist),
    )


def weighted(faces, base, count, besides):
    parts = [faces[n][pl.ds(base, count), :] * besides[n] for n in range(6)]
    return (parts[0] + parts[1]) + (parts[2] + parts[3]) + (parts[4] + parts[5])


def loop(low, high, width, body, late=True):
    assert (high - low) % width == 0

    def step(index, carry):
        first = low + index * width
        stores = []
        for m in range(width):
            stores += body(first + m)
            if not late or m == width - 1:
                for ref, index_, value in stores:
                    ref[index_] = value
                stores = []
        return carry

    if high - low == width:
        step(0, 0)
    else:
        lax.fori_loop(0, (high - low) // width, step, 0)


def at(base, count):
    return pl.ds(base, count), slice(None)


def pair_rows(ref, base, count, rows):
    got = [
        ref[pl.ds(base + offset, count, stride=2), :] for offset in (0, 1, rows, rows + 1)
    ]
    return (got[0] + got[1]) + (got[2] + got[3])


def pair_lanes(value, width):
    first = (lane_ids(value.shape[0]) // width) % 2 == 0
    return 0.125 * (value + jnp.where(first, turn(value, -width), turn(value, width)))


def kernel(
    counts, source, conductance, initial, out_field, out_resid,
    owners, raw_c, raw_u, raw_s, cf, uf, sf, u1, u2, fine, gf, df,
    c1, f1, e1, e1b, pe2, mid, w1, g1, d1, r1, c2, f2, e2, e2b, deep, g2, pe1,
    stage_f, stage_r, other_f, other_r, *rest,
):
    post, local_sem, send_sem, recv_sem = rest[:-3], rest[-3], rest[-2], rest[-1]
    me = lax.axis_index("box")
    a, j = me // 8, me % 8
    half = me % 2
    sibling = me + 1 - 2 * half
    across = {da: ((a + da + 16) % 16) * 8 for da in (-1, 0, 1)}
    along = {dj: (j + dj + 8) % 8 for dj in (-2, -1, 0, 1, 2)}

    def device(da, dj):
        return across[da] + along[dj]

    used = []

    def send(src, dst, target):
        number = len(used)
        copy = pltpu.make_async_remote_copy(
            src_ref=src, dst_ref=dst, send_sem=send_sem.at[number], recv_sem=recv_sem.at[number],
            device_id=(target,), device_id_type=pl.DeviceIdType.MESH,
        )
        copy.start()
        used.append(copy)
        return copy

    sent_upto = [0]

    def drain():
        for copy in used[sent_upto[0] :]:
            copy.wait_send()
        sent_upto[0] = len(used)

    raws = (raw_c, raw_u, raw_s)
    given = (conductance, initial, source)
    mine = pl.ds(pl.multiple_of(512 * half, 512), 512)
    theirs = pl.ds(pl.multiple_of(512 - 512 * half, 512), 512)
    held = pl.ds(3 * half, 3)
    locals_ = [pltpu.make_async_copy(counts, owners, local_sem.at[3])]
    for number in range(3):
        locals_.append(
            pltpu.make_async_copy(
                given[number].at[pl.ds(0, 3), :, mine], raws[number].at[held], local_sem.at[number]
            )
        )
    for copy in locals_:
        copy.start()

    barrier = pltpu.get_barrier_semaphore()
    for da, dj in FULL + FAR:
        pl.semaphore_signal(
            barrier, inc=1, device_id=(device(da, dj),), device_id_type=pl.DeviceIdType.MESH
        )
    pl.semaphore_wait(barrier, len(FULL + FAR))

    swaps = [
        send(given[number].at[pl.ds(0, 3), :, theirs], raws[number].at[held], sibling)
        for number in range(3)
    ]
    locals_[0].wait()
    split = owners[me - half]
    places = [jnp.where(p < split, p, jnp.clip(3 + p - split, 0, 5)) for p in range(4)]

    def bring(number, ref):
        locals_[1 + number].wait()
        swaps[number].wait_recv()
        raw = raws[number]

        def step(t):
            rows = pl.ds(pl.multiple_of(8 * t, 8), 8)
            out = []
            for q in range(4):
                four = [raw[places[p], rows, 128 * q : 128 * q + 128] for p in range(4)]
                for i, value in enumerate(transposed(four)):
                    out.append((ref, at(pl.multiple_of((4 + 4 * q + i) * RF + 8 + 8 * t, 8), 8), value))
            return out

        loop(0, 4, 2, step)

    ROWS = (RF, R1)
    OWN = ((4, 16, 8, 32), (8, 8, 8, 16))

    def near(first, count, side, depth):
        return first - 1 + depth if side < 0 else first + count - depth

    def far(first, count, side, depth):
        return first + count - 1 + depth if side < 0 else first - depth

    own2 = R2 + 2 * R2 + 8

    def there2(da, dj):
        return R2 + R2 * (2 - dj) + 8 * (1 - da)

    def pieces(strips, corners, block, da, dj, pick):
        out = []
        if block is not None:
            out.append((block, own2 if pick is near else there2(da, dj), 8, 1))
        if da == 0:
            for ref, level, depths in strips:
                plane, planes, row, rows = OWN[level]
                for d in depths:
                    out.append((ref, pick(plane, planes, dj, d) * ROWS[level] + row, rows, 1))
        elif dj == 0:
            for ref, level, depths in strips:
                plane, planes, row, rows = OWN[level]
                for d in depths:
                    out.append(
                        (ref, plane * ROWS[level] + pick(row, rows, da, d), planes, ROWS[level])
                    )
        else:
            for ref, level, depth, low, count in corners:
                plane, planes, row, rows = OWN[level]
                ends = [pick(row, rows, da, d) for d in (low, low + count - 1)]
                out.append((ref, pick(plane, planes, dj, depth) * ROWS[level] + min(ends), count, 1))
        return out

    def slab(ref, first, count, stride):
        return (pl.ds(first, count, stride=stride) if stride > 1 else pl.ds(first, count)), slice(None)

    spare = list(post)

    def exchange(strips, corners, block=None):
        boxes = [(spare.pop(0), spare.pop(0)) for _ in range(3)]
        started = []
        for number, (da, dj) in enumerate(FULL):
            kind = 2 if da and dj else 1 if da else 0
            slot = number % 2 if number < 4 else number - 4
            out, got = boxes[kind]
            offset = 0
            for ref, first, count, stride in pieces(strips, corners, block, da, dj, near):
                out[slot, pl.ds(offset, count), :] = ref[slab(ref, first, count, stride)]
                offset += count
            started.append((send(out.at[slot], got.at[slot], device(da, dj)), got, slot, da, dj))

        def land():
            for copy, got, slot, da, dj in started:
                copy.wait_recv()
                offset = 0
                for ref, first, count, stride in pieces(strips, corners, block, da, dj, far):
                    ref[slab(ref, first, count, stride)] = got[slot, pl.ds(offset, count), :]
                    offset += count

        return land

    def fine_corner(ref, depth):
        return [(ref, 0, d, 1, depth - d) for d in range(1, depth)]

    bring(0, cf)
    land_c = exchange(((cf, 0, (1, 2, 3)),), fine_corner(cf, 3))

    bring(1, uf)
    bring(2, sf)
    land_u = exchange(
        ((uf, 0, (1, 2, 3)), (sf, 0, (1, 2))), fine_corner(uf, 3) + fine_corner(sf, 2)
    )

    def coarse_c(i):
        total = pair_rows(cf, (4 + 2 * i) * RF + 8, 16, RF)
        return [(c1, at(pl.multiple_of((8 + i) * R1 + 8, 8), 16), pair_lanes(total, 1))]

    loop(0, 8, 8, coarse_c)

    def packed(ref):
        lanes = lane_ids(8) % 4
        total = jnp.zeros((8, LANES), F32)
        for i in range(4):
            value = pair_lanes(pair_rows(ref, (8 + 2 * i) * R1 + 8, 8, R1), 2)
            total = total + jnp.where(lanes == i, value, 0.0)
        return total

    def blocks2(ref, where):
        return [
            send(ref.at[pl.ds(own2, 8)], ref.at[pl.ds(there2(da, dj), 8)], device(da, dj))
            for da, dj in where
        ]

    c2[pl.ds(own2, 8), :] = packed(c1)
    land_c1 = exchange(
        ((c1, 1, (1, 2, 3, 4, 5, 6)),), [(c1, 1, d, 1, 6 - d) for d in range(1, 6)], c2
    )
    third = blocks2(c2, FAR)

    land_c()

    def edges(ref, first, side, count, rows, plane, row, low_y, high_y, low_x, high_x):
        for outside, there, here in (
            (low_y, plane - 1, plane), (high_y, plane + count, plane + count - 1)
        ):
            slab_there = at(there * rows + first, side)
            ref[slab_there] = jnp.where(outside, ref[at(here * rows + first, side)], ref[slab_there])
        lines = 24
        for outside, there, here in ((low_x, row[0] - 1, row[0]), (high_x, row[1] + 1, row[1])):
            slab_there = slab(ref, there, lines, rows)
            ref[slab_there] = jnp.where(outside, ref[slab(ref, here, lines, rows)], ref[slab_there])

    def cut(faces, first, side, count, rows, plane, row, low_y, high_y, low_x, high_x):
        for n, outside, here in ((0, low_y, plane), (1, high_y, plane + count - 1)):
            where = (n,) + at(here * rows + first, side)
            faces[where] = jnp.where(outside, 0.0, faces[where])
        for n, outside, here in ((2, low_x, row[0]), (3, high_x, row[1])):
            where = (n,) + slab(faces, here, 24, rows)
            faces[where] = jnp.where(outside, 0.0, faces[where])

    ends = (j == 0, j == 7, a == 0, a == 15)
    edges(cf, 4, 40, 16, RF, 4, (8, 39), *ends)
    fine_faces = [fine.at[n] for n in range(6)]

    def fine_coeffs(p):
        base = p * RF + 4
        centre, besides = around(cf, base, 40, RF, 1)
        z = lane_ids(40)
        inside = (None, None, None, None, z != 0, z != 127)
        faces, total, quarter = coefficients(centre, besides, inside)
        out = [(fine, (n,) + at(base, 40), faces[n]) for n in range(6)]
        out.append((gf, at(base, 40), 2.0 * quarter))
        out.append((df, at(base, 40), 1.25 * total))
        return out

    loop(2, 22, 2, fine_coeffs, late=False)
    cut(fine, 4, 40, 16, RF, 4, (8, 39), *ends)
    land_u()

    def sweep(src, dst, faces, right, low, high, width, rows, start, count, twist):
        def step(p):
            base = p * rows + start
            centre, besides = around(src, base, count, rows, twist)
            value = 0.2 * centre + right[pl.ds(base, count), :] + weighted(faces, base, count, besides)
            return [(dst, at(base, count), value)]

        loop(low, high, width, step)

    def leftover(src, dst, faces, right, diag, low, high, width, rows, start, count, twist):
        def step(p):
            base = p * rows + start
            centre, besides = around(src, base, count, rows, twist)
            value = diag[pl.ds(base, count), :] * (
                right[pl.ds(base, count), :] + weighted(faces, base, count, besides) - 0.8 * centre
            )
            return [(dst, at(base, count), value)]

        loop(low, high, width, step)

    def first_sweep(p):
        base = p * RF + 4
        centre, besides = around(uf, base, 40, RF, 1)
        right = gf[pl.ds(base, 40), :] * sf[pl.ds(base, 40), :]
        value = 0.2 * centre + right + weighted(fine_faces, base, 40, besides)
        return [(u1, at(base, 40), value), (gf, at(base, 40), right)]

    loop(2, 22, 4, first_sweep)
    sweep(u1, u2, fine_faces, gf, 3, 21, 6, RF, 4, 40, 1)
    leftover(u2, u1, fine_faces, gf, df, 4, 20, 4, RF, 8, 32, 1)

    def coarse_f(i):
        total = pair_rows(u1, (4 + 2 * i) * RF + 8, 16, RF)
        return [(f1, at(pl.multiple_of((8 + i) * R1 + 8, 8), 16), pair_lanes(total, 1))]

    loop(0, 8, 8, coarse_f)
    land_f = exchange(((f1, 1, (1, 2)),), [(f1, 1, 1, 1, 1)])
    land_rest = exchange(
        ((f1, 1, (3, 4, 5)), (u2, 0, (1, 2, 3))),
        [(f1, 1, 1, 2, 3), (f1, 1, 2, 1, 3), (f1, 1, 3, 1, 2), (f1, 1, 4, 1, 1)] + fine_corner(u2, 3),
    )

    drain()
    land_c1()
    edges(c1, 0, 32, 8, R1, 8, (8, 23), *ends)
    mid_faces = [mid.at[n] for n in range(6)]

    def mid_coeffs(p):
        base = p * R1
        centre, besides = around(c1, base, 32, R1, 2)
        z = lane_ids(32)
        inside = (None, None, None, None, z >= 2, z < 126)
        faces, total, quarter = coefficients(centre, besides, inside)
        out = [(mid, (n,) + at(base, 32), faces[n]) for n in range(6)]
        out.append((w1, at(base, 32), 8.0 * quarter))
        out.append((d1, at(base, 32), 0.3125 * total))
        return out

    loop(3, 21, 3, mid_coeffs, late=False)
    cut(mid, 0, 32, 8, R1, 8, (8, 23), *ends)

    for copy in third:
        copy.wait_recv()

    def around2(ref):
        lanes = lane_ids(5 * R2) % 4
        centre = ref[R2 : 6 * R2, :]
        return centre, (
            jnp.where(lanes == 0, turn(ref[0 : 5 * R2, :], -3), turn(centre, 1)),
            jnp.where(lanes == 3, turn(ref[2 * R2 : 7 * R2, :], 3), turn(centre, -1)),
            ref[pl.ds(R2 - 1, 5 * R2), :],
            ref[pl.ds(R2 + 1, 5 * R2), :],
            turn(centre, 4),
            turn(centre, -4),
        )

    rows2, lanes2 = row_ids(5 * R2), lane_ids(5 * R2)
    x = rows2 % R2 + (8 * a - 8)
    y = 4 * (rows2 // R2) + lanes2 % 4 + (4 * j - 8)
    inside2 = (y != 0, y != 31, x != 0, x != 127, lanes2 >= 4, lanes2 < 124)
    centre, besides = around2(c2)
    faces, total, quarter = coefficients(centre, besides, inside2)
    for n in range(6):
        deep[n] = faces[n]
    deep[6] = 32.0 * quarter

    def guess(p):
        base = p * R1
        return [(g1, at(base, 32), w1[pl.ds(base, 32), :] * f1[pl.ds(base, 32), :])]

    land_f()
    loop(6, 18, 12, guess)
    sweep(g1, e1, mid_faces, g1, 7, 17, 10, R1, 4, 24, 2)
    leftover(e1, r1, mid_faces, g1, d1, 8, 16, 8, R1, 8, 16, 2)
    f2[pl.ds(own2, 8), :] = packed(r1)
    sixth = blocks2(f2, FAR + FULL)

    land_rest()
    loop(3, 21, 9, guess)
    sweep(g1, e1, mid_faces, g1, 4, 20, 8, R1, 4, 24, 2)

    drain()
    for copy in sixth:
        copy.wait_recv()
    g2[...] = deep[6] * f2[R2 : 6 * R2, :]
    e2[R2 : 6 * R2, :] = g2[...]
    for src, dst in ((e2, e2b), (e2b, e2), (e2, e2b)):
        centre, besides = around2(src)
        parts = [deep[n] * besides[n] for n in range(6)]
        dst[R2 : 6 * R2, :] = (
            (0.2 * centre + g2[...]) + (parts[0] + parts[1]) + (parts[2] + parts[3]) + (parts[4] + parts[5])
        )

    lanes16 = lane_ids(16) % 4
    hops = ((1, 2), (-1, 2), (1, -2), (-1, -2))
    for number in range(8):
        block, i = (number + 6) // 4, (number + 6) % 4
        value = jnp.where(lanes16 == i, e2b[pl.ds(R2 + R2 * block + 4, 16), :], 0.0)
        value = value + turn(value, hops[i][0])
        value = value + turn(value, hops[i][1])
        pe2[pl.ds(32 * number, 16, stride=2), :] = value
        pe2[pl.ds(32 * number + 1, 16, stride=2), :] = value

    def corrected1(p):
        value = e1[pl.ds(p * R1 + 4, 24), :] + pe2[pl.ds((p // 2 - 2) * 32 + 4, 24), :]
        return [(e1, at(p * R1 + 4, 24), value)]

    loop(4, 20, 8, corrected1)
    sweep(e1, e1b, mid_faces, g1, 5, 19, 7, R1, 4, 24, 2)
    sweep(e1b, e1, mid_faces, g1, 6, 18, 6, R1, 4, 24, 2)

    def grown(i):
        value = e1[pl.ds((i + 6) * R1 + 4, 24), :]
        return [(pe1, (pl.ds(RF * i + odd, 24, stride=2), slice(None)), value) for odd in (0, 1)]

    loop(0, 12, 6, grown)

    def corrected0(p):
        base = p * RF + 4
        return [(u2, at(base, 40), u2[pl.ds(base, 40), :] + pe1[pl.ds((p // 2) * RF + 4, 40), :])]

    loop(1, 23, 2, corrected0)
    sweep(u2, u1, fine_faces, gf, 2, 22, 5, RF, 4, 40, 1)

    def give(ref, stage, other, quads):
        def step(t):
            rows = pl.ds(pl.multiple_of(8 * t, 8), 8)
            out = []
            for q in quads:
                four = [
                    ref[pl.ds(pl.multiple_of((4 + 4 * q + i) * RF + 8 + 8 * t, 8), 8), :]
                    for i in range(4)
                ]
                for p, value in enumerate(transposed(four)):
                    out.append((stage, (p, rows, slice(128 * q, 128 * q + 128)), value))
            return out

        loop(0, 4, 4, step)
        lanes = pl.ds(128 * quads[0], 128 * len(quads))
        return send(stage.at[pl.ds(1 - half, 3), :, lanes], other.at[:, :, lanes], sibling)

    own = jnp.where(half == 0, split, 4 - split)

    def keep(stage, out):
        for s in range(4):
            out[s, :, mine] = jnp.where(s < own, stage[jnp.clip(s + half * split, 0, 3)], 0.0)

    def take(copies, other, out):
        for copy in copies:
            copy.wait_recv()
        for s in range(4):
            out[s, :, theirs] = jnp.where(s < own, other[jnp.clip(s + half * (split - 1), 0, 2)], 0.0)

    last_f, last_r = [], []
    sweep(u1, u2, fine_faces, gf, 3, 12, 3, RF, 4, 40, 1)
    last_f.append(give(u2, stage_f, other_f, (0, 1)))
    sweep(u1, u2, fine_faces, gf, 12, 21, 3, RF, 4, 40, 1)
    last_f.append(give(u2, stage_f, other_f, (2, 3)))
    leftover(u2, u1, fine_faces, gf, df, 4, 12, 4, RF, 8, 32, 1)
    last_r.append(give(u1, stage_r, other_r, (0, 1)))
    leftover(u2, u1, fine_faces, gf, df, 12, 20, 4, RF, 8, 32, 1)
    last_r.append(give(u1, stage_r, other_r, (2, 3)))
    keep(stage_f, out_field)
    take(last_f, other_f, out_field)
    keep(stage_r, out_resid)
    take(last_r, other_r, out_resid)
    drain()


def vmem(*shape):
    return pltpu.VMEM(shape, F32)


def body(source, conductance, initial, box_counts):
    fine_field = vmem(PF * RF, LANES)
    mid_field = vmem(P1 * R1, LANES)
    deep_field = vmem(7 * R2, LANES)
    scratch = [pltpu.SMEM(box_counts.shape, jnp.int32)] + [vmem(6, 32, 512)] * 3
    scratch += [fine_field] * 5 + [vmem(6, PF * RF, LANES)] + [fine_field] * 2
    scratch += [mid_field] * 4 + [vmem(8 * 32, LANES), vmem(6, P1 * R1, LANES)] + [mid_field] * 4
    scratch += [deep_field] * 4 + [vmem(7, 5 * R2, LANES), vmem(5 * R2, LANES), vmem(12 * RF, LANES)]
    scratch += [vmem(4, 32, 512)] * 2 + [vmem(3, 32, 512)] * 2
    for big, middle, small in ((96, 48, 8), (160, 80, 8), (104, 56, 24), (32, 16, 8), (144, 72, 16)):
        for count, rows in ((2, big), (2, middle), (4, small)):
            scratch += [vmem(count, rows, LANES)] * 2
    messages = 3 + 5 * 8 + 6 + 14 + 4
    scratch += [pltpu.SemaphoreType.DMA((4,))] + [pltpu.SemaphoreType.DMA((messages,))] * 2
    hbm = pl.BlockSpec(memory_space=pltpu.HBM)
    shape = jax.ShapeDtypeStruct(source.shape, source.dtype)
    return pl.pallas_call(
        kernel,
        out_shape=(shape, shape),
        in_specs=[hbm] * 4,
        out_specs=(pl.BlockSpec(memory_space=pltpu.VMEM),) * 2,
        scratch_shapes=scratch,
        compiler_params=pltpu.CompilerParams(
            collective_id=0, has_side_effects=True, vmem_limit_bytes=40 * 2**20
        ),
        cost_estimate=pl.CostEstimate(flops=3 * 10**7, bytes_accessed=3 * 10**6, transcendentals=0),
    )(*[pltpu.with_memory_space_constraint(x, pltpu.HBM) for x in (box_counts, source, conductance, initial)])


def solution(mesh):
    return jax.shard_map(
        body,
        mesh=mesh,
        in_specs=(P("box", None, None), P("box", None, None), P("box", None, None), P()),
        out_specs=(P("box", None, None), P("box", None, None)),
        check_vma=False,
    )
```

```python
import functools

import jax
import jax.numpy as jnp
from jax import lax
from jax.experimental import pallas as pl
from jax.experimental.pallas import tpu as pltpu
from jax.sharding import PartitionSpec as P


RF, PF = 48, 24
R1, P1 = 32, 24
R2 = 24
LANES = 128
FULL = (1, 0), (-1, 0), (0, 1), (0, -1), (1, 1), (1, -1), (-1, 1), (-1, -1)
FAR = (0, 2), (0, -2), (1, 2), (1, -2), (-1, 2), (-1, -2)
F32 = jnp.float32


def lane_ids(rows):
    return lax.broadcasted_iota(jnp.int32, (rows, LANES), 1)


def row_ids(rows):
    return lax.broadcasted_iota(jnp.int32, (rows, LANES), 0)


def turn(value, steps):
    return pltpu.roll(value, steps % LANES, 1)


def transposed(four):
    lanes = lane_ids(four[0].shape[0])
    low = lanes < 64
    even = (lanes // 32) % 2 == 0
    a, b, c, d = four
    e = jnp.where(low, a, turn(c, 64))
    f = jnp.where(low, b, turn(d, 64))
    g = jnp.where(low, turn(a, 64), c)
    h = jnp.where(low, turn(b, 64), d)
    return (
        jnp.where(even, e, turn(f, 32)),
        jnp.where(even, turn(e, -32), f),
        jnp.where(even, g, turn(h, 32)),
        jnp.where(even, turn(g, -32), h),
    )


def coefficients(c, besides, inside):
    around_ = [
        beside if within is None else jnp.where(within, beside, c)
        for beside, within in zip(besides, inside)
    ]
    total = 3.0 * c + 0.5 * (
        (around_[0] + around_[1]) + (around_[2] + around_[3]) + (around_[4] + around_[5])
    )
    quarter = 0.4 / total
    faces = [
        (c + beside) * quarter if within is None else jnp.where(within, (c + beside) * quarter, 0.0)
        for beside, within in zip(besides, inside)
    ]
    return faces, total, quarter


def around(ref, base, count, rows, twist):
    centre = ref[pl.ds(base, count), :]
    return centre, (
        ref[pl.ds(base - rows, count), :],
        ref[pl.ds(base + rows, count), :],
        ref[pl.ds(base - 1, count), :],
        ref[pl.ds(base + 1, count), :],
        turn(centre, twist),
        turn(centre, -twist),
    )


def weighted(faces, base, count, besides):
    parts = [faces[n][pl.ds(base, count), :] * besides[n] for n in range(6)]
    return (parts[0] + parts[1]) + (parts[2] + parts[3]) + (parts[4] + parts[5])


def loop(low, high, width, body, group=None):
    assert (high - low) % width == 0
    group = group or width

    def step(index, carry):
        first = low + index * width
        stores = []
        for m in range(width):
            stores += body(first + m)
            if (m + 1) % group == 0 or m == width - 1:
                for ref, index_, value in stores:
                    ref[index_] = value
                stores = []
        return carry

    if high - low == width:
        step(0, 0)
    else:
        lax.fori_loop(0, (high - low) // width, step, 0)


def at(base, count):
    return pl.ds(base, count), slice(None)


def pair_rows(ref, base, count, rows):
    got = [
        ref[pl.ds(base + offset, count, stride=2), :] for offset in (0, 1, rows, rows + 1)
    ]
    return (got[0] + got[1]) + (got[2] + got[3])


def pair_lanes(value, width):
    first = (lane_ids(value.shape[0]) // width) % 2 == 0
    return 0.125 * (value + jnp.where(first, turn(value, -width), turn(value, width)))


def kernel(
    counts, source, conductance, initial, out_field, out_resid, out_held,
    owners, raw_c, raw_u, raw_s, cf, uf, sf, u1, u2, fine, gf, df,
    c1, f1, e1, e1b, pe2, mid, w1, g1, d1, r1, c2, f2, e2, e2b, deep, g2, pe1,
    stage_f, stage_r, other_f, other_r, *rest,
):
    post, local_sem, send_sem, recv_sem = rest[:-3], rest[-3], rest[-2], rest[-1]
    me = lax.axis_index("box")
    a, j = me // 8, me % 8
    half = me % 2
    sibling = me + 1 - 2 * half
    across = {da: ((a + da + 16) % 16) * 8 for da in (-1, 0, 1)}
    along = {dj: (j + dj + 8) % 8 for dj in (-2, -1, 0, 1, 2)}

    def device(da, dj):
        return across[da] + along[dj]

    used = []

    def send(src, dst, target):
        number = len(used)
        copy = pltpu.make_async_remote_copy(
            src_ref=src, dst_ref=dst, send_sem=send_sem.at[number], recv_sem=recv_sem.at[number],
            device_id=(target,), device_id_type=pl.DeviceIdType.MESH,
        )
        copy.start()
        used.append(copy)
        return copy

    sent_upto = [0]

    def drain():
        for copy in used[sent_upto[0] :]:
            copy.wait_send()
        sent_upto[0] = len(used)

    raws = (raw_c, raw_s, raw_u)
    given = (conductance, source, initial)
    mine = pl.ds(pl.multiple_of(512 * half, 512), 512)
    theirs = pl.ds(pl.multiple_of(512 - 512 * half, 512), 512)
    held = pl.ds(3 * half, 3)
    locals_ = [pltpu.make_async_copy(counts, owners, local_sem.at[3])]
    for number in range(3):
        locals_.append(
            pltpu.make_async_copy(
                given[number].at[pl.ds(0, 3), :, mine], raws[number].at[held], local_sem.at[number]
            )
        )
    for copy in locals_:
        copy.start()

    barrier = pltpu.get_barrier_semaphore()
    for da, dj in FULL + FAR:
        pl.semaphore_signal(
            barrier, inc=1, device_id=(device(da, dj),), device_id_type=pl.DeviceIdType.MESH
        )
    pl.semaphore_wait(barrier, len(FULL + FAR))

    swaps = [
        send(given[number].at[pl.ds(0, 3), :, theirs], raws[number].at[held], sibling)
        for number in range(3)
    ]
    locals_[0].wait()
    split = owners[me - half]
    own = jnp.where(half == 0, split, 4 - split)
    for s in range(4):
        out_held[s] = jnp.where(s < own, jnp.ones((32, 1024), F32), 0.0)
    places = [jnp.where(p < split, p, jnp.clip(3 + p - split, 0, 5)) for p in range(4)]

    def bring(number, ref):
        locals_[1 + number].wait()
        swaps[number].wait_recv()
        raw = raws[number]

        def step(t):
            rows = pl.ds(pl.multiple_of(8 * t, 8), 8)
            out = []
            for q in range(4):
                four = [raw[places[p], rows, 128 * q : 128 * q + 128] for p in range(4)]
                for i, value in enumerate(transposed(four)):
                    out.append((ref, at(pl.multiple_of((4 + 4 * q + i) * RF + 8 + 8 * t, 8), 8), value))
            return out

        loop(0, 4, 2, step)

    ROWS = (RF, R1)
    OWN = ((4, 16, 8, 32), (8, 8, 8, 16))

    def near(first, count, side, depth):
        return first - 1 + depth if side < 0 else first + count - depth

    def far(first, count, side, depth):
        return first + count - 1 + depth if side < 0 else first - depth

    own2 = R2 + 2 * R2 + 8

    def there2(da, dj):
        return R2 + R2 * (2 - dj) + 8 * (1 - da)

    def pieces(strips, corners, block, da, dj, pick):
        out = []
        if block is not None:
            out.append((block, own2 if pick is near else there2(da, dj), 8, 1))
        if da == 0:
            for ref, level, depths in strips:
                plane, planes, row, rows = OWN[level]
                for d in depths:
                    out.append((ref, pick(plane, planes, dj, d) * ROWS[level] + row, rows, 1))
        elif dj == 0:
            for ref, level, depths in strips:
                plane, planes, row, rows = OWN[level]
                for d in depths:
                    out.append(
                        (ref, plane * ROWS[level] + pick(row, rows, da, d), planes, ROWS[level])
                    )
        else:
            for ref, level, depth, low, count in corners:
                plane, planes, row, rows = OWN[level]
                ends = [pick(row, rows, da, d) for d in (low, low + count - 1)]
                out.append((ref, pick(plane, planes, dj, depth) * ROWS[level] + min(ends), count, 1))
        return out

    def slab(ref, first, count, stride):
        return (pl.ds(first, count, stride=stride) if stride > 1 else pl.ds(first, count)), slice(None)

    spare = list(post)

    def exchange(strips, corners, block=None):
        boxes = [(spare.pop(0), spare.pop(0)) for _ in range(3)]
        started = []
        for number, (da, dj) in enumerate(FULL):
            kind = 2 if da and dj else 1 if da else 0
            slot = number % 2 if number < 4 else number - 4
            out, got = boxes[kind]
            offset = 0
            for ref, first, count, stride in pieces(strips, corners, block, da, dj, near):
                out[slot, pl.ds(offset, count), :] = ref[slab(ref, first, count, stride)]
                offset += count
            started.append((send(out.at[slot], got.at[slot], device(da, dj)), got, slot, da, dj))

        def land():
            for copy, got, slot, da, dj in started:
                copy.wait_recv()
                offset = 0
                for ref, first, count, stride in pieces(strips, corners, block, da, dj, far):
                    ref[slab(ref, first, count, stride)] = got[slot, pl.ds(offset, count), :]
                    offset += count

        return land

    def fine_corner(ref, depth):
        return [(ref, 0, d, 1, depth - d) for d in range(1, depth)]

    bring(0, cf)
    bring(1, sf)
    land_c = exchange(
        ((cf, 0, (1, 2, 3)), (sf, 0, (1, 2))), fine_corner(cf, 3) + fine_corner(sf, 2)
    )
    bring(2, uf)
    land_u = exchange(((uf, 0, (1, 2, 3)),), fine_corner(uf, 3))

    def coarse_c(i):
        total = pair_rows(cf, (4 + 2 * i) * RF + 8, 16, RF)
        return [(c1, at(pl.multiple_of((8 + i) * R1 + 8, 8), 16), pair_lanes(total, 1))]

    loop(0, 8, 8, coarse_c)

    def packed(ref):
        lanes = lane_ids(8) % 4
        total = jnp.zeros((8, LANES), F32)
        for i in range(4):
            value = pair_lanes(pair_rows(ref, (8 + 2 * i) * R1 + 8, 8, R1), 2)
            total = total + jnp.where(lanes == i, value, 0.0)
        return total

    def blocks2(ref, where):
        return [
            send(ref.at[pl.ds(own2, 8)], ref.at[pl.ds(there2(da, dj), 8)], device(da, dj))
            for da, dj in where
        ]

    c2[pl.ds(own2, 8), :] = packed(c1)
    land_c1 = exchange(
        ((c1, 1, (1, 2, 3, 4, 5, 6)),), [(c1, 1, d, 1, 6 - d) for d in range(1, 6)], c2
    )
    third = blocks2(c2, FAR)

    land_c()

    def edges(ref, first, side, count, rows, plane, row, low_y, high_y, low_x, high_x):
        for outside, there, here in (
            (low_y, plane - 1, plane), (high_y, plane + count, plane + count - 1)
        ):
            slab_there = at(there * rows + first, side)
            ref[slab_there] = jnp.where(outside, ref[at(here * rows + first, side)], ref[slab_there])
        lines = 24
        for outside, there, here in ((low_x, row[0] - 1, row[0]), (high_x, row[1] + 1, row[1])):
            slab_there = slab(ref, there, lines, rows)
            ref[slab_there] = jnp.where(outside, ref[slab(ref, here, lines, rows)], ref[slab_there])

    def cut(faces, first, side, count, rows, plane, row, low_y, high_y, low_x, high_x):
        for n, outside, here in ((0, low_y, plane), (1, high_y, plane + count - 1)):
            where = (n,) + at(here * rows + first, side)
            faces[where] = jnp.where(outside, 0.0, faces[where])
        for n, outside, here in ((2, low_x, row[0]), (3, high_x, row[1])):
            where = (n,) + slab(faces, here, 24, rows)
            faces[where] = jnp.where(outside, 0.0, faces[where])

    ends = (j == 0, j == 7, a == 0, a == 15)
    edges(cf, 4, 40, 16, RF, 4, (8, 39), *ends)
    fine_faces = [fine.at[n] for n in range(6)]

    def fine_coeffs(p):
        base = p * RF + 4
        centre, besides = around(cf, base, 40, RF, 1)
        z = lane_ids(40)
        inside = (None, None, None, None, z != 0, z != 127)
        faces, total, quarter = coefficients(centre, besides, inside)
        out = [(fine, (n,) + at(base, 40), faces[n]) for n in range(6)]
        out.append((gf, at(base, 40), 2.0 * quarter))
        out.append((df, at(base, 40), 1.25 * total))
        return out

    loop(2, 22, 4, fine_coeffs, group=1)
    cut(fine, 4, 40, 16, RF, 4, (8, 39), *ends)
    land_u()

    def sweep(src, dst, faces, right, low, high, width, rows, start, count, twist):
        def step(p):
            base = p * rows + start
            centre, besides = around(src, base, count, rows, twist)
            value = 0.2 * centre + right[pl.ds(base, count), :] + weighted(faces, base, count, besides)
            return [(dst, at(base, count), value)]

        loop(low, high, width, step, group=5)

    def leftover(src, dst, faces, right, diag, low, high, width, rows, start, count, twist):
        def step(p):
            base = p * rows + start
            centre, besides = around(src, base, count, rows, twist)
            value = diag[pl.ds(base, count), :] * (
                right[pl.ds(base, count), :] + weighted(faces, base, count, besides) - 0.8 * centre
            )
            return [(dst, at(base, count), value)]

        loop(low, high, width, step, group=4)

    def first_sweep(p):
        base = p * RF + 4
        centre, besides = around(uf, base, 40, RF, 1)
        right = gf[pl.ds(base, 40), :] * sf[pl.ds(base, 40), :]
        value = 0.2 * centre + right + weighted(fine_faces, base, 40, besides)
        return [(u1, at(base, 40), value), (gf, at(base, 40), right)]

    loop(2, 22, 10, first_sweep, group=5)
    sweep(u1, u2, fine_faces, gf, 3, 21, 9, RF, 4, 40, 1)
    leftover(u2, u1, fine_faces, gf, df, 4, 20, 8, RF, 8, 32, 1)

    def coarse_f(i):
        total = pair_rows(u1, (4 + 2 * i) * RF + 8, 16, RF)
        return [(f1, at(pl.multiple_of((8 + i) * R1 + 8, 8), 16), pair_lanes(total, 1))]

    loop(0, 8, 8, coarse_f)
    land_f = exchange(((f1, 1, (1, 2)),), [(f1, 1, 1, 1, 1)])
    land_rest = exchange(
        ((f1, 1, (3, 4, 5)), (u2, 0, (1, 2, 3))),
        [(f1, 1, 1, 2, 3), (f1, 1, 2, 1, 3), (f1, 1, 3, 1, 2), (f1, 1, 4, 1, 1)] + fine_corner(u2, 3),
    )

    drain()
    land_c1()
    edges(c1, 0, 32, 8, R1, 8, (8, 23), *ends)
    mid_faces = [mid.at[n] for n in range(6)]

    def mid_coeffs(p):
        base = p * R1
        centre, besides = around(c1, base, 32, R1, 2)
        z = lane_ids(32)
        inside = (None, None, None, None, z >= 2, z < 126)
        faces, total, quarter = coefficients(centre, besides, inside)
        out = [(mid, (n,) + at(base, 32), faces[n]) for n in range(6)]
        out.append((w1, at(base, 32), 8.0 * quarter))
        out.append((d1, at(base, 32), 0.3125 * total))
        return out

    loop(3, 21, 3, mid_coeffs, group=1)
    cut(mid, 0, 32, 8, R1, 8, (8, 23), *ends)

    for copy in third:
        copy.wait_recv()

    def around2(ref):
        lanes = lane_ids(5 * R2) % 4
        centre = ref[R2 : 6 * R2, :]
        return centre, (
            jnp.where(lanes == 0, turn(ref[0 : 5 * R2, :], -3), turn(centre, 1)),
            jnp.where(lanes == 3, turn(ref[2 * R2 : 7 * R2, :], 3), turn(centre, -1)),
            ref[pl.ds(R2 - 1, 5 * R2), :],
            ref[pl.ds(R2 + 1, 5 * R2), :],
            turn(centre, 4),
            turn(centre, -4),
        )

    rows2, lanes2 = row_ids(5 * R2), lane_ids(5 * R2)
    x = rows2 % R2 + (8 * a - 8)
    y = 4 * (rows2 // R2) + lanes2 % 4 + (4 * j - 8)
    inside2 = (y != 0, y != 31, x != 0, x != 127, lanes2 >= 4, lanes2 < 124)
    centre, besides = around2(c2)
    faces, total, quarter = coefficients(centre, besides, inside2)
    for n in range(6):
        deep[n] = faces[n]
    deep[6] = 32.0 * quarter

    def guess(p):
        base = p * R1
        return [(g1, at(base, 32), w1[pl.ds(base, 32), :] * f1[pl.ds(base, 32), :])]

    land_f()
    loop(6, 18, 12, guess)
    sweep(g1, e1, mid_faces, g1, 7, 17, 10, R1, 4, 24, 2)
    leftover(e1, r1, mid_faces, g1, d1, 8, 16, 8, R1, 8, 16, 2)
    f2[pl.ds(own2, 8), :] = packed(r1)
    sixth = blocks2(f2, FAR + FULL)

    land_rest()
    loop(3, 21, 9, guess)
    sweep(g1, e1, mid_faces, g1, 4, 20, 8, R1, 4, 24, 2)

    drain()
    for copy in sixth:
        copy.wait_recv()
    g2[...] = deep[6] * f2[R2 : 6 * R2, :]
    e2[R2 : 6 * R2, :] = g2[...]
    for src, dst in ((e2, e2b), (e2b, e2), (e2, e2b)):
        centre, besides = around2(src)
        parts = [deep[n] * besides[n] for n in range(6)]
        dst[R2 : 6 * R2, :] = (
            (0.2 * centre + g2[...]) + (parts[0] + parts[1]) + (parts[2] + parts[3]) + (parts[4] + parts[5])
        )

    lanes16 = lane_ids(16) % 4
    hops = ((1, 2), (-1, 2), (1, -2), (-1, -2))
    for number in range(8):
        block, i = (number + 6) // 4, (number + 6) % 4
        value = jnp.where(lanes16 == i, e2b[pl.ds(R2 + R2 * block + 4, 16), :], 0.0)
        value = value + turn(value, hops[i][0])
        value = value + turn(value, hops[i][1])
        pe2[pl.ds(32 * number, 16, stride=2), :] = value
        pe2[pl.ds(32 * number + 1, 16, stride=2), :] = value

    def corrected1(p):
        value = e1[pl.ds(p * R1 + 4, 24), :] + pe2[pl.ds((p // 2 - 2) * 32 + 4, 24), :]
        return [(e1, at(p * R1 + 4, 24), value)]

    loop(4, 20, 16, corrected1)
    sweep(e1, e1b, mid_faces, g1, 5, 19, 14, R1, 4, 24, 2)
    sweep(e1b, e1, mid_faces, g1, 6, 18, 12, R1, 4, 24, 2)

    def grown(i):
        value = e1[pl.ds((i + 6) * R1 + 4, 24), :]
        return [(pe1, (pl.ds(RF * i + odd, 24, stride=2), slice(None)), value) for odd in (0, 1)]

    loop(0, 12, 12, grown)

    def corrected0(p):
        base = p * RF + 4
        return [(u2, at(base, 40), u2[pl.ds(base, 40), :] + pe1[pl.ds((p // 2) * RF + 4, 40), :])]

    loop(1, 23, 11, corrected0)
    sweep(u2, u1, fine_faces, gf, 2, 22, 10, RF, 4, 40, 1)

    def give(ref, stage, other, quads):
        def step(t):
            rows = pl.ds(pl.multiple_of(8 * t, 8), 8)
            out = []
            for q in quads:
                four = [
                    ref[pl.ds(pl.multiple_of((4 + 4 * q + i) * RF + 8 + 8 * t, 8), 8), :]
                    for i in range(4)
                ]
                for p, value in enumerate(transposed(four)):
                    out.append((stage, (p, rows, slice(128 * q, 128 * q + 128)), value))
            return out

        loop(0, 4, 4, step)
        lanes = pl.ds(128 * quads[0], 128 * len(quads))
        return send(stage.at[pl.ds(1 - half, 3), :, lanes], other.at[:, :, lanes], sibling)

    def keep(stage, out):
        for s in range(4):
            out[s, :, mine] = stage[jnp.clip(s + half * split, 0, 3)]

    def take(copies, other, out):
        for copy in copies:
            copy.wait_recv()
        for s in range(4):
            out[s, :, theirs] = other[jnp.clip(s + half * (split - 1), 0, 2)]

    last_f, last_r = [], []
    sweep(u1, u2, fine_faces, gf, 3, 12, 9, RF, 4, 40, 1)
    last_f.append(give(u2, stage_f, other_f, (0, 1)))
    sweep(u1, u2, fine_faces, gf, 12, 21, 9, RF, 4, 40, 1)
    last_f.append(give(u2, stage_f, other_f, (2, 3)))
    leftover(u2, u1, fine_faces, gf, df, 4, 12, 8, RF, 8, 32, 1)
    last_r.append(give(u1, stage_r, other_r, (0, 1)))
    leftover(u2, u1, fine_faces, gf, df, 12, 20, 8, RF, 8, 32, 1)
    last_r.append(give(u1, stage_r, other_r, (2, 3)))
    keep(stage_f, out_field)
    take(last_f, other_f, out_field)
    keep(stage_r, out_resid)
    take(last_r, other_r, out_resid)
    drain()


def vmem(*shape):
    return pltpu.VMEM(shape, F32)


def body(source, conductance, initial, box_counts):
    fine_field = vmem(PF * RF, LANES)
    mid_field = vmem(P1 * R1, LANES)
    deep_field = vmem(7 * R2, LANES)
    scratch = [pltpu.SMEM(box_counts.shape, jnp.int32)] + [vmem(6, 32, 512)] * 3
    scratch += [fine_field] * 5 + [vmem(6, PF * RF, LANES)] + [fine_field] * 2
    scratch += [mid_field] * 4 + [vmem(8 * 32, LANES), vmem(6, P1 * R1, LANES)] + [mid_field] * 4
    scratch += [deep_field] * 4 + [vmem(7, 5 * R2, LANES), vmem(5 * R2, LANES), vmem(12 * RF, LANES)]
    scratch += [vmem(4, 32, 512)] * 2 + [vmem(3, 32, 512)] * 2
    for big, middle, small in ((160, 80, 8), (96, 48, 8), (104, 56, 24), (32, 16, 8), (144, 72, 16)):
        for count, rows in ((2, big), (2, middle), (4, small)):
            scratch += [vmem(count, rows, LANES)] * 2
    messages = 3 + 5 * 8 + 6 + 14 + 4
    scratch += [pltpu.SemaphoreType.DMA((4,))] + [pltpu.SemaphoreType.DMA((messages,))] * 2
    hbm = pl.BlockSpec(memory_space=pltpu.HBM)
    shape = jax.ShapeDtypeStruct(source.shape, source.dtype)
    field, resid, held = pl.pallas_call(
        kernel,
        out_shape=(shape,) * 3,
        in_specs=[hbm] * 4,
        out_specs=(pl.BlockSpec(memory_space=pltpu.VMEM),) * 3,
        scratch_shapes=scratch,
        compiler_params=pltpu.CompilerParams(
            collective_id=0, has_side_effects=True, vmem_limit_bytes=40 * 2**20
        ),
        cost_estimate=pl.CostEstimate(flops=3 * 10**7, bytes_accessed=3 * 10**6, transcendentals=0),
    )(*[pltpu.with_memory_space_constraint(x, pltpu.HBM) for x in (box_counts, source, conductance, initial)])
    return jnp.where(held > 0.0, field, 0.0), jnp.where(held > 0.0, resid, 0.0)


def solution(mesh):
    return jax.shard_map(
        body,
        mesh=mesh,
        in_specs=(P("box", None, None), P("box", None, None), P("box", None, None), P()),
        out_specs=(P("box", None, None), P("box", None, None)),
        check_vma=False,
    )
```

```python
import functools

import jax
import jax.numpy as jnp
from jax import lax
from jax.experimental import pallas as pl
from jax.experimental.pallas import tpu as pltpu
from jax.sharding import PartitionSpec as P


RF, PF = 48, 24
R1, P1 = 32, 24
R2 = 24
LANES = 128
FULL = (1, 1), (1, -1), (-1, 1), (-1, -1), (1, 0), (-1, 0), (0, 1), (0, -1)
FAR = (1, 2), (1, -2), (-1, 2), (-1, -2), (0, 2), (0, -2)
F32 = jnp.float32
ROUNDS = 3 + 5 + 2 + 4


def lane_ids(rows):
    return lax.broadcasted_iota(jnp.int32, (rows, LANES), 1)


def row_ids(rows):
    return lax.broadcasted_iota(jnp.int32, (rows, LANES), 0)


def turn(value, steps):
    return pltpu.roll(value, steps % LANES, 1)


def transposed(four):
    lanes = lane_ids(four[0].shape[0])
    low = lanes < 64
    even = (lanes // 32) % 2 == 0
    a, b, c, d = four
    e = jnp.where(low, a, turn(c, 64))
    f = jnp.where(low, b, turn(d, 64))
    g = jnp.where(low, turn(a, 64), c)
    h = jnp.where(low, turn(b, 64), d)
    return (
        jnp.where(even, e, turn(f, 32)),
        jnp.where(even, turn(e, -32), f),
        jnp.where(even, g, turn(h, 32)),
        jnp.where(even, turn(g, -32), h),
    )


def coefficients(c, besides, inside):
    around_ = [
        beside if within is None else jnp.where(within, beside, c)
        for beside, within in zip(besides, inside)
    ]
    total = 3.0 * c + 0.5 * (
        (around_[0] + around_[1]) + (around_[2] + around_[3]) + (around_[4] + around_[5])
    )
    quarter = 0.4 / total
    faces = [
        (c + beside) * quarter if within is None else jnp.where(within, (c + beside) * quarter, 0.0)
        for beside, within in zip(besides, inside)
    ]
    return faces, total, quarter


def around(ref, base, count, rows, twist):
    centre = ref[pl.ds(base, count), :]
    return centre, (
        ref[pl.ds(base - rows, count), :],
        ref[pl.ds(base + rows, count), :],
        ref[pl.ds(base - 1, count), :],
        ref[pl.ds(base + 1, count), :],
        turn(centre, twist),
        turn(centre, -twist),
    )


def weighted(faces, base, count, besides):
    parts = [faces[n][pl.ds(base, count), :] * besides[n] for n in range(6)]
    return (parts[0] + parts[1]) + (parts[2] + parts[3]) + (parts[4] + parts[5])


def loop(low, high, width, body, group=None):
    assert (high - low) % width == 0
    group = group or width

    def step(index, carry):
        first = low + index * width
        stores = []
        for m in range(width):
            stores += body(first + m)
            if (m + 1) % group == 0 or m == width - 1:
                for ref, index_, value in stores:
                    ref[index_] = value
                stores = []
        return carry

    if high - low == width:
        step(0, 0)
    else:
        lax.fori_loop(0, (high - low) // width, step, 0)


def at(base, count):
    return pl.ds(base, count), slice(None)


def pair_rows(ref, base, count, rows):
    got = [
        ref[pl.ds(base + offset, count, stride=2), :] for offset in (0, 1, rows, rows + 1)
    ]
    return (got[0] + got[1]) + (got[2] + got[3])


def pair_lanes(value, width):
    first = (lane_ids(value.shape[0]) // width) % 2 == 0
    return 0.125 * (value + jnp.where(first, turn(value, -width), turn(value, width)))


def kernel(
    counts, source, conductance, initial, out_field, out_resid, out_held,
    owners, raw_c, raw_u, raw_s, cf, uf, sf, u1, u2, fine, gf, df,
    c1, f1, e1, e1b, pe2, mid, w1, g1, d1, r1, c2, f2, e2, e2b, deep, g2, pe1,
    stage_f, stage_r, other_f, other_r, *rest,
):
    post, local_sem, send_sem, recv_sem = rest[:-3], rest[-3], rest[-2], rest[-1]
    me = lax.axis_index("box")
    a, j = me // 8, me % 8
    half = me % 2
    sibling = me + 1 - 2 * half
    across = {da: ((a + da + 16) % 16) * 8 for da in (-1, 0, 1)}
    along = {dj: (j + dj + 8) % 8 for dj in (-2, -1, 0, 1, 2)}

    def device(da, dj):
        return across[da] + along[dj]

    numbers = iter(range(ROUNDS))
    leaving = []

    def describe(src, dst, number, target):
        return pltpu.make_async_remote_copy(
            src_ref=src, dst_ref=dst, send_sem=send_sem.at[number], recv_sem=recv_sem.at[number],
            device_id=(target,), device_id_type=pl.DeviceIdType.MESH,
        )

    def start(copies, whole):
        number = next(numbers)
        for src, dst, target in copies:
            describe(src, dst, number, target).start()
        everything = describe(whole, whole, number, sibling)
        leaving.append(everything.wait_send)
        return everything.wait_recv

    def drain():
        while leaving:
            leaving.pop(0)()

    raws = (raw_c, raw_s, raw_u)
    given = (conductance, source, initial)
    mine = pl.ds(pl.multiple_of(512 * half, 512), 512)
    theirs = pl.ds(pl.multiple_of(512 - 512 * half, 512), 512)
    held = pl.ds(3 * half, 3)
    locals_ = [pltpu.make_async_copy(counts, owners, local_sem.at[3])]
    for number in range(3):
        locals_.append(
            pltpu.make_async_copy(
                given[number].at[pl.ds(0, 3), :, mine], raws[number].at[held], local_sem.at[number]
            )
        )
    for copy in locals_:
        copy.start()

    barrier = pltpu.get_barrier_semaphore()
    for da, dj in FULL + FAR:
        pl.semaphore_signal(
            barrier, inc=1, device_id=(device(da, dj),), device_id_type=pl.DeviceIdType.MESH
        )
    pl.semaphore_wait(barrier, len(FULL + FAR))

    swaps = [
        start(
            [(given[number].at[pl.ds(0, 3), :, theirs], raws[number].at[held], sibling)],
            raws[number].at[held],
        )
        for number in range(3)
    ]
    locals_[0].wait()
    split = owners[me - half]
    own = jnp.where(half == 0, split, 4 - split)
    for s in range(4):
        out_held[s] = jnp.where(s < own, jnp.ones((32, 1024), F32), 0.0)
    places = [jnp.where(p < split, p, jnp.clip(3 + p - split, 0, 5)) for p in range(4)]

    def bring(number, ref):
        locals_[1 + number].wait()
        swaps[number]()
        raw = raws[number]

        def step(t):
            rows = pl.ds(pl.multiple_of(8 * t, 8), 8)
            out = []
            for q in range(4):
                four = [raw[places[p], rows, 128 * q : 128 * q + 128] for p in range(4)]
                for i, value in enumerate(transposed(four)):
                    out.append((ref, at(pl.multiple_of((4 + 4 * q + i) * RF + 8 + 8 * t, 8), 8), value))
            return out

        loop(0, 4, 4, step, group=1)

    ROWS = (RF, R1)
    OWN = ((4, 16, 8, 32), (8, 8, 8, 16))

    def near(first, count, side, depth):
        return first - 1 + depth if side < 0 else first + count - depth

    def far(first, count, side, depth):
        return first + count - 1 + depth if side < 0 else first - depth

    own2 = R2 + 2 * R2 + 8

    def there2(da, dj):
        return R2 + R2 * (2 - dj) + 8 * (1 - da)

    def pieces(strips, corners, block, da, dj, pick):
        out = []
        if block is not None:
            out.append((block, own2 if pick is near else there2(da, dj), 8, 1))
        if da == 0:
            for ref, level, depths in strips:
                plane, planes, row, rows = OWN[level]
                for d in depths:
                    out.append((ref, pick(plane, planes, dj, d) * ROWS[level] + row, rows, 1))
        elif dj == 0:
            for ref, level, depths in strips:
                plane, planes, row, rows = OWN[level]
                for d in depths:
                    out.append(
                        (ref, plane * ROWS[level] + pick(row, rows, da, d), planes, ROWS[level])
                    )
        else:
            for ref, level, depth, low, count in corners:
                plane, planes, row, rows = OWN[level]
                ends = [pick(row, rows, da, d) for d in (low, low + count - 1)]
                out.append((ref, pick(plane, planes, dj, depth) * ROWS[level] + min(ends), count, 1))
        return out

    def slab(ref, first, count, stride):
        return (pl.ds(first, count, stride=stride) if stride > 1 else pl.ds(first, count)), slice(None)

    spare = list(post)

    def exchange(strips, corners, block=None):
        out, got = spare.pop(0), spare.pop(0)
        copies, filled = [], []
        offset = 0
        for da, dj in FULL:
            first_row = offset
            for ref, first, count, stride in pieces(strips, corners, block, da, dj, near):
                out[pl.ds(offset, count), :] = ref[slab(ref, first, count, stride)]
                offset += count
            offset += -offset % 8
            rows = pl.ds(first_row, offset - first_row)
            copies.append((out.at[rows], got.at[rows], device(da, dj)))
            filled.append((first_row, da, dj))
        assert out.shape == (offset, LANES)
        arrived = start(copies, got)

        def land():
            arrived()
            for offset, da, dj in filled:
                for ref, first, count, stride in pieces(strips, corners, block, da, dj, far):
                    ref[slab(ref, first, count, stride)] = got[pl.ds(offset, count), :]
                    offset += count

        return land

    def fine_corner(ref, depth):
        return [(ref, 0, d, 1, depth - d) for d in range(1, depth)]

    bring(0, cf)
    bring(1, sf)
    land_c = exchange(
        ((cf, 0, (1, 2, 3)), (sf, 0, (1, 2))), fine_corner(cf, 3) + fine_corner(sf, 2)
    )
    bring(2, uf)
    land_u = exchange(((uf, 0, (1, 2, 3)),), fine_corner(uf, 3))

    def coarse_c(i):
        total = pair_rows(cf, (4 + 2 * i) * RF + 8, 16, RF)
        return [(c1, at(pl.multiple_of((8 + i) * R1 + 8, 8), 16), pair_lanes(total, 1))]

    loop(0, 8, 8, coarse_c)

    def packed(ref):
        lanes = lane_ids(8) % 4
        total = jnp.zeros((8, LANES), F32)
        for i in range(4):
            value = pair_lanes(pair_rows(ref, (8 + 2 * i) * R1 + 8, 8, R1), 2)
            total = total + jnp.where(lanes == i, value, 0.0)
        return total

    def blocks2(ref, where):
        copies = [
            (ref.at[pl.ds(own2, 8)], ref.at[pl.ds(there2(da, dj), 8)], device(da, dj))
            for da, dj in where
        ]
        return start(copies, ref.at[pl.ds(0, 8 * len(where))])

    c2[pl.ds(own2, 8), :] = packed(c1)
    land_c1 = exchange(
        ((c1, 1, (1, 2, 3, 4, 5, 6)),), [(c1, 1, d, 1, 6 - d) for d in range(1, 6)], c2
    )
    third = blocks2(c2, FAR)

    land_c()

    def edges(ref, first, side, count, rows, plane, row, low_y, high_y, low_x, high_x):
        for outside, there, here in (
            (low_y, plane - 1, plane), (high_y, plane + count, plane + count - 1)
        ):
            slab_there = at(there * rows + first, side)
            ref[slab_there] = jnp.where(outside, ref[at(here * rows + first, side)], ref[slab_there])
        lines = 24
        for outside, there, here in ((low_x, row[0] - 1, row[0]), (high_x, row[1] + 1, row[1])):
            slab_there = slab(ref, there, lines, rows)
            ref[slab_there] = jnp.where(outside, ref[slab(ref, here, lines, rows)], ref[slab_there])

    def cut(faces, first, side, count, rows, plane, row, low_y, high_y, low_x, high_x):
        for n, outside, here in ((0, low_y, plane), (1, high_y, plane + count - 1)):
            where = (n,) + at(here * rows + first, side)
            faces[where] = jnp.where(outside, 0.0, faces[where])
        for n, outside, here in ((2, low_x, row[0]), (3, high_x, row[1])):
            where = (n,) + slab(faces, here, 24, rows)
            faces[where] = jnp.where(outside, 0.0, faces[where])

    ends = (j == 0, j == 7, a == 0, a == 15)
    edges(cf, 4, 40, 16, RF, 4, (8, 39), *ends)
    fine_faces = [fine.at[n] for n in range(6)]

    def fine_coeffs(p):
        base = p * RF + 4
        centre, besides = around(cf, base, 40, RF, 1)
        z = lane_ids(40)
        inside = (None, None, None, None, z != 0, z != 127)
        faces, total, quarter = coefficients(centre, besides, inside)
        out = [(fine, (n,) + at(base, 40), faces[n]) for n in range(6)]
        out.append((gf, at(base, 40), 2.0 * quarter))
        out.append((df, at(base, 40), 1.25 * total))
        return out

    loop(2, 22, 4, fine_coeffs, group=1)
    cut(fine, 4, 40, 16, RF, 4, (8, 39), *ends)
    land_u()

    def sweep(src, dst, faces, right, low, high, width, rows, start, count, twist):
        def step(p):
            base = p * rows + start
            centre, besides = around(src, base, count, rows, twist)
            value = 0.2 * centre + right[pl.ds(base, count), :] + weighted(faces, base, count, besides)
            return [(dst, at(base, count), value)]

        loop(low, high, width, step, group=5)

    def leftover(src, dst, faces, right, diag, low, high, width, rows, start, count, twist):
        def step(p):
            base = p * rows + start
            centre, besides = around(src, base, count, rows, twist)
            value = diag[pl.ds(base, count), :] * (
                right[pl.ds(base, count), :] + weighted(faces, base, count, besides) - 0.8 * centre
            )
            return [(dst, at(base, count), value)]

        loop(low, high, width, step, group=4)

    def first_sweep(p):
        base = p * RF + 4
        centre, besides = around(uf, base, 40, RF, 1)
        right = gf[pl.ds(base, 40), :] * sf[pl.ds(base, 40), :]
        value = 0.2 * centre + right + weighted(fine_faces, base, 40, besides)
        return [(u1, at(base, 40), value), (gf, at(base, 40), right)]

    loop(2, 22, 10, first_sweep, group=5)
    sweep(u1, u2, fine_faces, gf, 3, 21, 9, RF, 4, 40, 1)
    leftover(u2, u1, fine_faces, gf, df, 4, 20, 8, RF, 8, 32, 1)

    def coarse_f(i):
        total = pair_rows(u1, (4 + 2 * i) * RF + 8, 16, RF)
        return [(f1, at(pl.multiple_of((8 + i) * R1 + 8, 8), 16), pair_lanes(total, 1))]

    loop(0, 8, 8, coarse_f)
    land_f = exchange(((f1, 1, (1, 2)),), [(f1, 1, 1, 1, 1)])
    land_rest = exchange(
        ((f1, 1, (3, 4, 5)), (u2, 0, (1, 2, 3))),
        [(f1, 1, 1, 2, 3), (f1, 1, 2, 1, 3), (f1, 1, 3, 1, 2), (f1, 1, 4, 1, 1)] + fine_corner(u2, 3),
    )

    drain()
    land_c1()
    edges(c1, 0, 32, 8, R1, 8, (8, 23), *ends)
    mid_faces = [mid.at[n] for n in range(6)]

    def mid_coeffs(p):
        base = p * R1
        centre, besides = around(c1, base, 32, R1, 2)
        z = lane_ids(32)
        inside = (None, None, None, None, z >= 2, z < 126)
        faces, total, quarter = coefficients(centre, besides, inside)
        out = [(mid, (n,) + at(base, 32), faces[n]) for n in range(6)]
        out.append((w1, at(base, 32), 8.0 * quarter))
        out.append((d1, at(base, 32), 0.3125 * total))
        return out

    loop(3, 21, 3, mid_coeffs, group=1)
    cut(mid, 0, 32, 8, R1, 8, (8, 23), *ends)

    third()

    def around2(ref):
        lanes = lane_ids(5 * R2) % 4
        centre = ref[R2 : 6 * R2, :]
        return centre, (
            jnp.where(lanes == 0, turn(ref[0 : 5 * R2, :], -3), turn(centre, 1)),
            jnp.where(lanes == 3, turn(ref[2 * R2 : 7 * R2, :], 3), turn(centre, -1)),
            ref[pl.ds(R2 - 1, 5 * R2), :],
            ref[pl.ds(R2 + 1, 5 * R2), :],
            turn(centre, 4),
            turn(centre, -4),
        )

    rows2, lanes2 = row_ids(5 * R2), lane_ids(5 * R2)
    x = rows2 % R2 + (8 * a - 8)
    y = 4 * (rows2 // R2) + lanes2 % 4 + (4 * j - 8)
    inside2 = (y != 0, y != 31, x != 0, x != 127, lanes2 >= 4, lanes2 < 124)
    centre, besides = around2(c2)
    faces, total, quarter = coefficients(centre, besides, inside2)
    for n in range(6):
        deep[n] = faces[n]
    deep[6] = 32.0 * quarter

    def guess(p):
        base = p * R1
        return [(g1, at(base, 32), w1[pl.ds(base, 32), :] * f1[pl.ds(base, 32), :])]

    land_f()
    loop(6, 18, 12, guess)
    sweep(g1, e1, mid_faces, g1, 7, 17, 10, R1, 4, 24, 2)
    leftover(e1, r1, mid_faces, g1, d1, 8, 16, 8, R1, 8, 16, 2)
    f2[pl.ds(own2, 8), :] = packed(r1)
    sixth = blocks2(f2, FAR + FULL)

    land_rest()
    loop(3, 21, 9, guess)
    sweep(g1, e1, mid_faces, g1, 4, 20, 8, R1, 4, 24, 2)

    drain()
    sixth()
    g2[...] = deep[6] * f2[R2 : 6 * R2, :]
    e2[R2 : 6 * R2, :] = g2[...]
    for src, dst in ((e2, e2b), (e2b, e2), (e2, e2b)):
        centre, besides = around2(src)
        parts = [deep[n] * besides[n] for n in range(6)]
        dst[R2 : 6 * R2, :] = (
            (0.2 * centre + g2[...]) + (parts[0] + parts[1]) + (parts[2] + parts[3]) + (parts[4] + parts[5])
        )

    lanes16 = lane_ids(16) % 4
    hops = ((1, 2), (-1, 2), (1, -2), (-1, -2))
    for number in range(8):
        block, i = (number + 6) // 4, (number + 6) % 4
        value = jnp.where(lanes16 == i, e2b[pl.ds(R2 + R2 * block + 4, 16), :], 0.0)
        value = value + turn(value, hops[i][0])
        value = value + turn(value, hops[i][1])
        pe2[pl.ds(32 * number, 16, stride=2), :] = value
        pe2[pl.ds(32 * number + 1, 16, stride=2), :] = value

    def corrected1(p):
        value = e1[pl.ds(p * R1 + 4, 24), :] + pe2[pl.ds((p // 2 - 2) * 32 + 4, 24), :]
        return [(e1, at(p * R1 + 4, 24), value)]

    loop(4, 20, 16, corrected1)
    sweep(e1, e1b, mid_faces, g1, 5, 19, 14, R1, 4, 24, 2)
    sweep(e1b, e1, mid_faces, g1, 6, 18, 12, R1, 4, 24, 2)

    def grown(i):
        value = e1[pl.ds((i + 6) * R1 + 4, 24), :]
        return [(pe1, (pl.ds(RF * i + odd, 24, stride=2), slice(None)), value) for odd in (0, 1)]

    loop(0, 12, 12, grown)

    def corrected0(p):
        base = p * RF + 4
        return [(u2, at(base, 40), u2[pl.ds(base, 40), :] + pe1[pl.ds((p // 2) * RF + 4, 40), :])]

    loop(1, 23, 11, corrected0)
    sweep(u2, u1, fine_faces, gf, 2, 22, 10, RF, 4, 40, 1)

    def give(ref, stage, other, quads):
        def step(t):
            rows = pl.ds(pl.multiple_of(8 * t, 8), 8)
            out = []
            for q in quads:
                four = [
                    ref[pl.ds(pl.multiple_of((4 + 4 * q + i) * RF + 8 + 8 * t, 8), 8), :]
                    for i in range(4)
                ]
                for p, value in enumerate(transposed(four)):
                    out.append((stage, (p, rows, slice(128 * q, 128 * q + 128)), value))
            return out

        loop(0, 4, 4, step)
        lanes = pl.ds(128 * quads[0], 128 * len(quads))
        return stage.at[pl.ds(1 - half, 3), :, lanes], other.at[:, :, lanes], sibling

    def keep(stage, out):
        for s in range(4):
            out[s, :, mine] = stage[jnp.clip(s + half * split, 0, 3)]

    def take(other, out):
        for s in range(4):
            out[s, :, theirs] = other[jnp.clip(s + half * (split - 1), 0, 2)]

    last = []
    sweep(u1, u2, fine_faces, gf, 3, 12, 9, RF, 4, 40, 1)
    last.append(start([give(u2, stage_f, other_f, (0, 1))], other_f.at[:, :, pl.ds(0, 256)]))
    sweep(u1, u2, fine_faces, gf, 12, 21, 9, RF, 4, 40, 1)
    last.append(start([give(u2, stage_f, other_f, (2, 3))], other_f.at[:, :, pl.ds(256, 256)]))
    leftover(u2, u1, fine_faces, gf, df, 4, 12, 8, RF, 8, 32, 1)
    last.append(start([give(u1, stage_r, other_r, (0, 1))], other_r.at[:, :, pl.ds(0, 256)]))
    leftover(u2, u1, fine_faces, gf, df, 12, 20, 8, RF, 8, 32, 1)
    last.append(start([give(u1, stage_r, other_r, (2, 3))], other_r.at[:, :, pl.ds(256, 256)]))
    keep(stage_f, out_field)
    last[0]()
    last[1]()
    take(other_f, out_field)
    keep(stage_r, out_resid)
    last[2]()
    last[3]()
    take(other_r, out_resid)
    drain()


def vmem(*shape):
    return pltpu.VMEM(shape, F32)


def body(source, conductance, initial, box_counts):
    fine_field = vmem(PF * RF, LANES)
    mid_field = vmem(P1 * R1, LANES)
    deep_field = vmem(7 * R2, LANES)
    scratch = [pltpu.SMEM(box_counts.shape, jnp.int32)] + [vmem(6, 32, 512)] * 3
    scratch += [fine_field] * 5 + [vmem(6, PF * RF, LANES)] + [fine_field] * 2
    scratch += [mid_field] * 4 + [vmem(8 * 32, LANES), vmem(6, P1 * R1, LANES)] + [mid_field] * 4
    scratch += [deep_field] * 4 + [vmem(7, 5 * R2, LANES), vmem(5 * R2, LANES), vmem(12 * RF, LANES)]
    scratch += [vmem(4, 32, 512)] * 2 + [vmem(3, 32, 512)] * 2
    for big, middle, small in ((160, 80, 8), (96, 48, 8), (104, 56, 24), (32, 16, 8), (144, 72, 16)):
        scratch += [vmem(2 * big + 2 * middle + 4 * small, LANES)] * 2
    scratch += [pltpu.SemaphoreType.DMA((4,))] + [pltpu.SemaphoreType.DMA((ROUNDS,))] * 2
    hbm = pl.BlockSpec(memory_space=pltpu.HBM)
    shape = jax.ShapeDtypeStruct(source.shape, source.dtype)
    field, resid, held = pl.pallas_call(
        kernel,
        out_shape=(shape,) * 3,
        in_specs=[hbm] * 4,
        out_specs=(pl.BlockSpec(memory_space=pltpu.VMEM),) * 3,
        scratch_shapes=scratch,
        compiler_params=pltpu.CompilerParams(
            collective_id=0, has_side_effects=True, vmem_limit_bytes=40 * 2**20
        ),
        cost_estimate=pl.CostEstimate(flops=3 * 10**7, bytes_accessed=3 * 10**6, transcendentals=0),
    )(*[pltpu.with_memory_space_constraint(x, pltpu.HBM) for x in (box_counts, source, conductance, initial)])
    return field * held, resid * held


def solution(mesh):
    return jax.shard_map(
        body,
        mesh=mesh,
        in_specs=(P("box", None, None), P("box", None, None), P("box", None, None), P()),
        out_specs=(P("box", None, None), P("box", None, None)),
        check_vma=False,
    )
```

```python
import functools

import jax
import jax.numpy as jnp
from jax import lax
from jax.experimental import pallas as pl
from jax.experimental.pallas import tpu as pltpu
from jax.sharding import PartitionSpec as P


RF, PF = 48, 24
R1, P1 = 32, 24
R2 = 24
LANES = 128
FULL = (1, 1), (1, -1), (-1, 1), (-1, -1), (1, 0), (-1, 0), (0, 1), (0, -1)
FAR = (1, 2), (1, -2), (-1, 2), (-1, -2), (0, 2), (0, -2)
F32 = jnp.float32
ROUNDS = 3 + 5 + 3 + 4


def lane_ids(rows):
    return lax.broadcasted_iota(jnp.int32, (rows, LANES), 1)


def row_ids(rows):
    return lax.broadcasted_iota(jnp.int32, (rows, LANES), 0)


def turn(value, steps):
    return pltpu.roll(value, steps % LANES, 1)


def transposed(four):
    lanes = lane_ids(four[0].shape[0])
    low = lanes < 64
    even = (lanes // 32) % 2 == 0
    a, b, c, d = four
    e = jnp.where(low, a, turn(c, 64))
    f = jnp.where(low, b, turn(d, 64))
    g = jnp.where(low, turn(a, 64), c)
    h = jnp.where(low, turn(b, 64), d)
    return (
        jnp.where(even, e, turn(f, 32)),
        jnp.where(even, turn(e, -32), f),
        jnp.where(even, g, turn(h, 32)),
        jnp.where(even, turn(g, -32), h),
    )


def coefficients(c, besides, inside):
    around_ = [
        beside if within is None else jnp.where(within, beside, c)
        for beside, within in zip(besides, inside)
    ]
    total = 3.0 * c + 0.5 * (
        (around_[0] + around_[1]) + (around_[2] + around_[3]) + (around_[4] + around_[5])
    )
    quarter = 0.4 / total
    faces = [
        (c + beside) * quarter if within is None else jnp.where(within, (c + beside) * quarter, 0.0)
        for beside, within in zip(besides, inside)
    ]
    return faces, total, quarter


def around(ref, base, count, rows, twist):
    centre = ref[pl.ds(base, count), :]
    return centre, (
        ref[pl.ds(base - rows, count), :],
        ref[pl.ds(base + rows, count), :],
        ref[pl.ds(base - 1, count), :],
        ref[pl.ds(base + 1, count), :],
        turn(centre, twist),
        turn(centre, -twist),
    )


def weighted(faces, base, count, besides):
    parts = [faces[n][pl.ds(base, count), :] * besides[n] for n in range(6)]
    return (parts[0] + parts[1]) + (parts[2] + parts[3]) + (parts[4] + parts[5])


def planes_loop(low, high, width, body, group=None, base=0):
    assert (high - low) % width == 0
    group = group or width

    def step(index, carry):
        first = base + low + index * width
        stores = []
        for m in range(width):
            stores += body(first + m)
            if (m + 1) % group == 0 or m == width - 1:
                for ref, index_, value in stores:
                    ref[index_] = value
                stores = []
        return carry

    if high - low == width:
        step(0, 0)
    else:
        lax.fori_loop(0, (high - low) // width, step, 0)


def at(base, count):
    return pl.ds(base, count), slice(None)


def pair_rows(ref, base, count, rows):
    got = [
        ref[pl.ds(base + offset, count, stride=2), :] for offset in (0, 1, rows, rows + 1)
    ]
    return (got[0] + got[1]) + (got[2] + got[3])


def pair_lanes(value, width):
    first = (lane_ids(value.shape[0]) // width) % 2 == 0
    return 0.125 * (value + jnp.where(first, turn(value, -width), turn(value, width)))


def kernel(
    counts, source, conductance, initial, out_field, out_resid, out_held,
    owners, raw_c, raw_u, raw_s, cf, uf, sf, u1, u2, fine, gf, df,
    c1, f1, e1, e1b, pe2, mid, w1, g1, d1, r1, c2, f2, e2, e2b, deep, g2, pe1,
    stage_f, stage_r, other_f, other_r, *rest,
):
    post, local_sem, send_sem, recv_sem = rest[:-3], rest[-3], rest[-2], rest[-1]
    me = lax.axis_index("box")
    a, j = me // 8, me % 8
    half = me % 2
    sibling = me + 1 - 2 * half
    zero = me // 1024
    loop = functools.partial(planes_loop, base=zero)
    across = {da: ((a + da + 16) % 16) * 8 for da in (-1, 0, 1)}
    along = {dj: (j + dj + 8) % 8 for dj in (-2, -1, 0, 1, 2)}

    def device(da, dj):
        return across[da] + along[dj]

    numbers = iter(range(ROUNDS))
    leaving = []

    def describe(src, dst, number, target):
        return pltpu.make_async_remote_copy(
            src_ref=src, dst_ref=dst, send_sem=send_sem.at[number], recv_sem=recv_sem.at[number],
            device_id=(target,), device_id_type=pl.DeviceIdType.MESH,
        )

    def start(copies, whole):
        number = next(numbers)
        for src, dst, target in copies:
            describe(src, dst, number, target).start()
        everything = describe(whole, whole, number, sibling)
        leaving.append(everything.wait_send)
        return everything.wait_recv

    def drain():
        while leaving:
            leaving.pop(0)()

    raws = (raw_c, raw_s, raw_u)
    given = (conductance, source, initial)
    mine = pl.ds(pl.multiple_of(512 * half, 512), 512)
    theirs = pl.ds(pl.multiple_of(512 - 512 * half, 512), 512)
    held = pl.ds(3 * half, 3)
    locals_ = [pltpu.make_async_copy(counts, owners, local_sem.at[3])]
    for number in range(3):
        locals_.append(
            pltpu.make_async_copy(
                given[number].at[pl.ds(0, 3), :, mine], raws[number].at[held], local_sem.at[number]
            )
        )
    for copy in locals_:
        copy.start()

    barrier = pltpu.get_barrier_semaphore()
    for da, dj in FULL + FAR:
        pl.semaphore_signal(
            barrier, inc=1, device_id=(device(da, dj),), device_id_type=pl.DeviceIdType.MESH
        )
    pl.semaphore_wait(barrier, len(FULL + FAR))

    swaps = [
        start(
            [(given[number].at[pl.ds(0, 3), :, theirs], raws[number].at[held], sibling)],
            raws[number].at[held],
        )
        for number in range(3)
    ]
    locals_[0].wait()
    split = owners[me - half]
    own = jnp.where(half == 0, split, 4 - split)
    for s in range(4):
        out_held[s] = jnp.where(s < own, jnp.ones((32, 1024), F32), 0.0)
    places = [jnp.where(p < split, p, jnp.clip(3 + p - split, 0, 5)) for p in range(4)]

    def bring(number, ref):
        locals_[1 + number].wait()
        swaps[number]()
        raw = raws[number]

        def step(t):
            rows = pl.ds(pl.multiple_of(8 * t, 8), 8)
            out = []
            for q in range(4):
                four = [raw[places[p], rows, 128 * q : 128 * q + 128] for p in range(4)]
                for i, value in enumerate(transposed(four)):
                    out.append((ref, at(pl.multiple_of((4 + 4 * q + i) * RF + 8 + 8 * t, 8), 8), value))
            return out

        loop(0, 4, 4, step, group=1)

    ROWS = (RF, R1)
    OWN = ((4, 16, 8, 32), (8, 8, 8, 16))

    def near(first, count, side, depth):
        return first - 1 + depth if side < 0 else first + count - depth

    def far(first, count, side, depth):
        return first + count - 1 + depth if side < 0 else first - depth

    own2 = R2 + 2 * R2 + 8

    def there2(da, dj):
        return R2 + R2 * (2 - dj) + 8 * (1 - da)

    def pieces(strips, corners, block, da, dj, pick):
        out = []
        if block is not None:
            out.append((block, own2 if pick is near else there2(da, dj), 8, 1))
        if da == 0:
            for ref, level, depths in strips:
                plane, planes, row, rows = OWN[level]
                for d in depths:
                    out.append((ref, pick(plane, planes, dj, d) * ROWS[level] + row, rows, 1))
        elif dj == 0:
            for ref, level, depths in strips:
                plane, planes, row, rows = OWN[level]
                for d in depths:
                    out.append(
                        (ref, plane * ROWS[level] + pick(row, rows, da, d), planes, ROWS[level])
                    )
        else:
            for ref, level, depth, low, count in corners:
                plane, planes, row, rows = OWN[level]
                ends = [pick(row, rows, da, d) for d in (low, low + count - 1)]
                out.append((ref, pick(plane, planes, dj, depth) * ROWS[level] + min(ends), count, 1))
        return out

    def slab(ref, first, count, stride):
        return (pl.ds(first, count, stride=stride) if stride > 1 else pl.ds(first, count)), slice(None)

    spare = list(post)

    def exchange(strips, corners, block=None, where=FULL):
        out, got = spare.pop(0), spare.pop(0)
        copies, filled = [], []
        offset = 0
        for da, dj in where:
            first_row = offset
            for ref, first, count, stride in pieces(strips, corners, block, da, dj, near):
                out[pl.ds(offset, count), :] = ref[slab(ref, first, count, stride)]
                offset += count
            offset += -offset % 8
            rows = pl.ds(first_row, offset - first_row)
            copies.append((out.at[rows], got.at[rows], device(da, dj)))
            filled.append((first_row, da, dj))
        assert out.shape == (offset, LANES)
        arrived = start(copies, got)

        def land():
            arrived()
            for offset, da, dj in filled:
                for ref, first, count, stride in pieces(strips, corners, block, da, dj, far):
                    ref[slab(ref, first, count, stride)] = got[pl.ds(offset, count), :]
                    offset += count

        return land

    def fine_corner(ref, depth):
        return [(ref, 0, d, 1, depth - d) for d in range(1, depth)]

    bring(0, cf)
    bring(1, sf)
    land_c = exchange(
        ((cf, 0, (1, 2, 3)), (sf, 0, (1, 2))), fine_corner(cf, 3) + fine_corner(sf, 2)
    )
    bring(2, uf)
    land_u = exchange(((uf, 0, (1, 2, 3)),), fine_corner(uf, 3))

    def coarse_c(i):
        total = pair_rows(cf, (4 + 2 * i) * RF + 8, 16, RF)
        return [(c1, at(pl.multiple_of((8 + i) * R1 + 8, 8), 16), pair_lanes(total, 1))]

    loop(0, 8, 8, coarse_c)

    def packed(ref):
        lanes = lane_ids(8) % 4
        total = jnp.zeros((8, LANES), F32)
        for i in range(4):
            value = pair_lanes(pair_rows(ref, (8 + 2 * i) * R1 + 8, 8, R1), 2)
            total = total + jnp.where(lanes == i, value, 0.0)
        return total

    def blocks2(ref, where):
        copies = [
            (ref.at[pl.ds(own2, 8)], ref.at[pl.ds(there2(da, dj), 8)], device(da, dj))
            for da, dj in where
        ]
        return start(copies, ref.at[pl.ds(0, 8 * len(where))])

    c2[pl.ds(own2, 8), :] = packed(c1)
    land_c1 = exchange(((c1, 1, (1, 2, 3, 4, 5, 6)),), (), c2, ((1, 0), (-1, 0)))

    land_c()

    def edges(ref, first, side, count, rows, plane, row, low_y, high_y, low_x, high_x):
        for outside, there, here in (
            (low_y, plane - 1, plane), (high_y, plane + count, plane + count - 1)
        ):
            slab_there = at(there * rows + first, side)
            ref[slab_there] = jnp.where(outside, ref[at(here * rows + first, side)], ref[slab_there])
        lines = 24
        for outside, there, here in ((low_x, row[0] - 1, row[0]), (high_x, row[1] + 1, row[1])):
            slab_there = slab(ref, there, lines, rows)
            ref[slab_there] = jnp.where(outside, ref[slab(ref, here, lines, rows)], ref[slab_there])

    def cut(faces, first, side, count, rows, plane, row, low_y, high_y, low_x, high_x):
        for n, outside, here in ((0, low_y, plane), (1, high_y, plane + count - 1)):
            where = (n,) + at(here * rows + first, side)
            faces[where] = jnp.where(outside, 0.0, faces[where])
        for n, outside, here in ((2, low_x, row[0]), (3, high_x, row[1])):
            where = (n,) + slab(faces, here, 24, rows)
            faces[where] = jnp.where(outside, 0.0, faces[where])

    ends = (j == 0, j == 7, a == 0, a == 15)
    edges(cf, 4, 40, 16, RF, 4, (8, 39), *ends)
    fine_faces = [fine.at[n] for n in range(6)]

    def fine_coeffs(p):
        base = p * RF + 4
        centre, besides = around(cf, base, 40, RF, 1)
        z = lane_ids(40)
        inside = (None, None, None, None, z != 0, z != 127)
        faces, total, quarter = coefficients(centre, besides, inside)
        out = [(fine, (n,) + at(base, 40), faces[n]) for n in range(6)]
        out.append((gf, at(base, 40), 2.0 * quarter))
        out.append((df, at(base, 40), 1.25 * total))
        return out

    loop(2, 22, 4, fine_coeffs, group=1)
    cut(fine, 4, 40, 16, RF, 4, (8, 39), *ends)
    land_u()

    def sweep(src, dst, faces, right, low, high, width, rows, start, count, twist):
        def step(p):
            base = p * rows + start
            centre, besides = around(src, base, count, rows, twist)
            value = 0.2 * centre + right[pl.ds(base, count), :] + weighted(faces, base, count, besides)
            return [(dst, at(base, count), value)]

        loop(low, high, width, step, group=5)

    def leftover(src, dst, faces, right, diag, low, high, width, rows, start, count, twist):
        def step(p):
            base = p * rows + start
            centre, besides = around(src, base, count, rows, twist)
            value = diag[pl.ds(base, count), :] * (
                right[pl.ds(base, count), :] + weighted(faces, base, count, besides) - 0.8 * centre
            )
            return [(dst, at(base, count), value)]

        loop(low, high, width, step, group=4)

    def first_sweep(p):
        base = p * RF + 4
        centre, besides = around(uf, base, 40, RF, 1)
        right = gf[pl.ds(base, 40), :] * sf[pl.ds(base, 40), :]
        value = 0.2 * centre + right + weighted(fine_faces, base, 40, besides)
        return [(u1, at(base, 40), value), (gf, at(base, 40), right)]

    loop(2, 22, 10, first_sweep, group=5)

    land_c1()
    third = [
        start(
            [
                (c1.at[pl.ds(8 * R1, 6 * R1)], c1.at[pl.ds(16 * R1, 6 * R1)], device(0, -1)),
                (c1.at[pl.ds(10 * R1, 6 * R1)], c1.at[pl.ds(2 * R1, 6 * R1)], device(0, 1)),
            ],
            c1.at[pl.ds(0, 12 * R1)],
        ),
        start(
            [
                (c2.at[pl.ds(3 * R2, R2)], c2.at[pl.ds(R2 * (3 - dj), R2)], device(0, dj))
                for dj in (2, -2, 1, -1)
            ],
            c2.at[pl.ds(0, 4 * R2)],
        ),
    ]
    sweep(u1, u2, fine_faces, gf, 3, 21, 9, RF, 4, 40, 1)
    leftover(u2, u1, fine_faces, gf, df, 4, 20, 8, RF, 8, 32, 1)

    def coarse_f(i):
        total = pair_rows(u1, (4 + 2 * i) * RF + 8, 16, RF)
        return [(f1, at(pl.multiple_of((8 + i) * R1 + 8, 8), 16), pair_lanes(total, 1))]

    loop(0, 8, 8, coarse_f)
    land_f = exchange(((f1, 1, (1, 2)),), [(f1, 1, 1, 1, 1)])
    land_rest = exchange(
        ((f1, 1, (3, 4, 5)), (u2, 0, (1, 2, 3))),
        [(f1, 1, 1, 2, 3), (f1, 1, 2, 1, 3), (f1, 1, 3, 1, 2), (f1, 1, 4, 1, 1)] + fine_corner(u2, 3),
    )

    drain()
    third[0]()
    edges(c1, 0, 32, 8, R1, 8, (8, 23), *ends)
    mid_faces = [mid.at[n] for n in range(6)]

    def mid_coeffs(p):
        base = p * R1
        centre, besides = around(c1, base, 32, R1, 2)
        z = lane_ids(32)
        inside = (None, None, None, None, z >= 2, z < 126)
        faces, total, quarter = coefficients(centre, besides, inside)
        out = [(mid, (n,) + at(base, 32), faces[n]) for n in range(6)]
        out.append((w1, at(base, 32), 8.0 * quarter))
        out.append((d1, at(base, 32), 0.3125 * total))
        return out

    loop(3, 21, 3, mid_coeffs, group=1)
    cut(mid, 0, 32, 8, R1, 8, (8, 23), *ends)

    third[1]()

    def around2(ref):
        lanes = lane_ids(5 * R2) % 4
        centre = ref[R2 : 6 * R2, :]
        return centre, (
            jnp.where(lanes == 0, turn(ref[0 : 5 * R2, :], -3), turn(centre, 1)),
            jnp.where(lanes == 3, turn(ref[2 * R2 : 7 * R2, :], 3), turn(centre, -1)),
            ref[pl.ds(zero + (R2 - 1), 5 * R2), :],
            ref[pl.ds(zero + (R2 + 1), 5 * R2), :],
            turn(centre, 4),
            turn(centre, -4),
        )

    rows2, lanes2 = row_ids(5 * R2), lane_ids(5 * R2)
    x = rows2 % R2 + (8 * a - 8)
    y = 4 * (rows2 // R2) + lanes2 % 4 + (4 * j - 8)
    inside2 = (y != 0, y != 31, x != 0, x != 127, lanes2 >= 4, lanes2 < 124)
    centre, besides = around2(c2)
    faces, total, quarter = coefficients(centre, besides, inside2)
    for n in range(6):
        deep[n] = faces[n]
    deep[6] = 32.0 * quarter

    def guess(p):
        base = p * R1
        return [(g1, at(base, 32), w1[pl.ds(base, 32), :] * f1[pl.ds(base, 32), :])]

    land_f()
    loop(6, 18, 12, guess)
    sweep(g1, e1, mid_faces, g1, 7, 17, 10, R1, 4, 24, 2)
    leftover(e1, r1, mid_faces, g1, d1, 8, 16, 8, R1, 8, 16, 2)
    f2[pl.ds(own2, 8), :] = packed(r1)
    sixth = blocks2(f2, FAR + FULL)

    land_rest()
    loop(3, 21, 9, guess)
    sweep(g1, e1, mid_faces, g1, 4, 20, 8, R1, 4, 24, 2)

    drain()
    sixth()
    g2[...] = deep[6] * f2[R2 : 6 * R2, :]
    e2[R2 : 6 * R2, :] = g2[...]
    for src, dst in ((e2, e2b), (e2b, e2), (e2, e2b)):
        centre, besides = around2(src)
        parts = [deep[n] * besides[n] for n in range(6)]
        dst[R2 : 6 * R2, :] = (
            (0.2 * centre + g2[...]) + (parts[0] + parts[1]) + (parts[2] + parts[3]) + (parts[4] + parts[5])
        )

    lanes16 = lane_ids(16) % 4
    hops = ((1, 2), (-1, 2), (1, -2), (-1, -2))
    for number in range(8):
        block, i = (number + 6) // 4, (number + 6) % 4
        value = jnp.where(lanes16 == i, e2b[pl.ds(zero + (R2 + R2 * block + 4), 16), :], 0.0)
        value = value + turn(value, hops[i][0])
        value = value + turn(value, hops[i][1])
        pe2[pl.ds(32 * number, 16, stride=2), :] = value
        pe2[pl.ds(32 * number + 1, 16, stride=2), :] = value

    def corrected1(p):
        value = e1[pl.ds(p * R1 + 4, 24), :] + pe2[pl.ds((p // 2 - 2) * 32 + 4, 24), :]
        return [(e1, at(p * R1 + 4, 24), value)]

    loop(4, 20, 16, corrected1)
    sweep(e1, e1b, mid_faces, g1, 5, 19, 14, R1, 4, 24, 2)
    sweep(e1b, e1, mid_faces, g1, 6, 18, 12, R1, 4, 24, 2)

    def grown(i):
        value = e1[pl.ds((i + 6) * R1 + 4, 24), :]
        return [(pe1, (pl.ds(RF * i + odd, 24, stride=2), slice(None)), value) for odd in (0, 1)]

    loop(0, 12, 12, grown)

    def corrected0(p):
        base = p * RF + 4
        return [(u2, at(base, 40), u2[pl.ds(base, 40), :] + pe1[pl.ds((p // 2) * RF + 4, 40), :])]

    loop(1, 23, 11, corrected0)
    sweep(u2, u1, fine_faces, gf, 2, 22, 10, RF, 4, 40, 1)

    def give(ref, stage, other, quads):
        def step(t):
            rows = pl.ds(pl.multiple_of(8 * t, 8), 8)
            out = []
            for q in quads:
                four = [
                    ref[pl.ds(pl.multiple_of((4 + 4 * q + i) * RF + 8 + 8 * t, 8), 8), :]
                    for i in range(4)
                ]
                for p, value in enumerate(transposed(four)):
                    out.append((stage, (p, rows, slice(128 * q, 128 * q + 128)), value))
            return out

        loop(0, 4, 4, step)
        lanes = pl.ds(128 * quads[0], 128 * len(quads))
        return stage.at[pl.ds(1 - half, 3), :, lanes], other.at[:, :, lanes], sibling

    def keep(stage, out):
        for s in range(4):
            out[s, :, mine] = stage[jnp.clip(s + half * split, 0, 3)]

    def take(other, out):
        for s in range(4):
            out[s, :, theirs] = other[jnp.clip(s + half * (split - 1), 0, 2)]

    last = []
    sweep(u1, u2, fine_faces, gf, 3, 12, 9, RF, 4, 40, 1)
    last.append(start([give(u2, stage_f, other_f, (0, 1))], other_f.at[:, :, pl.ds(0, 256)]))
    sweep(u1, u2, fine_faces, gf, 12, 21, 9, RF, 4, 40, 1)
    last.append(start([give(u2, stage_f, other_f, (2, 3))], other_f.at[:, :, pl.ds(256, 256)]))
    leftover(u2, u1, fine_faces, gf, df, 4, 12, 8, RF, 8, 32, 1)
    last.append(start([give(u1, stage_r, other_r, (0, 1))], other_r.at[:, :, pl.ds(0, 256)]))
    leftover(u2, u1, fine_faces, gf, df, 12, 20, 8, RF, 8, 32, 1)
    last.append(start([give(u1, stage_r, other_r, (2, 3))], other_r.at[:, :, pl.ds(256, 256)]))
    keep(stage_f, out_field)
    last[0]()
    last[1]()
    take(other_f, out_field)
    keep(stage_r, out_resid)
    last[2]()
    last[3]()
    take(other_r, out_resid)
    drain()


def vmem(*shape):
    return pltpu.VMEM(shape, F32)


def body(source, conductance, initial, box_counts):
    fine_field = vmem(PF * RF, LANES)
    mid_field = vmem(P1 * R1, LANES)
    deep_field = vmem(7 * R2, LANES)
    scratch = [pltpu.SMEM(box_counts.shape, jnp.int32)] + [vmem(6, 32, 512)] * 3
    scratch += [fine_field] * 5 + [vmem(6, PF * RF, LANES)] + [fine_field] * 2
    scratch += [mid_field] * 4 + [vmem(8 * 32, LANES), vmem(6, P1 * R1, LANES)] + [mid_field] * 4
    scratch += [deep_field] * 4 + [vmem(7, 5 * R2, LANES), vmem(5 * R2, LANES), vmem(12 * RF, LANES)]
    scratch += [vmem(4, 32, 512)] * 2 + [vmem(3, 32, 512)] * 2
    for big, middle, small in ((160, 80, 8), (96, 48, 8), (0, 56, 0), (32, 16, 8), (144, 72, 16)):
        scratch += [vmem(2 * big + 2 * middle + 4 * small, LANES)] * 2
    scratch += [pltpu.SemaphoreType.DMA((4,))] + [pltpu.SemaphoreType.DMA((ROUNDS,))] * 2
    hbm = pl.BlockSpec(memory_space=pltpu.HBM)
    shape = jax.ShapeDtypeStruct(source.shape, source.dtype)
    field, resid, held = pl.pallas_call(
        kernel,
        out_shape=(shape,) * 3,
        in_specs=[hbm] * 4,
        out_specs=(pl.BlockSpec(memory_space=pltpu.VMEM),) * 3,
        scratch_shapes=scratch,
        compiler_params=pltpu.CompilerParams(
            collective_id=0, has_side_effects=True, vmem_limit_bytes=40 * 2**20
        ),
        cost_estimate=pl.CostEstimate(flops=3 * 10**7, bytes_accessed=3 * 10**6, transcendentals=0),
    )(*[pltpu.with_memory_space_constraint(x, pltpu.HBM) for x in (box_counts, source, conductance, initial)])
    return field * held, resid * held


def solution(mesh):
    return jax.shard_map(
        body,
        mesh=mesh,
        in_specs=(P("box", None, None), P("box", None, None), P("box", None, None), P()),
        out_specs=(P("box", None, None), P("box", None, None)),
        check_vma=False,
    )
```

```python
import functools

import jax
import jax.numpy as jnp
from jax import lax
from jax.experimental import pallas as pl
from jax.experimental.pallas import tpu as pltpu
from jax.sharding import PartitionSpec as P


RF, PF = 48, 24
R1, P1 = 32, 24
R2 = 24
LANES = 128
FULL = (1, 1), (1, -1), (-1, 1), (-1, -1), (1, 0), (-1, 0), (0, 1), (0, -1)
FAR = (1, 2), (1, -2), (-1, 2), (-1, -2), (0, 2), (0, -2)
F32 = jnp.float32
ROUNDS = 3 + 5 + 2 + 4


def lane_ids(rows):
    return lax.broadcasted_iota(jnp.int32, (rows, LANES), 1)


def row_ids(rows):
    return lax.broadcasted_iota(jnp.int32, (rows, LANES), 0)


def turn(value, steps):
    return pltpu.roll(value, steps % LANES, 1)


def transposed(four):
    lanes = lane_ids(four[0].shape[0])
    low = lanes < 64
    even = (lanes // 32) % 2 == 0
    a, b, c, d = four
    e = jnp.where(low, a, turn(c, 64))
    f = jnp.where(low, b, turn(d, 64))
    g = jnp.where(low, turn(a, 64), c)
    h = jnp.where(low, turn(b, 64), d)
    return (
        jnp.where(even, e, turn(f, 32)),
        jnp.where(even, turn(e, -32), f),
        jnp.where(even, g, turn(h, 32)),
        jnp.where(even, turn(g, -32), h),
    )


def coefficients(c, besides, inside):
    around_ = [
        beside if within is None else jnp.where(within, beside, c)
        for beside, within in zip(besides, inside)
    ]
    total = 3.0 * c + 0.5 * (
        (around_[0] + around_[1]) + (around_[2] + around_[3]) + (around_[4] + around_[5])
    )
    quarter = 0.4 / total
    faces = [
        (c + beside) * quarter if within is None else jnp.where(within, (c + beside) * quarter, 0.0)
        for beside, within in zip(besides, inside)
    ]
    return faces, total, quarter


def around(ref, base, count, rows, twist):
    centre = ref[pl.ds(base, count), :]
    return centre, (
        ref[pl.ds(base - rows, count), :],
        ref[pl.ds(base + rows, count), :],
        ref[pl.ds(base - 1, count), :],
        ref[pl.ds(base + 1, count), :],
        turn(centre, twist),
        turn(centre, -twist),
    )


def weighted(faces, base, count, besides):
    parts = [faces[n][pl.ds(base, count), :] * besides[n] for n in range(6)]
    return (parts[0] + parts[1]) + (parts[2] + parts[3]) + (parts[4] + parts[5])


def planes_loop(low, high, width, body, group=None, base=0):
    assert (high - low) % width == 0
    group = group or width

    def step(index, carry):
        first = base + low + index * width
        stores = []
        for m in range(width):
            stores += body(first + m)
            if (m + 1) % group == 0 or m == width - 1:
                for ref, index_, value in stores:
                    ref[index_] = value
                stores = []
        return carry

    if high - low == width:
        step(0, 0)
    else:
        lax.fori_loop(0, (high - low) // width, step, 0)


def at(base, count):
    return pl.ds(base, count), slice(None)


def pair_rows(ref, base, count, rows):
    got = [
        ref[pl.ds(base + offset, count, stride=2), :] for offset in (0, 1, rows, rows + 1)
    ]
    return (got[0] + got[1]) + (got[2] + got[3])


def pair_lanes(value, width):
    first = (lane_ids(value.shape[0]) // width) % 2 == 0
    return 0.125 * (value + jnp.where(first, turn(value, -width), turn(value, width)))


def kernel(
    counts, source, conductance, initial, out_field, out_resid, out_held,
    owners, raw_c, raw_u, raw_s, cf, uf, sf, u1, u2, fine, gf, df,
    c1, f1, e1, e1b, pe2, mid, w1, g1, d1, r1, c2, f2, e2, e2b, deep, g2, pe1,
    stage_f, stage_r, other_f, other_r, *rest,
):
    post, local_sem, send_sem, recv_sem = rest[:-3], rest[-3], rest[-2], rest[-1]
    me = lax.axis_index("box")
    a, j = me // 8, me % 8
    half = me % 2
    sibling = me + 1 - 2 * half
    zero = me // 1024
    loop = functools.partial(planes_loop, base=zero)
    across = {da: ((a + da + 16) % 16) * 8 for da in (-1, 0, 1)}
    along = {dj: (j + dj + 8) % 8 for dj in (-2, -1, 0, 1, 2)}

    def device(da, dj):
        return across[da] + along[dj]

    numbers = iter(range(ROUNDS))
    leaving = []

    def describe(src, dst, number, target):
        return pltpu.make_async_remote_copy(
            src_ref=src, dst_ref=dst, send_sem=send_sem.at[number], recv_sem=recv_sem.at[number],
            device_id=(target,), device_id_type=pl.DeviceIdType.MESH,
        )

    def start(copies, whole):
        number = next(numbers)
        for src, dst, target in copies:
            describe(src, dst, number, target).start()
        everything = describe(whole, whole, number, sibling)
        leaving.append(everything.wait_send)
        return everything.wait_recv

    def drain():
        while leaving:
            leaving.pop(0)()

    raws = (raw_c, raw_s, raw_u)
    given = (conductance, source, initial)
    mine = pl.ds(pl.multiple_of(512 * half, 512), 512)
    theirs = pl.ds(pl.multiple_of(512 - 512 * half, 512), 512)
    held = pl.ds(3 * half, 3)
    locals_ = [pltpu.make_async_copy(counts, owners, local_sem.at[3])]
    for number in range(3):
        locals_.append(
            pltpu.make_async_copy(
                given[number].at[pl.ds(0, 3), :, mine], raws[number].at[held], local_sem.at[number]
            )
        )
    for copy in locals_:
        copy.start()

    barrier = pltpu.get_barrier_semaphore()
    for da, dj in FULL[::-1] + FAR:
        pl.semaphore_signal(
            barrier, inc=1, device_id=(device(da, dj),), device_id_type=pl.DeviceIdType.MESH
        )
    pl.semaphore_wait(barrier, len(FULL + FAR))

    swaps = [
        start(
            [(given[number].at[pl.ds(0, 3), :, theirs], raws[number].at[held], sibling)],
            raws[number].at[held],
        )
        for number in range(3)
    ]
    locals_[0].wait()
    split = owners[me - half]
    own = jnp.where(half == 0, split, 4 - split)
    for s in range(4):
        out_held[s] = jnp.where(s < own, jnp.ones((32, 1024), F32), 0.0)
    places = [jnp.where(p < split, p, jnp.clip(3 + p - split, 0, 5)) for p in range(4)]

    def bring(number, ref):
        locals_[1 + number].wait()
        swaps[number]()
        raw = raws[number]

        def step(t):
            rows = pl.ds(pl.multiple_of(8 * t, 8), 8)
            out = []
            for q in range(4):
                four = [raw[places[p], rows, 128 * q : 128 * q + 128] for p in range(4)]
                for i, value in enumerate(transposed(four)):
                    out.append((ref, at(pl.multiple_of((4 + 4 * q + i) * RF + 8 + 8 * t, 8), 8), value))
            return out

        loop(0, 4, 4, step, group=1)

    ROWS = (RF, R1)
    OWN = ((4, 16, 8, 32), (8, 8, 8, 16))

    def near(first, count, side, depth):
        return first - 1 + depth if side < 0 else first + count - depth

    def far(first, count, side, depth):
        return first + count - 1 + depth if side < 0 else first - depth

    own2 = R2 + 2 * R2 + 8

    def there2(da, dj):
        return R2 + R2 * (2 - dj) + 8 * (1 - da)

    def pieces(strips, corners, block, da, dj, pick):
        out = []
        if block is not None:
            out.append((block, own2 if pick is near else there2(da, dj), 8, 1))
        if da == 0:
            for ref, level, depths in strips:
                plane, planes, row, rows = OWN[level]
                for d in depths:
                    out.append((ref, pick(plane, planes, dj, d) * ROWS[level] + row, rows, 1))
        elif dj == 0:
            for ref, level, depths in strips:
                plane, planes, row, rows = OWN[level]
                for d in depths:
                    out.append(
                        (ref, plane * ROWS[level] + pick(row, rows, da, d), planes, ROWS[level])
                    )
        else:
            for ref, level, depth, low, count in corners:
                plane, planes, row, rows = OWN[level]
                ends = [pick(row, rows, da, d) for d in (low, low + count - 1)]
                out.append((ref, pick(plane, planes, dj, depth) * ROWS[level] + min(ends), count, 1))
        return out

    def slab(ref, first, count, stride):
        return (pl.ds(first, count, stride=stride) if stride > 1 else pl.ds(first, count)), slice(None)

    spare = list(post)

    def exchange(strips, corners, block=None, where=FULL):
        out, got = spare.pop(0), spare.pop(0)
        copies, filled = [], []
        offset = 0
        for da, dj in where:
            first_row = offset
            for ref, first, count, stride in pieces(strips, corners, block, da, dj, near):
                out[pl.ds(offset, count), :] = ref[slab(ref, first, count, stride)]
                offset += count
            offset += -offset % 8
            rows = pl.ds(first_row, offset - first_row)
            copies.append((out.at[rows], got.at[rows], device(da, dj)))
            filled.append((first_row, da, dj))
        assert out.shape == (offset, LANES)
        arrived = start(copies, got)

        def land():
            arrived()
            for offset, da, dj in filled:
                for ref, first, count, stride in pieces(strips, corners, block, da, dj, far):
                    ref[slab(ref, first, count, stride)] = got[pl.ds(offset, count), :]
                    offset += count

        return land

    def fine_corner(ref, depth):
        return [(ref, 0, d, 1, depth - d) for d in range(1, depth)]

    bring(0, cf)
    bring(1, sf)
    land_c = exchange(
        ((cf, 0, (1, 2, 3)), (sf, 0, (1, 2))), fine_corner(cf, 3) + fine_corner(sf, 2)
    )
    bring(2, uf)
    land_u = exchange(((uf, 0, (1, 2, 3)),), fine_corner(uf, 3))

    def coarse_c(i):
        total = pair_rows(cf, (4 + 2 * i) * RF + 8, 16, RF)
        return [(c1, at(pl.multiple_of((8 + i) * R1 + 8, 8), 16), pair_lanes(total, 1))]

    loop(0, 8, 8, coarse_c)

    def packed(ref):
        lanes = lane_ids(8) % 4
        total = jnp.zeros((8, LANES), F32)
        for i in range(4):
            value = pair_lanes(pair_rows(ref, (8 + 2 * i) * R1 + 8, 8, R1), 2)
            total = total + jnp.where(lanes == i, value, 0.0)
        return total

    def blocks2(ref, where):
        copies = [
            (ref.at[pl.ds(own2, 8)], ref.at[pl.ds(there2(da, dj), 8)], device(da, dj))
            for da, dj in where
        ]
        return start(copies, ref.at[pl.ds(0, 8 * len(where))])

    c2[pl.ds(own2, 8), :] = packed(c1)
    land_c1 = exchange(
        ((c1, 1, (1, 2, 3, 4, 5, 6)),), [(c1, 1, d, 1, 6 - d) for d in range(1, 6)], c2
    )
    far_c2 = blocks2(c2, FAR)

    land_c()

    def edges(ref, first, side, count, rows, plane, row, low_y, high_y, low_x, high_x):
        for outside, there, here in (
            (low_y, plane - 1, plane), (high_y, plane + count, plane + count - 1)
        ):
            slab_there = at(there * rows + first, side)
            ref[slab_there] = jnp.where(outside, ref[at(here * rows + first, side)], ref[slab_there])
        lines = 24
        for outside, there, here in ((low_x, row[0] - 1, row[0]), (high_x, row[1] + 1, row[1])):
            slab_there = slab(ref, there, lines, rows)
            ref[slab_there] = jnp.where(outside, ref[slab(ref, here, lines, rows)], ref[slab_there])

    def cut(faces, first, side, count, rows, plane, row, low_y, high_y, low_x, high_x):
        for n, outside, here in ((0, low_y, plane), (1, high_y, plane + count - 1)):
            where = (n,) + at(here * rows + first, side)
            faces[where] = jnp.where(outside, 0.0, faces[where])
        for n, outside, here in ((2, low_x, row[0]), (3, high_x, row[1])):
            where = (n,) + slab(faces, here, 24, rows)
            faces[where] = jnp.where(outside, 0.0, faces[where])

    ends = (j == 0, j == 7, a == 0, a == 15)
    edges(cf, 4, 40, 16, RF, 4, (8, 39), *ends)
    fine_faces = [fine.at[n] for n in range(6)]

    def fine_coeffs(p):
        base = p * RF + 4
        centre, besides = around(cf, base, 40, RF, 1)
        z = lane_ids(40)
        inside = (None, None, None, None, z != 0, z != 127)
        faces, total, quarter = coefficients(centre, besides, inside)
        out = [(fine, (n,) + at(base, 40), faces[n]) for n in range(6)]
        out.append((gf, at(base, 40), 2.0 * quarter))
        out.append((df, at(base, 40), 1.25 * total))
        return out

    loop(2, 22, 4, fine_coeffs, group=1)
    cut(fine, 4, 40, 16, RF, 4, (8, 39), *ends)
    land_u()

    def sweep(src, dst, faces, right, low, high, width, rows, start, count, twist):
        def step(p):
            base = p * rows + start
            centre, besides = around(src, base, count, rows, twist)
            value = 0.2 * centre + right[pl.ds(base, count), :] + weighted(faces, base, count, besides)
            return [(dst, at(base, count), value)]

        loop(low, high, width, step, group=5)

    def leftover(src, dst, faces, right, diag, low, high, width, rows, start, count, twist):
        def step(p):
            base = p * rows + start
            centre, besides = around(src, base, count, rows, twist)
            value = diag[pl.ds(base, count), :] * (
                right[pl.ds(base, count), :] + weighted(faces, base, count, besides) - 0.8 * centre
            )
            return [(dst, at(base, count), value)]

        loop(low, high, width, step, group=4)

    def first_sweep(p):
        base = p * RF + 4
        centre, besides = around(uf, base, 40, RF, 1)
        right = gf[pl.ds(base, 40), :] * sf[pl.ds(base, 40), :]
        value = 0.2 * centre + right + weighted(fine_faces, base, 40, besides)
        return [(u1, at(base, 40), value), (gf, at(base, 40), right)]

    loop(2, 22, 10, first_sweep, group=5)
    sweep(u1, u2, fine_faces, gf, 3, 21, 9, RF, 4, 40, 1)
    leftover(u2, u1, fine_faces, gf, df, 4, 20, 8, RF, 8, 32, 1)

    def coarse_f(i):
        total = pair_rows(u1, (4 + 2 * i) * RF + 8, 16, RF)
        return [(f1, at(pl.multiple_of((8 + i) * R1 + 8, 8), 16), pair_lanes(total, 1))]

    loop(0, 8, 8, coarse_f)
    land_f = exchange(((f1, 1, (1, 2)),), [(f1, 1, 1, 1, 1)])
    land_rest = exchange(
        ((f1, 1, (3, 4, 5)), (u2, 0, (1, 2, 3))),
        [(f1, 1, 1, 2, 3), (f1, 1, 2, 1, 3), (f1, 1, 3, 1, 2), (f1, 1, 4, 1, 1)] + fine_corner(u2, 3),
    )

    drain()
    land_c1()
    edges(c1, 0, 32, 8, R1, 8, (8, 23), *ends)
    mid_faces = [mid.at[n] for n in range(6)]

    def mid_coeffs(p):
        base = p * R1
        centre, besides = around(c1, base, 32, R1, 2)
        z = lane_ids(32)
        inside = (None, None, None, None, z >= 2, z < 126)
        faces, total, quarter = coefficients(centre, besides, inside)
        out = [(mid, (n,) + at(base, 32), faces[n]) for n in range(6)]
        out.append((w1, at(base, 32), 8.0 * quarter))
        out.append((d1, at(base, 32), 0.3125 * total))
        return out

    loop(6, 18, 3, mid_coeffs, group=1)
    cut(mid, 0, 32, 8, R1, 8, (8, 23), *ends)

    def guess(p):
        base = p * R1
        return [(g1, at(base, 32), w1[pl.ds(base, 32), :] * f1[pl.ds(base, 32), :])]

    land_f()
    loop(6, 18, 12, guess)
    sweep(g1, e1, mid_faces, g1, 7, 17, 10, R1, 4, 24, 2)
    leftover(e1, r1, mid_faces, g1, d1, 8, 16, 8, R1, 8, 16, 2)
    f2[pl.ds(own2, 8), :] = packed(r1)
    sixth = blocks2(f2, FAR + FULL)

    loop(3, 6, 3, mid_coeffs, group=1)
    loop(18, 21, 3, mid_coeffs, group=1)
    cut(mid, 0, 32, 8, R1, 8, (8, 23), *ends)
    far_c2()

    def around2(ref):
        lanes = lane_ids(5 * R2) % 4
        centre = ref[R2 : 6 * R2, :]
        return centre, (
            jnp.where(lanes == 0, turn(ref[0 : 5 * R2, :], -3), turn(centre, 1)),
            jnp.where(lanes == 3, turn(ref[2 * R2 : 7 * R2, :], 3), turn(centre, -1)),
            ref[pl.ds(zero + (R2 - 1), 5 * R2), :],
            ref[pl.ds(zero + (R2 + 1), 5 * R2), :],
            turn(centre, 4),
            turn(centre, -4),
        )

    rows2, lanes2 = row_ids(5 * R2), lane_ids(5 * R2)
    x = rows2 % R2 + (8 * a - 8)
    y = 4 * (rows2 // R2) + lanes2 % 4 + (4 * j - 8)
    inside2 = (y != 0, y != 31, x != 0, x != 127, lanes2 >= 4, lanes2 < 124)
    centre, besides = around2(c2)
    faces, total, quarter = coefficients(centre, besides, inside2)
    for n in range(6):
        deep[n] = faces[n]
    deep[6] = 32.0 * quarter

    drain()
    land_rest()
    loop(3, 21, 9, guess)
    sweep(g1, e1, mid_faces, g1, 4, 20, 8, R1, 4, 24, 2)

    sixth()
    g2[...] = deep[6] * f2[R2 : 6 * R2, :]
    e2[R2 : 6 * R2, :] = g2[...]
    for src, dst in ((e2, e2b), (e2b, e2), (e2, e2b)):
        centre, besides = around2(src)
        parts = [deep[n] * besides[n] for n in range(6)]
        dst[R2 : 6 * R2, :] = (
            (0.2 * centre + g2[...]) + (parts[0] + parts[1]) + (parts[2] + parts[3]) + (parts[4] + parts[5])
        )

    lanes16 = lane_ids(16) % 4
    hops = ((1, 2), (-1, 2), (1, -2), (-1, -2))
    for number in range(8):
        block, i = (number + 6) // 4, (number + 6) % 4
        value = jnp.where(lanes16 == i, e2b[pl.ds(zero + (R2 + R2 * block + 4), 16), :], 0.0)
        value = value + turn(value, hops[i][0])
        value = value + turn(value, hops[i][1])
        pe2[pl.ds(32 * number, 16, stride=2), :] = value
        pe2[pl.ds(32 * number + 1, 16, stride=2), :] = value

    def corrected1(p):
        value = e1[pl.ds(p * R1 + 4, 24), :] + pe2[pl.ds((p // 2 - 2) * 32 + 4, 24), :]
        return [(e1, at(p * R1 + 4, 24), value)]

    loop(4, 20, 16, corrected1)
    sweep(e1, e1b, mid_faces, g1, 5, 19, 14, R1, 4, 24, 2)
    sweep(e1b, e1, mid_faces, g1, 6, 18, 12, R1, 4, 24, 2)

    def grown(i):
        value = e1[pl.ds((i + 6) * R1 + 4, 24), :]
        return [(pe1, (pl.ds(RF * i + odd, 24, stride=2), slice(None)), value) for odd in (0, 1)]

    loop(0, 12, 12, grown)

    def corrected0(p):
        base = p * RF + 4
        return [(u2, at(base, 40), u2[pl.ds(base, 40), :] + pe1[pl.ds((p // 2) * RF + 4, 40), :])]

    loop(1, 23, 11, corrected0)
    sweep(u2, u1, fine_faces, gf, 2, 22, 10, RF, 4, 40, 1)

    def give(ref, stage, other, quads):
        def step(t):
            rows = pl.ds(pl.multiple_of(8 * t, 8), 8)
            out = []
            for q in quads:
                four = [
                    ref[pl.ds(pl.multiple_of((4 + 4 * q + i) * RF + 8 + 8 * t, 8), 8), :]
                    for i in range(4)
                ]
                for p, value in enumerate(transposed(four)):
                    out.append((stage, (p, rows, slice(128 * q, 128 * q + 128)), value))
            return out

        loop(0, 4, 4, step)
        lanes = pl.ds(128 * quads[0], 128 * len(quads))
        return stage.at[pl.ds(1 - half, 3), :, lanes], other.at[:, :, lanes], sibling

    def keep(stage, out):
        for s in range(4):
            out[s, :, mine] = stage[jnp.clip(s + half * split, 0, 3)]

    def take(other, out):
        for s in range(4):
            out[s, :, theirs] = other[jnp.clip(s + half * (split - 1), 0, 2)]

    last = []
    sweep(u1, u2, fine_faces, gf, 3, 12, 9, RF, 4, 40, 1)
    last.append(start([give(u2, stage_f, other_f, (0, 1))], other_f.at[:, :, pl.ds(0, 256)]))
    sweep(u1, u2, fine_faces, gf, 12, 21, 9, RF, 4, 40, 1)
    last.append(start([give(u2, stage_f, other_f, (2, 3))], other_f.at[:, :, pl.ds(256, 256)]))
    leftover(u2, u1, fine_faces, gf, df, 4, 12, 8, RF, 8, 32, 1)
    last.append(start([give(u1, stage_r, other_r, (0, 1))], other_r.at[:, :, pl.ds(0, 256)]))
    leftover(u2, u1, fine_faces, gf, df, 12, 20, 8, RF, 8, 32, 1)
    last.append(start([give(u1, stage_r, other_r, (2, 3))], other_r.at[:, :, pl.ds(256, 256)]))
    keep(stage_f, out_field)
    last[0]()
    last[1]()
    take(other_f, out_field)
    keep(stage_r, out_resid)
    last[2]()
    last[3]()
    take(other_r, out_resid)
    drain()


def vmem(*shape):
    return pltpu.VMEM(shape, F32)


def body(source, conductance, initial, box_counts):
    fine_field = vmem(PF * RF, LANES)
    mid_field = vmem(P1 * R1, LANES)
    deep_field = vmem(7 * R2, LANES)
    scratch = [pltpu.SMEM(box_counts.shape, jnp.int32)] + [vmem(6, 32, 512)] * 3
    scratch += [fine_field] * 5 + [vmem(6, PF * RF, LANES)] + [fine_field] * 2
    scratch += [mid_field] * 4 + [vmem(8 * 32, LANES), vmem(6, P1 * R1, LANES)] + [mid_field] * 4
    scratch += [deep_field] * 4 + [vmem(7, 5 * R2, LANES), vmem(5 * R2, LANES), vmem(12 * RF, LANES)]
    scratch += [vmem(4, 32, 512)] * 2 + [vmem(3, 32, 512)] * 2
    for big, middle, small in ((160, 80, 8), (96, 48, 8), (104, 56, 24), (32, 16, 8), (144, 72, 16)):
        scratch += [vmem(2 * big + 2 * middle + 4 * small, LANES)] * 2
    scratch += [pltpu.SemaphoreType.DMA((4,))] + [pltpu.SemaphoreType.DMA((ROUNDS,))] * 2
    hbm = pl.BlockSpec(memory_space=pltpu.HBM)
    shape = jax.ShapeDtypeStruct(source.shape, source.dtype)
    field, resid, held = pl.pallas_call(
        kernel,
        out_shape=(shape,) * 3,
        in_specs=[hbm] * 4,
        out_specs=(pl.BlockSpec(memory_space=pltpu.VMEM),) * 3,
        scratch_shapes=scratch,
        compiler_params=pltpu.CompilerParams(
            collective_id=0, has_side_effects=True, vmem_limit_bytes=40 * 2**20
        ),
        cost_estimate=pl.CostEstimate(flops=3 * 10**7, bytes_accessed=3 * 10**6, transcendentals=0),
    )(*[pltpu.with_memory_space_constraint(x, pltpu.HBM) for x in (box_counts, source, conductance, initial)])
    return field * held, resid * held


def solution(mesh):
    return jax.shard_map(
        body,
        mesh=mesh,
        in_specs=(P("box", None, None), P("box", None, None), P("box", None, None), P()),
        out_specs=(P("box", None, None), P("box", None, None)),
        check_vma=False,
    )
```

```python
import functools

import jax
import jax.numpy as jnp
from jax import lax
from jax.experimental import pallas as pl
from jax.experimental.pallas import tpu as pltpu
from jax.sharding import PartitionSpec as P


RF, PF = 48, 24
R1, P1 = 32, 24
R2 = 24
LANES = 128
FULL = (1, 1), (1, -1), (-1, 1), (-1, -1), (1, 0), (-1, 0), (0, 1), (0, -1)
FAR = (1, 2), (1, -2), (-1, 2), (-1, -2), (0, 2), (0, -2)
F32 = jnp.float32
ROUNDS = 3 + 5 + 2 + 4


def lane_ids(rows):
    return lax.broadcasted_iota(jnp.int32, (rows, LANES), 1)


def row_ids(rows):
    return lax.broadcasted_iota(jnp.int32, (rows, LANES), 0)


def turn(value, steps):
    return pltpu.roll(value, steps % LANES, 1)


def transposed(four):
    lanes = lane_ids(four[0].shape[0])
    low = lanes < 64
    even = (lanes // 32) % 2 == 0
    a, b, c, d = four
    e = jnp.where(low, a, turn(c, 64))
    f = jnp.where(low, b, turn(d, 64))
    g = jnp.where(low, turn(a, 64), c)
    h = jnp.where(low, turn(b, 64), d)
    return (
        jnp.where(even, e, turn(f, 32)),
        jnp.where(even, turn(e, -32), f),
        jnp.where(even, g, turn(h, 32)),
        jnp.where(even, turn(g, -32), h),
    )


def coefficients(c, besides, inside):
    around_ = [
        beside if within is None else jnp.where(within, beside, c)
        for beside, within in zip(besides, inside)
    ]
    total = 3.0 * c + 0.5 * (
        (around_[0] + around_[1]) + (around_[2] + around_[3]) + (around_[4] + around_[5])
    )
    quarter = 0.4 / total
    faces = [
        (c + beside) * quarter if within is None else jnp.where(within, (c + beside) * quarter, 0.0)
        for beside, within in zip(besides, inside)
    ]
    return faces, total, quarter


def around(ref, base, count, rows, twist):
    centre = ref[pl.ds(base, count), :]
    return centre, (
        ref[pl.ds(base - rows, count), :],
        ref[pl.ds(base + rows, count), :],
        ref[pl.ds(base - 1, count), :],
        ref[pl.ds(base + 1, count), :],
        turn(centre, twist),
        turn(centre, -twist),
    )


def weighted(faces, base, count, besides):
    parts = [faces[n][pl.ds(base, count), :] * besides[n] for n in range(6)]
    return (parts[0] + parts[1]) + (parts[2] + parts[3]) + (parts[4] + parts[5])


def planes_loop(low, high, width, body, group=None, base=0):
    assert (high - low) % width == 0
    group = group or width

    def step(index, carry):
        first = base + low + index * width
        stores = []
        for m in range(width):
            stores += body(first + m)
            if (m + 1) % group == 0 or m == width - 1:
                for ref, index_, value in stores:
                    ref[index_] = value
                stores = []
        return carry

    if high - low == width:
        step(0, 0)
    else:
        lax.fori_loop(0, (high - low) // width, step, 0)


def at(base, count):
    return pl.ds(base, count), slice(None)


def pair_rows(ref, base, count, rows):
    got = [
        ref[pl.ds(base + offset, count, stride=2), :] for offset in (0, 1, rows, rows + 1)
    ]
    return (got[0] + got[1]) + (got[2] + got[3])


def pair_lanes(value, width):
    first = (lane_ids(value.shape[0]) // width) % 2 == 0
    return 0.125 * (value + jnp.where(first, turn(value, -width), turn(value, width)))


def kernel(
    counts, source, conductance, initial, out_field, out_resid, out_held,
    owners, raw_c, raw_u, raw_s, cf, uf, sf, u1, u2, fine, gf, df,
    c1, f1, e1, e1b, pe2, mid, w1, g1, d1, r1, c2, f2, e2, e2b, deep, g2, pe1,
    stage_f, stage_r, other_f, other_r, *rest,
):
    post, local_sem, send_sem, recv_sem = rest[:-3], rest[-3], rest[-2], rest[-1]
    me = lax.axis_index("box")
    a, j = me // 8, me % 8
    half = me % 2
    sibling = me + 1 - 2 * half
    zero = me // 1024
    loop = functools.partial(planes_loop, base=zero)
    across = {da: ((a + da + 16) % 16) * 8 for da in (-1, 0, 1)}
    along = {dj: (j + dj + 8) % 8 for dj in (-2, -1, 0, 1, 2)}

    sibling_far = across[0] + (j - 1 + 2 * half + 8) % 8

    def device(da, dj):
        return across[da] + along[dj]

    numbers = iter(range(ROUNDS))
    leaving = []

    def describe(src, dst, number, target):
        return pltpu.make_async_remote_copy(
            src_ref=src, dst_ref=dst, send_sem=send_sem.at[number], recv_sem=recv_sem.at[number],
            device_id=(target,), device_id_type=pl.DeviceIdType.MESH,
        )

    def start(copies, whole):
        number = next(numbers)
        for src, dst, target in copies:
            describe(src, dst, number, target).start()
        everything = describe(whole, whole, number, sibling)
        leaving.append(everything.wait_send)
        return everything.wait_recv

    def drain(but=0):
        while len(leaving) > but:
            leaving.pop(0)()

    barrier = pltpu.get_barrier_semaphore()
    for target in (sibling,) + tuple(device(da, dj) for da, dj in FULL[:6]) + (sibling_far,):
        pl.semaphore_signal(barrier, inc=1, device_id=(target,), device_id_type=pl.DeviceIdType.MESH)

    raws = (raw_c, raw_s, raw_u)
    given = (conductance, source, initial)
    mine = pl.ds(pl.multiple_of(512 * half, 512), 512)
    theirs = pl.ds(pl.multiple_of(512 - 512 * half, 512), 512)
    held = pl.ds(3 * half, 3)
    locals_ = [pltpu.make_async_copy(counts, owners, local_sem.at[3])]
    for number in range(3):
        locals_.append(
            pltpu.make_async_copy(
                given[number].at[pl.ds(0, 3), :, mine], raws[number].at[held], local_sem.at[number]
            )
        )
    for copy in locals_:
        copy.start()

    pl.semaphore_wait(barrier, len(FULL))

    swaps = [
        start(
            [(given[number].at[pl.ds(0, 3), :, theirs], raws[number].at[held], sibling)],
            raws[number].at[held],
        )
        for number in range(3)
    ]
    locals_[0].wait()
    split = owners[me - half]
    own = jnp.where(half == 0, split, 4 - split)
    for s in range(4):
        out_held[s] = jnp.where(s < own, jnp.ones((32, 1024), F32), 0.0)
    places = [jnp.where(p < split, p, jnp.clip(3 + p - split, 0, 5)) for p in range(4)]

    def bring(number, ref):
        locals_[1 + number].wait()
        swaps[number]()
        raw = raws[number]

        def step(t):
            rows = pl.ds(pl.multiple_of(8 * t, 8), 8)
            out = []
            for q in range(4):
                four = [raw[places[p], rows, 128 * q : 128 * q + 128] for p in range(4)]
                for i, value in enumerate(transposed(four)):
                    out.append((ref, at(pl.multiple_of((4 + 4 * q + i) * RF + 8 + 8 * t, 8), 8), value))
            return out

        loop(0, 4, 4, step, group=1)

    ROWS = (RF, R1)
    OWN = ((4, 16, 8, 32), (8, 8, 8, 16))

    def near(first, count, side, depth):
        return first - 1 + depth if side < 0 else first + count - depth

    def far(first, count, side, depth):
        return first + count - 1 + depth if side < 0 else first - depth

    own2 = R2 + 2 * R2 + 8

    def there2(da, dj):
        return R2 + R2 * (2 - dj) + 8 * (1 - da)

    def pieces(strips, corners, block, da, dj, pick):
        out = []
        if block is not None:
            out.append((block, own2 if pick is near else there2(da, dj), 8, 1))
        if da == 0:
            for ref, level, depths in strips:
                plane, planes, row, rows = OWN[level]
                for d in depths:
                    out.append((ref, pick(plane, planes, dj, d) * ROWS[level] + row, rows, 1))
        elif dj == 0:
            for ref, level, depths in strips:
                plane, planes, row, rows = OWN[level]
                for d in depths:
                    out.append(
                        (ref, plane * ROWS[level] + pick(row, rows, da, d), planes, ROWS[level])
                    )
        else:
            for ref, level, depth, low, count in corners:
                plane, planes, row, rows = OWN[level]
                ends = [pick(row, rows, da, d) for d in (low, low + count - 1)]
                out.append((ref, pick(plane, planes, dj, depth) * ROWS[level] + min(ends), count, 1))
        return out

    def slab(ref, first, count, stride):
        return (pl.ds(first, count, stride=stride) if stride > 1 else pl.ds(first, count)), slice(None)

    spare = list(post)

    def exchange(strips, corners, block=None, where=FULL):
        out, got = spare.pop(0), spare.pop(0)
        copies, filled = [], []
        offset = 0
        for da, dj in where:
            first_row = offset
            for ref, first, count, stride in pieces(strips, corners, block, da, dj, near):
                out[pl.ds(offset, count), :] = ref[slab(ref, first, count, stride)]
                offset += count
            offset += -offset % 8
            rows = pl.ds(first_row, offset - first_row)
            copies.append((out.at[rows], got.at[rows], device(da, dj)))
            filled.append((first_row, da, dj))
        assert out.shape == (offset, LANES)
        arrived = start(copies, got)

        def land():
            arrived()
            for offset, da, dj in filled:
                for ref, first, count, stride in pieces(strips, corners, block, da, dj, far):
                    ref[slab(ref, first, count, stride)] = got[pl.ds(offset, count), :]
                    offset += count

        return land

    def fine_corner(ref, depth):
        return [(ref, 0, d, 1, depth - d) for d in range(1, depth)]

    bring(0, cf)
    bring(1, sf)
    land_c = exchange(
        ((cf, 0, (1, 2, 3)), (sf, 0, (1, 2))), fine_corner(cf, 3) + fine_corner(sf, 2)
    )
    bring(2, uf)
    land_u = exchange(((uf, 0, (1, 2, 3)),), fine_corner(uf, 3))

    def coarse_c(i):
        total = pair_rows(cf, (4 + 2 * i) * RF + 8, 16, RF)
        return [(c1, at(pl.multiple_of((8 + i) * R1 + 8, 8), 16), pair_lanes(total, 1))]

    loop(0, 8, 8, coarse_c)

    def packed(ref):
        lanes = lane_ids(8) % 4
        total = jnp.zeros((8, LANES), F32)
        for i in range(4):
            value = pair_lanes(pair_rows(ref, (8 + 2 * i) * R1 + 8, 8, R1), 2)
            total = total + jnp.where(lanes == i, value, 0.0)
        return total

    def blocks2(ref, where):
        copies = [
            (ref.at[pl.ds(own2, 8)], ref.at[pl.ds(there2(da, dj), 8)], device(da, dj))
            for da, dj in where
        ]
        return start(copies, ref.at[pl.ds(0, 8 * len(where))])

    c2[pl.ds(own2, 8), :] = packed(c1)
    land_c1 = exchange(
        ((c1, 1, (1, 2, 3, 4, 5, 6)),), [(c1, 1, d, 1, 6 - d) for d in range(1, 6)], c2
    )

    land_c()
    far_c2 = blocks2(c2, FAR)

    def edges(ref, first, side, count, rows, plane, row, low_y, high_y, low_x, high_x):
        for outside, there, here in (
            (low_y, plane - 1, plane), (high_y, plane + count, plane + count - 1)
        ):
            slab_there = at(there * rows + first, side)
            ref[slab_there] = jnp.where(outside, ref[at(here * rows + first, side)], ref[slab_there])
        lines = 24
        for outside, there, here in ((low_x, row[0] - 1, row[0]), (high_x, row[1] + 1, row[1])):
            slab_there = slab(ref, there, lines, rows)
            ref[slab_there] = jnp.where(outside, ref[slab(ref, here, lines, rows)], ref[slab_there])

    def cut(faces, first, side, count, rows, plane, row, low_y, high_y, low_x, high_x):
        for n, outside, here in ((0, low_y, plane), (1, high_y, plane + count - 1)):
            where = (n,) + at(here * rows + first, side)
            faces[where] = jnp.where(outside, 0.0, faces[where])
        for n, outside, here in ((2, low_x, row[0]), (3, high_x, row[1])):
            where = (n,) + slab(faces, here, 24, rows)
            faces[where] = jnp.where(outside, 0.0, faces[where])

    ends = (j == 0, j == 7, a == 0, a == 15)
    edges(cf, 4, 40, 16, RF, 4, (8, 39), *ends)
    fine_faces = [fine.at[n] for n in range(6)]

    def fine_coeffs(p):
        base = p * RF + 4
        centre, besides = around(cf, base, 40, RF, 1)
        z = lane_ids(40)
        inside = (None, None, None, None, z != 0, z != 127)
        faces, total, quarter = coefficients(centre, besides, inside)
        out = [(fine, (n,) + at(base, 40), faces[n]) for n in range(6)]
        out.append((gf, at(base, 40), 2.0 * quarter))
        out.append((df, at(base, 40), 1.25 * total))
        return out

    loop(2, 22, 4, fine_coeffs, group=1)
    cut(fine, 4, 40, 16, RF, 4, (8, 39), *ends)
    land_u()

    def sweep(src, dst, faces, right, low, high, width, rows, start, count, twist):
        def step(p):
            base = p * rows + start
            centre, besides = around(src, base, count, rows, twist)
            value = 0.2 * centre + right[pl.ds(base, count), :] + weighted(faces, base, count, besides)
            return [(dst, at(base, count), value)]

        loop(low, high, width, step, group=5)

    def leftover(src, dst, faces, right, diag, low, high, width, rows, start, count, twist):
        def step(p):
            base = p * rows + start
            centre, besides = around(src, base, count, rows, twist)
            value = diag[pl.ds(base, count), :] * (
                right[pl.ds(base, count), :] + weighted(faces, base, count, besides) - 0.8 * centre
            )
            return [(dst, at(base, count), value)]

        loop(low, high, width, step, group=4)

    def first_sweep(p):
        base = p * RF + 4
        centre, besides = around(uf, base, 40, RF, 1)
        right = gf[pl.ds(base, 40), :] * sf[pl.ds(base, 40), :]
        value = 0.2 * centre + right + weighted(fine_faces, base, 40, besides)
        return [(u1, at(base, 40), value), (gf, at(base, 40), right)]

    loop(2, 22, 10, first_sweep, group=5)
    sweep(u1, u2, fine_faces, gf, 3, 21, 9, RF, 4, 40, 1)
    leftover(u2, u1, fine_faces, gf, df, 4, 20, 8, RF, 8, 32, 1)

    def coarse_f(i):
        total = pair_rows(u1, (4 + 2 * i) * RF + 8, 16, RF)
        return [(f1, at(pl.multiple_of((8 + i) * R1 + 8, 8), 16), pair_lanes(total, 1))]

    loop(0, 8, 8, coarse_f)
    land_f = exchange(((f1, 1, (1, 2)),), [(f1, 1, 1, 1, 1)])
    land_rest = exchange(
        ((f1, 1, (3, 4, 5)), (u2, 0, (1, 2, 3))),
        [(f1, 1, 1, 2, 3), (f1, 1, 2, 1, 3), (f1, 1, 3, 1, 2), (f1, 1, 4, 1, 1)] + fine_corner(u2, 3),
    )

    drain(but=2)
    land_c1()
    edges(c1, 0, 32, 8, R1, 8, (8, 23), *ends)
    mid_faces = [mid.at[n] for n in range(6)]

    def mid_coeffs(p):
        base = p * R1
        centre, besides = around(c1, base, 32, R1, 2)
        z = lane_ids(32)
        inside = (None, None, None, None, z >= 2, z < 126)
        faces, total, quarter = coefficients(centre, besides, inside)
        out = [(mid, (n,) + at(base, 32), faces[n]) for n in range(6)]
        out.append((w1, at(base, 32), 8.0 * quarter))
        out.append((d1, at(base, 32), 0.3125 * total))
        return out

    loop(6, 18, 3, mid_coeffs, group=1)
    cut(mid, 0, 32, 8, R1, 8, (8, 23), *ends)

    def guess(p):
        base = p * R1
        return [(g1, at(base, 32), w1[pl.ds(base, 32), :] * f1[pl.ds(base, 32), :])]

    land_f()
    loop(6, 18, 12, guess)
    sweep(g1, e1, mid_faces, g1, 7, 17, 10, R1, 4, 24, 2)
    leftover(e1, r1, mid_faces, g1, d1, 8, 16, 8, R1, 8, 16, 2)
    f2[pl.ds(own2, 8), :] = packed(r1)
    sixth = blocks2(f2, FAR + FULL)

    loop(3, 6, 3, mid_coeffs, group=1)
    loop(18, 21, 3, mid_coeffs, group=1)
    cut(mid, 0, 32, 8, R1, 8, (8, 23), *ends)
    far_c2()

    def around2(ref):
        lanes = lane_ids(5 * R2) % 4
        centre = ref[R2 : 6 * R2, :]
        return centre, (
            jnp.where(lanes == 0, turn(ref[0 : 5 * R2, :], -3), turn(centre, 1)),
            jnp.where(lanes == 3, turn(ref[2 * R2 : 7 * R2, :], 3), turn(centre, -1)),
            ref[pl.ds(zero + (R2 - 1), 5 * R2), :],
            ref[pl.ds(zero + (R2 + 1), 5 * R2), :],
            turn(centre, 4),
            turn(centre, -4),
        )

    rows2, lanes2 = row_ids(5 * R2), lane_ids(5 * R2)
    x = rows2 % R2 + (8 * a - 8)
    y = 4 * (rows2 // R2) + lanes2 % 4 + (4 * j - 8)
    inside2 = (y != 0, y != 31, x != 0, x != 127, lanes2 >= 4, lanes2 < 124)
    centre, besides = around2(c2)
    faces, total, quarter = coefficients(centre, besides, inside2)
    for n in range(6):
        deep[n] = faces[n]
    deep[6] = 32.0 * quarter

    drain(but=1)
    land_rest()
    loop(3, 21, 9, guess)
    sweep(g1, e1, mid_faces, g1, 4, 20, 8, R1, 4, 24, 2)

    sixth()
    g2[...] = deep[6] * f2[R2 : 6 * R2, :]
    e2[R2 : 6 * R2, :] = g2[...]
    for src, dst in ((e2, e2b), (e2b, e2), (e2, e2b)):
        centre, besides = around2(src)
        parts = [deep[n] * besides[n] for n in range(6)]
        dst[R2 : 6 * R2, :] = (
            (0.2 * centre + g2[...]) + (parts[0] + parts[1]) + (parts[2] + parts[3]) + (parts[4] + parts[5])
        )

    lanes16 = lane_ids(16) % 4
    hops = ((1, 2), (-1, 2), (1, -2), (-1, -2))
    for number in range(8):
        block, i = (number + 6) // 4, (number + 6) % 4
        value = jnp.where(lanes16 == i, e2b[pl.ds(zero + (R2 + R2 * block + 4), 16), :], 0.0)
        value = value + turn(value, hops[i][0])
        value = value + turn(value, hops[i][1])
        pe2[pl.ds(32 * number, 16, stride=2), :] = value
        pe2[pl.ds(32 * number + 1, 16, stride=2), :] = value

    def corrected1(p):
        value = e1[pl.ds(p * R1 + 4, 24), :] + pe2[pl.ds((p // 2 - 2) * 32 + 4, 24), :]
        return [(e1, at(p * R1 + 4, 24), value)]

    loop(4, 20, 16, corrected1)
    sweep(e1, e1b, mid_faces, g1, 5, 19, 14, R1, 4, 24, 2)
    sweep(e1b, e1, mid_faces, g1, 6, 18, 12, R1, 4, 24, 2)

    def grown(i):
        value = e1[pl.ds((i + 6) * R1 + 4, 24), :]
        return [(pe1, (pl.ds(RF * i + odd, 24, stride=2), slice(None)), value) for odd in (0, 1)]

    loop(0, 12, 12, grown)

    def corrected0(p):
        base = p * RF + 4
        return [(u2, at(base, 40), u2[pl.ds(base, 40), :] + pe1[pl.ds((p // 2) * RF + 4, 40), :])]

    loop(1, 23, 11, corrected0)
    sweep(u2, u1, fine_faces, gf, 2, 22, 10, RF, 4, 40, 1)

    def give(ref, stage, other, quads):
        def step(t):
            rows = pl.ds(pl.multiple_of(8 * t, 8), 8)
            out = []
            for q in quads:
                four = [
                    ref[pl.ds(pl.multiple_of((4 + 4 * q + i) * RF + 8 + 8 * t, 8), 8), :]
                    for i in range(4)
                ]
                for p, value in enumerate(transposed(four)):
                    out.append((stage, (p, rows, slice(128 * q, 128 * q + 128)), value))
            return out

        loop(0, 4, 4, step)
        lanes = pl.ds(128 * quads[0], 128 * len(quads))
        return stage.at[pl.ds(1 - half, 3), :, lanes], other.at[:, :, lanes], sibling

    def keep(stage, out):
        for s in range(4):
            out[s, :, mine] = stage[jnp.clip(s + half * split, 0, 3)]

    def take(other, out):
        for s in range(4):
            out[s, :, theirs] = other[jnp.clip(s + half * (split - 1), 0, 2)]

    last = []
    sweep(u1, u2, fine_faces, gf, 3, 12, 9, RF, 4, 40, 1)
    last.append(start([give(u2, stage_f, other_f, (0, 1))], other_f.at[:, :, pl.ds(0, 256)]))
    sweep(u1, u2, fine_faces, gf, 12, 21, 9, RF, 4, 40, 1)
    last.append(start([give(u2, stage_f, other_f, (2, 3))], other_f.at[:, :, pl.ds(256, 256)]))
    leftover(u2, u1, fine_faces, gf, df, 4, 12, 8, RF, 8, 32, 1)
    last.append(start([give(u1, stage_r, other_r, (0, 1))], other_r.at[:, :, pl.ds(0, 256)]))
    leftover(u2, u1, fine_faces, gf, df, 12, 20, 8, RF, 8, 32, 1)
    last.append(start([give(u1, stage_r, other_r, (2, 3))], other_r.at[:, :, pl.ds(256, 256)]))
    keep(stage_f, out_field)
    last[0]()
    last[1]()
    take(other_f, out_field)
    keep(stage_r, out_resid)
    last[2]()
    last[3]()
    take(other_r, out_resid)
    drain()


def vmem(*shape):
    return pltpu.VMEM(shape, F32)


def body(source, conductance, initial, box_counts):
    fine_field = vmem(PF * RF, LANES)
    mid_field = vmem(P1 * R1, LANES)
    deep_field = vmem(7 * R2, LANES)
    scratch = [pltpu.SMEM(box_counts.shape, jnp.int32)] + [vmem(6, 32, 512)] * 3
    scratch += [fine_field] * 5 + [vmem(6, PF * RF, LANES)] + [fine_field] * 2
    scratch += [mid_field] * 4 + [vmem(8 * 32, LANES), vmem(6, P1 * R1, LANES)] + [mid_field] * 4
    scratch += [deep_field] * 4 + [vmem(7, 5 * R2, LANES), vmem(5 * R2, LANES), vmem(12 * RF, LANES)]
    scratch += [vmem(4, 32, 512)] * 2 + [vmem(3, 32, 512)] * 2
    for big, middle, small in ((160, 80, 8), (96, 48, 8), (104, 56, 24), (32, 16, 8), (144, 72, 16)):
        scratch += [vmem(2 * big + 2 * middle + 4 * small, LANES)] * 2
    scratch += [pltpu.SemaphoreType.DMA((4,))] + [pltpu.SemaphoreType.DMA((ROUNDS,))] * 2
    hbm = pl.BlockSpec(memory_space=pltpu.HBM)
    shape = jax.ShapeDtypeStruct(source.shape, source.dtype)
    field, resid, held = pl.pallas_call(
        kernel,
        out_shape=(shape,) * 3,
        in_specs=[hbm] * 4,
        out_specs=(pl.BlockSpec(memory_space=pltpu.VMEM),) * 3,
        scratch_shapes=scratch,
        compiler_params=pltpu.CompilerParams(
            collective_id=0, has_side_effects=True, vmem_limit_bytes=40 * 2**20
        ),
        cost_estimate=pl.CostEstimate(flops=3 * 10**7, bytes_accessed=3 * 10**6, transcendentals=0),
    )(*[pltpu.with_memory_space_constraint(x, pltpu.HBM) for x in (box_counts, source, conductance, initial)])
    return field * held, resid * held


def solution(mesh):
    return jax.shard_map(
        body,
        mesh=mesh,
        in_specs=(P("box", None, None), P("box", None, None), P("box", None, None), P()),
        out_specs=(P("box", None, None), P("box", None, None)),
        check_vma=False,
    )
```

```python
import functools

import jax
import jax.numpy as jnp
from jax import lax
from jax.experimental import pallas as pl
from jax.experimental.pallas import tpu as pltpu
from jax.sharding import PartitionSpec as P


RF, PF = 48, 24
R1, P1 = 32, 24
R2 = 24
LANES = 128
FULL = (1, 1), (1, -1), (-1, 1), (-1, -1), (1, 0), (-1, 0), (0, 1), (0, -1)
FAR = (1, 2), (1, -2), (-1, 2), (-1, -2), (0, 2), (0, -2)
F32 = jnp.float32
ROUNDS = 3 + 5 + 2 + 6


def lane_ids(rows):
    return lax.broadcasted_iota(jnp.int32, (rows, LANES), 1)


def row_ids(rows):
    return lax.broadcasted_iota(jnp.int32, (rows, LANES), 0)


def turn(value, steps):
    return pltpu.roll(value, steps % LANES, 1)


def transposed(four):
    lanes = lane_ids(four[0].shape[0])
    low = lanes < 64
    even = (lanes // 32) % 2 == 0
    a, b, c, d = four
    e = jnp.where(low, a, turn(c, 64))
    f = jnp.where(low, b, turn(d, 64))
    g = jnp.where(low, turn(a, 64), c)
    h = jnp.where(low, turn(b, 64), d)
    return (
        jnp.where(even, e, turn(f, 32)),
        jnp.where(even, turn(e, -32), f),
        jnp.where(even, g, turn(h, 32)),
        jnp.where(even, turn(g, -32), h),
    )


def coefficients(c, besides, inside):
    around_ = [
        beside if within is None else jnp.where(within, beside, c)
        for beside, within in zip(besides, inside)
    ]
    total = 3.0 * c + 0.5 * (
        (around_[0] + around_[1]) + (around_[2] + around_[3]) + (around_[4] + around_[5])
    )
    quarter = 0.4 / total
    faces = [
        (c + beside) * quarter if within is None else jnp.where(within, (c + beside) * quarter, 0.0)
        for beside, within in zip(besides, inside)
    ]
    return faces, total, quarter


class Planes:
    def __init__(self):
        self.held = {}
        self.step = 0

    def load(self, ref, base, count, rows, ahead):
        key = (id(ref), count, self.step + ahead)
        if key not in self.held:
            self.held[key] = ref[pl.ds(base + rows * ahead, count), :]
        return self.held[key]


def around(ref, base, count, rows, twist, planes):
    centre = planes.load(ref, base, count, rows, 0)
    return centre, (
        planes.load(ref, base, count, rows, -1),
        planes.load(ref, base, count, rows, 1),
        ref[pl.ds(base - 1, count), :],
        ref[pl.ds(base + 1, count), :],
        turn(centre, twist),
        turn(centre, -twist),
    )


def weighted(faces, base, count, besides):
    parts = [faces[n][pl.ds(base, count), :] * besides[n] for n in range(6)]
    return (parts[0] + parts[1]) + (parts[2] + parts[3]) + (parts[4] + parts[5])


def planes_loop(low, high, width, body, group=None, base=0):
    assert (high - low) % width == 0
    group = group or width

    def step(index, carry):
        first = base + low + index * width
        stores, planes = [], Planes()
        for m in range(width):
            planes.step = m
            stores += body(first + m, planes)
            if (m + 1) % group == 0 or m == width - 1:
                for ref, index_, value in stores:
                    ref[index_] = value
                stores, planes = [], Planes()
        return carry

    if high - low == width:
        step(0, 0)
    else:
        lax.fori_loop(0, (high - low) // width, step, 0)


def at(base, count):
    return pl.ds(base, count), slice(None)


def pair_rows(ref, base, count, rows):
    got = [
        ref[pl.ds(base + offset, count, stride=2), :] for offset in (0, 1, rows, rows + 1)
    ]
    return (got[0] + got[1]) + (got[2] + got[3])


def pair_lanes(value, width):
    first = (lane_ids(value.shape[0]) // width) % 2 == 0
    return 0.125 * (value + jnp.where(first, turn(value, -width), turn(value, width)))


def kernel(
    counts, source, conductance, initial, out_field, out_resid, out_held,
    owners, raw_c, raw_u, raw_s, cf, uf, sf, u1, u2, fine, gf, df,
    c1, f1, e1, e1b, pe2, mid, w1, g1, d1, r1, c2, f2, e2, e2b, deep, g2, pe1,
    stage_f, stage_r, other_f, other_r, *rest,
):
    post, local_sem, send_sem, recv_sem = rest[:-3], rest[-3], rest[-2], rest[-1]
    me = lax.axis_index("box")
    a, j = me // 8, me % 8
    half = me % 2
    sibling = me + 1 - 2 * half
    zero = me // 1024
    loop = functools.partial(planes_loop, base=zero)
    across = {da: ((a + da + 16) % 16) * 8 for da in (-1, 0, 1)}
    along = {dj: (j + dj + 8) % 8 for dj in (-2, -1, 0, 1, 2)}

    sibling_far = across[0] + (j - 1 + 2 * half + 8) % 8

    def device(da, dj):
        return across[da] + along[dj]

    numbers = iter(range(ROUNDS))
    leaving = []

    def describe(src, dst, number, target):
        return pltpu.make_async_remote_copy(
            src_ref=src, dst_ref=dst, send_sem=send_sem.at[number], recv_sem=recv_sem.at[number],
            device_id=(target,), device_id_type=pl.DeviceIdType.MESH,
        )

    def start(copies, whole):
        number = next(numbers)
        for src, dst, target in copies:
            describe(src, dst, number, target).start()
        everything = describe(whole, whole, number, sibling)
        leaving.append(everything.wait_send)
        return everything.wait_recv

    def drain(but=0):
        while len(leaving) > but:
            leaving.pop(0)()

    barrier = pltpu.get_barrier_semaphore()
    for target in (sibling,) + tuple(device(da, dj) for da, dj in FULL[:6]) + (sibling_far,):
        pl.semaphore_signal(barrier, inc=1, device_id=(target,), device_id_type=pl.DeviceIdType.MESH)

    raws = (raw_c, raw_s, raw_u)
    given = (conductance, source, initial)
    mine = pl.ds(pl.multiple_of(512 * half, 512), 512)
    theirs = pl.ds(pl.multiple_of(512 - 512 * half, 512), 512)
    held = pl.ds(3 * half, 3)
    locals_ = [pltpu.make_async_copy(counts, owners, local_sem.at[3])]
    for number in range(3):
        locals_.append(
            pltpu.make_async_copy(
                given[number].at[pl.ds(0, 3), :, mine], raws[number].at[held], local_sem.at[number]
            )
        )
    for copy in locals_:
        copy.start()

    pl.semaphore_wait(barrier, len(FULL))

    def swap(number):
        return start(
            [(given[number].at[pl.ds(0, 3), :, theirs], raws[number].at[held], sibling)],
            raws[number].at[held],
        )

    swaps = [swap(0), swap(1)]
    locals_[0].wait()
    split = owners[me - half]
    own = jnp.where(half == 0, split, 4 - split)
    for s in range(4):
        out_held[s] = jnp.where(s < own, jnp.ones((32, 1024), F32), 0.0)
    places = [jnp.where(p < split, p, jnp.clip(3 + p - split, 0, 5)) for p in range(4)]

    def bring(number, ref):
        locals_[1 + number].wait()
        swaps[number]()
        if number == 0:
            swaps.append(swap(2))
        raw = raws[number]

        def step(t, planes):
            rows = pl.ds(pl.multiple_of(8 * t, 8), 8)
            out = []
            for q in range(4):
                four = [raw[places[p], rows, 128 * q : 128 * q + 128] for p in range(4)]
                for i, value in enumerate(transposed(four)):
                    out.append((ref, at(pl.multiple_of((4 + 4 * q + i) * RF + 8 + 8 * t, 8), 8), value))
            return out

        loop(0, 4, 4, step, group=1)

    ROWS = (RF, R1)
    OWN = ((4, 16, 8, 32), (8, 8, 8, 16))

    def near(first, count, side, depth):
        return first - 1 + depth if side < 0 else first + count - depth

    def far(first, count, side, depth):
        return first + count - 1 + depth if side < 0 else first - depth

    own2 = R2 + 2 * R2 + 8

    def there2(da, dj):
        return R2 + R2 * (2 - dj) + 8 * (1 - da)

    def pieces(strips, corners, block, da, dj, pick):
        out = []
        if block is not None:
            out.append((block, own2 if pick is near else there2(da, dj), 8, 1))
        if da == 0:
            for ref, level, depths in strips:
                plane, planes, row, rows = OWN[level]
                for d in depths:
                    out.append((ref, pick(plane, planes, dj, d) * ROWS[level] + row, rows, 1))
        elif dj == 0:
            for ref, level, depths in strips:
                plane, planes, row, rows = OWN[level]
                for d in depths:
                    out.append(
                        (ref, plane * ROWS[level] + pick(row, rows, da, d), planes, ROWS[level])
                    )
        else:
            for ref, level, depth, low, count in corners:
                plane, planes, row, rows = OWN[level]
                ends = [pick(row, rows, da, d) for d in (low, low + count - 1)]
                out.append((ref, pick(plane, planes, dj, depth) * ROWS[level] + min(ends), count, 1))
        return out

    def slab(ref, first, count, stride):
        return (pl.ds(first, count, stride=stride) if stride > 1 else pl.ds(first, count)), slice(None)

    spare = list(post)

    def exchange(strips, corners, block=None, where=FULL):
        out, got = spare.pop(0), spare.pop(0)
        copies, filled = [], []
        offset = 0
        for da, dj in where:
            first_row = offset
            for ref, first, count, stride in pieces(strips, corners, block, da, dj, near):
                out[pl.ds(offset, count), :] = ref[slab(ref, first, count, stride)]
                offset += count
            offset += -offset % 8
            rows = pl.ds(first_row, offset - first_row)
            copies.append((out.at[rows], got.at[rows], device(da, dj)))
            filled.append((first_row, da, dj))
        assert out.shape == (offset, LANES)
        arrived = start(copies, got)

        def land():
            arrived()
            for offset, da, dj in filled:
                for ref, first, count, stride in pieces(strips, corners, block, da, dj, far):
                    ref[slab(ref, first, count, stride)] = got[pl.ds(offset, count), :]
                    offset += count

        return land

    def fine_corner(ref, depth):
        return [(ref, 0, d, 1, depth - d) for d in range(1, depth)]

    bring(0, cf)
    bring(1, sf)
    land_c = exchange(
        ((cf, 0, (1, 2, 3)), (sf, 0, (1, 2))), fine_corner(cf, 3) + fine_corner(sf, 2)
    )
    bring(2, uf)
    land_u = exchange(((uf, 0, (1, 2, 3)),), fine_corner(uf, 3))

    def coarse_c(i, planes):
        total = pair_rows(cf, (4 + 2 * i) * RF + 8, 16, RF)
        return [(c1, at(pl.multiple_of((8 + i) * R1 + 8, 8), 16), pair_lanes(total, 1))]

    loop(0, 8, 8, coarse_c)

    def packed(ref):
        lanes = lane_ids(8) % 4
        total = jnp.zeros((8, LANES), F32)
        for i in range(4):
            value = pair_lanes(pair_rows(ref, (8 + 2 * i) * R1 + 8, 8, R1), 2)
            total = total + jnp.where(lanes == i, value, 0.0)
        return total

    def blocks2(ref, where):
        copies = [
            (ref.at[pl.ds(own2, 8)], ref.at[pl.ds(there2(da, dj), 8)], device(da, dj))
            for da, dj in where
        ]
        return start(copies, ref.at[pl.ds(0, 8 * len(where))])

    c2[pl.ds(own2, 8), :] = packed(c1)
    land_c1 = exchange(
        ((c1, 1, (1, 2, 3, 4, 5, 6)),), [(c1, 1, d, 1, 6 - d) for d in range(1, 6)], c2
    )

    fine_faces = [fine.at[n] for n in range(6)]

    def fine_coeffs(*windows):
        def body(p, planes):
            out = []
            for start_row, count in windows:
                base = p * RF + start_row
                centre, besides = around(cf, base, count, RF, 1, Planes())
                z = lane_ids(count)
                inside = (None, None, None, None, z != 0, z != 127)
                faces, total, quarter = coefficients(centre, besides, inside)
                out += [(fine, (n,) + at(base, count), faces[n]) for n in range(6)]
                out.append((gf, at(base, count), 2.0 * quarter))
                out.append((df, at(base, count), 1.25 * total))
            return out

        return body

    loop(5, 19, 7, fine_coeffs((12, 24)), group=1)
    land_c()
    far_c2 = blocks2(c2, FAR)

    def edges(ref, first, side, count, rows, plane, row, low_y, high_y, low_x, high_x):
        for outside, there, here in (
            (low_y, plane - 1, plane), (high_y, plane + count, plane + count - 1)
        ):
            slab_there = at(there * rows + first, side)
            ref[slab_there] = jnp.where(outside, ref[at(here * rows + first, side)], ref[slab_there])
        lines = 24
        for outside, there, here in ((low_x, row[0] - 1, row[0]), (high_x, row[1] + 1, row[1])):
            slab_there = slab(ref, there, lines, rows)
            ref[slab_there] = jnp.where(outside, ref[slab(ref, here, lines, rows)], ref[slab_there])

    def cut(faces, first, side, count, rows, plane, row, low_y, high_y, low_x, high_x):
        for n, outside, here in ((0, low_y, plane), (1, high_y, plane + count - 1)):
            where = (n,) + at(here * rows + first, side)
            faces[where] = jnp.where(outside, 0.0, faces[where])
        for n, outside, here in ((2, low_x, row[0]), (3, high_x, row[1])):
            where = (n,) + slab(faces, here, 24, rows)
            faces[where] = jnp.where(outside, 0.0, faces[where])

    ends = (j == 0, j == 7, a == 0, a == 15)
    edges(cf, 4, 40, 16, RF, 4, (8, 39), *ends)
    loop(5, 19, 7, fine_coeffs((4, 8), (36, 8)), group=1)
    for low in (2, 19):
        loop(low, low + 3, 3, fine_coeffs((4, 40)), group=1)
    cut(fine, 4, 40, 16, RF, 4, (8, 39), *ends)

    def first_sweep(*windows):
        def body(p, planes):
            out = []
            for start_row, count in windows:
                base = p * RF + start_row
                centre, besides = around(uf, base, count, RF, 1, planes if len(windows) == 1 else Planes())
                right = gf[pl.ds(base, count), :] * sf[pl.ds(base, count), :]
                value = 0.2 * centre + right + weighted(fine_faces, base, count, besides)
                out += [(u1, at(base, count), value), (gf, at(base, count), right)]
            return out

        return body

    loop(5, 19, 7, first_sweep((12, 24)))
    land_u()
    loop(5, 19, 7, first_sweep((4, 8), (36, 8)))
    for low in (2, 19):
        loop(low, low + 3, 3, first_sweep((4, 40)))

    def sweep(src, dst, faces, right, low, high, width, rows, start, count, twist):
        def step(p, planes):
            base = p * rows + start
            centre, besides = around(src, base, count, rows, twist, planes)
            value = 0.2 * centre + right[pl.ds(base, count), :] + weighted(faces, base, count, besides)
            return [(dst, at(base, count), value)]

        loop(low, high, width, step, group=5)

    def leftover(src, dst, faces, right, diag, low, high, width, rows, start, count, twist):
        def step(p, planes):
            base = p * rows + start
            centre, besides = around(src, base, count, rows, twist, planes)
            value = diag[pl.ds(base, count), :] * (
                right[pl.ds(base, count), :] + weighted(faces, base, count, besides) - 0.8 * centre
            )
            return [(dst, at(base, count), value)]

        loop(low, high, width, step, group=4)

    sweep(u1, u2, fine_faces, gf, 3, 21, 9, RF, 4, 40, 1)
    leftover(u2, u1, fine_faces, gf, df, 4, 20, 8, RF, 8, 32, 1)

    def coarse_f(i, planes):
        total = pair_rows(u1, (4 + 2 * i) * RF + 8, 16, RF)
        return [(f1, at(pl.multiple_of((8 + i) * R1 + 8, 8), 16), pair_lanes(total, 1))]

    loop(0, 8, 8, coarse_f)
    land_f = exchange(((f1, 1, (1, 2)),), [(f1, 1, 1, 1, 1)])
    land_rest = exchange(
        ((f1, 1, (3, 4, 5)), (u2, 0, (1, 2, 3))),
        [(f1, 1, 1, 2, 3), (f1, 1, 2, 1, 3), (f1, 1, 3, 1, 2), (f1, 1, 4, 1, 1)] + fine_corner(u2, 3),
    )

    drain(but=2)
    land_c1()
    edges(c1, 0, 32, 8, R1, 8, (8, 23), *ends)
    mid_faces = [mid.at[n] for n in range(6)]

    def mid_coeffs(p, planes):
        base = p * R1
        centre, besides = around(c1, base, 32, R1, 2, planes)
        z = lane_ids(32)
        inside = (None, None, None, None, z >= 2, z < 126)
        faces, total, quarter = coefficients(centre, besides, inside)
        out = [(mid, (n,) + at(base, 32), faces[n]) for n in range(6)]
        out.append((w1, at(base, 32), 8.0 * quarter))
        out.append((d1, at(base, 32), 0.3125 * total))
        return out

    loop(6, 18, 3, mid_coeffs, group=1)
    cut(mid, 0, 32, 8, R1, 8, (8, 23), *ends)

    def guess(p, planes):
        base = p * R1
        return [(g1, at(base, 32), w1[pl.ds(base, 32), :] * f1[pl.ds(base, 32), :])]

    land_f()
    loop(6, 18, 12, guess)
    sweep(g1, e1, mid_faces, g1, 7, 17, 10, R1, 4, 24, 2)
    leftover(e1, r1, mid_faces, g1, d1, 8, 16, 8, R1, 8, 16, 2)
    f2[pl.ds(own2, 8), :] = packed(r1)
    sixth = blocks2(f2, FAR + FULL)

    loop(3, 6, 3, mid_coeffs, group=1)
    loop(18, 21, 3, mid_coeffs, group=1)
    cut(mid, 0, 32, 8, R1, 8, (8, 23), *ends)
    far_c2()

    def around2(ref):
        lanes = lane_ids(5 * R2) % 4
        centre = ref[R2 : 6 * R2, :]
        return centre, (
            jnp.where(lanes == 0, turn(ref[0 : 5 * R2, :], -3), turn(centre, 1)),
            jnp.where(lanes == 3, turn(ref[2 * R2 : 7 * R2, :], 3), turn(centre, -1)),
            ref[pl.ds(zero + (R2 - 1), 5 * R2), :],
            ref[pl.ds(zero + (R2 + 1), 5 * R2), :],
            turn(centre, 4),
            turn(centre, -4),
        )

    rows2, lanes2 = row_ids(5 * R2), lane_ids(5 * R2)
    x = rows2 % R2 + (8 * a - 8)
    y = 4 * (rows2 // R2) + lanes2 % 4 + (4 * j - 8)
    inside2 = (y != 0, y != 31, x != 0, x != 127, lanes2 >= 4, lanes2 < 124)
    centre, besides = around2(c2)
    faces, total, quarter = coefficients(centre, besides, inside2)
    for n in range(6):
        deep[n] = faces[n]
    deep[6] = 32.0 * quarter

    drain(but=1)
    land_rest()
    loop(3, 21, 9, guess)
    sweep(g1, e1, mid_faces, g1, 4, 20, 8, R1, 4, 24, 2)

    sixth()
    g2[...] = deep[6] * f2[R2 : 6 * R2, :]
    e2[R2 : 6 * R2, :] = g2[...]
    for src, dst in ((e2, e2b), (e2b, e2), (e2, e2b)):
        centre, besides = around2(src)
        parts = [deep[n] * besides[n] for n in range(6)]
        dst[R2 : 6 * R2, :] = (
            (0.2 * centre + g2[...]) + (parts[0] + parts[1]) + (parts[2] + parts[3]) + (parts[4] + parts[5])
        )

    lanes16 = lane_ids(16) % 4
    hops = ((1, 2), (-1, 2), (1, -2), (-1, -2))
    for number in range(8):
        block, i = (number + 6) // 4, (number + 6) % 4
        value = jnp.where(lanes16 == i, e2b[pl.ds(zero + (R2 + R2 * block + 4), 16), :], 0.0)
        value = value + turn(value, hops[i][0])
        value = value + turn(value, hops[i][1])
        pe2[pl.ds(32 * number, 16, stride=2), :] = value
        pe2[pl.ds(32 * number + 1, 16, stride=2), :] = value

    def corrected1(p, planes):
        value = e1[pl.ds(p * R1 + 4, 24), :] + pe2[pl.ds((p // 2 - 2) * 32 + 4, 24), :]
        return [(e1, at(p * R1 + 4, 24), value)]

    loop(4, 20, 16, corrected1)
    sweep(e1, e1b, mid_faces, g1, 5, 19, 14, R1, 4, 24, 2)
    sweep(e1b, e1, mid_faces, g1, 6, 18, 12, R1, 4, 24, 2)

    def grown(i, planes):
        value = e1[pl.ds((i + 6) * R1 + 4, 24), :]
        return [(pe1, (pl.ds(RF * i + odd, 24, stride=2), slice(None)), value) for odd in (0, 1)]

    loop(0, 12, 12, grown)

    def corrected0(p, planes):
        base = p * RF + 4
        return [(u2, at(base, 40), u2[pl.ds(base, 40), :] + pe1[pl.ds((p // 2) * RF + 4, 40), :])]

    loop(1, 23, 11, corrected0)
    sweep(u2, u1, fine_faces, gf, 2, 22, 10, RF, 4, 40, 1)

    def give(ref, stage, other, quads):
        def step(t, planes):
            rows = pl.ds(pl.multiple_of(8 * t, 8), 8)
            out = []
            for q in quads:
                four = [
                    ref[pl.ds(pl.multiple_of((4 + 4 * q + i) * RF + 8 + 8 * t, 8), 8), :]
                    for i in range(4)
                ]
                for p, value in enumerate(transposed(four)):
                    out.append((stage, (p, rows, slice(128 * q, 128 * q + 128)), value))
            return out

        loop(0, 4, 4, step)
        lanes = pl.ds(128 * quads[0], 128 * len(quads))
        return stage.at[pl.ds(1 - half, 3), :, lanes], other.at[:, :, lanes], sibling

    def keep(stage, out):
        for s in range(4):
            out[s, :, mine] = stage[jnp.clip(s + half * split, 0, 3)]

    def take(other, out):
        for s in range(4):
            out[s, :, theirs] = other[jnp.clip(s + half * (split - 1), 0, 2)]

    last = []
    sweep(u1, u2, fine_faces, gf, 3, 12, 9, RF, 4, 40, 1)
    last.append(start([give(u2, stage_f, other_f, (0, 1))], other_f.at[:, :, pl.ds(0, 256)]))
    sweep(u1, u2, fine_faces, gf, 12, 21, 9, RF, 4, 40, 1)
    last.append(start([give(u2, stage_f, other_f, (2, 3))], other_f.at[:, :, pl.ds(256, 256)]))
    for q in range(4):
        leftover(u2, u1, fine_faces, gf, df, 4 + 4 * q, 8 + 4 * q, 4, RF, 8, 32, 1)
        last.append(start([give(u1, stage_r, other_r, (q,))], other_r.at[:, :, pl.ds(128 * q, 128)]))
    keep(stage_f, out_field)
    last[0]()
    last[1]()
    take(other_f, out_field)
    keep(stage_r, out_resid)
    for arrived in last[2:]:
        arrived()
    take(other_r, out_resid)
    drain()


def vmem(*shape):
    return pltpu.VMEM(shape, F32)


def body(source, conductance, initial, box_counts):
    fine_field = vmem(PF * RF, LANES)
    mid_field = vmem(P1 * R1, LANES)
    deep_field = vmem(7 * R2, LANES)
    scratch = [pltpu.SMEM(box_counts.shape, jnp.int32)] + [vmem(6, 32, 512)] * 3
    scratch += [fine_field] * 5 + [vmem(6, PF * RF, LANES)] + [fine_field] * 2
    scratch += [mid_field] * 4 + [vmem(8 * 32, LANES), vmem(6, P1 * R1, LANES)] + [mid_field] * 4
    scratch += [deep_field] * 4 + [vmem(7, 5 * R2, LANES), vmem(5 * R2, LANES), vmem(12 * RF, LANES)]
    scratch += [vmem(4, 32, 512)] * 2 + [vmem(3, 32, 512)] * 2
    for big, middle, small in ((160, 80, 8), (96, 48, 8), (104, 56, 24), (32, 16, 8), (144, 72, 16)):
        scratch += [vmem(2 * big + 2 * middle + 4 * small, LANES)] * 2
    scratch += [pltpu.SemaphoreType.DMA((4,))] + [pltpu.SemaphoreType.DMA((ROUNDS,))] * 2
    hbm = pl.BlockSpec(memory_space=pltpu.HBM)
    shape = jax.ShapeDtypeStruct(source.shape, source.dtype)
    field, resid, held = pl.pallas_call(
        kernel,
        out_shape=(shape,) * 3,
        in_specs=[hbm] * 4,
        out_specs=(pl.BlockSpec(memory_space=pltpu.VMEM),) * 3,
        scratch_shapes=scratch,
        compiler_params=pltpu.CompilerParams(
            collective_id=0, has_side_effects=True, vmem_limit_bytes=40 * 2**20
        ),
        cost_estimate=pl.CostEstimate(flops=3 * 10**7, bytes_accessed=3 * 10**6, transcendentals=0),
    )(*[pltpu.with_memory_space_constraint(x, pltpu.HBM) for x in (box_counts, source, conductance, initial)])
    return field * held, resid * held


def solution(mesh):
    return jax.shard_map(
        body,
        mesh=mesh,
        in_specs=(P("box", None, None), P("box", None, None), P("box", None, None), P()),
        out_specs=(P("box", None, None), P("box", None, None)),
        check_vma=False,
    )
```

```python
import functools

import jax
import jax.numpy as jnp
from jax import lax
from jax.experimental import pallas as pl
from jax.experimental.pallas import tpu as pltpu
from jax.sharding import PartitionSpec as P


RF, PF = 48, 24
R1, P1 = 32, 24
R2 = 24
LANES = 128
FULL = (1, 1), (1, -1), (-1, 1), (-1, -1), (1, 0), (-1, 0), (0, 1), (0, -1)
FAR = (1, 2), (1, -2), (-1, 2), (-1, -2), (0, 2), (0, -2)
F32 = jnp.float32
ROUNDS = 3 + 5 + 2 + 6


def lane_ids(rows):
    return lax.broadcasted_iota(jnp.int32, (rows, LANES), 1)


def row_ids(rows):
    return lax.broadcasted_iota(jnp.int32, (rows, LANES), 0)


def turn(value, steps):
    return pltpu.roll(value, steps % LANES, 1)


def transposed(four):
    lanes = lane_ids(four[0].shape[0])
    low = lanes < 64
    even = (lanes // 32) % 2 == 0
    a, b, c, d = four
    e = jnp.where(low, a, turn(c, 64))
    f = jnp.where(low, b, turn(d, 64))
    g = jnp.where(low, turn(a, 64), c)
    h = jnp.where(low, turn(b, 64), d)
    return (
        jnp.where(even, e, turn(f, 32)),
        jnp.where(even, turn(e, -32), f),
        jnp.where(even, g, turn(h, 32)),
        jnp.where(even, turn(g, -32), h),
    )


def coefficients(c, besides, inside):
    around_ = [
        beside if within is None else jnp.where(within, beside, c)
        for beside, within in zip(besides, inside)
    ]
    total = 3.0 * c + 0.5 * (
        (around_[0] + around_[1]) + (around_[2] + around_[3]) + (around_[4] + around_[5])
    )
    quarter = 0.4 / total
    faces = [
        (c + beside) * quarter if within is None else jnp.where(within, (c + beside) * quarter, 0.0)
        for beside, within in zip(besides, inside)
    ]
    return faces, total, quarter


class Planes:
    def __init__(self):
        self.held = {}
        self.step = 0

    def load(self, ref, base, count, rows, ahead):
        key = (id(ref), count, self.step + ahead)
        if key not in self.held:
            self.held[key] = ref[pl.ds(base + rows * ahead, count), :]
        return self.held[key]


def around(ref, base, count, rows, twist, planes):
    centre = planes.load(ref, base, count, rows, 0)
    return centre, (
        planes.load(ref, base, count, rows, -1),
        planes.load(ref, base, count, rows, 1),
        ref[pl.ds(base - 1, count), :],
        ref[pl.ds(base + 1, count), :],
        turn(centre, twist),
        turn(centre, -twist),
    )


def weighted(faces, base, count, besides):
    parts = [faces[n][pl.ds(base, count), :] * besides[n] for n in range(6)]
    return (parts[0] + parts[1]) + (parts[2] + parts[3]) + (parts[4] + parts[5])


def planes_loop(low, high, width, body, group=None, base=0):
    assert (high - low) % width == 0
    group = group or width

    def step(index, carry):
        first = base + low + index * width
        stores, planes = [], Planes()
        for m in range(width):
            planes.step = m
            stores += body(first + m, planes)
            if (m + 1) % group == 0 or m == width - 1:
                for ref, index_, value in stores:
                    ref[index_] = value
                stores, planes = [], Planes()
        return carry

    if high - low == width:
        step(0, 0)
    else:
        lax.fori_loop(0, (high - low) // width, step, 0)


def at(base, count):
    return pl.ds(base, count), slice(None)


def pair_rows(ref, base, count, rows):
    got = [
        ref[pl.ds(base + offset, count, stride=2), :] for offset in (0, 1, rows, rows + 1)
    ]
    return (got[0] + got[1]) + (got[2] + got[3])


def pair_lanes(value, width):
    first = (lane_ids(value.shape[0]) // width) % 2 == 0
    return 0.125 * (value + jnp.where(first, turn(value, -width), turn(value, width)))


def kernel(
    counts, source, conductance, initial, out_field, out_resid, out_held,
    owners, raw_c, raw_u, raw_s, cf, uf, sf, u1, u2, fine, gf, df,
    c1, f1, e1, e1b, pe2, mid, w1, g1, d1, r1, c2, f2, e2, e2b, deep, g2, pe1,
    stage_f, stage_r, other_f, other_r, *rest,
):
    post, local_sem, send_sem, recv_sem = rest[:-3], rest[-3], rest[-2], rest[-1]
    me = lax.axis_index("box")
    a, j = me // 8, me % 8
    half = me % 2
    sibling = me + 1 - 2 * half
    zero = me // 1024
    loop = functools.partial(planes_loop, base=zero)
    across = {da: ((a + da + 16) % 16) * 8 for da in (-1, 0, 1)}
    along = {dj: (j + dj + 8) % 8 for dj in (-2, -1, 0, 1, 2)}

    sibling_far = across[0] + (j - 1 + 2 * half + 8) % 8

    def device(da, dj):
        return across[da] + along[dj]

    numbers = iter(range(ROUNDS))
    leaving = []

    def describe(src, dst, number, target):
        return pltpu.make_async_remote_copy(
            src_ref=src, dst_ref=dst, send_sem=send_sem.at[number], recv_sem=recv_sem.at[number],
            device_id=(target,), device_id_type=pl.DeviceIdType.MESH,
        )

    def start(copies, whole):
        number = next(numbers)
        for src, dst, target in copies:
            describe(src, dst, number, target).start()
        everything = describe(whole, whole, number, sibling)
        leaving.append(everything.wait_send)
        return everything.wait_recv

    def drain(but=0):
        while len(leaving) > but:
            leaving.pop(0)()

    barrier = pltpu.get_barrier_semaphore()
    for target in (sibling,) + tuple(device(da, dj) for da, dj in FULL[:6]) + (sibling_far,):
        pl.semaphore_signal(barrier, inc=1, device_id=(target,), device_id_type=pl.DeviceIdType.MESH)

    raws = (raw_c, raw_s, raw_u)
    given = (conductance, source, initial)
    mine = pl.ds(pl.multiple_of(512 * half, 512), 512)
    theirs = pl.ds(pl.multiple_of(512 - 512 * half, 512), 512)
    held = pl.ds(3 * half, 3)
    locals_ = [pltpu.make_async_copy(counts, owners, local_sem.at[3])]
    for number in range(3):
        locals_.append(
            pltpu.make_async_copy(
                given[number].at[pl.ds(0, 3), :, mine], raws[number].at[held], local_sem.at[number]
            )
        )
    for copy in locals_:
        copy.start()

    pl.semaphore_wait(barrier, len(FULL))

    def swap(number):
        return start(
            [(given[number].at[pl.ds(0, 3), :, theirs], raws[number].at[held], sibling)],
            raws[number].at[held],
        )

    swaps = [swap(number) for number in range(3)]
    locals_[0].wait()
    split = owners[me - half]
    own = jnp.where(half == 0, split, 4 - split)
    for s in range(4):
        out_held[s] = jnp.where(s < own, jnp.ones((32, 1024), F32), 0.0)
    places = [jnp.where(p < split, p, jnp.clip(3 + p - split, 0, 5)) for p in range(4)]

    def bring(number, ref):
        locals_[1 + number].wait()
        swaps[number]()
        raw = raws[number]

        def step(t, planes):
            rows = pl.ds(pl.multiple_of(8 * t, 8), 8)
            out = []
            for q in range(4):
                four = [raw[places[p], rows, 128 * q : 128 * q + 128] for p in range(4)]
                for i, value in enumerate(transposed(four)):
                    out.append((ref, at(pl.multiple_of((4 + 4 * q + i) * RF + 8 + 8 * t, 8), 8), value))
            return out

        loop(0, 4, 4, step, group=1)

    ROWS = (RF, R1)
    OWN = ((4, 16, 8, 32), (8, 8, 8, 16))

    def near(first, count, side, depth):
        return first - 1 + depth if side < 0 else first + count - depth

    def far(first, count, side, depth):
        return first + count - 1 + depth if side < 0 else first - depth

    own2 = R2 + 2 * R2 + 8

    def there2(da, dj):
        return R2 + R2 * (2 - dj) + 8 * (1 - da)

    def pieces(strips, corners, block, da, dj, pick):
        out = []
        if block is not None:
            out.append((block, own2 if pick is near else there2(da, dj), 8, 1))
        if da == 0:
            for ref, level, depths in strips:
                plane, planes, row, rows = OWN[level]
                for d in depths:
                    out.append((ref, pick(plane, planes, dj, d) * ROWS[level] + row, rows, 1))
        elif dj == 0:
            for ref, level, depths in strips:
                plane, planes, row, rows = OWN[level]
                for d in depths:
                    out.append(
                        (ref, plane * ROWS[level] + pick(row, rows, da, d), planes, ROWS[level])
                    )
        else:
            for ref, level, depth, low, count in corners:
                plane, planes, row, rows = OWN[level]
                ends = [pick(row, rows, da, d) for d in (low, low + count - 1)]
                out.append((ref, pick(plane, planes, dj, depth) * ROWS[level] + min(ends), count, 1))
        return out

    def slab(ref, first, count, stride):
        return (pl.ds(first, count, stride=stride) if stride > 1 else pl.ds(first, count)), slice(None)

    spare = list(post)

    def exchange(strips, corners, block=None, where=FULL):
        out, got = spare.pop(0), spare.pop(0)
        copies, filled = [], []
        offset = 0
        for da, dj in where:
            first_row = offset
            for ref, first, count, stride in pieces(strips, corners, block, da, dj, near):
                out[pl.ds(offset, count), :] = ref[slab(ref, first, count, stride)]
                offset += count
            offset += -offset % 8
            rows = pl.ds(first_row, offset - first_row)
            copies.append((out.at[rows], got.at[rows], device(da, dj)))
            filled.append((first_row, da, dj))
        assert out.shape == (offset, LANES)
        arrived = start(copies, got)

        def land():
            arrived()
            for offset, da, dj in filled:
                for ref, first, count, stride in pieces(strips, corners, block, da, dj, far):
                    ref[slab(ref, first, count, stride)] = got[pl.ds(offset, count), :]
                    offset += count

        return land

    def fine_corner(ref, depth):
        return [(ref, 0, d, 1, depth - d) for d in range(1, depth)]

    bring(0, cf)
    bring(1, sf)
    land_c = exchange(
        ((cf, 0, (1, 2, 3)), (sf, 0, (1, 2))), fine_corner(cf, 3) + fine_corner(sf, 2)
    )
    bring(2, uf)
    land_u = exchange(((uf, 0, (1, 2, 3)),), fine_corner(uf, 3))

    def coarse_c(i, planes):
        total = pair_rows(cf, (4 + 2 * i) * RF + 8, 16, RF)
        return [(c1, at(pl.multiple_of((8 + i) * R1 + 8, 8), 16), pair_lanes(total, 1))]

    loop(0, 8, 8, coarse_c)

    def packed(ref):
        lanes = lane_ids(8) % 4
        total = jnp.zeros((8, LANES), F32)
        for i in range(4):
            value = pair_lanes(pair_rows(ref, (8 + 2 * i) * R1 + 8, 8, R1), 2)
            total = total + jnp.where(lanes == i, value, 0.0)
        return total

    def blocks2(ref, where):
        copies = [
            (ref.at[pl.ds(own2, 8)], ref.at[pl.ds(there2(da, dj), 8)], device(da, dj))
            for da, dj in where
        ]
        return start(copies, ref.at[pl.ds(0, 8 * len(where))])

    c2[pl.ds(own2, 8), :] = packed(c1)
    land_c1 = exchange(
        ((c1, 1, (1, 2, 3, 4, 5, 6)),), [(c1, 1, d, 1, 6 - d) for d in range(1, 6)], c2
    )

    fine_faces = [fine.at[n] for n in range(6)]

    def fine_coeffs(*windows):
        def body(p, planes):
            out = []
            for start_row, count in windows:
                base = p * RF + start_row
                centre, besides = around(cf, base, count, RF, 1, Planes())
                z = lane_ids(count)
                inside = (None, None, None, None, z != 0, z != 127)
                faces, total, quarter = coefficients(centre, besides, inside)
                out += [(fine, (n,) + at(base, count), faces[n]) for n in range(6)]
                out.append((gf, at(base, count), 2.0 * quarter))
                out.append((df, at(base, count), 1.25 * total))
            return out

        return body

    loop(5, 19, 7, fine_coeffs((12, 24)), group=1)
    land_c()
    far_c2 = blocks2(c2, FAR)

    def edges(ref, first, side, count, rows, plane, row, low_y, high_y, low_x, high_x):
        for outside, there, here in (
            (low_y, plane - 1, plane), (high_y, plane + count, plane + count - 1)
        ):
            slab_there = at(there * rows + first, side)
            ref[slab_there] = jnp.where(outside, ref[at(here * rows + first, side)], ref[slab_there])
        lines = 24
        for outside, there, here in ((low_x, row[0] - 1, row[0]), (high_x, row[1] + 1, row[1])):
            slab_there = slab(ref, there, lines, rows)
            ref[slab_there] = jnp.where(outside, ref[slab(ref, here, lines, rows)], ref[slab_there])

    def cut(faces, first, side, count, rows, plane, row, low_y, high_y, low_x, high_x):
        for n, outside, here in ((0, low_y, plane), (1, high_y, plane + count - 1)):
            where = (n,) + at(here * rows + first, side)
            faces[where] = jnp.where(outside, 0.0, faces[where])
        for n, outside, here in ((2, low_x, row[0]), (3, high_x, row[1])):
            where = (n,) + slab(faces, here, 24, rows)
            faces[where] = jnp.where(outside, 0.0, faces[where])

    ends = (j == 0, j == 7, a == 0, a == 15)
    edges(cf, 4, 40, 16, RF, 4, (8, 39), *ends)
    loop(5, 19, 7, fine_coeffs((4, 8), (36, 8)), group=1)
    for low in (2, 19):
        loop(low, low + 3, 3, fine_coeffs((4, 40)), group=1)
    cut(fine, 4, 40, 16, RF, 4, (8, 39), *ends)

    def first_sweep(*windows):
        def body(p, planes):
            out = []
            for start_row, count in windows:
                base = p * RF + start_row
                centre, besides = around(uf, base, count, RF, 1, planes if len(windows) == 1 else Planes())
                right = gf[pl.ds(base, count), :] * sf[pl.ds(base, count), :]
                value = 0.2 * centre + right + weighted(fine_faces, base, count, besides)
                out += [(u1, at(base, count), value), (gf, at(base, count), right)]
            return out

        return body

    loop(5, 19, 7, first_sweep((12, 24)))
    land_u()
    loop(5, 19, 7, first_sweep((4, 8), (36, 8)))
    for low in (2, 19):
        loop(low, low + 3, 3, first_sweep((4, 40)))

    def sweep(src, dst, faces, right, low, high, width, rows, start, count, twist):
        def step(p, planes):
            base = p * rows + start
            centre, besides = around(src, base, count, rows, twist, planes)
            value = 0.2 * centre + right[pl.ds(base, count), :] + weighted(faces, base, count, besides)
            return [(dst, at(base, count), value)]

        loop(low, high, width, step, group=5)

    def leftover(src, dst, faces, right, diag, low, high, width, rows, start, count, twist):
        def step(p, planes):
            base = p * rows + start
            centre, besides = around(src, base, count, rows, twist, planes)
            value = diag[pl.ds(base, count), :] * (
                right[pl.ds(base, count), :] + weighted(faces, base, count, besides) - 0.8 * centre
            )
            return [(dst, at(base, count), value)]

        loop(low, high, width, step, group=4)

    sweep(u1, u2, fine_faces, gf, 3, 21, 9, RF, 4, 40, 1)
    leftover(u2, u1, fine_faces, gf, df, 4, 20, 8, RF, 8, 32, 1)

    def coarse_f(i, planes):
        total = pair_rows(u1, (4 + 2 * i) * RF + 8, 16, RF)
        return [(f1, at(pl.multiple_of((8 + i) * R1 + 8, 8), 16), pair_lanes(total, 1))]

    loop(0, 8, 8, coarse_f)
    land_f = exchange(((f1, 1, (1, 2)),), [(f1, 1, 1, 1, 1)])
    land_rest = exchange(
        ((f1, 1, (3, 4, 5)), (u2, 0, (1, 2, 3))),
        [(f1, 1, 1, 2, 3), (f1, 1, 2, 1, 3), (f1, 1, 3, 1, 2), (f1, 1, 4, 1, 1)] + fine_corner(u2, 3),
    )

    drain(but=2)
    land_c1()
    edges(c1, 0, 32, 8, R1, 8, (8, 23), *ends)
    mid_faces = [mid.at[n] for n in range(6)]

    def mid_coeffs(p, planes):
        base = p * R1
        centre, besides = around(c1, base, 32, R1, 2, planes)
        z = lane_ids(32)
        inside = (None, None, None, None, z >= 2, z < 126)
        faces, total, quarter = coefficients(centre, besides, inside)
        out = [(mid, (n,) + at(base, 32), faces[n]) for n in range(6)]
        out.append((w1, at(base, 32), 8.0 * quarter))
        out.append((d1, at(base, 32), 0.3125 * total))
        return out

    loop(6, 18, 3, mid_coeffs, group=1)
    cut(mid, 0, 32, 8, R1, 8, (8, 23), *ends)

    def guess(p, planes):
        base = p * R1
        return [(g1, at(base, 32), w1[pl.ds(base, 32), :] * f1[pl.ds(base, 32), :])]

    land_f()
    loop(6, 18, 12, guess)
    sweep(g1, e1, mid_faces, g1, 7, 17, 10, R1, 4, 24, 2)
    leftover(e1, r1, mid_faces, g1, d1, 8, 16, 8, R1, 8, 16, 2)
    f2[pl.ds(own2, 8), :] = packed(r1)
    sixth = blocks2(f2, FAR + FULL)

    loop(3, 6, 3, mid_coeffs, group=1)
    loop(18, 21, 3, mid_coeffs, group=1)
    cut(mid, 0, 32, 8, R1, 8, (8, 23), *ends)
    far_c2()

    def around2(ref):
        lanes = lane_ids(5 * R2) % 4
        centre = ref[R2 : 6 * R2, :]
        return centre, (
            jnp.where(lanes == 0, turn(ref[0 : 5 * R2, :], -3), turn(centre, 1)),
            jnp.where(lanes == 3, turn(ref[2 * R2 : 7 * R2, :], 3), turn(centre, -1)),
            ref[pl.ds(zero + (R2 - 1), 5 * R2), :],
            ref[pl.ds(zero + (R2 + 1), 5 * R2), :],
            turn(centre, 4),
            turn(centre, -4),
        )

    rows2, lanes2 = row_ids(5 * R2), lane_ids(5 * R2)
    x = rows2 % R2 + (8 * a - 8)
    y = 4 * (rows2 // R2) + lanes2 % 4 + (4 * j - 8)
    inside2 = (y != 0, y != 31, x != 0, x != 127, lanes2 >= 4, lanes2 < 124)
    centre, besides = around2(c2)
    faces, total, quarter = coefficients(centre, besides, inside2)
    for n in range(6):
        deep[n] = faces[n]
    deep[6] = 32.0 * quarter

    drain(but=1)
    land_rest()
    loop(3, 21, 9, guess)
    sweep(g1, e1, mid_faces, g1, 4, 20, 8, R1, 4, 24, 2)

    sixth()
    g2[...] = deep[6] * f2[R2 : 6 * R2, :]
    e2[R2 : 6 * R2, :] = g2[...]
    for src, dst in ((e2, e2b), (e2b, e2), (e2, e2b)):
        centre, besides = around2(src)
        parts = [deep[n] * besides[n] for n in range(6)]
        dst[R2 : 6 * R2, :] = (
            (0.2 * centre + g2[...]) + (parts[0] + parts[1]) + (parts[2] + parts[3]) + (parts[4] + parts[5])
        )

    lanes16 = lane_ids(16) % 4
    hops = ((1, 2), (-1, 2), (1, -2), (-1, -2))
    for number in range(8):
        block, i = (number + 6) // 4, (number + 6) % 4
        value = jnp.where(lanes16 == i, e2b[pl.ds(zero + (R2 + R2 * block + 4), 16), :], 0.0)
        value = value + turn(value, hops[i][0])
        value = value + turn(value, hops[i][1])
        pe2[pl.ds(32 * number, 16, stride=2), :] = value
        pe2[pl.ds(32 * number + 1, 16, stride=2), :] = value

    def corrected1(p, planes):
        value = e1[pl.ds(p * R1 + 4, 24), :] + pe2[pl.ds((p // 2 - 2) * 32 + 4, 24), :]
        return [(e1, at(p * R1 + 4, 24), value)]

    loop(4, 20, 16, corrected1)
    sweep(e1, e1b, mid_faces, g1, 5, 19, 14, R1, 4, 24, 2)
    sweep(e1b, e1, mid_faces, g1, 6, 18, 12, R1, 4, 24, 2)

    def grown(i, planes):
        value = e1[pl.ds((i + 6) * R1 + 4, 24), :]
        return [(pe1, (pl.ds(RF * i + odd, 24, stride=2), slice(None)), value) for odd in (0, 1)]

    loop(0, 12, 12, grown)

    def corrected0(p, planes):
        base = p * RF + 4
        return [(u2, at(base, 40), u2[pl.ds(base, 40), :] + pe1[pl.ds((p // 2) * RF + 4, 40), :])]

    loop(1, 23, 11, corrected0)
    sweep(u2, u1, fine_faces, gf, 2, 22, 10, RF, 4, 40, 1)

    def give(ref, stage, other, quads):
        def step(t, planes):
            rows = pl.ds(pl.multiple_of(8 * t, 8), 8)
            out = []
            for q in quads:
                four = [
                    ref[pl.ds(pl.multiple_of((4 + 4 * q + i) * RF + 8 + 8 * t, 8), 8), :]
                    for i in range(4)
                ]
                for p, value in enumerate(transposed(four)):
                    out.append((stage, (p, rows, slice(128 * q, 128 * q + 128)), value))
            return out

        loop(0, 4, 4, step)
        lanes = pl.ds(128 * quads[0], 128 * len(quads))
        return stage.at[pl.ds(1 - half, 3), :, lanes], other.at[:, :, lanes], sibling

    def keep(stage, out):
        for s in range(4):
            out[s, :, mine] = stage[jnp.clip(s + half * split, 0, 3)]

    def take(other, out):
        for s in range(4):
            out[s, :, theirs] = other[jnp.clip(s + half * (split - 1), 0, 2)]

    last = []
    sweep(u1, u2, fine_faces, gf, 3, 12, 9, RF, 4, 40, 1)
    last.append(start([give(u2, stage_f, other_f, (0, 1))], other_f.at[:, :, pl.ds(0, 256)]))
    sweep(u1, u2, fine_faces, gf, 12, 21, 9, RF, 4, 40, 1)
    last.append(start([give(u2, stage_f, other_f, (2, 3))], other_f.at[:, :, pl.ds(256, 256)]))
    for q in range(4):
        leftover(u2, u1, fine_faces, gf, df, 4 + 4 * q, 8 + 4 * q, 4, RF, 8, 32, 1)
        last.append(start([give(u1, stage_r, other_r, (q,))], other_r.at[:, :, pl.ds(128 * q, 128)]))
    keep(stage_f, out_field)
    last[0]()
    last[1]()
    take(other_f, out_field)
    keep(stage_r, out_resid)
    for arrived in last[2:]:
        arrived()
    take(other_r, out_resid)
    drain()


def vmem(*shape):
    return pltpu.VMEM(shape, F32)


def body(source, conductance, initial, box_counts):
    fine_field = vmem(PF * RF, LANES)
    mid_field = vmem(P1 * R1, LANES)
    deep_field = vmem(7 * R2, LANES)
    scratch = [pltpu.SMEM(box_counts.shape, jnp.int32)] + [vmem(6, 32, 512)] * 3
    scratch += [fine_field] * 5 + [vmem(6, PF * RF, LANES)] + [fine_field] * 2
    scratch += [mid_field] * 4 + [vmem(8 * 32, LANES), vmem(6, P1 * R1, LANES)] + [mid_field] * 4
    scratch += [deep_field] * 4 + [vmem(7, 5 * R2, LANES), vmem(5 * R2, LANES), vmem(12 * RF, LANES)]
    scratch += [vmem(4, 32, 512)] * 2 + [vmem(3, 32, 512)] * 2
    for big, middle, small in ((160, 80, 8), (96, 48, 8), (104, 56, 24), (32, 16, 8), (144, 72, 16)):
        scratch += [vmem(2 * big + 2 * middle + 4 * small, LANES)] * 2
    scratch += [pltpu.SemaphoreType.DMA((4,))] + [pltpu.SemaphoreType.DMA((ROUNDS,))] * 2
    hbm = pl.BlockSpec(memory_space=pltpu.HBM)
    shape = jax.ShapeDtypeStruct(source.shape, source.dtype)
    field, resid, held = pl.pallas_call(
        kernel,
        out_shape=(shape,) * 3,
        in_specs=[hbm] * 4,
        out_specs=(pl.BlockSpec(memory_space=pltpu.VMEM),) * 3,
        scratch_shapes=scratch,
        compiler_params=pltpu.CompilerParams(
            collective_id=0, has_side_effects=True, vmem_limit_bytes=40 * 2**20
        ),
        cost_estimate=pl.CostEstimate(flops=3 * 10**7, bytes_accessed=3 * 10**6, transcendentals=0),
    )(*[pltpu.with_memory_space_constraint(x, pltpu.HBM) for x in (box_counts, source, conductance, initial)])
    return field * held, resid * held


def solution(mesh):
    return jax.shard_map(
        body,
        mesh=mesh,
        in_specs=(P("box", None, None), P("box", None, None), P("box", None, None), P()),
        out_specs=(P("box", None, None), P("box", None, None)),
        check_vma=False,
    )
```

```python
import functools

import jax
import jax.numpy as jnp
from jax import lax
from jax.experimental import pallas as pl
from jax.experimental.pallas import tpu as pltpu
from jax.sharding import PartitionSpec as P


RF, PF = 48, 24
R1, P1 = 32, 24
R2 = 24
LANES = 128
FULL = (1, 1), (1, -1), (1, 0), (-1, 1), (-1, -1), (-1, 0), (0, 1), (0, -1)
FAR = (1, 2), (1, -2), (-1, 2), (-1, -2), (0, 2), (0, -2)
F32 = jnp.float32
ROUNDS = 3 + 3 * (5 + 2) + 4


def lane_ids(rows):
    return lax.broadcasted_iota(jnp.int32, (rows, LANES), 1)


def row_ids(rows):
    return lax.broadcasted_iota(jnp.int32, (rows, LANES), 0)


def turn(value, steps):
    return pltpu.roll(value, steps % LANES, 1)


def transposed(four):
    lanes = lane_ids(four[0].shape[0])
    low = lanes < 64
    even = (lanes // 32) % 2 == 0
    a, b, c, d = four
    e = jnp.where(low, a, turn(c, 64))
    f = jnp.where(low, b, turn(d, 64))
    g = jnp.where(low, turn(a, 64), c)
    h = jnp.where(low, turn(b, 64), d)
    return (
        jnp.where(even, e, turn(f, 32)),
        jnp.where(even, turn(e, -32), f),
        jnp.where(even, g, turn(h, 32)),
        jnp.where(even, turn(g, -32), h),
    )


def coefficients(c, besides, inside):
    around_ = [
        beside if within is None else jnp.where(within, beside, c)
        for beside, within in zip(besides, inside)
    ]
    total = 3.0 * c + 0.5 * (
        (around_[0] + around_[1]) + (around_[2] + around_[3]) + (around_[4] + around_[5])
    )
    quarter = 0.4 / total
    faces = [
        (c + beside) * quarter if within is None else jnp.where(within, (c + beside) * quarter, 0.0)
        for beside, within in zip(besides, inside)
    ]
    return faces, total, quarter


def around(ref, base, count, rows, twist):
    centre = ref[pl.ds(base, count), :]
    return centre, (
        ref[pl.ds(base - rows, count), :],
        ref[pl.ds(base + rows, count), :],
        ref[pl.ds(base - 1, count), :],
        ref[pl.ds(base + 1, count), :],
        turn(centre, twist),
        turn(centre, -twist),
    )


def weighted(faces, base, count, besides):
    parts = [faces[n][pl.ds(base, count), :] * besides[n] for n in range(6)]
    return (parts[0] + parts[1]) + (parts[2] + parts[3]) + (parts[4] + parts[5])


def planes_loop(low, high, width, body, group=None, base=0):
    assert (high - low) % width == 0
    group = group or width

    def step(index, carry):
        first = base + low + index * width
        stores = []
        for m in range(width):
            stores += body(first + m)
            if (m + 1) % group == 0 or m == width - 1:
                for ref, index_, value in stores:
                    ref[index_] = value
                stores = []
        return carry

    if high - low == width:
        step(0, 0)
    else:
        lax.fori_loop(0, (high - low) // width, step, 0)


def at(base, count):
    return pl.ds(base, count), slice(None)


def pair_rows(ref, base, count, rows):
    got = [
        ref[pl.ds(base + offset, count, stride=2), :] for offset in (0, 1, rows, rows + 1)
    ]
    return (got[0] + got[1]) + (got[2] + got[3])


def pair_lanes(value, width):
    first = (lane_ids(value.shape[0]) // width) % 2 == 0
    return 0.125 * (value + jnp.where(first, turn(value, -width), turn(value, width)))


def kernel(
    counts, source, conductance, initial, out_field, out_resid, out_held,
    owners, raw_c, raw_u, raw_s, cf, uf, sf, u1, u2, fine, gf, df,
    c1, f1, e1, e1b, pe2, mid, w1, g1, d1, r1, c2, f2, e2, e2b, deep, g2, pe1,
    stage_f, stage_r, other_f, other_r, *rest,
):
    post, local_sem, send_sem, recv_sem = rest[:-3], rest[-3], rest[-2], rest[-1]
    me = lax.axis_index("box")
    a, j = me // 8, me % 8
    half = me % 2
    sibling = me + 1 - 2 * half
    zero = me // 1024
    loop = functools.partial(planes_loop, base=zero)
    across = {da: ((a + da + 16) % 16) * 8 for da in (-1, 0, 1)}
    along = {dj: (j + dj + 8) % 8 for dj in (-2, -1, 0, 1, 2)}

    sibling_far = across[0] + (j - 1 + 2 * half + 8) % 8

    def device(da, dj):
        return across[da] + along[dj]

    numbers = iter(range(ROUNDS))
    leaving = []

    def describe(src, dst, number, target):
        return pltpu.make_async_remote_copy(
            src_ref=src, dst_ref=dst, send_sem=send_sem.at[number], recv_sem=recv_sem.at[number],
            device_id=(target,), device_id_type=pl.DeviceIdType.MESH,
        )

    leaves = {1: a < 15, -1: a > 0}
    comes = {1: a > 0, -1: a < 15}

    def start(copies, whole, da=0, without=None):
        number = next(numbers)
        everything = describe(whole, whole, number, sibling)

        def go():
            for src, dst, target in copies:
                describe(src, dst, number, target).start()

        if da == 0:
            go()
            leaving.append(everything.wait_send)
            return everything.wait_recv
        pl.when(leaves[da])(go)
        leaving.append(lambda: pl.when(leaves[da])(everything.wait_send))

        def arrived():
            pl.when(comes[da])(everything.wait_recv)
            pl.when(jnp.logical_not(comes[da]))(without)

        return arrived

    def drain(but=0):
        while len(leaving) > but:
            leaving.pop(0)()

    barrier = pltpu.get_barrier_semaphore()

    def here(*targets):
        for target in targets:
            pl.semaphore_signal(
                barrier, inc=1, device_id=(target,), device_id_type=pl.DeviceIdType.MESH
            )

    here(sibling, sibling_far)
    for da in (1, -1):
        pl.when(leaves[da])(lambda: here(*[device(da, dj) for dj in (1, -1, 0)]))

    raws = (raw_c, raw_s, raw_u)
    given = (conductance, source, initial)
    mine = pl.ds(pl.multiple_of(512 * half, 512), 512)
    theirs = pl.ds(pl.multiple_of(512 - 512 * half, 512), 512)
    held = pl.ds(3 * half, 3)
    locals_ = [pltpu.make_async_copy(counts, owners, local_sem.at[3])]
    for number in range(3):
        locals_.append(
            pltpu.make_async_copy(
                given[number].at[pl.ds(0, 3), :, mine], raws[number].at[held], local_sem.at[number]
            )
        )
    for copy in locals_:
        copy.start()

    pl.semaphore_wait(barrier, 2 + 3 * (a > 0).astype(jnp.int32) + 3 * (a < 15).astype(jnp.int32))

    swaps = [
        start(
            [(given[number].at[pl.ds(0, 3), :, theirs], raws[number].at[held], sibling)],
            raws[number].at[held],
        )
        for number in range(3)
    ]
    locals_[0].wait()
    split = owners[me - half]
    own = jnp.where(half == 0, split, 4 - split)
    for s in range(4):
        out_held[s] = jnp.where(s < own, jnp.ones((32, 1024), F32), 0.0)
    places = [jnp.where(p < split, p, jnp.clip(3 + p - split, 0, 5)) for p in range(4)]

    def bring(number, ref):
        locals_[1 + number].wait()
        swaps[number]()
        raw = raws[number]

        def step(t):
            rows = pl.ds(pl.multiple_of(8 * t, 8), 8)
            out = []
            for q in range(4):
                four = [raw[places[p], rows, 128 * q : 128 * q + 128] for p in range(4)]
                for i, value in enumerate(transposed(four)):
                    out.append((ref, at(pl.multiple_of((4 + 4 * q + i) * RF + 8 + 8 * t, 8), 8), value))
            return out

        loop(0, 4, 4, step, group=1)

    ROWS = (RF, R1)
    OWN = ((4, 16, 8, 32), (8, 8, 8, 16))

    def near(first, count, side, depth):
        return first - 1 + depth if side < 0 else first + count - depth

    def far(first, count, side, depth):
        return first + count - 1 + depth if side < 0 else first - depth

    own2 = R2 + 2 * R2 + 8

    def there2(da, dj):
        return R2 + R2 * (2 - dj) + 8 * (1 - da)

    def pieces(strips, corners, block, da, dj, pick):
        out = []
        if block is not None:
            out.append((block, own2 if pick is near else there2(da, dj), 8, 1))
        if da == 0:
            for ref, level, depths in strips:
                plane, planes, row, rows = OWN[level]
                for d in depths:
                    out.append((ref, pick(plane, planes, dj, d) * ROWS[level] + row, rows, 1))
        elif dj == 0:
            for ref, level, depths in strips:
                plane, planes, row, rows = OWN[level]
                for d in depths:
                    out.append(
                        (ref, plane * ROWS[level] + pick(row, rows, da, d), planes, ROWS[level])
                    )
        else:
            for ref, level, depth, low, count in corners:
                plane, planes, row, rows = OWN[level]
                ends = [pick(row, rows, da, d) for d in (low, low + count - 1)]
                out.append((ref, pick(plane, planes, dj, depth) * ROWS[level] + min(ends), count, 1))
        return out

    def slab(ref, first, count, stride):
        return (pl.ds(first, count, stride=stride) if stride > 1 else pl.ds(first, count)), slice(None)

    spare = list(post)

    def ones(ref, *slabs):
        for rows in slabs:
            ref[rows, :] = jnp.ones((rows.size, LANES), F32)

    def exchange(strips, corners, block=None, where=FULL):
        out, got = spare.pop(0), spare.pop(0)
        arrivals, filled = [], []
        offset = 0
        for step_x in (1, -1, 0):
            copies, group_row = [], offset
            for da, dj in FULL:
                if da != step_x:
                    continue
                first_row = offset
                for ref, first, count, stride in pieces(strips, corners, block, da, dj, near):
                    out[pl.ds(offset, count), :] = ref[slab(ref, first, count, stride)]
                    offset += count
                offset += -offset % 8
                rows = pl.ds(first_row, offset - first_row)
                copies.append((out.at[rows], got.at[rows], device(da, dj)))
                filled.append((first_row, da, dj))
            group = pl.ds(group_row, offset - group_row)
            arrivals.append(start(copies, got.at[group], step_x, functools.partial(ones, got, group)))
        assert out.shape == (offset, LANES)

        def land():
            for arrived in arrivals:
                arrived()
            for offset, da, dj in filled:
                for ref, first, count, stride in pieces(strips, corners, block, da, dj, far):
                    ref[slab(ref, first, count, stride)] = got[pl.ds(offset, count), :]
                    offset += count

        return land

    def fine_corner(ref, depth):
        return [(ref, 0, d, 1, depth - d) for d in range(1, depth)]

    bring(0, cf)
    bring(1, sf)
    land_c = exchange(
        ((cf, 0, (1, 2, 3)), (sf, 0, (1, 2))), fine_corner(cf, 3) + fine_corner(sf, 2)
    )
    bring(2, uf)
    land_u = exchange(((uf, 0, (1, 2, 3)),), fine_corner(uf, 3))

    def coarse_c(i):
        total = pair_rows(cf, (4 + 2 * i) * RF + 8, 16, RF)
        return [(c1, at(pl.multiple_of((8 + i) * R1 + 8, 8), 16), pair_lanes(total, 1))]

    loop(0, 8, 8, coarse_c)

    def packed(ref):
        lanes = lane_ids(8) % 4
        total = jnp.zeros((8, LANES), F32)
        for i in range(4):
            value = pair_lanes(pair_rows(ref, (8 + 2 * i) * R1 + 8, 8, R1), 2)
            total = total + jnp.where(lanes == i, value, 0.0)
        return total

    def blocks2(ref, where):
        arrivals = []
        for step_x in (1, -1, 0):
            places_ = [(da, dj) for da, dj in where if da == step_x]
            copies = [
                (ref.at[pl.ds(own2, 8)], ref.at[pl.ds(there2(da, dj), 8)], device(da, dj))
                for da, dj in places_
            ]
            slabs = [pl.ds(there2(da, dj), 8) for da, dj in places_]
            arrivals.append(
                start(
                    copies, ref.at[pl.ds(0, 8 * len(copies))], step_x,
                    functools.partial(ones, ref, *slabs),
                )
            )

        def arrived():
            for part in arrivals:
                part()

        return arrived

    c2[pl.ds(own2, 8), :] = packed(c1)
    land_c1 = exchange(
        ((c1, 1, (1, 2, 3, 4, 5, 6)),), [(c1, 1, d, 1, 6 - d) for d in range(1, 6)], c2
    )

    land_c()
    far_c2 = blocks2(c2, FAR)

    def edges(ref, first, side, count, rows, plane, row, low_y, high_y, low_x, high_x):
        for outside, there, here in (
            (low_y, plane - 1, plane), (high_y, plane + count, plane + count - 1)
        ):
            slab_there = at(there * rows + first, side)
            ref[slab_there] = jnp.where(outside, ref[at(here * rows + first, side)], ref[slab_there])
        lines = 24
        for outside, there, here in ((low_x, row[0] - 1, row[0]), (high_x, row[1] + 1, row[1])):
            slab_there = slab(ref, there, lines, rows)
            ref[slab_there] = jnp.where(outside, ref[slab(ref, here, lines, rows)], ref[slab_there])

    def cut(faces, first, side, count, rows, plane, row, low_y, high_y, low_x, high_x):
        for n, outside, here in ((0, low_y, plane), (1, high_y, plane + count - 1)):
            where = (n,) + at(here * rows + first, side)
            faces[where] = jnp.where(outside, 0.0, faces[where])
        for n, outside, here in ((2, low_x, row[0]), (3, high_x, row[1])):
            where = (n,) + slab(faces, here, 24, rows)
            faces[where] = jnp.where(outside, 0.0, faces[where])

    ends = (j == 0, j == 7, a == 0, a == 15)
    edges(cf, 4, 40, 16, RF, 4, (8, 39), *ends)
    fine_faces = [fine.at[n] for n in range(6)]

    def fine_coeffs(p):
        base = p * RF + 4
        centre, besides = around(cf, base, 40, RF, 1)
        z = lane_ids(40)
        inside = (None, None, None, None, z != 0, z != 127)
        faces, total, quarter = coefficients(centre, besides, inside)
        out = [(fine, (n,) + at(base, 40), faces[n]) for n in range(6)]
        out.append((gf, at(base, 40), 2.0 * quarter))
        out.append((df, at(base, 40), 1.25 * total))
        return out

    loop(2, 22, 4, fine_coeffs, group=1)
    cut(fine, 4, 40, 16, RF, 4, (8, 39), *ends)
    land_u()

    def sweep(src, dst, faces, right, low, high, width, rows, start, count, twist):
        def step(p):
            base = p * rows + start
            centre, besides = around(src, base, count, rows, twist)
            value = 0.2 * centre + right[pl.ds(base, count), :] + weighted(faces, base, count, besides)
            return [(dst, at(base, count), value)]

        loop(low, high, width, step, group=5)

    def leftover(src, dst, faces, right, diag, low, high, width, rows, start, count, twist):
        def step(p):
            base = p * rows + start
            centre, besides = around(src, base, count, rows, twist)
            value = diag[pl.ds(base, count), :] * (
                right[pl.ds(base, count), :] + weighted(faces, base, count, besides) - 0.8 * centre
            )
            return [(dst, at(base, count), value)]

        loop(low, high, width, step, group=4)

    def first_sweep(p):
        base = p * RF + 4
        centre, besides = around(uf, base, 40, RF, 1)
        right = gf[pl.ds(base, 40), :] * sf[pl.ds(base, 40), :]
        value = 0.2 * centre + right + weighted(fine_faces, base, 40, besides)
        return [(u1, at(base, 40), value), (gf, at(base, 40), right)]

    loop(2, 22, 10, first_sweep, group=5)
    sweep(u1, u2, fine_faces, gf, 3, 21, 9, RF, 4, 40, 1)
    leftover(u2, u1, fine_faces, gf, df, 4, 20, 8, RF, 8, 32, 1)

    def coarse_f(i):
        total = pair_rows(u1, (4 + 2 * i) * RF + 8, 16, RF)
        return [(f1, at(pl.multiple_of((8 + i) * R1 + 8, 8), 16), pair_lanes(total, 1))]

    loop(0, 8, 8, coarse_f)
    land_f = exchange(((f1, 1, (1, 2)),), [(f1, 1, 1, 1, 1)])
    land_rest = exchange(
        ((f1, 1, (3, 4, 5)), (u2, 0, (1, 2, 3))),
        [(f1, 1, 1, 2, 3), (f1, 1, 2, 1, 3), (f1, 1, 3, 1, 2), (f1, 1, 4, 1, 1)] + fine_corner(u2, 3),
    )

    drain(but=6)
    land_c1()
    edges(c1, 0, 32, 8, R1, 8, (8, 23), *ends)
    mid_faces = [mid.at[n] for n in range(6)]

    def mid_coeffs(p):
        base = p * R1
        centre, besides = around(c1, base, 32, R1, 2)
        z = lane_ids(32)
        inside = (None, None, None, None, z >= 2, z < 126)
        faces, total, quarter = coefficients(centre, besides, inside)
        out = [(mid, (n,) + at(base, 32), faces[n]) for n in range(6)]
        out.append((w1, at(base, 32), 8.0 * quarter))
        out.append((d1, at(base, 32), 0.3125 * total))
        return out

    loop(6, 18, 3, mid_coeffs, group=1)
    cut(mid, 0, 32, 8, R1, 8, (8, 23), *ends)

    def guess(p):
        base = p * R1
        return [(g1, at(base, 32), w1[pl.ds(base, 32), :] * f1[pl.ds(base, 32), :])]

    land_f()
    loop(6, 18, 12, guess)
    sweep(g1, e1, mid_faces, g1, 7, 17, 10, R1, 4, 24, 2)
    leftover(e1, r1, mid_faces, g1, d1, 8, 16, 8, R1, 8, 16, 2)
    f2[pl.ds(own2, 8), :] = packed(r1)
    sixth = blocks2(f2, FAR + FULL)

    loop(3, 6, 3, mid_coeffs, group=1)
    loop(18, 21, 3, mid_coeffs, group=1)
    cut(mid, 0, 32, 8, R1, 8, (8, 23), *ends)
    far_c2()

    def around2(ref):
        lanes = lane_ids(5 * R2) % 4
        centre = ref[R2 : 6 * R2, :]
        return centre, (
            jnp.where(lanes == 0, turn(ref[0 : 5 * R2, :], -3), turn(centre, 1)),
            jnp.where(lanes == 3, turn(ref[2 * R2 : 7 * R2, :], 3), turn(centre, -1)),
            ref[pl.ds(zero + (R2 - 1), 5 * R2), :],
            ref[pl.ds(zero + (R2 + 1), 5 * R2), :],
            turn(centre, 4),
            turn(centre, -4),
        )

    rows2, lanes2 = row_ids(5 * R2), lane_ids(5 * R2)
    x = rows2 % R2 + (8 * a - 8)
    y = 4 * (rows2 // R2) + lanes2 % 4 + (4 * j - 8)
    inside2 = (y != 0, y != 31, x != 0, x != 127, lanes2 >= 4, lanes2 < 124)
    centre, besides = around2(c2)
    faces, total, quarter = coefficients(centre, besides, inside2)
    for n in range(6):
        deep[n] = faces[n]
    deep[6] = 32.0 * quarter

    drain(but=3)
    land_rest()
    loop(3, 21, 9, guess)
    sweep(g1, e1, mid_faces, g1, 4, 20, 8, R1, 4, 24, 2)

    sixth()
    g2[...] = deep[6] * f2[R2 : 6 * R2, :]
    e2[R2 : 6 * R2, :] = g2[...]
    for src, dst in ((e2, e2b), (e2b, e2), (e2, e2b)):
        centre, besides = around2(src)
        parts = [deep[n] * besides[n] for n in range(6)]
        dst[R2 : 6 * R2, :] = (
            (0.2 * centre + g2[...]) + (parts[0] + parts[1]) + (parts[2] + parts[3]) + (parts[4] + parts[5])
        )

    lanes16 = lane_ids(16) % 4
    hops = ((1, 2), (-1, 2), (1, -2), (-1, -2))
    for number in range(8):
        block, i = (number + 6) // 4, (number + 6) % 4
        value = jnp.where(lanes16 == i, e2b[pl.ds(zero + (R2 + R2 * block + 4), 16), :], 0.0)
        value = value + turn(value, hops[i][0])
        value = value + turn(value, hops[i][1])
        pe2[pl.ds(32 * number, 16, stride=2), :] = value
        pe2[pl.ds(32 * number + 1, 16, stride=2), :] = value

    def corrected1(p):
        value = e1[pl.ds(p * R1 + 4, 24), :] + pe2[pl.ds((p // 2 - 2) * 32 + 4, 24), :]
        return [(e1, at(p * R1 + 4, 24), value)]

    loop(4, 20, 16, corrected1)
    sweep(e1, e1b, mid_faces, g1, 5, 19, 14, R1, 4, 24, 2)
    sweep(e1b, e1, mid_faces, g1, 6, 18, 12, R1, 4, 24, 2)

    def grown(i):
        value = e1[pl.ds((i + 6) * R1 + 4, 24), :]
        return [(pe1, (pl.ds(RF * i + odd, 24, stride=2), slice(None)), value) for odd in (0, 1)]

    loop(0, 12, 12, grown)

    def corrected0(p):
        base = p * RF + 4
        return [(u2, at(base, 40), u2[pl.ds(base, 40), :] + pe1[pl.ds((p // 2) * RF + 4, 40), :])]

    loop(1, 23, 11, corrected0)
    sweep(u2, u1, fine_faces, gf, 2, 22, 10, RF, 4, 40, 1)

    def give(ref, stage, other, quads):
        def step(t):
            rows = pl.ds(pl.multiple_of(8 * t, 8), 8)
            out = []
            for q in quads:
                four = [
                    ref[pl.ds(pl.multiple_of((4 + 4 * q + i) * RF + 8 + 8 * t, 8), 8), :]
                    for i in range(4)
                ]
                for p, value in enumerate(transposed(four)):
                    out.append((stage, (p, rows, slice(128 * q, 128 * q + 128)), value))
            return out

        loop(0, 4, 4, step)
        lanes = pl.ds(128 * quads[0], 128 * len(quads))
        return stage.at[pl.ds(1 - half, 3), :, lanes], other.at[:, :, lanes], sibling

    def keep(stage, out):
        for s in range(4):
            out[s, :, mine] = stage[jnp.clip(s + half * split, 0, 3)]

    def take(other, out):
        for s in range(4):
            out[s, :, theirs] = other[jnp.clip(s + half * (split - 1), 0, 2)]

    last = []
    sweep(u1, u2, fine_faces, gf, 3, 12, 9, RF, 4, 40, 1)
    last.append(start([give(u2, stage_f, other_f, (0, 1))], other_f.at[:, :, pl.ds(0, 256)]))
    sweep(u1, u2, fine_faces, gf, 12, 21, 9, RF, 4, 40, 1)
    last.append(start([give(u2, stage_f, other_f, (2, 3))], other_f.at[:, :, pl.ds(256, 256)]))
    leftover(u2, u1, fine_faces, gf, df, 4, 12, 8, RF, 8, 32, 1)
    last.append(start([give(u1, stage_r, other_r, (0, 1))], other_r.at[:, :, pl.ds(0, 256)]))
    leftover(u2, u1, fine_faces, gf, df, 12, 20, 8, RF, 8, 32, 1)
    last.append(start([give(u1, stage_r, other_r, (2, 3))], other_r.at[:, :, pl.ds(256, 256)]))
    keep(stage_f, out_field)
    last[0]()
    last[1]()
    take(other_f, out_field)
    keep(stage_r, out_resid)
    last[2]()
    last[3]()
    take(other_r, out_resid)
    drain()


def vmem(*shape):
    return pltpu.VMEM(shape, F32)


def body(source, conductance, initial, box_counts):
    fine_field = vmem(PF * RF, LANES)
    mid_field = vmem(P1 * R1, LANES)
    deep_field = vmem(7 * R2, LANES)
    scratch = [pltpu.SMEM(box_counts.shape, jnp.int32)] + [vmem(6, 32, 512)] * 3
    scratch += [fine_field] * 5 + [vmem(6, PF * RF, LANES)] + [fine_field] * 2
    scratch += [mid_field] * 4 + [vmem(8 * 32, LANES), vmem(6, P1 * R1, LANES)] + [mid_field] * 4
    scratch += [deep_field] * 4 + [vmem(7, 5 * R2, LANES), vmem(5 * R2, LANES), vmem(12 * RF, LANES)]
    scratch += [vmem(4, 32, 512)] * 2 + [vmem(3, 32, 512)] * 2
    for big, middle, small in ((160, 80, 8), (96, 48, 8), (104, 56, 24), (32, 16, 8), (144, 72, 16)):
        scratch += [vmem(2 * big + 2 * middle + 4 * small, LANES)] * 2
    scratch += [pltpu.SemaphoreType.DMA((4,))] + [pltpu.SemaphoreType.DMA((ROUNDS,))] * 2
    hbm = pl.BlockSpec(memory_space=pltpu.HBM)
    shape = jax.ShapeDtypeStruct(source.shape, source.dtype)
    field, resid, held = pl.pallas_call(
        kernel,
        out_shape=(shape,) * 3,
        in_specs=[hbm] * 4,
        out_specs=(pl.BlockSpec(memory_space=pltpu.VMEM),) * 3,
        scratch_shapes=scratch,
        compiler_params=pltpu.CompilerParams(
            collective_id=0, has_side_effects=True, vmem_limit_bytes=40 * 2**20
        ),
        cost_estimate=pl.CostEstimate(flops=3 * 10**7, bytes_accessed=3 * 10**6, transcendentals=0),
    )(*[pltpu.with_memory_space_constraint(x, pltpu.HBM) for x in (box_counts, source, conductance, initial)])
    return field * held, resid * held


def solution(mesh):
    return jax.shard_map(
        body,
        mesh=mesh,
        in_specs=(P("box", None, None), P("box", None, None), P("box", None, None), P()),
        out_specs=(P("box", None, None), P("box", None, None)),
        check_vma=False,
    )
```

```python
import functools

import jax
import jax.numpy as jnp
from jax import lax
from jax.experimental import pallas as pl
from jax.experimental.pallas import tpu as pltpu
from jax.sharding import PartitionSpec as P


RF, PF = 48, 24
R1, P1 = 32, 24
R2 = 24
LANES = 128
FULL = (1, 1), (1, -1), (1, 0), (-1, 1), (-1, -1), (-1, 0), (0, 1), (0, -1)
FAR = (1, 2), (1, -2), (-1, 2), (-1, -2), (0, 2), (0, -2)
F32 = jnp.float32
ROUNDS = 3 + 3 * (5 + 2) + 4


def lane_ids(rows):
    return lax.broadcasted_iota(jnp.int32, (rows, LANES), 1)


def row_ids(rows):
    return lax.broadcasted_iota(jnp.int32, (rows, LANES), 0)


def turn(value, steps):
    return pltpu.roll(value, steps % LANES, 1)


def transposed(four):
    lanes = lane_ids(four[0].shape[0])
    low = lanes < 64
    even = (lanes // 32) % 2 == 0
    a, b, c, d = four
    e = jnp.where(low, a, turn(c, 64))
    f = jnp.where(low, b, turn(d, 64))
    g = jnp.where(low, turn(a, 64), c)
    h = jnp.where(low, turn(b, 64), d)
    return (
        jnp.where(even, e, turn(f, 32)),
        jnp.where(even, turn(e, -32), f),
        jnp.where(even, g, turn(h, 32)),
        jnp.where(even, turn(g, -32), h),
    )


def coefficients(c, besides, inside):
    around_ = [
        beside if within is None else jnp.where(within, beside, c)
        for beside, within in zip(besides, inside)
    ]
    total = 3.0 * c + 0.5 * (
        (around_[0] + around_[1]) + (around_[2] + around_[3]) + (around_[4] + around_[5])
    )
    quarter = 0.4 / total
    faces = [
        (c + beside) * quarter if within is None else jnp.where(within, (c + beside) * quarter, 0.0)
        for beside, within in zip(besides, inside)
    ]
    return faces, total, quarter


def around(ref, base, count, rows, twist):
    centre = ref[pl.ds(base, count), :]
    return centre, (
        ref[pl.ds(base - rows, count), :],
        ref[pl.ds(base + rows, count), :],
        ref[pl.ds(base - 1, count), :],
        ref[pl.ds(base + 1, count), :],
        turn(centre, twist),
        turn(centre, -twist),
    )


def weighted(faces, base, count, besides):
    parts = [faces[n][pl.ds(base, count), :] * besides[n] for n in range(6)]
    return (parts[0] + parts[1]) + (parts[2] + parts[3]) + (parts[4] + parts[5])


def planes_loop(low, high, width, body, group=None, base=0):
    assert (high - low) % width == 0
    group = group or width

    def step(index, carry):
        first = base + low + index * width
        stores = []
        for m in range(width):
            stores += body(first + m)
            if (m + 1) % group == 0 or m == width - 1:
                for ref, index_, value in stores:
                    ref[index_] = value
                stores = []
        return carry

    if high - low == width:
        step(0, 0)
    else:
        lax.fori_loop(0, (high - low) // width, step, 0)


def at(base, count):
    return pl.ds(base, count), slice(None)


def pair_rows(ref, base, count, rows):
    got = [
        ref[pl.ds(base + offset, count, stride=2), :] for offset in (0, 1, rows, rows + 1)
    ]
    return (got[0] + got[1]) + (got[2] + got[3])


def pair_lanes(value, width):
    first = (lane_ids(value.shape[0]) // width) % 2 == 0
    return 0.125 * (value + jnp.where(first, turn(value, -width), turn(value, width)))


def kernel(
    counts, source, conductance, initial, out_field, out_resid, out_held,
    owners, raw_c, raw_u, raw_s, cf, uf, sf, u1, u2, fine, gf, df,
    c1, f1, e1, e1b, pe2, mid, w1, g1, d1, r1, c2, f2, e2, e2b, deep, g2, pe1,
    stage_f, stage_r, other_f, other_r, *rest,
):
    post, local_sem, send_sem, recv_sem = rest[:-3], rest[-3], rest[-2], rest[-1]
    me = lax.axis_index("box")
    a, j = me // 8, me % 8
    half = me % 2
    sibling = me + 1 - 2 * half
    zero = me // 1024
    loop = functools.partial(planes_loop, base=zero)
    across = {da: ((a + da + 16) % 16) * 8 for da in (-1, 0, 1)}
    along = {dj: (j + dj + 8) % 8 for dj in (-2, -1, 0, 1, 2)}

    sibling_far = across[0] + (j - 1 + 2 * half + 8) % 8

    def device(da, dj):
        return across[da] + along[dj]

    numbers = iter(range(ROUNDS))
    leaving = []

    def describe(src, dst, number, target):
        return pltpu.make_async_remote_copy(
            src_ref=src, dst_ref=dst, send_sem=send_sem.at[number], recv_sem=recv_sem.at[number],
            device_id=(target,), device_id_type=pl.DeviceIdType.MESH,
        )

    leaves = {1: a < 15, -1: a > 0}
    comes = {1: a > 0, -1: a < 15}

    def inside(column):
        return jnp.logical_and(column >= 0, column < 8)

    def sized(messages, whole, sign, act):
        sizes = {}
        for column in range(8):
            rows = sum(rows for rows, da, dj in messages if 0 <= column + sign * dj < 8)
            sizes.setdefault(rows, []).append(column)
        for rows, columns in sizes.items():
            if len(columns) == 8:
                act(rows)
            else:
                there = functools.reduce(jnp.logical_or, [j == column for column in columns])
                pl.when(there)(functools.partial(act, rows))

    def start(copies, ref, first_row, messages, without):
        number = next(numbers)
        step_x = messages[0][1]

        def some(rows):
            part = ref.at[pl.ds(first_row, rows)]
            return describe(part, part, number, sibling)

        def go():
            for src, dst, target, dj in copies:
                begin = describe(src, dst, number, target).start
                if dj == 0:
                    begin()
                else:
                    pl.when(inside(j + dj))(begin)

        def gone():
            sized(messages, ref, 1, lambda rows: some(rows).wait_send())

        def come():
            sized(messages, ref, -1, lambda rows: some(rows).wait_recv())
            for dj in sorted({dj for rows, da, dj in messages}):
                if dj != 0:
                    gaps = [n for n, item in enumerate(messages) if item[2] == dj]
                    pl.when(jnp.logical_not(inside(j - dj)))(functools.partial(without, *gaps))

        if step_x == 0:
            go()
            leaving.append(gone)
            return come
        pl.when(leaves[step_x])(go)
        leaving.append(lambda: pl.when(leaves[step_x])(gone))

        def arrived():
            pl.when(comes[step_x])(come)
            pl.when(jnp.logical_not(comes[step_x]))(functools.partial(without, *range(len(messages))))

        return arrived

    def hand(src, dst, whole):
        number = next(numbers)
        describe(src, dst, number, sibling).start()
        everything = describe(whole, whole, number, sibling)
        leaving.append(everything.wait_send)
        return everything.wait_recv

    def drain(but=0):
        while len(leaving) > but:
            leaving.pop(0)()

    barrier = pltpu.get_barrier_semaphore()

    def here(*targets):
        for target in targets:
            pl.semaphore_signal(
                barrier, inc=1, device_id=(target,), device_id_type=pl.DeviceIdType.MESH
            )

    here(sibling)
    pl.when(inside(j - 1 + 2 * half))(lambda: here(sibling_far))
    for da in (1, -1):

        def beside():
            here(device(da, 0))
            for dj in (1, -1):
                pl.when(inside(j + dj))(lambda: here(device(da, dj)))

        pl.when(leaves[da])(beside)

    raws = (raw_c, raw_s, raw_u)
    given = (conductance, source, initial)
    mine = pl.ds(pl.multiple_of(512 * half, 512), 512)
    theirs = pl.ds(pl.multiple_of(512 - 512 * half, 512), 512)
    held = pl.ds(3 * half, 3)
    locals_ = [pltpu.make_async_copy(counts, owners, local_sem.at[3])]
    for number in range(3):
        locals_.append(
            pltpu.make_async_copy(
                given[number].at[pl.ds(0, 3), :, mine], raws[number].at[held], local_sem.at[number]
            )
        )
    for copy in locals_:
        copy.start()

    around_x = 1 + (a > 0).astype(jnp.int32) + (a < 15).astype(jnp.int32)
    around_y = 1 + (j > 0).astype(jnp.int32) + (j < 7).astype(jnp.int32)
    pl.semaphore_wait(barrier, around_x * around_y - 1)

    swaps = [
        hand(given[number].at[pl.ds(0, 3), :, theirs], raws[number].at[held], raws[number].at[held])
        for number in range(3)
    ]
    locals_[0].wait()
    split = owners[me - half]
    own = jnp.where(half == 0, split, 4 - split)
    for s in range(4):
        out_held[s] = jnp.where(s < own, jnp.ones((32, 1024), F32), 0.0)
    places = [jnp.where(p < split, p, jnp.clip(3 + p - split, 0, 5)) for p in range(4)]

    def bring(number, ref):
        locals_[1 + number].wait()
        swaps[number]()
        raw = raws[number]

        def step(t):
            rows = pl.ds(pl.multiple_of(8 * t, 8), 8)
            out = []
            for q in range(4):
                four = [raw[places[p], rows, 128 * q : 128 * q + 128] for p in range(4)]
                for i, value in enumerate(transposed(four)):
                    out.append((ref, at(pl.multiple_of((4 + 4 * q + i) * RF + 8 + 8 * t, 8), 8), value))
            return out

        loop(0, 4, 4, step, group=1)

    ROWS = (RF, R1)
    OWN = ((4, 16, 8, 32), (8, 8, 8, 16))

    def near(first, count, side, depth):
        return first - 1 + depth if side < 0 else first + count - depth

    def far(first, count, side, depth):
        return first + count - 1 + depth if side < 0 else first - depth

    own2 = R2 + 2 * R2 + 8

    def there2(da, dj):
        return R2 + R2 * (2 - dj) + 8 * (1 - da)

    def pieces(strips, corners, block, da, dj, pick):
        out = []
        if block is not None:
            out.append((block, own2 if pick is near else there2(da, dj), 8, 1))
        if da == 0:
            for ref, level, depths in strips:
                plane, planes, row, rows = OWN[level]
                for d in depths:
                    out.append((ref, pick(plane, planes, dj, d) * ROWS[level] + row, rows, 1))
        elif dj == 0:
            for ref, level, depths in strips:
                plane, planes, row, rows = OWN[level]
                for d in depths:
                    out.append(
                        (ref, plane * ROWS[level] + pick(row, rows, da, d), planes, ROWS[level])
                    )
        else:
            for ref, level, depth, low, count in corners:
                plane, planes, row, rows = OWN[level]
                ends = [pick(row, rows, da, d) for d in (low, low + count - 1)]
                out.append((ref, pick(plane, planes, dj, depth) * ROWS[level] + min(ends), count, 1))
        return out

    def slab(ref, first, count, stride):
        return (pl.ds(first, count, stride=stride) if stride > 1 else pl.ds(first, count)), slice(None)

    spare = list(post)

    def filler(ref, firsts, messages):
        def without(*gaps):
            for n in gaps:
                ref[pl.ds(firsts[n], messages[n][0]), :] = jnp.ones((messages[n][0], LANES), F32)

        return without

    def exchange(strips, corners, block=None, where=FULL):
        out, got = spare.pop(0), spare.pop(0)
        arrivals, filled = [], []
        offset = 0
        for step_x in (1, -1, 0):
            copies, messages, group_row = [], [], offset
            for da, dj in FULL:
                if da != step_x:
                    continue
                first_row = offset
                for ref, first, count, stride in pieces(strips, corners, block, da, dj, near):
                    out[pl.ds(offset, count), :] = ref[slab(ref, first, count, stride)]
                    offset += count
                offset += -offset % 8
                rows = pl.ds(first_row, offset - first_row)
                copies.append((out.at[rows], got.at[rows], device(da, dj), dj))
                messages.append((rows.size, da, dj))
                filled.append((first_row, da, dj))
            firsts = [first for first, da, dj in filled if da == step_x]
            arrivals.append(start(copies, got, group_row, messages, filler(got, firsts, messages)))
        assert out.shape == (offset, LANES)

        def land():
            for arrived in arrivals:
                arrived()
            for offset, da, dj in filled:
                for ref, first, count, stride in pieces(strips, corners, block, da, dj, far):
                    ref[slab(ref, first, count, stride)] = got[pl.ds(offset, count), :]
                    offset += count

        return land

    def fine_corner(ref, depth):
        return [(ref, 0, d, 1, depth - d) for d in range(1, depth)]

    bring(0, cf)
    bring(1, sf)
    land_c = exchange(
        ((cf, 0, (1, 2, 3)), (sf, 0, (1, 2))), fine_corner(cf, 3) + fine_corner(sf, 2)
    )
    bring(2, uf)
    land_u = exchange(((uf, 0, (1, 2, 3)),), fine_corner(uf, 3))

    def coarse_c(i):
        total = pair_rows(cf, (4 + 2 * i) * RF + 8, 16, RF)
        return [(c1, at(pl.multiple_of((8 + i) * R1 + 8, 8), 16), pair_lanes(total, 1))]

    loop(0, 8, 8, coarse_c)

    def packed(ref):
        lanes = lane_ids(8) % 4
        total = jnp.zeros((8, LANES), F32)
        for i in range(4):
            value = pair_lanes(pair_rows(ref, (8 + 2 * i) * R1 + 8, 8, R1), 2)
            total = total + jnp.where(lanes == i, value, 0.0)
        return total

    def blocks2(ref, where):
        arrivals = []
        for step_x in (1, -1, 0):
            places_ = [(da, dj) for da, dj in where if da == step_x]
            copies = [
                (ref.at[pl.ds(own2, 8)], ref.at[pl.ds(there2(da, dj), 8)], device(da, dj), dj)
                for da, dj in places_
            ]
            firsts = [there2(da, dj) for da, dj in places_]
            messages = [(8, da, dj) for da, dj in places_]
            arrivals.append(start(copies, ref, 0, messages, filler(ref, firsts, messages)))

        def arrived():
            for part in arrivals:
                part()

        return arrived

    c2[pl.ds(own2, 8), :] = packed(c1)
    land_c1 = exchange(
        ((c1, 1, (1, 2, 3, 4, 5, 6)),), [(c1, 1, d, 1, 6 - d) for d in range(1, 6)], c2
    )

    land_c()
    far_c2 = blocks2(c2, FAR)

    def edges(ref, first, side, count, rows, plane, row, low_y, high_y, low_x, high_x):
        for outside, there, here in (
            (low_y, plane - 1, plane), (high_y, plane + count, plane + count - 1)
        ):
            slab_there = at(there * rows + first, side)
            ref[slab_there] = jnp.where(outside, ref[at(here * rows + first, side)], ref[slab_there])
        lines = 24
        for outside, there, here in ((low_x, row[0] - 1, row[0]), (high_x, row[1] + 1, row[1])):
            slab_there = slab(ref, there, lines, rows)
            ref[slab_there] = jnp.where(outside, ref[slab(ref, here, lines, rows)], ref[slab_there])

    def cut(faces, first, side, count, rows, plane, row, low_y, high_y, low_x, high_x):
        for n, outside, here in ((0, low_y, plane), (1, high_y, plane + count - 1)):
            where = (n,) + at(here * rows + first, side)
            faces[where] = jnp.where(outside, 0.0, faces[where])
        for n, outside, here in ((2, low_x, row[0]), (3, high_x, row[1])):
            where = (n,) + slab(faces, here, 24, rows)
            faces[where] = jnp.where(outside, 0.0, faces[where])

    ends = (j == 0, j == 7, a == 0, a == 15)
    edges(cf, 4, 40, 16, RF, 4, (8, 39), *ends)
    fine_faces = [fine.at[n] for n in range(6)]

    def fine_coeffs(p):
        base = p * RF + 4
        centre, besides = around(cf, base, 40, RF, 1)
        z = lane_ids(40)
        inside = (None, None, None, None, z != 0, z != 127)
        faces, total, quarter = coefficients(centre, besides, inside)
        out = [(fine, (n,) + at(base, 40), faces[n]) for n in range(6)]
        out.append((gf, at(base, 40), 2.0 * quarter))
        out.append((df, at(base, 40), 1.25 * total))
        return out

    loop(2, 22, 4, fine_coeffs, group=1)
    cut(fine, 4, 40, 16, RF, 4, (8, 39), *ends)
    land_u()

    def sweep(src, dst, faces, right, low, high, width, rows, start, count, twist):
        def step(p):
            base = p * rows + start
            centre, besides = around(src, base, count, rows, twist)
            value = 0.2 * centre + right[pl.ds(base, count), :] + weighted(faces, base, count, besides)
            return [(dst, at(base, count), value)]

        loop(low, high, width, step, group=5)

    def leftover(src, dst, faces, right, diag, low, high, width, rows, start, count, twist):
        def step(p):
            base = p * rows + start
            centre, besides = around(src, base, count, rows, twist)
            value = diag[pl.ds(base, count), :] * (
                right[pl.ds(base, count), :] + weighted(faces, base, count, besides) - 0.8 * centre
            )
            return [(dst, at(base, count), value)]

        loop(low, high, width, step, group=4)

    def first_sweep(p):
        base = p * RF + 4
        centre, besides = around(uf, base, 40, RF, 1)
        right = gf[pl.ds(base, 40), :] * sf[pl.ds(base, 40), :]
        value = 0.2 * centre + right + weighted(fine_faces, base, 40, besides)
        return [(u1, at(base, 40), value), (gf, at(base, 40), right)]

    loop(2, 22, 10, first_sweep, group=5)
    sweep(u1, u2, fine_faces, gf, 3, 21, 9, RF, 4, 40, 1)
    leftover(u2, u1, fine_faces, gf, df, 4, 20, 8, RF, 8, 32, 1)

    def coarse_f(i):
        total = pair_rows(u1, (4 + 2 * i) * RF + 8, 16, RF)
        return [(f1, at(pl.multiple_of((8 + i) * R1 + 8, 8), 16), pair_lanes(total, 1))]

    loop(0, 8, 8, coarse_f)
    land_f = exchange(((f1, 1, (1, 2)),), [(f1, 1, 1, 1, 1)])
    land_rest = exchange(
        ((f1, 1, (3, 4, 5)), (u2, 0, (1, 2, 3))),
        [(f1, 1, 1, 2, 3), (f1, 1, 2, 1, 3), (f1, 1, 3, 1, 2), (f1, 1, 4, 1, 1)] + fine_corner(u2, 3),
    )

    drain(but=6)
    land_c1()
    edges(c1, 0, 32, 8, R1, 8, (8, 23), *ends)
    mid_faces = [mid.at[n] for n in range(6)]

    def mid_coeffs(p):
        base = p * R1
        centre, besides = around(c1, base, 32, R1, 2)
        z = lane_ids(32)
        inside = (None, None, None, None, z >= 2, z < 126)
        faces, total, quarter = coefficients(centre, besides, inside)
        out = [(mid, (n,) + at(base, 32), faces[n]) for n in range(6)]
        out.append((w1, at(base, 32), 8.0 * quarter))
        out.append((d1, at(base, 32), 0.3125 * total))
        return out

    loop(6, 18, 3, mid_coeffs, group=1)
    cut(mid, 0, 32, 8, R1, 8, (8, 23), *ends)

    def guess(p):
        base = p * R1
        return [(g1, at(base, 32), w1[pl.ds(base, 32), :] * f1[pl.ds(base, 32), :])]

    land_f()
    loop(6, 18, 12, guess)
    sweep(g1, e1, mid_faces, g1, 7, 17, 10, R1, 4, 24, 2)
    leftover(e1, r1, mid_faces, g1, d1, 8, 16, 8, R1, 8, 16, 2)
    f2[pl.ds(own2, 8), :] = packed(r1)
    sixth = blocks2(f2, FAR + FULL)

    loop(3, 6, 3, mid_coeffs, group=1)
    loop(18, 21, 3, mid_coeffs, group=1)
    cut(mid, 0, 32, 8, R1, 8, (8, 23), *ends)
    far_c2()

    def around2(ref):
        lanes = lane_ids(5 * R2) % 4
        centre = ref[R2 : 6 * R2, :]
        return centre, (
            jnp.where(lanes == 0, turn(ref[0 : 5 * R2, :], -3), turn(centre, 1)),
            jnp.where(lanes == 3, turn(ref[2 * R2 : 7 * R2, :], 3), turn(centre, -1)),
            ref[pl.ds(zero + (R2 - 1), 5 * R2), :],
            ref[pl.ds(zero + (R2 + 1), 5 * R2), :],
            turn(centre, 4),
            turn(centre, -4),
        )

    rows2, lanes2 = row_ids(5 * R2), lane_ids(5 * R2)
    x = rows2 % R2 + (8 * a - 8)
    y = 4 * (rows2 // R2) + lanes2 % 4 + (4 * j - 8)
    inside2 = (y != 0, y != 31, x != 0, x != 127, lanes2 >= 4, lanes2 < 124)
    centre, besides = around2(c2)
    faces, total, quarter = coefficients(centre, besides, inside2)
    for n in range(6):
        deep[n] = faces[n]
    deep[6] = 32.0 * quarter

    drain(but=3)
    land_rest()
    loop(3, 21, 9, guess)
    sweep(g1, e1, mid_faces, g1, 4, 20, 8, R1, 4, 24, 2)

    sixth()
    g2[...] = deep[6] * f2[R2 : 6 * R2, :]
    e2[R2 : 6 * R2, :] = g2[...]
    for src, dst in ((e2, e2b), (e2b, e2), (e2, e2b)):
        centre, besides = around2(src)
        parts = [deep[n] * besides[n] for n in range(6)]
        dst[R2 : 6 * R2, :] = (
            (0.2 * centre + g2[...]) + (parts[0] + parts[1]) + (parts[2] + parts[3]) + (parts[4] + parts[5])
        )

    lanes16 = lane_ids(16) % 4
    hops = ((1, 2), (-1, 2), (1, -2), (-1, -2))
    for number in range(8):
        block, i = (number + 6) // 4, (number + 6) % 4
        value = jnp.where(lanes16 == i, e2b[pl.ds(zero + (R2 + R2 * block + 4), 16), :], 0.0)
        value = value + turn(value, hops[i][0])
        value = value + turn(value, hops[i][1])
        pe2[pl.ds(32 * number, 16, stride=2), :] = value
        pe2[pl.ds(32 * number + 1, 16, stride=2), :] = value

    def corrected1(p):
        value = e1[pl.ds(p * R1 + 4, 24), :] + pe2[pl.ds((p // 2 - 2) * 32 + 4, 24), :]
        return [(e1, at(p * R1 + 4, 24), value)]

    loop(4, 20, 16, corrected1)
    sweep(e1, e1b, mid_faces, g1, 5, 19, 14, R1, 4, 24, 2)
    sweep(e1b, e1, mid_faces, g1, 6, 18, 12, R1, 4, 24, 2)

    def grown(i):
        value = e1[pl.ds((i + 6) * R1 + 4, 24), :]
        return [(pe1, (pl.ds(RF * i + odd, 24, stride=2), slice(None)), value) for odd in (0, 1)]

    loop(0, 12, 12, grown)

    def corrected0(p):
        base = p * RF + 4
        return [(u2, at(base, 40), u2[pl.ds(base, 40), :] + pe1[pl.ds((p // 2) * RF + 4, 40), :])]

    loop(1, 23, 11, corrected0)
    sweep(u2, u1, fine_faces, gf, 2, 22, 10, RF, 4, 40, 1)

    def give(ref, stage, other, quads):
        def step(t):
            rows = pl.ds(pl.multiple_of(8 * t, 8), 8)
            out = []
            for q in quads:
                four = [
                    ref[pl.ds(pl.multiple_of((4 + 4 * q + i) * RF + 8 + 8 * t, 8), 8), :]
                    for i in range(4)
                ]
                for p, value in enumerate(transposed(four)):
                    out.append((stage, (p, rows, slice(128 * q, 128 * q + 128)), value))
            return out

        loop(0, 4, 4, step)
        lanes = pl.ds(128 * quads[0], 128 * len(quads))
        return stage.at[pl.ds(1 - half, 3), :, lanes], other.at[:, :, lanes], other.at[:, :, lanes]

    def keep(stage, out):
        for s in range(4):
            out[s, :, mine] = stage[jnp.clip(s + half * split, 0, 3)]

    def take(other, out):
        for s in range(4):
            out[s, :, theirs] = other[jnp.clip(s + half * (split - 1), 0, 2)]

    last = []
    sweep(u1, u2, fine_faces, gf, 3, 12, 9, RF, 4, 40, 1)
    last.append(hand(*give(u2, stage_f, other_f, (0, 1))))
    sweep(u1, u2, fine_faces, gf, 12, 21, 9, RF, 4, 40, 1)
    last.append(hand(*give(u2, stage_f, other_f, (2, 3))))
    leftover(u2, u1, fine_faces, gf, df, 4, 12, 8, RF, 8, 32, 1)
    last.append(hand(*give(u1, stage_r, other_r, (0, 1))))
    leftover(u2, u1, fine_faces, gf, df, 12, 20, 8, RF, 8, 32, 1)
    last.append(hand(*give(u1, stage_r, other_r, (2, 3))))
    keep(stage_f, out_field)
    last[0]()
    last[1]()
    take(other_f, out_field)
    keep(stage_r, out_resid)
    last[2]()
    last[3]()
    take(other_r, out_resid)
    drain()


def vmem(*shape):
    return pltpu.VMEM(shape, F32)


def body(source, conductance, initial, box_counts):
    fine_field = vmem(PF * RF, LANES)
    mid_field = vmem(P1 * R1, LANES)
    deep_field = vmem(7 * R2, LANES)
    scratch = [pltpu.SMEM(box_counts.shape, jnp.int32)] + [vmem(6, 32, 512)] * 3
    scratch += [fine_field] * 5 + [vmem(6, PF * RF, LANES)] + [fine_field] * 2
    scratch += [mid_field] * 4 + [vmem(8 * 32, LANES), vmem(6, P1 * R1, LANES)] + [mid_field] * 4
    scratch += [deep_field] * 4 + [vmem(7, 5 * R2, LANES), vmem(5 * R2, LANES), vmem(12 * RF, LANES)]
    scratch += [vmem(4, 32, 512)] * 2 + [vmem(3, 32, 512)] * 2
    for big, middle, small in ((160, 80, 8), (96, 48, 8), (104, 56, 24), (32, 16, 8), (144, 72, 16)):
        scratch += [vmem(2 * big + 2 * middle + 4 * small, LANES)] * 2
    scratch += [pltpu.SemaphoreType.DMA((4,))] + [pltpu.SemaphoreType.DMA((ROUNDS,))] * 2
    hbm = pl.BlockSpec(memory_space=pltpu.HBM)
    shape = jax.ShapeDtypeStruct(source.shape, source.dtype)
    field, resid, held = pl.pallas_call(
        kernel,
        out_shape=(shape,) * 3,
        in_specs=[hbm] * 4,
        out_specs=(pl.BlockSpec(memory_space=pltpu.VMEM),) * 3,
        scratch_shapes=scratch,
        compiler_params=pltpu.CompilerParams(
            collective_id=0, has_side_effects=True, vmem_limit_bytes=40 * 2**20
        ),
        cost_estimate=pl.CostEstimate(flops=3 * 10**7, bytes_accessed=3 * 10**6, transcendentals=0),
    )(*[pltpu.with_memory_space_constraint(x, pltpu.HBM) for x in (box_counts, source, conductance, initial)])
    return field * held, resid * held


def solution(mesh):
    return jax.shard_map(
        body,
        mesh=mesh,
        in_specs=(P("box", None, None), P("box", None, None), P("box", None, None), P()),
        out_specs=(P("box", None, None), P("box", None, None)),
        check_vma=False,
    )
```

```python
import functools

import jax
import jax.numpy as jnp
from jax import lax
from jax.experimental import pallas as pl
from jax.experimental.pallas import tpu as pltpu
from jax.sharding import PartitionSpec as P


RF, PF = 48, 24
R1, P1 = 32, 24
R2 = 24
LANES = 128
FULL = (1, 1), (1, -1), (1, 0), (-1, 1), (-1, -1), (-1, 0), (0, 1), (0, -1)
FAR = (1, 2), (1, -2), (-1, 2), (-1, -2), (0, 2), (0, -2)
F32 = jnp.float32
ROUNDS = 3 + 3 * (5 + 2) + 6


def lane_ids(rows):
    return lax.broadcasted_iota(jnp.int32, (rows, LANES), 1)


def row_ids(rows):
    return lax.broadcasted_iota(jnp.int32, (rows, LANES), 0)


def turn(value, steps):
    return pltpu.roll(value, steps % LANES, 1)


def transposed(four):
    lanes = lane_ids(four[0].shape[0])
    low = lanes < 64
    even = (lanes // 32) % 2 == 0
    a, b, c, d = four
    e = jnp.where(low, a, turn(c, 64))
    f = jnp.where(low, b, turn(d, 64))
    g = jnp.where(low, turn(a, 64), c)
    h = jnp.where(low, turn(b, 64), d)
    return (
        jnp.where(even, e, turn(f, 32)),
        jnp.where(even, turn(e, -32), f),
        jnp.where(even, g, turn(h, 32)),
        jnp.where(even, turn(g, -32), h),
    )


def coefficients(c, besides, inside):
    around_ = [
        beside if within is None else jnp.where(within, beside, c)
        for beside, within in zip(besides, inside)
    ]
    total = 3.0 * c + 0.5 * (
        (around_[0] + around_[1]) + (around_[2] + around_[3]) + (around_[4] + around_[5])
    )
    quarter = 0.4 / total
    faces = [
        (c + beside) * quarter if within is None else jnp.where(within, (c + beside) * quarter, 0.0)
        for beside, within in zip(besides, inside)
    ]
    return faces, total, quarter


class Planes:
    def __init__(self):
        self.held = {}
        self.step = 0

    def load(self, ref, base, count, rows, ahead):
        key = (id(ref), count, self.step + ahead)
        if key not in self.held:
            self.held[key] = ref[pl.ds(base + rows * ahead, count), :]
        return self.held[key]


def around(ref, base, count, rows, twist, planes):
    centre = planes.load(ref, base, count, rows, 0)
    return centre, (
        planes.load(ref, base, count, rows, -1),
        planes.load(ref, base, count, rows, 1),
        ref[pl.ds(base - 1, count), :],
        ref[pl.ds(base + 1, count), :],
        turn(centre, twist),
        turn(centre, -twist),
    )


def weighted(faces, base, count, besides):
    parts = [faces[n][pl.ds(base, count), :] * besides[n] for n in range(6)]
    return (parts[0] + parts[1]) + (parts[2] + parts[3]) + (parts[4] + parts[5])


def planes_loop(low, high, width, body, group=None, base=0):
    assert (high - low) % width == 0
    group = group or width

    def step(index, carry):
        first = base + low + index * width
        stores, planes = [], Planes()
        for m in range(width):
            planes.step = m
            stores += body(first + m, planes)
            if (m + 1) % group == 0 or m == width - 1:
                for ref, index_, value in stores:
                    ref[index_] = value
                stores, planes = [], Planes()
        return carry

    if high - low == width:
        step(0, 0)
    else:
        lax.fori_loop(0, (high - low) // width, step, 0)


def at(base, count):
    return pl.ds(base, count), slice(None)


def pair_rows(ref, base, count, rows):
    got = [
        ref[pl.ds(base + offset, count, stride=2), :] for offset in (0, 1, rows, rows + 1)
    ]
    return (got[0] + got[1]) + (got[2] + got[3])


def pair_lanes(value, width):
    first = (lane_ids(value.shape[0]) // width) % 2 == 0
    return 0.125 * (value + jnp.where(first, turn(value, -width), turn(value, width)))


def kernel(
    counts, source, conductance, initial, out_field, out_resid, out_held,
    owners, raw_c, raw_u, raw_s, cf, uf, sf, u1, u2, fine, gf, df,
    c1, f1, e1, e1b, pe2, mid, w1, g1, d1, r1, c2, f2, e2, e2b, deep, g2, pe1,
    stage_f, stage_r, other_f, other_r, *rest,
):
    post, local_sem, send_sem, recv_sem = rest[:-3], rest[-3], rest[-2], rest[-1]
    me = lax.axis_index("box")
    a, j = me // 8, me % 8
    half = me % 2
    sibling = me + 1 - 2 * half
    zero = me // 1024
    loop = functools.partial(planes_loop, base=zero)
    across = {da: ((a + da + 16) % 16) * 8 for da in (-1, 0, 1)}
    along = {dj: (j + dj + 8) % 8 for dj in (-2, -1, 0, 1, 2)}

    sibling_far = across[0] + (j - 1 + 2 * half + 8) % 8

    def device(da, dj):
        return across[da] + along[dj]

    numbers = iter(range(ROUNDS))
    leaving = []

    def describe(src, dst, number, target):
        return pltpu.make_async_remote_copy(
            src_ref=src, dst_ref=dst, send_sem=send_sem.at[number], recv_sem=recv_sem.at[number],
            device_id=(target,), device_id_type=pl.DeviceIdType.MESH,
        )

    leaves = {1: a < 15, -1: a > 0}
    comes = {1: a > 0, -1: a < 15}

    def inside(column):
        return jnp.logical_and(column >= 0, column < 8)

    def sized(messages, whole, sign, act):
        sizes = {}
        for column in range(8):
            rows = sum(rows for rows, da, dj in messages if 0 <= column + sign * dj < 8)
            sizes.setdefault(rows, []).append(column)
        for rows, columns in sizes.items():
            if len(columns) == 8:
                act(rows)
            else:
                there = functools.reduce(jnp.logical_or, [j == column for column in columns])
                pl.when(there)(functools.partial(act, rows))

    def start(copies, ref, first_row, messages, without):
        number = next(numbers)
        step_x = messages[0][1]

        def some(rows):
            part = ref.at[pl.ds(first_row, rows)]
            return describe(part, part, number, sibling)

        def go():
            for src, dst, target, dj in copies:
                begin = describe(src, dst, number, target).start
                if dj == 0:
                    begin()
                else:
                    pl.when(inside(j + dj))(begin)

        def gone():
            sized(messages, ref, 1, lambda rows: some(rows).wait_send())

        def come():
            sized(messages, ref, -1, lambda rows: some(rows).wait_recv())
            for dj in sorted({dj for rows, da, dj in messages}):
                if dj != 0:
                    gaps = [n for n, item in enumerate(messages) if item[2] == dj]
                    pl.when(jnp.logical_not(inside(j - dj)))(functools.partial(without, *gaps))

        if step_x == 0:
            go()
            leaving.append(gone)
            return come
        pl.when(leaves[step_x])(go)
        leaving.append(lambda: pl.when(leaves[step_x])(gone))

        def arrived():
            pl.when(comes[step_x])(come)
            pl.when(jnp.logical_not(comes[step_x]))(functools.partial(without, *range(len(messages))))

        return arrived

    def hand(src, dst, whole):
        number = next(numbers)
        describe(src, dst, number, sibling).start()
        everything = describe(whole, whole, number, sibling)
        leaving.append(everything.wait_send)
        return everything.wait_recv

    def drain(but=0):
        while len(leaving) > but:
            leaving.pop(0)()

    barrier = pltpu.get_barrier_semaphore()

    def here(*targets):
        for target in targets:
            pl.semaphore_signal(
                barrier, inc=1, device_id=(target,), device_id_type=pl.DeviceIdType.MESH
            )

    here(sibling)
    pl.when(inside(j - 1 + 2 * half))(lambda: here(sibling_far))
    for da in (1, -1):

        def beside():
            here(device(da, 0))
            for dj in (1, -1):
                pl.when(inside(j + dj))(lambda: here(device(da, dj)))

        pl.when(leaves[da])(beside)

    raws = (raw_c, raw_s, raw_u)
    given = (conductance, source, initial)
    mine = pl.ds(pl.multiple_of(512 * half, 512), 512)
    theirs = pl.ds(pl.multiple_of(512 - 512 * half, 512), 512)
    held = pl.ds(3 * half, 3)
    locals_ = [pltpu.make_async_copy(counts, owners, local_sem.at[3])]
    for number in range(3):
        locals_.append(
            pltpu.make_async_copy(
                given[number].at[pl.ds(0, 3), :, mine], raws[number].at[held], local_sem.at[number]
            )
        )
    for copy in locals_:
        copy.start()

    around_x = 1 + (a > 0).astype(jnp.int32) + (a < 15).astype(jnp.int32)
    around_y = 1 + (j > 0).astype(jnp.int32) + (j < 7).astype(jnp.int32)
    pl.semaphore_wait(barrier, around_x * around_y - 1)

    swaps = [
        hand(given[number].at[pl.ds(0, 3), :, theirs], raws[number].at[held], raws[number].at[held])
        for number in range(3)
    ]
    locals_[0].wait()
    split = owners[me - half]
    own = jnp.where(half == 0, split, 4 - split)
    for s in range(4):
        out_held[s] = jnp.where(s < own, jnp.ones((32, 1024), F32), 0.0)
    places = [jnp.where(p < split, p, jnp.clip(3 + p - split, 0, 5)) for p in range(4)]

    def bring(number, ref):
        locals_[1 + number].wait()
        swaps[number]()
        raw = raws[number]

        def step(t, planes):
            rows = pl.ds(pl.multiple_of(8 * t, 8), 8)
            out = []
            for q in range(4):
                four = [raw[places[p], rows, 128 * q : 128 * q + 128] for p in range(4)]
                for i, value in enumerate(transposed(four)):
                    out.append((ref, at(pl.multiple_of((4 + 4 * q + i) * RF + 8 + 8 * t, 8), 8), value))
            return out

        loop(0, 4, 4, step, group=1)

    ROWS = (RF, R1)
    OWN = ((4, 16, 8, 32), (8, 8, 8, 16))

    def near(first, count, side, depth):
        return first - 1 + depth if side < 0 else first + count - depth

    def far(first, count, side, depth):
        return first + count - 1 + depth if side < 0 else first - depth

    own2 = R2 + 2 * R2 + 8

    def there2(da, dj):
        return R2 + R2 * (2 - dj) + 8 * (1 - da)

    def pieces(strips, corners, block, da, dj, pick):
        out = []
        if block is not None:
            out.append((block, own2 if pick is near else there2(da, dj), 8, 1))
        if da == 0:
            for ref, level, depths in strips:
                plane, planes, row, rows = OWN[level]
                for d in depths:
                    out.append((ref, pick(plane, planes, dj, d) * ROWS[level] + row, rows, 1))
        elif dj == 0:
            for ref, level, depths in strips:
                plane, planes, row, rows = OWN[level]
                for d in depths:
                    out.append(
                        (ref, plane * ROWS[level] + pick(row, rows, da, d), planes, ROWS[level])
                    )
        else:
            for ref, level, depth, low, count in corners:
                plane, planes, row, rows = OWN[level]
                ends = [pick(row, rows, da, d) for d in (low, low + count - 1)]
                out.append((ref, pick(plane, planes, dj, depth) * ROWS[level] + min(ends), count, 1))
        return out

    def slab(ref, first, count, stride):
        return (pl.ds(first, count, stride=stride) if stride > 1 else pl.ds(first, count)), slice(None)

    spare = list(post)

    def filler(ref, firsts, messages):
        def without(*gaps):
            for n in gaps:
                ref[pl.ds(firsts[n], messages[n][0]), :] = jnp.ones((messages[n][0], LANES), F32)

        return without

    def exchange(strips, corners, block=None, where=FULL):
        out, got = spare.pop(0), spare.pop(0)
        arrivals, filled = [], []
        offset = 0
        for step_x in (1, -1, 0):
            copies, messages, group_row = [], [], offset
            for da, dj in FULL:
                if da != step_x:
                    continue
                first_row = offset
                for ref, first, count, stride in pieces(strips, corners, block, da, dj, near):
                    out[pl.ds(offset, count), :] = ref[slab(ref, first, count, stride)]
                    offset += count
                offset += -offset % 8
                rows = pl.ds(first_row, offset - first_row)
                copies.append((out.at[rows], got.at[rows], device(da, dj), dj))
                messages.append((rows.size, da, dj))
                filled.append((first_row, da, dj))
            firsts = [first for first, da, dj in filled if da == step_x]
            arrivals.append(start(copies, got, group_row, messages, filler(got, firsts, messages)))
        assert out.shape == (offset, LANES)

        def land():
            for arrived in arrivals:
                arrived()
            for offset, da, dj in filled:
                for ref, first, count, stride in pieces(strips, corners, block, da, dj, far):
                    ref[slab(ref, first, count, stride)] = got[pl.ds(offset, count), :]
                    offset += count

        return land

    def fine_corner(ref, depth):
        return [(ref, 0, d, 1, depth - d) for d in range(1, depth)]

    bring(0, cf)
    bring(1, sf)
    land_c = exchange(
        ((cf, 0, (1, 2, 3)), (sf, 0, (1, 2))), fine_corner(cf, 3) + fine_corner(sf, 2)
    )
    bring(2, uf)
    land_u = exchange(((uf, 0, (1, 2, 3)),), fine_corner(uf, 3))

    def coarse_c(i, planes):
        total = pair_rows(cf, (4 + 2 * i) * RF + 8, 16, RF)
        return [(c1, at(pl.multiple_of((8 + i) * R1 + 8, 8), 16), pair_lanes(total, 1))]

    loop(0, 8, 8, coarse_c)

    def packed(ref):
        lanes = lane_ids(8) % 4
        total = jnp.zeros((8, LANES), F32)
        for i in range(4):
            value = pair_lanes(pair_rows(ref, (8 + 2 * i) * R1 + 8, 8, R1), 2)
            total = total + jnp.where(lanes == i, value, 0.0)
        return total

    def blocks2(ref, where):
        arrivals = []
        for step_x in (1, -1, 0):
            places_ = [(da, dj) for da, dj in where if da == step_x]
            copies = [
                (ref.at[pl.ds(own2, 8)], ref.at[pl.ds(there2(da, dj), 8)], device(da, dj), dj)
                for da, dj in places_
            ]
            firsts = [there2(da, dj) for da, dj in places_]
            messages = [(8, da, dj) for da, dj in places_]
            arrivals.append(start(copies, ref, 0, messages, filler(ref, firsts, messages)))

        def arrived():
            for part in arrivals:
                part()

        return arrived

    c2[pl.ds(own2, 8), :] = packed(c1)
    land_c1 = exchange(
        ((c1, 1, (1, 2, 3, 4, 5, 6)),), [(c1, 1, d, 1, 6 - d) for d in range(1, 6)], c2
    )

    fine_faces = [fine.at[n] for n in range(6)]

    def fine_coeffs(*windows):
        def body(p, planes):
            out = []
            for start_row, count in windows:
                base = p * RF + start_row
                centre, besides = around(cf, base, count, RF, 1, Planes())
                z = lane_ids(count)
                inside = (None, None, None, None, z != 0, z != 127)
                faces, total, quarter = coefficients(centre, besides, inside)
                out += [(fine, (n,) + at(base, count), faces[n]) for n in range(6)]
                out.append((gf, at(base, count), 2.0 * quarter))
                out.append((df, at(base, count), 1.25 * total))
            return out

        return body

    loop(5, 19, 7, fine_coeffs((12, 24)), group=1)
    land_c()
    far_c2 = blocks2(c2, FAR)

    def edges(ref, first, side, count, rows, plane, row, low_y, high_y, low_x, high_x):
        for outside, there, here in (
            (low_y, plane - 1, plane), (high_y, plane + count, plane + count - 1)
        ):
            slab_there = at(there * rows + first, side)
            ref[slab_there] = jnp.where(outside, ref[at(here * rows + first, side)], ref[slab_there])
        lines = 24
        for outside, there, here in ((low_x, row[0] - 1, row[0]), (high_x, row[1] + 1, row[1])):
            slab_there = slab(ref, there, lines, rows)
            ref[slab_there] = jnp.where(outside, ref[slab(ref, here, lines, rows)], ref[slab_there])

    def cut(faces, first, side, count, rows, plane, row, low_y, high_y, low_x, high_x):
        for n, outside, here in ((0, low_y, plane), (1, high_y, plane + count - 1)):
            where = (n,) + at(here * rows + first, side)
            faces[where] = jnp.where(outside, 0.0, faces[where])
        for n, outside, here in ((2, low_x, row[0]), (3, high_x, row[1])):
            where = (n,) + slab(faces, here, 24, rows)
            faces[where] = jnp.where(outside, 0.0, faces[where])

    ends = (j == 0, j == 7, a == 0, a == 15)
    edges(cf, 4, 40, 16, RF, 4, (8, 39), *ends)
    loop(5, 19, 7, fine_coeffs((4, 8), (36, 8)), group=1)
    for low in (2, 19):
        loop(low, low + 3, 3, fine_coeffs((4, 40)), group=1)
    cut(fine, 4, 40, 16, RF, 4, (8, 39), *ends)

    def first_sweep(*windows):
        def body(p, planes):
            out = []
            for start_row, count in windows:
                base = p * RF + start_row
                centre, besides = around(uf, base, count, RF, 1, planes if len(windows) == 1 else Planes())
                right = gf[pl.ds(base, count), :] * sf[pl.ds(base, count), :]
                value = 0.2 * centre + right + weighted(fine_faces, base, count, besides)
                out += [(u1, at(base, count), value), (gf, at(base, count), right)]
            return out

        return body

    loop(5, 19, 7, first_sweep((12, 24)))
    land_u()
    loop(5, 19, 7, first_sweep((4, 8), (36, 8)))
    for low in (2, 19):
        loop(low, low + 3, 3, first_sweep((4, 40)))

    def sweep(src, dst, faces, right, low, high, width, rows, start, count, twist):
        def step(p, planes):
            base = p * rows + start
            centre, besides = around(src, base, count, rows, twist, planes)
            value = 0.2 * centre + right[pl.ds(base, count), :] + weighted(faces, base, count, besides)
            return [(dst, at(base, count), value)]

        loop(low, high, width, step, group=5)

    def leftover(src, dst, faces, right, diag, low, high, width, rows, start, count, twist):
        def step(p, planes):
            base = p * rows + start
            centre, besides = around(src, base, count, rows, twist, planes)
            value = diag[pl.ds(base, count), :] * (
                right[pl.ds(base, count), :] + weighted(faces, base, count, besides) - 0.8 * centre
            )
            return [(dst, at(base, count), value)]

        loop(low, high, width, step, group=4)

    sweep(u1, u2, fine_faces, gf, 3, 21, 9, RF, 4, 40, 1)
    leftover(u2, u1, fine_faces, gf, df, 4, 20, 8, RF, 8, 32, 1)

    def coarse_f(i, planes):
        total = pair_rows(u1, (4 + 2 * i) * RF + 8, 16, RF)
        return [(f1, at(pl.multiple_of((8 + i) * R1 + 8, 8), 16), pair_lanes(total, 1))]

    loop(0, 8, 8, coarse_f)
    land_f = exchange(((f1, 1, (1, 2)),), [(f1, 1, 1, 1, 1)])
    land_rest = exchange(
        ((f1, 1, (3, 4, 5)), (u2, 0, (1, 2, 3))),
        [(f1, 1, 1, 2, 3), (f1, 1, 2, 1, 3), (f1, 1, 3, 1, 2), (f1, 1, 4, 1, 1)] + fine_corner(u2, 3),
    )

    drain(but=6)
    land_c1()
    edges(c1, 0, 32, 8, R1, 8, (8, 23), *ends)
    mid_faces = [mid.at[n] for n in range(6)]

    def mid_coeffs(p, planes):
        base = p * R1
        centre, besides = around(c1, base, 32, R1, 2, planes)
        z = lane_ids(32)
        inside = (None, None, None, None, z >= 2, z < 126)
        faces, total, quarter = coefficients(centre, besides, inside)
        out = [(mid, (n,) + at(base, 32), faces[n]) for n in range(6)]
        out.append((w1, at(base, 32), 8.0 * quarter))
        out.append((d1, at(base, 32), 0.3125 * total))
        return out

    loop(6, 18, 3, mid_coeffs, group=1)
    cut(mid, 0, 32, 8, R1, 8, (8, 23), *ends)

    def guess(p, planes):
        base = p * R1
        return [(g1, at(base, 32), w1[pl.ds(base, 32), :] * f1[pl.ds(base, 32), :])]

    land_f()
    loop(6, 18, 12, guess)
    sweep(g1, e1, mid_faces, g1, 7, 17, 10, R1, 4, 24, 2)
    leftover(e1, r1, mid_faces, g1, d1, 8, 16, 8, R1, 8, 16, 2)
    f2[pl.ds(own2, 8), :] = packed(r1)
    sixth = blocks2(f2, FAR + FULL)

    loop(3, 6, 3, mid_coeffs, group=1)
    loop(18, 21, 3, mid_coeffs, group=1)
    cut(mid, 0, 32, 8, R1, 8, (8, 23), *ends)
    far_c2()

    def around2(ref):
        lanes = lane_ids(5 * R2) % 4
        centre = ref[R2 : 6 * R2, :]
        return centre, (
            jnp.where(lanes == 0, turn(ref[0 : 5 * R2, :], -3), turn(centre, 1)),
            jnp.where(lanes == 3, turn(ref[2 * R2 : 7 * R2, :], 3), turn(centre, -1)),
            ref[pl.ds(zero + (R2 - 1), 5 * R2), :],
            ref[pl.ds(zero + (R2 + 1), 5 * R2), :],
            turn(centre, 4),
            turn(centre, -4),
        )

    rows2, lanes2 = row_ids(5 * R2), lane_ids(5 * R2)
    x = rows2 % R2 + (8 * a - 8)
    y = 4 * (rows2 // R2) + lanes2 % 4 + (4 * j - 8)
    inside2 = (y != 0, y != 31, x != 0, x != 127, lanes2 >= 4, lanes2 < 124)
    centre, besides = around2(c2)
    faces, total, quarter = coefficients(centre, besides, inside2)
    for n in range(6):
        deep[n] = faces[n]
    deep[6] = 32.0 * quarter

    drain(but=3)
    land_rest()
    loop(3, 21, 9, guess)
    sweep(g1, e1, mid_faces, g1, 4, 20, 8, R1, 4, 24, 2)

    sixth()
    g2[...] = deep[6] * f2[R2 : 6 * R2, :]
    e2[R2 : 6 * R2, :] = g2[...]
    for src, dst in ((e2, e2b), (e2b, e2), (e2, e2b)):
        centre, besides = around2(src)
        parts = [deep[n] * besides[n] for n in range(6)]
        dst[R2 : 6 * R2, :] = (
            (0.2 * centre + g2[...]) + (parts[0] + parts[1]) + (parts[2] + parts[3]) + (parts[4] + parts[5])
        )

    lanes16 = lane_ids(16) % 4
    hops = ((1, 2), (-1, 2), (1, -2), (-1, -2))
    for number in range(8):
        block, i = (number + 6) // 4, (number + 6) % 4
        value = jnp.where(lanes16 == i, e2b[pl.ds(zero + (R2 + R2 * block + 4), 16), :], 0.0)
        value = value + turn(value, hops[i][0])
        value = value + turn(value, hops[i][1])
        pe2[pl.ds(32 * number, 16, stride=2), :] = value
        pe2[pl.ds(32 * number + 1, 16, stride=2), :] = value

    def corrected1(p, planes):
        value = e1[pl.ds(p * R1 + 4, 24), :] + pe2[pl.ds((p // 2 - 2) * 32 + 4, 24), :]
        return [(e1, at(p * R1 + 4, 24), value)]

    loop(4, 20, 16, corrected1)
    sweep(e1, e1b, mid_faces, g1, 5, 19, 14, R1, 4, 24, 2)
    sweep(e1b, e1, mid_faces, g1, 6, 18, 12, R1, 4, 24, 2)

    def grown(i, planes):
        value = e1[pl.ds((i + 6) * R1 + 4, 24), :]
        return [(pe1, (pl.ds(RF * i + odd, 24, stride=2), slice(None)), value) for odd in (0, 1)]

    loop(0, 12, 12, grown)

    def corrected0(p, planes):
        base = p * RF + 4
        return [(u2, at(base, 40), u2[pl.ds(base, 40), :] + pe1[pl.ds((p // 2) * RF + 4, 40), :])]

    loop(1, 23, 11, corrected0)
    sweep(u2, u1, fine_faces, gf, 2, 22, 10, RF, 4, 40, 1)

    def give(ref, stage, other, quads):
        def step(t, planes):
            rows = pl.ds(pl.multiple_of(8 * t, 8), 8)
            out = []
            for q in quads:
                four = [
                    ref[pl.ds(pl.multiple_of((4 + 4 * q + i) * RF + 8 + 8 * t, 8), 8), :]
                    for i in range(4)
                ]
                for p, value in enumerate(transposed(four)):
                    out.append((stage, (p, rows, slice(128 * q, 128 * q + 128)), value))
            return out

        loop(0, 4, 4, step)
        lanes = pl.ds(128 * quads[0], 128 * len(quads))
        return stage.at[pl.ds(1 - half, 3), :, lanes], other.at[:, :, lanes], other.at[:, :, lanes]

    def keep(stage, out):
        for s in range(4):
            out[s, :, mine] = stage[jnp.clip(s + half * split, 0, 3)]

    def take(other, out):
        for s in range(4):
            out[s, :, theirs] = other[jnp.clip(s + half * (split - 1), 0, 2)]

    last = []
    sweep(u1, u2, fine_faces, gf, 3, 12, 9, RF, 4, 40, 1)
    last.append(hand(*give(u2, stage_f, other_f, (0, 1))))
    sweep(u1, u2, fine_faces, gf, 12, 21, 9, RF, 4, 40, 1)
    last.append(hand(*give(u2, stage_f, other_f, (2, 3))))
    for q in range(4):
        leftover(u2, u1, fine_faces, gf, df, 4 + 4 * q, 8 + 4 * q, 4, RF, 8, 32, 1)
        last.append(hand(*give(u1, stage_r, other_r, (q,))))
    keep(stage_f, out_field)
    last[0]()
    last[1]()
    take(other_f, out_field)
    keep(stage_r, out_resid)
    for arrived in last[2:]:
        arrived()
    take(other_r, out_resid)
    drain()


def vmem(*shape):
    return pltpu.VMEM(shape, F32)


def body(source, conductance, initial, box_counts):
    fine_field = vmem(PF * RF, LANES)
    mid_field = vmem(P1 * R1, LANES)
    deep_field = vmem(7 * R2, LANES)
    scratch = [pltpu.SMEM(box_counts.shape, jnp.int32)] + [vmem(6, 32, 512)] * 3
    scratch += [fine_field] * 5 + [vmem(6, PF * RF, LANES)] + [fine_field] * 2
    scratch += [mid_field] * 4 + [vmem(8 * 32, LANES), vmem(6, P1 * R1, LANES)] + [mid_field] * 4
    scratch += [deep_field] * 4 + [vmem(7, 5 * R2, LANES), vmem(5 * R2, LANES), vmem(12 * RF, LANES)]
    scratch += [vmem(4, 32, 512)] * 2 + [vmem(3, 32, 512)] * 2
    for big, middle, small in ((160, 80, 8), (96, 48, 8), (104, 56, 24), (32, 16, 8), (144, 72, 16)):
        scratch += [vmem(2 * big + 2 * middle + 4 * small, LANES)] * 2
    scratch += [pltpu.SemaphoreType.DMA((4,))] + [pltpu.SemaphoreType.DMA((ROUNDS,))] * 2
    hbm = pl.BlockSpec(memory_space=pltpu.HBM)
    shape = jax.ShapeDtypeStruct(source.shape, source.dtype)
    field, resid, held = pl.pallas_call(
        kernel,
        out_shape=(shape,) * 3,
        in_specs=[hbm] * 4,
        out_specs=(pl.BlockSpec(memory_space=pltpu.VMEM),) * 3,
        scratch_shapes=scratch,
        compiler_params=pltpu.CompilerParams(
            collective_id=0, has_side_effects=True, vmem_limit_bytes=40 * 2**20
        ),
        cost_estimate=pl.CostEstimate(flops=3 * 10**7, bytes_accessed=3 * 10**6, transcendentals=0),
    )(*[pltpu.with_memory_space_constraint(x, pltpu.HBM) for x in (box_counts, source, conductance, initial)])
    return field * held, resid * held


def solution(mesh):
    return jax.shard_map(
        body,
        mesh=mesh,
        in_specs=(P("box", None, None), P("box", None, None), P("box", None, None), P()),
        out_specs=(P("box", None, None), P("box", None, None)),
        check_vma=False,
    )
```

```python
import functools

import jax
import jax.numpy as jnp
from jax import lax
from jax.experimental import pallas as pl
from jax.experimental.pallas import tpu as pltpu
from jax.sharding import PartitionSpec as P


RF, PF = 48, 24
R1, P1 = 32, 24
R2 = 24
LANES = 128
FULL = (1, 1), (1, -1), (1, 0), (-1, 1), (-1, -1), (-1, 0), (0, 1), (0, -1)
FAR = (1, 2), (1, -2), (-1, 2), (-1, -2), (0, 2), (0, -2)
F32 = jnp.float32
ROUNDS = 3 + 3 * (5 + 2) + 4


def lane_ids(rows):
    return lax.broadcasted_iota(jnp.int32, (rows, LANES), 1)


def row_ids(rows):
    return lax.broadcasted_iota(jnp.int32, (rows, LANES), 0)


def turn(value, steps):
    return pltpu.roll(value, steps % LANES, 1)


def transposed(four):
    lanes = lane_ids(four[0].shape[0])
    low = lanes < 64
    even = (lanes // 32) % 2 == 0
    a, b, c, d = four
    e = jnp.where(low, a, turn(c, 64))
    f = jnp.where(low, b, turn(d, 64))
    g = jnp.where(low, turn(a, 64), c)
    h = jnp.where(low, turn(b, 64), d)
    return (
        jnp.where(even, e, turn(f, 32)),
        jnp.where(even, turn(e, -32), f),
        jnp.where(even, g, turn(h, 32)),
        jnp.where(even, turn(g, -32), h),
    )


def coefficients(c, besides, inside):
    around_ = [
        beside if within is None else jnp.where(within, beside, c)
        for beside, within in zip(besides, inside)
    ]
    total = 3.0 * c + 0.5 * (
        (around_[0] + around_[1]) + (around_[2] + around_[3]) + (around_[4] + around_[5])
    )
    quarter = 0.4 / total
    faces = [
        (c + beside) * quarter if within is None else jnp.where(within, (c + beside) * quarter, 0.0)
        for beside, within in zip(besides, inside)
    ]
    return faces, total, quarter


def around(ref, base, count, rows, twist):
    centre = ref[pl.ds(base, count), :]
    return centre, (
        ref[pl.ds(base - rows, count), :],
        ref[pl.ds(base + rows, count), :],
        ref[pl.ds(base - 1, count), :],
        ref[pl.ds(base + 1, count), :],
        turn(centre, twist),
        turn(centre, -twist),
    )


def weighted(faces, base, count, besides):
    parts = [faces[n][pl.ds(base, count), :] * besides[n] for n in range(6)]
    return (parts[0] + parts[1]) + (parts[2] + parts[3]) + (parts[4] + parts[5])


def planes_loop(low, high, width, body, group=None, base=0):
    assert (high - low) % width == 0
    group = group or width

    def step(index, carry):
        first = base + low + index * width
        stores = []
        for m in range(width):
            stores += body(first + m)
            if (m + 1) % group == 0 or m == width - 1:
                for ref, index_, value in stores:
                    ref[index_] = value
                stores = []
        return carry

    if high - low == width:
        step(0, 0)
    else:
        lax.fori_loop(0, (high - low) // width, step, 0)


def at(base, count):
    return pl.ds(base, count), slice(None)


def pair_rows(ref, base, count, rows):
    got = [
        ref[pl.ds(base + offset, count, stride=2), :] for offset in (0, 1, rows, rows + 1)
    ]
    return (got[0] + got[1]) + (got[2] + got[3])


def pair_lanes(value, width):
    first = (lane_ids(value.shape[0]) // width) % 2 == 0
    return 0.125 * (value + jnp.where(first, turn(value, -width), turn(value, width)))


def kernel(
    counts, source, conductance, initial, out_field, out_resid, out_held,
    owners, raw_c, raw_u, raw_s, cf, uf, sf, u1, u2, fine, gf, df,
    c1, f1, e1, e1b, pe2, mid, w1, g1, d1, r1, c2, f2, e2, e2b, deep, g2, pe1,
    stage_f, stage_r, other_f, other_r, *rest,
):
    post, local_sem, send_sem, recv_sem = rest[:-3], rest[-3], rest[-2], rest[-1]
    me = lax.axis_index("box")
    a, j = me // 8, me % 8
    half = me % 2
    sibling = me + 1 - 2 * half
    zero = me // 1024
    loop = functools.partial(planes_loop, base=zero)
    across = {da: ((a + da + 16) % 16) * 8 for da in (-1, 0, 1)}
    along = {dj: (j + dj + 8) % 8 for dj in (-2, -1, 0, 1, 2)}

    sibling_far = across[0] + (j - 1 + 2 * half + 8) % 8

    def device(da, dj):
        return across[da] + along[dj]

    numbers = iter(range(ROUNDS))
    leaving = []

    def describe(src, dst, number, target):
        return pltpu.make_async_remote_copy(
            src_ref=src, dst_ref=dst, send_sem=send_sem.at[number], recv_sem=recv_sem.at[number],
            device_id=(target,), device_id_type=pl.DeviceIdType.MESH,
        )

    leaves = {1: a < 15, -1: a > 0}
    comes = {1: a > 0, -1: a < 15}

    def inside(column):
        return jnp.logical_and(column >= 0, column < 8)

    def sized(messages, whole, sign, act):
        sizes = {}
        for column in range(8):
            rows = sum(rows for rows, da, dj in messages if 0 <= column + sign * dj < 8)
            sizes.setdefault(rows, []).append(column)
        for rows, columns in sizes.items():
            if len(columns) == 8:
                act(rows)
            else:
                there = functools.reduce(jnp.logical_or, [j == column for column in columns])
                pl.when(there)(functools.partial(act, rows))

    def start(copies, ref, first_row, messages, without):
        number = next(numbers)
        step_x = messages[0][1]

        def some(rows):
            part = ref.at[pl.ds(first_row, rows)]
            return describe(part, part, number, sibling)

        def go():
            for src, dst, target, dj in copies:
                begin = describe(src, dst, number, target).start
                if dj == 0:
                    begin()
                else:
                    pl.when(inside(j + dj))(begin)

        def gone():
            sized(messages, ref, 1, lambda rows: some(rows).wait_send())

        def come():
            sized(messages, ref, -1, lambda rows: some(rows).wait_recv())
            for dj in sorted({dj for rows, da, dj in messages}):
                if dj != 0:
                    gaps = [n for n, item in enumerate(messages) if item[2] == dj]
                    pl.when(jnp.logical_not(inside(j - dj)))(functools.partial(without, *gaps))

        if step_x == 0:
            leaving.append(gone)
            return go, come
        leaving.append(lambda: pl.when(leaves[step_x])(gone))

        def arrived():
            pl.when(comes[step_x])(come)
            pl.when(jnp.logical_not(comes[step_x]))(functools.partial(without, *range(len(messages))))

        return go, arrived

    seam = a % 4 == 0

    def depart(plus, minus):
        pl.when(jnp.logical_and(leaves[-1], seam))(minus)
        pl.when(leaves[1])(plus)
        pl.when(jnp.logical_and(leaves[-1], jnp.logical_not(seam)))(minus)

    def hand(src, dst, whole):
        number = next(numbers)
        describe(src, dst, number, sibling).start()
        everything = describe(whole, whole, number, sibling)
        leaving.append(everything.wait_send)
        return everything.wait_recv

    def drain(but=0):
        while len(leaving) > but:
            leaving.pop(0)()

    barrier = pltpu.get_barrier_semaphore()

    def here(*targets):
        for target in targets:
            pl.semaphore_signal(
                barrier, inc=1, device_id=(target,), device_id_type=pl.DeviceIdType.MESH
            )

    here(sibling)
    pl.when(inside(j - 1 + 2 * half))(lambda: here(sibling_far))
    for da in (1, -1):

        def beside():
            here(device(da, 0))
            for dj in (1, -1):
                pl.when(inside(j + dj))(lambda: here(device(da, dj)))

        pl.when(leaves[da])(beside)

    raws = (raw_c, raw_s, raw_u)
    given = (conductance, source, initial)
    mine = pl.ds(pl.multiple_of(512 * half, 512), 512)
    theirs = pl.ds(pl.multiple_of(512 - 512 * half, 512), 512)
    held = pl.ds(3 * half, 3)
    locals_ = [pltpu.make_async_copy(counts, owners, local_sem.at[3])]
    for number in range(3):
        locals_.append(
            pltpu.make_async_copy(
                given[number].at[pl.ds(0, 3), :, mine], raws[number].at[held], local_sem.at[number]
            )
        )
    for copy in locals_:
        copy.start()

    around_x = 1 + (a > 0).astype(jnp.int32) + (a < 15).astype(jnp.int32)
    around_y = 1 + (j > 0).astype(jnp.int32) + (j < 7).astype(jnp.int32)
    pl.semaphore_wait(barrier, around_x * around_y - 1)

    swaps = [
        hand(given[number].at[pl.ds(0, 3), :, theirs], raws[number].at[held], raws[number].at[held])
        for number in range(3)
    ]
    locals_[0].wait()
    split = owners[me - half]
    own = jnp.where(half == 0, split, 4 - split)
    for s in range(4):
        out_held[s] = jnp.where(s < own, jnp.ones((32, 1024), F32), 0.0)
    places = [jnp.where(p < split, p, jnp.clip(3 + p - split, 0, 5)) for p in range(4)]

    def bring(number, ref):
        locals_[1 + number].wait()
        swaps[number]()
        raw = raws[number]

        def step(t):
            rows = pl.ds(pl.multiple_of(8 * t, 8), 8)
            out = []
            for q in range(4):
                four = [raw[places[p], rows, 128 * q : 128 * q + 128] for p in range(4)]
                for i, value in enumerate(transposed(four)):
                    out.append((ref, at(pl.multiple_of((4 + 4 * q + i) * RF + 8 + 8 * t, 8), 8), value))
            return out

        loop(0, 4, 4, step, group=1)

    ROWS = (RF, R1)
    OWN = ((4, 16, 8, 32), (8, 8, 8, 16))

    def near(first, count, side, depth):
        return first - 1 + depth if side < 0 else first + count - depth

    def far(first, count, side, depth):
        return first + count - 1 + depth if side < 0 else first - depth

    own2 = R2 + 2 * R2 + 8

    def there2(da, dj):
        return R2 + R2 * (2 - dj) + 8 * (1 - da)

    def pieces(strips, corners, block, da, dj, pick):
        out = []
        if block is not None:
            out.append((block, own2 if pick is near else there2(da, dj), 8, 1))
        if da == 0:
            for ref, level, depths in strips:
                plane, planes, row, rows = OWN[level]
                for d in depths:
                    out.append((ref, pick(plane, planes, dj, d) * ROWS[level] + row, rows, 1))
        elif dj == 0:
            for ref, level, depths in strips:
                plane, planes, row, rows = OWN[level]
                for d in depths:
                    out.append(
                        (ref, plane * ROWS[level] + pick(row, rows, da, d), planes, ROWS[level])
                    )
        else:
            for ref, level, depth, low, count in corners:
                plane, planes, row, rows = OWN[level]
                ends = [pick(row, rows, da, d) for d in (low, low + count - 1)]
                out.append((ref, pick(plane, planes, dj, depth) * ROWS[level] + min(ends), count, 1))
        return out

    def slab(ref, first, count, stride):
        return (pl.ds(first, count, stride=stride) if stride > 1 else pl.ds(first, count)), slice(None)

    spare = list(post)

    def filler(ref, firsts, messages):
        def without(*gaps):
            for n in gaps:
                ref[pl.ds(firsts[n], messages[n][0]), :] = jnp.ones((messages[n][0], LANES), F32)

        return without

    def exchange(strips, corners, block=None, where=FULL):
        out, got = spare.pop(0), spare.pop(0)
        arrivals, filled = [], []
        offset = 0
        for step_x in (1, -1, 0):
            copies, messages, group_row = [], [], offset
            for da, dj in FULL:
                if da != step_x:
                    continue
                first_row = offset
                for ref, first, count, stride in pieces(strips, corners, block, da, dj, near):
                    out[pl.ds(offset, count), :] = ref[slab(ref, first, count, stride)]
                    offset += count
                offset += -offset % 8
                rows = pl.ds(first_row, offset - first_row)
                copies.append((out.at[rows], got.at[rows], device(da, dj), dj))
                messages.append((rows.size, da, dj))
                filled.append((first_row, da, dj))
            firsts = [first for first, da, dj in filled if da == step_x]
            go, arrived = start(copies, got, group_row, messages, filler(got, firsts, messages))
            arrivals.append(arrived)
            if step_x == 1:
                plus = go
            elif step_x == -1:
                depart(plus, go)
            else:
                go()
        assert out.shape == (offset, LANES)

        def land():
            for arrived in arrivals:
                arrived()
            for offset, da, dj in filled:
                for ref, first, count, stride in pieces(strips, corners, block, da, dj, far):
                    ref[slab(ref, first, count, stride)] = got[pl.ds(offset, count), :]
                    offset += count

        return land

    def fine_corner(ref, depth):
        return [(ref, 0, d, 1, depth - d) for d in range(1, depth)]

    bring(0, cf)
    bring(1, sf)
    land_c = exchange(
        ((cf, 0, (1, 2, 3)), (sf, 0, (1, 2))), fine_corner(cf, 3) + fine_corner(sf, 2)
    )
    bring(2, uf)
    land_u = exchange(((uf, 0, (1, 2, 3)),), fine_corner(uf, 3))

    def coarse_c(i):
        total = pair_rows(cf, (4 + 2 * i) * RF + 8, 16, RF)
        return [(c1, at(pl.multiple_of((8 + i) * R1 + 8, 8), 16), pair_lanes(total, 1))]

    loop(0, 8, 8, coarse_c)

    def packed(ref):
        lanes = lane_ids(8) % 4
        total = jnp.zeros((8, LANES), F32)
        for i in range(4):
            value = pair_lanes(pair_rows(ref, (8 + 2 * i) * R1 + 8, 8, R1), 2)
            total = total + jnp.where(lanes == i, value, 0.0)
        return total

    def blocks2(ref, where):
        arrivals = []
        for step_x in (1, -1, 0):
            places_ = [(da, dj) for da, dj in where if da == step_x]
            copies = [
                (ref.at[pl.ds(own2, 8)], ref.at[pl.ds(there2(da, dj), 8)], device(da, dj), dj)
                for da, dj in places_
            ]
            firsts = [there2(da, dj) for da, dj in places_]
            messages = [(8, da, dj) for da, dj in places_]
            go, arrived = start(copies, ref, 0, messages, filler(ref, firsts, messages))
            arrivals.append(arrived)
            if step_x == 1:
                plus = go
            elif step_x == -1:
                depart(plus, go)
            else:
                go()

        def arrived():
            for part in arrivals:
                part()

        return arrived

    c2[pl.ds(own2, 8), :] = packed(c1)
    land_c1 = exchange(
        ((c1, 1, (1, 2, 3, 4, 5, 6)),), [(c1, 1, d, 1, 6 - d) for d in range(1, 6)], c2
    )

    land_c()
    far_c2 = blocks2(c2, FAR)

    def edges(ref, first, side, count, rows, plane, row, low_y, high_y, low_x, high_x):
        for outside, there, here in (
            (low_y, plane - 1, plane), (high_y, plane + count, plane + count - 1)
        ):
            slab_there = at(there * rows + first, side)
            ref[slab_there] = jnp.where(outside, ref[at(here * rows + first, side)], ref[slab_there])
        lines = 24
        for outside, there, here in ((low_x, row[0] - 1, row[0]), (high_x, row[1] + 1, row[1])):
            slab_there = slab(ref, there, lines, rows)
            ref[slab_there] = jnp.where(outside, ref[slab(ref, here, lines, rows)], ref[slab_there])

    def cut(faces, first, side, count, rows, plane, row, low_y, high_y, low_x, high_x):
        for n, outside, here in ((0, low_y, plane), (1, high_y, plane + count - 1)):
            where = (n,) + at(here * rows + first, side)
            faces[where] = jnp.where(outside, 0.0, faces[where])
        for n, outside, here in ((2, low_x, row[0]), (3, high_x, row[1])):
            where = (n,) + slab(faces, here, 24, rows)
            faces[where] = jnp.where(outside, 0.0, faces[where])

    ends = (j == 0, j == 7, a == 0, a == 15)
    edges(cf, 4, 40, 16, RF, 4, (8, 39), *ends)
    fine_faces = [fine.at[n] for n in range(6)]

    def fine_coeffs(p):
        base = p * RF + 4
        centre, besides = around(cf, base, 40, RF, 1)
        z = lane_ids(40)
        inside = (None, None, None, None, z != 0, z != 127)
        faces, total, quarter = coefficients(centre, besides, inside)
        out = [(fine, (n,) + at(base, 40), faces[n]) for n in range(6)]
        out.append((gf, at(base, 40), 2.0 * quarter))
        out.append((df, at(base, 40), 1.25 * total))
        return out

    loop(2, 22, 4, fine_coeffs, group=1)
    cut(fine, 4, 40, 16, RF, 4, (8, 39), *ends)
    land_u()

    def sweep(src, dst, faces, right, low, high, width, rows, start, count, twist):
        def step(p):
            base = p * rows + start
            centre, besides = around(src, base, count, rows, twist)
            value = 0.2 * centre + right[pl.ds(base, count), :] + weighted(faces, base, count, besides)
            return [(dst, at(base, count), value)]

        loop(low, high, width, step, group=5)

    def leftover(src, dst, faces, right, diag, low, high, width, rows, start, count, twist):
        def step(p):
            base = p * rows + start
            centre, besides = around(src, base, count, rows, twist)
            value = diag[pl.ds(base, count), :] * (
                right[pl.ds(base, count), :] + weighted(faces, base, count, besides) - 0.8 * centre
            )
            return [(dst, at(base, count), value)]

        loop(low, high, width, step, group=4)

    def first_sweep(p):
        base = p * RF + 4
        centre, besides = around(uf, base, 40, RF, 1)
        right = gf[pl.ds(base, 40), :] * sf[pl.ds(base, 40), :]
        value = 0.2 * centre + right + weighted(fine_faces, base, 40, besides)
        return [(u1, at(base, 40), value), (gf, at(base, 40), right)]

    loop(2, 22, 10, first_sweep, group=5)
    sweep(u1, u2, fine_faces, gf, 3, 21, 9, RF, 4, 40, 1)
    leftover(u2, u1, fine_faces, gf, df, 4, 20, 8, RF, 8, 32, 1)

    def coarse_f(i):
        total = pair_rows(u1, (4 + 2 * i) * RF + 8, 16, RF)
        return [(f1, at(pl.multiple_of((8 + i) * R1 + 8, 8), 16), pair_lanes(total, 1))]

    loop(0, 8, 8, coarse_f)
    land_f = exchange(((f1, 1, (1, 2)),), [(f1, 1, 1, 1, 1)])
    land_rest = exchange(
        ((f1, 1, (3, 4, 5)), (u2, 0, (1, 2, 3))),
        [(f1, 1, 1, 2, 3), (f1, 1, 2, 1, 3), (f1, 1, 3, 1, 2), (f1, 1, 4, 1, 1)] + fine_corner(u2, 3),
    )

    drain(but=6)
    land_c1()
    edges(c1, 0, 32, 8, R1, 8, (8, 23), *ends)
    mid_faces = [mid.at[n] for n in range(6)]

    def mid_coeffs(p):
        base = p * R1
        centre, besides = around(c1, base, 32, R1, 2)
        z = lane_ids(32)
        inside = (None, None, None, None, z >= 2, z < 126)
        faces, total, quarter = coefficients(centre, besides, inside)
        out = [(mid, (n,) + at(base, 32), faces[n]) for n in range(6)]
        out.append((w1, at(base, 32), 8.0 * quarter))
        out.append((d1, at(base, 32), 0.3125 * total))
        return out

    loop(6, 18, 3, mid_coeffs, group=1)
    cut(mid, 0, 32, 8, R1, 8, (8, 23), *ends)

    def guess(p):
        base = p * R1
        return [(g1, at(base, 32), w1[pl.ds(base, 32), :] * f1[pl.ds(base, 32), :])]

    land_f()
    loop(6, 18, 12, guess)
    sweep(g1, e1, mid_faces, g1, 7, 17, 10, R1, 4, 24, 2)
    leftover(e1, r1, mid_faces, g1, d1, 8, 16, 8, R1, 8, 16, 2)
    f2[pl.ds(own2, 8), :] = packed(r1)
    sixth = blocks2(f2, FAR + FULL)

    loop(3, 6, 3, mid_coeffs, group=1)
    loop(18, 21, 3, mid_coeffs, group=1)
    cut(mid, 0, 32, 8, R1, 8, (8, 23), *ends)
    far_c2()

    def around2(ref):
        lanes = lane_ids(5 * R2) % 4
        centre = ref[R2 : 6 * R2, :]
        return centre, (
            jnp.where(lanes == 0, turn(ref[0 : 5 * R2, :], -3), turn(centre, 1)),
            jnp.where(lanes == 3, turn(ref[2 * R2 : 7 * R2, :], 3), turn(centre, -1)),
            ref[pl.ds(zero + (R2 - 1), 5 * R2), :],
            ref[pl.ds(zero + (R2 + 1), 5 * R2), :],
            turn(centre, 4),
            turn(centre, -4),
        )

    rows2, lanes2 = row_ids(5 * R2), lane_ids(5 * R2)
    x = rows2 % R2 + (8 * a - 8)
    y = 4 * (rows2 // R2) + lanes2 % 4 + (4 * j - 8)
    inside2 = (y != 0, y != 31, x != 0, x != 127, lanes2 >= 4, lanes2 < 124)
    centre, besides = around2(c2)
    faces, total, quarter = coefficients(centre, besides, inside2)
    for n in range(6):
        deep[n] = faces[n]
    deep[6] = 32.0 * quarter

    drain(but=3)
    land_rest()
    loop(3, 21, 9, guess)
    sweep(g1, e1, mid_faces, g1, 4, 20, 8, R1, 4, 24, 2)

    sixth()
    g2[...] = deep[6] * f2[R2 : 6 * R2, :]
    e2[R2 : 6 * R2, :] = g2[...]
    for src, dst in ((e2, e2b), (e2b, e2), (e2, e2b)):
        centre, besides = around2(src)
        parts = [deep[n] * besides[n] for n in range(6)]
        dst[R2 : 6 * R2, :] = (
            (0.2 * centre + g2[...]) + (parts[0] + parts[1]) + (parts[2] + parts[3]) + (parts[4] + parts[5])
        )

    lanes16 = lane_ids(16) % 4
    hops = ((1, 2), (-1, 2), (1, -2), (-1, -2))
    for number in range(8):
        block, i = (number + 6) // 4, (number + 6) % 4
        value = jnp.where(lanes16 == i, e2b[pl.ds(zero + (R2 + R2 * block + 4), 16), :], 0.0)
        value = value + turn(value, hops[i][0])
        value = value + turn(value, hops[i][1])
        pe2[pl.ds(32 * number, 16, stride=2), :] = value
        pe2[pl.ds(32 * number + 1, 16, stride=2), :] = value

    def corrected1(p):
        value = e1[pl.ds(p * R1 + 4, 24), :] + pe2[pl.ds((p // 2 - 2) * 32 + 4, 24), :]
        return [(e1, at(p * R1 + 4, 24), value)]

    loop(4, 20, 16, corrected1)
    sweep(e1, e1b, mid_faces, g1, 5, 19, 14, R1, 4, 24, 2)
    sweep(e1b, e1, mid_faces, g1, 6, 18, 12, R1, 4, 24, 2)

    def grown(i):
        value = e1[pl.ds((i + 6) * R1 + 4, 24), :]
        return [(pe1, (pl.ds(RF * i + odd, 24, stride=2), slice(None)), value) for odd in (0, 1)]

    loop(0, 12, 12, grown)

    def corrected0(p):
        base = p * RF + 4
        return [(u2, at(base, 40), u2[pl.ds(base, 40), :] + pe1[pl.ds((p // 2) * RF + 4, 40), :])]

    loop(1, 23, 11, corrected0)
    sweep(u2, u1, fine_faces, gf, 2, 22, 10, RF, 4, 40, 1)

    def give(ref, stage, other, quads):
        def step(t):
            rows = pl.ds(pl.multiple_of(8 * t, 8), 8)
            out = []
            for q in quads:
                four = [
                    ref[pl.ds(pl.multiple_of((4 + 4 * q + i) * RF + 8 + 8 * t, 8), 8), :]
                    for i in range(4)
                ]
                for p, value in enumerate(transposed(four)):
                    out.append((stage, (p, rows, slice(128 * q, 128 * q + 128)), value))
            return out

        loop(0, 4, 4, step)
        lanes = pl.ds(128 * quads[0], 128 * len(quads))
        return stage.at[pl.ds(1 - half, 3), :, lanes], other.at[:, :, lanes], other.at[:, :, lanes]

    def keep(stage, out):
        for s in range(4):
            out[s, :, mine] = stage[jnp.clip(s + half * split, 0, 3)]

    def take(other, out):
        for s in range(4):
            out[s, :, theirs] = other[jnp.clip(s + half * (split - 1), 0, 2)]

    last = []
    sweep(u1, u2, fine_faces, gf, 3, 12, 9, RF, 4, 40, 1)
    last.append(hand(*give(u2, stage_f, other_f, (0, 1))))
    sweep(u1, u2, fine_faces, gf, 12, 21, 9, RF, 4, 40, 1)
    last.append(hand(*give(u2, stage_f, other_f, (2, 3))))
    leftover(u2, u1, fine_faces, gf, df, 4, 12, 8, RF, 8, 32, 1)
    last.append(hand(*give(u1, stage_r, other_r, (0, 1))))
    leftover(u2, u1, fine_faces, gf, df, 12, 20, 8, RF, 8, 32, 1)
    last.append(hand(*give(u1, stage_r, other_r, (2, 3))))
    keep(stage_f, out_field)
    last[0]()
    last[1]()
    take(other_f, out_field)
    keep(stage_r, out_resid)
    last[2]()
    last[3]()
    take(other_r, out_resid)
    drain()


def vmem(*shape):
    return pltpu.VMEM(shape, F32)


def body(source, conductance, initial, box_counts):
    fine_field = vmem(PF * RF, LANES)
    mid_field = vmem(P1 * R1, LANES)
    deep_field = vmem(7 * R2, LANES)
    scratch = [pltpu.SMEM(box_counts.shape, jnp.int32)] + [vmem(6, 32, 512)] * 3
    scratch += [fine_field] * 5 + [vmem(6, PF * RF, LANES)] + [fine_field] * 2
    scratch += [mid_field] * 4 + [vmem(8 * 32, LANES), vmem(6, P1 * R1, LANES)] + [mid_field] * 4
    scratch += [deep_field] * 4 + [vmem(7, 5 * R2, LANES), vmem(5 * R2, LANES), vmem(12 * RF, LANES)]
    scratch += [vmem(4, 32, 512)] * 2 + [vmem(3, 32, 512)] * 2
    for big, middle, small in ((160, 80, 8), (96, 48, 8), (104, 56, 24), (32, 16, 8), (144, 72, 16)):
        scratch += [vmem(2 * big + 2 * middle + 4 * small, LANES)] * 2
    scratch += [pltpu.SemaphoreType.DMA((4,))] + [pltpu.SemaphoreType.DMA((ROUNDS,))] * 2
    hbm = pl.BlockSpec(memory_space=pltpu.HBM)
    shape = jax.ShapeDtypeStruct(source.shape, source.dtype)
    field, resid, held = pl.pallas_call(
        kernel,
        out_shape=(shape,) * 3,
        in_specs=[hbm] * 4,
        out_specs=(pl.BlockSpec(memory_space=pltpu.VMEM),) * 3,
        scratch_shapes=scratch,
        compiler_params=pltpu.CompilerParams(
            collective_id=0, has_side_effects=True, vmem_limit_bytes=40 * 2**20
        ),
        cost_estimate=pl.CostEstimate(flops=3 * 10**7, bytes_accessed=3 * 10**6, transcendentals=0),
    )(*[pltpu.with_memory_space_constraint(x, pltpu.HBM) for x in (box_counts, source, conductance, initial)])
    return field * held, resid * held


def solution(mesh):
    return jax.shard_map(
        body,
        mesh=mesh,
        in_specs=(P("box", None, None), P("box", None, None), P("box", None, None), P()),
        out_specs=(P("box", None, None), P("box", None, None)),
        check_vma=False,
    )
```

```python
import functools

import jax
import jax.numpy as jnp
from jax import lax
from jax.experimental import pallas as pl
from jax.experimental.pallas import tpu as pltpu
from jax.sharding import PartitionSpec as P


RF, PF = 48, 24
R1, P1 = 32, 24
R2 = 24
LANES = 128
FULL = (1, 1), (1, -1), (1, 0), (-1, 1), (-1, -1), (-1, 0), (0, 1), (0, -1)
FAR = (1, 2), (1, -2), (-1, 2), (-1, -2), (0, 2), (0, -2)
F32 = jnp.float32
ROUNDS = 3 + 3 * (5 + 2) + 4


def lane_ids(rows):
    return lax.broadcasted_iota(jnp.int32, (rows, LANES), 1)


def row_ids(rows):
    return lax.broadcasted_iota(jnp.int32, (rows, LANES), 0)


def turn(value, steps):
    return pltpu.roll(value, steps % LANES, 1)


def transposed(four):
    lanes = lane_ids(four[0].shape[0])
    low = lanes < 64
    even = (lanes // 32) % 2 == 0
    a, b, c, d = four
    e = jnp.where(low, a, turn(c, 64))
    f = jnp.where(low, b, turn(d, 64))
    g = jnp.where(low, turn(a, 64), c)
    h = jnp.where(low, turn(b, 64), d)
    return (
        jnp.where(even, e, turn(f, 32)),
        jnp.where(even, turn(e, -32), f),
        jnp.where(even, g, turn(h, 32)),
        jnp.where(even, turn(g, -32), h),
    )


def coefficients(c, besides, inside):
    around_ = [
        beside if within is None else jnp.where(within, beside, c)
        for beside, within in zip(besides, inside)
    ]
    total = 3.0 * c + 0.5 * (
        (around_[0] + around_[1]) + (around_[2] + around_[3]) + (around_[4] + around_[5])
    )
    quarter = 0.4 / total
    faces = [
        (c + beside) * quarter if within is None else jnp.where(within, (c + beside) * quarter, 0.0)
        for beside, within in zip(besides, inside)
    ]
    return faces, total, quarter


def around(ref, base, count, rows, twist):
    centre = ref[pl.ds(base, count), :]
    return centre, (
        ref[pl.ds(base - rows, count), :],
        ref[pl.ds(base + rows, count), :],
        ref[pl.ds(base - 1, count), :],
        ref[pl.ds(base + 1, count), :],
        turn(centre, twist),
        turn(centre, -twist),
    )


def weighted(faces, base, count, besides):
    parts = [faces[n][pl.ds(base, count), :] * besides[n] for n in range(6)]
    return (parts[0] + parts[1]) + (parts[2] + parts[3]) + (parts[4] + parts[5])


def planes_loop(low, high, width, body, group=None, base=0):
    assert (high - low) % width == 0
    group = group or width

    def step(index, carry):
        first = base + low + index * width
        stores = []
        for m in range(width):
            stores += body(first + m)
            if (m + 1) % group == 0 or m == width - 1:
                for ref, index_, value in stores:
                    ref[index_] = value
                stores = []
        return carry

    if high - low == width:
        step(0, 0)
    else:
        lax.fori_loop(0, (high - low) // width, step, 0)


def at(base, count):
    return pl.ds(base, count), slice(None)


def pair_rows(ref, base, count, rows):
    got = [
        ref[pl.ds(base + offset, count, stride=2), :] for offset in (0, 1, rows, rows + 1)
    ]
    return (got[0] + got[1]) + (got[2] + got[3])


def pair_lanes(value, width):
    first = (lane_ids(value.shape[0]) // width) % 2 == 0
    return 0.125 * (value + jnp.where(first, turn(value, -width), turn(value, width)))


def kernel(
    counts, source, conductance, initial, out_field, out_resid, out_held,
    owners, raw_c, raw_u, raw_s, cf, uf, sf, u1, u2, fine, gf, df,
    c1, f1, e1, e1b, mid, w1, g1, d1, r1, c2, f2, e2, e2b, deep, g2,
    stage_f, stage_r, other_f, other_r, *rest,
):
    post, local_sem, send_sem, recv_sem = rest[:-3], rest[-3], rest[-2], rest[-1]
    me = lax.axis_index("box")
    a, j = me // 8, me % 8
    half = me % 2
    sibling = me + 1 - 2 * half
    zero = me // 1024
    loop = functools.partial(planes_loop, base=zero)
    across = {da: ((a + da + 16) % 16) * 8 for da in (-1, 0, 1)}
    along = {dj: (j + dj + 8) % 8 for dj in (-2, -1, 0, 1, 2)}

    sibling_far = across[0] + (j - 1 + 2 * half + 8) % 8

    def device(da, dj):
        return across[da] + along[dj]

    numbers = iter(range(ROUNDS))
    leaving = []

    def describe(src, dst, number, target):
        return pltpu.make_async_remote_copy(
            src_ref=src, dst_ref=dst, send_sem=send_sem.at[number], recv_sem=recv_sem.at[number],
            device_id=(target,), device_id_type=pl.DeviceIdType.MESH,
        )

    leaves = {1: a < 15, -1: a > 0}
    comes = {1: a > 0, -1: a < 15}

    def inside(column):
        return jnp.logical_and(column >= 0, column < 8)

    def sized(messages, whole, sign, act):
        sizes = {}
        for column in range(8):
            rows = sum(rows for rows, da, dj in messages if 0 <= column + sign * dj < 8)
            sizes.setdefault(rows, []).append(column)
        for rows, columns in sizes.items():
            if len(columns) == 8:
                act(rows)
            else:
                there = functools.reduce(jnp.logical_or, [j == column for column in columns])
                pl.when(there)(functools.partial(act, rows))

    def start(copies, ref, first_row, messages, without):
        number = next(numbers)
        step_x = messages[0][1]

        def some(rows):
            part = ref.at[pl.ds(first_row, rows)]
            return describe(part, part, number, sibling)

        def go():
            for src, dst, target, dj in copies:
                begin = describe(src, dst, number, target).start
                if dj == 0:
                    begin()
                else:
                    pl.when(inside(j + dj))(begin)

        def gone():
            sized(messages, ref, 1, lambda rows: some(rows).wait_send())

        def come():
            sized(messages, ref, -1, lambda rows: some(rows).wait_recv())
            for dj in sorted({dj for rows, da, dj in messages}):
                if dj != 0:
                    gaps = [n for n, item in enumerate(messages) if item[2] == dj]
                    pl.when(jnp.logical_not(inside(j - dj)))(functools.partial(without, *gaps))

        if step_x == 0:
            go()
            leaving.append(gone)
            return come
        pl.when(leaves[step_x])(go)
        leaving.append(lambda: pl.when(leaves[step_x])(gone))

        def arrived():
            pl.when(comes[step_x])(come)
            pl.when(jnp.logical_not(comes[step_x]))(functools.partial(without, *range(len(messages))))

        return arrived

    def hand(src, dst, whole):
        number = next(numbers)
        describe(src, dst, number, sibling).start()
        everything = describe(whole, whole, number, sibling)
        leaving.append(everything.wait_send)
        return everything.wait_recv

    def drain(but=0):
        while len(leaving) > but:
            leaving.pop(0)()

    barrier = pltpu.get_barrier_semaphore()

    def here(*targets):
        for target in targets:
            pl.semaphore_signal(
                barrier, inc=1, device_id=(target,), device_id_type=pl.DeviceIdType.MESH
            )

    here(sibling)
    pl.when(inside(j - 1 + 2 * half))(lambda: here(sibling_far))
    for da in (1, -1):

        def beside():
            here(device(da, 0))
            for dj in (1, -1):
                pl.when(inside(j + dj))(lambda: here(device(da, dj)))

        pl.when(leaves[da])(beside)

    raws = (raw_c, raw_s, raw_u)
    given = (conductance, source, initial)
    mine = pl.ds(pl.multiple_of(512 * half, 512), 512)
    theirs = pl.ds(pl.multiple_of(512 - 512 * half, 512), 512)
    held = pl.ds(3 * half, 3)
    locals_ = [pltpu.make_async_copy(counts, owners, local_sem.at[3])]
    for number in range(3):
        locals_.append(
            pltpu.make_async_copy(
                given[number].at[pl.ds(0, 3), :, mine], raws[number].at[held], local_sem.at[number]
            )
        )
    for copy in locals_:
        copy.start()

    around_x = 1 + (a > 0).astype(jnp.int32) + (a < 15).astype(jnp.int32)
    around_y = 1 + (j > 0).astype(jnp.int32) + (j < 7).astype(jnp.int32)
    pl.semaphore_wait(barrier, around_x * around_y - 1)

    swaps = [
        hand(given[number].at[pl.ds(0, 3), :, theirs], raws[number].at[held], raws[number].at[held])
        for number in range(3)
    ]
    locals_[0].wait()
    split = owners[me - half]
    own = jnp.where(half == 0, split, 4 - split)
    for s in range(4):
        out_held[s] = jnp.where(s < own, jnp.ones((32, 1024), F32), 0.0)
    places = [jnp.where(p < split, p, jnp.clip(3 + p - split, 0, 5)) for p in range(4)]

    def bring(number, ref):
        locals_[1 + number].wait()
        swaps[number]()
        raw = raws[number]

        def step(t):
            rows = pl.ds(pl.multiple_of(8 * t, 8), 8)
            out = []
            for q in range(4):
                four = [raw[places[p], rows, 128 * q : 128 * q + 128] for p in range(4)]
                for i, value in enumerate(transposed(four)):
                    out.append((ref, at(pl.multiple_of((4 + 4 * q + i) * RF + 8 + 8 * t, 8), 8), value))
            return out

        loop(0, 4, 4, step, group=1)

    ROWS = (RF, R1)
    OWN = ((4, 16, 8, 32), (8, 8, 8, 16))

    def near(first, count, side, depth):
        return first - 1 + depth if side < 0 else first + count - depth

    def far(first, count, side, depth):
        return first + count - 1 + depth if side < 0 else first - depth

    own2 = R2 + 2 * R2 + 8

    def there2(da, dj):
        return R2 + R2 * (2 - dj) + 8 * (1 - da)

    def pieces(strips, corners, block, da, dj, pick):
        out = []
        if block is not None:
            out.append((block, own2 if pick is near else there2(da, dj), 8, 1))
        if da == 0:
            for ref, level, depths in strips:
                plane, planes, row, rows = OWN[level]
                for d in depths:
                    out.append((ref, pick(plane, planes, dj, d) * ROWS[level] + row, rows, 1))
        elif dj == 0:
            for ref, level, depths in strips:
                plane, planes, row, rows = OWN[level]
                for d in depths:
                    out.append(
                        (ref, plane * ROWS[level] + pick(row, rows, da, d), planes, ROWS[level])
                    )
        else:
            for ref, level, depth, low, count in corners:
                plane, planes, row, rows = OWN[level]
                ends = [pick(row, rows, da, d) for d in (low, low + count - 1)]
                out.append((ref, pick(plane, planes, dj, depth) * ROWS[level] + min(ends), count, 1))
        return out

    def slab(ref, first, count, stride):
        return (pl.ds(first, count, stride=stride) if stride > 1 else pl.ds(first, count)), slice(None)

    spare = list(post)

    def filler(ref, firsts, messages):
        def without(*gaps):
            for n in gaps:
                ref[pl.ds(firsts[n], messages[n][0]), :] = jnp.ones((messages[n][0], LANES), F32)

        return without

    def exchange(strips, corners, block=None, where=FULL):
        out, got = spare.pop(0), spare.pop(0)
        arrivals, filled = [], []
        offset = 0
        for step_x in (1, -1, 0):
            copies, messages, group_row = [], [], offset
            for da, dj in FULL:
                if da != step_x:
                    continue
                first_row = offset
                for ref, first, count, stride in pieces(strips, corners, block, da, dj, near):
                    out[pl.ds(offset, count), :] = ref[slab(ref, first, count, stride)]
                    offset += count
                offset += -offset % 8
                rows = pl.ds(first_row, offset - first_row)
                copies.append((out.at[rows], got.at[rows], device(da, dj), dj))
                messages.append((rows.size, da, dj))
                filled.append((first_row, da, dj))
            firsts = [first for first, da, dj in filled if da == step_x]
            arrivals.append(start(copies, got, group_row, messages, filler(got, firsts, messages)))
        assert out.shape == (offset, LANES)

        def land():
            for arrived in arrivals:
                arrived()
            for offset, da, dj in filled:
                for ref, first, count, stride in pieces(strips, corners, block, da, dj, far):
                    ref[slab(ref, first, count, stride)] = got[pl.ds(offset, count), :]
                    offset += count

        return land

    def fine_corner(ref, depth):
        return [(ref, 0, d, 1, depth - d) for d in range(1, depth)]

    bring(0, cf)
    bring(1, sf)
    land_c = exchange(
        ((cf, 0, (1, 2, 3)), (sf, 0, (1, 2))), fine_corner(cf, 3) + fine_corner(sf, 2)
    )
    bring(2, uf)
    land_u = exchange(((uf, 0, (1, 2, 3)),), fine_corner(uf, 3))

    def coarse_c(i):
        total = pair_rows(cf, (4 + 2 * i) * RF + 8, 16, RF)
        return [(c1, at(pl.multiple_of((8 + i) * R1 + 8, 8), 16), pair_lanes(total, 1))]

    loop(0, 8, 8, coarse_c)

    def packed(ref):
        lanes = lane_ids(8) % 4
        total = jnp.zeros((8, LANES), F32)
        for i in range(4):
            value = pair_lanes(pair_rows(ref, (8 + 2 * i) * R1 + 8, 8, R1), 2)
            total = total + jnp.where(lanes == i, value, 0.0)
        return total

    def blocks2(ref, where):
        arrivals = []
        for step_x in (1, -1, 0):
            places_ = [(da, dj) for da, dj in where if da == step_x]
            copies = [
                (ref.at[pl.ds(own2, 8)], ref.at[pl.ds(there2(da, dj), 8)], device(da, dj), dj)
                for da, dj in places_
            ]
            firsts = [there2(da, dj) for da, dj in places_]
            messages = [(8, da, dj) for da, dj in places_]
            arrivals.append(start(copies, ref, 0, messages, filler(ref, firsts, messages)))

        def arrived():
            for part in arrivals:
                part()

        return arrived

    c2[pl.ds(own2, 8), :] = packed(c1)
    land_c1 = exchange(
        ((c1, 1, (1, 2, 3, 4, 5, 6)),), [(c1, 1, d, 1, 6 - d) for d in range(1, 6)], c2
    )

    land_c()
    far_c2 = blocks2(c2, FAR)

    def edges(ref, first, side, count, rows, plane, row, low_y, high_y, low_x, high_x):
        for outside, there, here in (
            (low_y, plane - 1, plane), (high_y, plane + count, plane + count - 1)
        ):
            slab_there = at(there * rows + first, side)
            ref[slab_there] = jnp.where(outside, ref[at(here * rows + first, side)], ref[slab_there])
        lines = 24
        for outside, there, here in ((low_x, row[0] - 1, row[0]), (high_x, row[1] + 1, row[1])):
            slab_there = slab(ref, there, lines, rows)
            ref[slab_there] = jnp.where(outside, ref[slab(ref, here, lines, rows)], ref[slab_there])

    def cut(faces, first, side, count, rows, plane, row, low_y, high_y, low_x, high_x):
        for n, outside, here in ((0, low_y, plane), (1, high_y, plane + count - 1)):
            where = (n,) + at(here * rows + first, side)
            faces[where] = jnp.where(outside, 0.0, faces[where])
        for n, outside, here in ((2, low_x, row[0]), (3, high_x, row[1])):
            where = (n,) + slab(faces, here, 24, rows)
            faces[where] = jnp.where(outside, 0.0, faces[where])

    ends = (j == 0, j == 7, a == 0, a == 15)
    edges(cf, 4, 40, 16, RF, 4, (8, 39), *ends)
    fine_faces = [fine.at[n] for n in range(6)]

    def fine_coeffs(p):
        base = p * RF + 4
        centre, besides = around(cf, base, 40, RF, 1)
        z = lane_ids(40)
        inside = (None, None, None, None, z != 0, z != 127)
        faces, total, quarter = coefficients(centre, besides, inside)
        out = [(fine, (n,) + at(base, 40), faces[n]) for n in range(6)]
        out.append((gf, at(base, 40), 2.0 * quarter))
        out.append((df, at(base, 40), 1.25 * total))
        return out

    loop(2, 22, 4, fine_coeffs, group=1)
    cut(fine, 4, 40, 16, RF, 4, (8, 39), *ends)
    land_u()

    def sweep(src, dst, faces, right, low, high, width, rows, start, count, twist):
        def step(p):
            base = p * rows + start
            centre, besides = around(src, base, count, rows, twist)
            value = 0.2 * centre + right[pl.ds(base, count), :] + weighted(faces, base, count, besides)
            return [(dst, at(base, count), value)]

        loop(low, high, width, step, group=5)

    def leftover(src, dst, faces, right, diag, low, high, width, rows, start, count, twist):
        def step(p):
            base = p * rows + start
            centre, besides = around(src, base, count, rows, twist)
            value = diag[pl.ds(base, count), :] * (
                right[pl.ds(base, count), :] + weighted(faces, base, count, besides) - 0.8 * centre
            )
            return [(dst, at(base, count), value)]

        loop(low, high, width, step, group=4)

    def first_sweep(p):
        base = p * RF + 4
        centre, besides = around(uf, base, 40, RF, 1)
        right = gf[pl.ds(base, 40), :] * sf[pl.ds(base, 40), :]
        value = 0.2 * centre + right + weighted(fine_faces, base, 40, besides)
        return [(u1, at(base, 40), value), (gf, at(base, 40), right)]

    loop(2, 22, 10, first_sweep, group=5)
    sweep(u1, u2, fine_faces, gf, 3, 21, 9, RF, 4, 40, 1)
    leftover(u2, u1, fine_faces, gf, df, 4, 20, 8, RF, 8, 32, 1)

    def coarse_f(i):
        total = pair_rows(u1, (4 + 2 * i) * RF + 8, 16, RF)
        return [(f1, at(pl.multiple_of((8 + i) * R1 + 8, 8), 16), pair_lanes(total, 1))]

    loop(0, 8, 8, coarse_f)
    land_f = exchange(((f1, 1, (1, 2)),), [(f1, 1, 1, 1, 1)])
    land_rest = exchange(
        ((f1, 1, (3, 4, 5)), (u2, 0, (1, 2, 3))),
        [(f1, 1, 1, 2, 3), (f1, 1, 2, 1, 3), (f1, 1, 3, 1, 2), (f1, 1, 4, 1, 1)] + fine_corner(u2, 3),
    )

    drain(but=6)
    land_c1()
    edges(c1, 0, 32, 8, R1, 8, (8, 23), *ends)
    mid_faces = [mid.at[n] for n in range(6)]

    def mid_coeffs(p):
        base = p * R1
        centre, besides = around(c1, base, 32, R1, 2)
        z = lane_ids(32)
        inside = (None, None, None, None, z >= 2, z < 126)
        faces, total, quarter = coefficients(centre, besides, inside)
        out = [(mid, (n,) + at(base, 32), faces[n]) for n in range(6)]
        out.append((w1, at(base, 32), 8.0 * quarter))
        out.append((d1, at(base, 32), 0.3125 * total))
        return out

    loop(6, 18, 3, mid_coeffs, group=1)
    cut(mid, 0, 32, 8, R1, 8, (8, 23), *ends)

    def guess(p):
        base = p * R1
        return [(g1, at(base, 32), w1[pl.ds(base, 32), :] * f1[pl.ds(base, 32), :])]

    land_f()
    loop(6, 18, 12, guess)
    sweep(g1, e1, mid_faces, g1, 7, 17, 10, R1, 4, 24, 2)
    leftover(e1, r1, mid_faces, g1, d1, 8, 16, 8, R1, 8, 16, 2)
    f2[pl.ds(own2, 8), :] = packed(r1)
    sixth = blocks2(f2, FAR + FULL)

    loop(3, 6, 3, mid_coeffs, group=1)
    loop(18, 21, 3, mid_coeffs, group=1)
    cut(mid, 0, 32, 8, R1, 8, (8, 23), *ends)
    far_c2()

    def around2(ref):
        lanes = lane_ids(5 * R2) % 4
        centre = ref[R2 : 6 * R2, :]
        return centre, (
            jnp.where(lanes == 0, turn(ref[0 : 5 * R2, :], -3), turn(centre, 1)),
            jnp.where(lanes == 3, turn(ref[2 * R2 : 7 * R2, :], 3), turn(centre, -1)),
            ref[pl.ds(zero + (R2 - 1), 5 * R2), :],
            ref[pl.ds(zero + (R2 + 1), 5 * R2), :],
            turn(centre, 4),
            turn(centre, -4),
        )

    rows2, lanes2 = row_ids(5 * R2), lane_ids(5 * R2)
    x = rows2 % R2 + (8 * a - 8)
    y = 4 * (rows2 // R2) + lanes2 % 4 + (4 * j - 8)
    inside2 = (y != 0, y != 31, x != 0, x != 127, lanes2 >= 4, lanes2 < 124)
    centre, besides = around2(c2)
    faces, total, quarter = coefficients(centre, besides, inside2)
    for n in range(6):
        deep[n] = faces[n]
    deep[6] = 32.0 * quarter

    drain(but=3)
    land_rest()
    loop(3, 21, 9, guess)
    sweep(g1, e1, mid_faces, g1, 4, 20, 8, R1, 4, 24, 2)

    sixth()
    g2[...] = deep[6] * f2[R2 : 6 * R2, :]
    e2[R2 : 6 * R2, :] = g2[...]
    for src, dst in ((e2, e2b), (e2b, e2), (e2, e2b)):
        centre, besides = around2(src)
        parts = [deep[n] * besides[n] for n in range(6)]
        dst[R2 : 6 * R2, :] = (
            (0.2 * centre + g2[...]) + (parts[0] + parts[1]) + (parts[2] + parts[3]) + (parts[4] + parts[5])
        )

    def spread(ref, first, count, rows, value):
        slabs = [slab(ref, first + offset, count, 2) for offset in (0, 1, rows, rows + 1)]
        return [(ref, where, ref[where] + value) for where in slabs]

    lanes16 = lane_ids(16) % 4
    hops = ((1, 2), (-1, 2), (1, -2), (-1, -2))
    added = []
    for number in range(8):
        block, i = (number + 6) // 4, (number + 6) % 4
        value = jnp.where(lanes16 == i, e2b[pl.ds(zero + (R2 + R2 * block + 4), 16), :], 0.0)
        value = value + turn(value, hops[i][0])
        value = value + turn(value, hops[i][1])
        added += spread(e1, (4 + 2 * number) * R1, 16, R1, value)
        if number % 4 == 3:
            for ref, where, total in added:
                ref[where] = total
            added = []

    sweep(e1, e1b, mid_faces, g1, 5, 19, 14, R1, 4, 24, 2)
    sweep(e1b, e1, mid_faces, g1, 6, 18, 12, R1, 4, 24, 2)

    def grown(i):
        return spread(u2, 2 * i * RF, 24, RF, e1[pl.ds((i + 6) * R1 + 4, 24), :])

    loop(0, 12, 6, grown, group=3)
    sweep(u2, u1, fine_faces, gf, 2, 22, 10, RF, 4, 40, 1)

    def give(ref, stage, other, quads):
        def step(t):
            rows = pl.ds(pl.multiple_of(8 * t, 8), 8)
            out = []
            for q in quads:
                four = [
                    ref[pl.ds(pl.multiple_of((4 + 4 * q + i) * RF + 8 + 8 * t, 8), 8), :]
                    for i in range(4)
                ]
                for p, value in enumerate(transposed(four)):
                    out.append((stage, (p, rows, slice(128 * q, 128 * q + 128)), value))
            return out

        loop(0, 4, 4, step)
        lanes = pl.ds(128 * quads[0], 128 * len(quads))
        return stage.at[pl.ds(1 - half, 3), :, lanes], other.at[:, :, lanes], other.at[:, :, lanes]

    def keep(stage, out):
        for s in range(4):
            out[s, :, mine] = stage[jnp.clip(s + half * split, 0, 3)]

    def take(other, out):
        for s in range(4):
            out[s, :, theirs] = other[jnp.clip(s + half * (split - 1), 0, 2)]

    last = []
    sweep(u1, u2, fine_faces, gf, 3, 12, 9, RF, 4, 40, 1)
    last.append(hand(*give(u2, stage_f, other_f, (0, 1))))
    sweep(u1, u2, fine_faces, gf, 12, 21, 9, RF, 4, 40, 1)
    last.append(hand(*give(u2, stage_f, other_f, (2, 3))))
    leftover(u2, u1, fine_faces, gf, df, 4, 12, 8, RF, 8, 32, 1)
    last.append(hand(*give(u1, stage_r, other_r, (0, 1))))
    leftover(u2, u1, fine_faces, gf, df, 12, 20, 8, RF, 8, 32, 1)
    last.append(hand(*give(u1, stage_r, other_r, (2, 3))))
    keep(stage_f, out_field)
    last[0]()
    last[1]()
    take(other_f, out_field)
    keep(stage_r, out_resid)
    last[2]()
    last[3]()
    take(other_r, out_resid)
    drain()


def vmem(*shape):
    return pltpu.VMEM(shape, F32)


def body(source, conductance, initial, box_counts):
    fine_field = vmem(PF * RF, LANES)
    mid_field = vmem(P1 * R1, LANES)
    deep_field = vmem(7 * R2, LANES)
    scratch = [pltpu.SMEM(box_counts.shape, jnp.int32)] + [vmem(6, 32, 512)] * 3
    scratch += [fine_field] * 5 + [vmem(6, PF * RF, LANES)] + [fine_field] * 2
    scratch += [mid_field] * 4 + [vmem(6, P1 * R1, LANES)] + [mid_field] * 4
    scratch += [deep_field] * 4 + [vmem(7, 5 * R2, LANES), vmem(5 * R2, LANES)]
    scratch += [vmem(4, 32, 512)] * 2 + [vmem(3, 32, 512)] * 2
    for big, middle, small in ((160, 80, 8), (96, 48, 8), (104, 56, 24), (32, 16, 8), (144, 72, 16)):
        scratch += [vmem(2 * big + 2 * middle + 4 * small, LANES)] * 2
    scratch += [pltpu.SemaphoreType.DMA((4,))] + [pltpu.SemaphoreType.DMA((ROUNDS,))] * 2
    hbm = pl.BlockSpec(memory_space=pltpu.HBM)
    shape = jax.ShapeDtypeStruct(source.shape, source.dtype)
    field, resid, held = pl.pallas_call(
        kernel,
        out_shape=(shape,) * 3,
        in_specs=[hbm] * 4,
        out_specs=(pl.BlockSpec(memory_space=pltpu.VMEM),) * 3,
        scratch_shapes=scratch,
        compiler_params=pltpu.CompilerParams(
            collective_id=0, has_side_effects=True, vmem_limit_bytes=40 * 2**20
        ),
        cost_estimate=pl.CostEstimate(flops=3 * 10**7, bytes_accessed=3 * 10**6, transcendentals=0),
    )(*[pltpu.with_memory_space_constraint(x, pltpu.HBM) for x in (box_counts, source, conductance, initial)])
    return field * held, resid * held


def solution(mesh):
    return jax.shard_map(
        body,
        mesh=mesh,
        in_specs=(P("box", None, None), P("box", None, None), P("box", None, None), P()),
        out_specs=(P("box", None, None), P("box", None, None)),
        check_vma=False,
    )
```

```python
import functools

import jax
import jax.numpy as jnp
from jax import lax
from jax.experimental import pallas as pl
from jax.experimental.pallas import tpu as pltpu
from jax.sharding import PartitionSpec as P


RF, PF = 48, 24
R1, P1 = 32, 24
R2 = 24
LANES = 128
FULL = (1, 1), (1, -1), (1, 0), (-1, 1), (-1, -1), (-1, 0), (0, 1), (0, -1)
FAR = (1, 2), (1, -2), (-1, 2), (-1, -2), (0, 2), (0, -2)
F32 = jnp.float32
ROUNDS = 3 + 3 * (5 + 2) + 4


def lane_ids(rows):
    return lax.broadcasted_iota(jnp.int32, (rows, LANES), 1)


def row_ids(rows):
    return lax.broadcasted_iota(jnp.int32, (rows, LANES), 0)


def turn(value, steps):
    return pltpu.roll(value, steps % LANES, 1)


def transposed(four):
    lanes = lane_ids(four[0].shape[0])
    low = lanes < 64
    even = (lanes // 32) % 2 == 0
    a, b, c, d = four
    e = jnp.where(low, a, turn(c, 64))
    f = jnp.where(low, b, turn(d, 64))
    g = jnp.where(low, turn(a, 64), c)
    h = jnp.where(low, turn(b, 64), d)
    return (
        jnp.where(even, e, turn(f, 32)),
        jnp.where(even, turn(e, -32), f),
        jnp.where(even, g, turn(h, 32)),
        jnp.where(even, turn(g, -32), h),
    )


def coefficients(c, besides, inside):
    around_ = [
        beside if within is None else jnp.where(within, beside, c)
        for beside, within in zip(besides, inside)
    ]
    total = 3.0 * c + 0.5 * (
        (around_[0] + around_[1]) + (around_[2] + around_[3]) + (around_[4] + around_[5])
    )
    quarter = 0.4 / total
    faces = [
        (c + beside) * quarter if within is None else jnp.where(within, (c + beside) * quarter, 0.0)
        for beside, within in zip(besides, inside)
    ]
    return faces, total, quarter


def around(ref, base, count, rows, twist):
    centre = ref[pl.ds(base, count), :]
    return centre, (
        ref[pl.ds(base - rows, count), :],
        ref[pl.ds(base + rows, count), :],
        ref[pl.ds(base - 1, count), :],
        ref[pl.ds(base + 1, count), :],
        turn(centre, twist),
        turn(centre, -twist),
    )


def weighted(faces, base, count, besides):
    parts = [faces[n][pl.ds(base, count), :] * besides[n] for n in range(6)]
    return (parts[0] + parts[1]) + (parts[2] + parts[3]) + (parts[4] + parts[5])


def planes_loop(low, high, width, body, group=None, base=0):
    assert (high - low) % width == 0
    group = group or width

    def step(index, carry):
        first = base + low + index * width
        stores = []
        for m in range(width):
            stores += body(first + m)
            if (m + 1) % group == 0 or m == width - 1:
                for ref, index_, value in stores:
                    ref[index_] = value
                stores = []
        return carry

    if high - low == width:
        step(0, 0)
    else:
        lax.fori_loop(0, (high - low) // width, step, 0)


def at(base, count):
    return pl.ds(base, count), slice(None)


def pair_rows(ref, base, count, rows):
    got = [
        ref[pl.ds(base + offset, count, stride=2), :] for offset in (0, 1, rows, rows + 1)
    ]
    return (got[0] + got[1]) + (got[2] + got[3])


def pair_lanes(value, width):
    first = (lane_ids(value.shape[0]) // width) % 2 == 0
    return 0.125 * (value + jnp.where(first, turn(value, -width), turn(value, width)))


def kernel(
    counts, source, conductance, initial, out_field, out_resid, out_held,
    owners, raw_c, raw_u, raw_s, cf, uf, sf, u1, u2, fine, gf, df,
    c1, f1, e1, e1b, mid, w1, g1, d1, r1, c2, f2, e2, e2b, deep, g2,
    stage_f, stage_r, other_f, other_r, *rest,
):
    post, local_sem, send_sem, recv_sem = rest[:-3], rest[-3], rest[-2], rest[-1]
    me = lax.axis_index("box")
    a, j = me // 8, me % 8
    half = me % 2
    sibling = me + 1 - 2 * half
    zero = me // 1024
    loop = functools.partial(planes_loop, base=zero)
    across = {da: ((a + da + 16) % 16) * 8 for da in (-1, 0, 1)}
    along = {dj: (j + dj + 8) % 8 for dj in (-2, -1, 0, 1, 2)}

    sibling_far = across[0] + (j - 1 + 2 * half + 8) % 8

    def device(da, dj):
        return across[da] + along[dj]

    numbers = iter(range(ROUNDS))
    leaving = []

    def describe(src, dst, number, target):
        return pltpu.make_async_remote_copy(
            src_ref=src, dst_ref=dst, send_sem=send_sem.at[number], recv_sem=recv_sem.at[number],
            device_id=(target,), device_id_type=pl.DeviceIdType.MESH,
        )

    leaves = {1: a < 15, -1: a > 0}
    comes = {1: a > 0, -1: a < 15}

    def inside(column):
        return jnp.logical_and(column >= 0, column < 8)

    def sized(messages, whole, sign, act):
        sizes = {}
        for column in range(8):
            rows = sum(rows for rows, da, dj in messages if 0 <= column + sign * dj < 8)
            sizes.setdefault(rows, []).append(column)
        for rows, columns in sizes.items():
            if len(columns) == 8:
                act(rows)
            else:
                there = functools.reduce(jnp.logical_or, [j == column for column in columns])
                pl.when(there)(functools.partial(act, rows))

    def start(copies, ref, first_row, messages, without):
        number = next(numbers)
        step_x = messages[0][1]

        def some(rows):
            part = ref.at[pl.ds(first_row, rows)]
            return describe(part, part, number, sibling)

        def go():
            for src, dst, target, dj in copies:
                begin = describe(src, dst, number, target).start
                if dj == 0:
                    begin()
                else:
                    pl.when(inside(j + dj))(begin)

        def gone():
            sized(messages, ref, 1, lambda rows: some(rows).wait_send())

        def come():
            sized(messages, ref, -1, lambda rows: some(rows).wait_recv())
            for dj in sorted({dj for rows, da, dj in messages}):
                if dj != 0:
                    gaps = [n for n, item in enumerate(messages) if item[2] == dj]
                    pl.when(jnp.logical_not(inside(j - dj)))(functools.partial(without, *gaps))

        if step_x == 0:
            go()
            leaving.append(gone)
            return come
        pl.when(leaves[step_x])(go)
        leaving.append(lambda: pl.when(leaves[step_x])(gone))

        def arrived():
            pl.when(comes[step_x])(come)
            pl.when(jnp.logical_not(comes[step_x]))(functools.partial(without, *range(len(messages))))

        return arrived

    def hand(copies, whole):
        number = next(numbers)
        for src, dst in copies:
            describe(src, dst, number, sibling).start()
        everything = describe(whole, whole, number, sibling)
        leaving.append(everything.wait_send)
        return everything.wait_recv

    def drain(but=0):
        while len(leaving) > but:
            leaving.pop(0)()

    barrier = pltpu.get_barrier_semaphore()

    def here(*targets):
        for target in targets:
            pl.semaphore_signal(
                barrier, inc=1, device_id=(target,), device_id_type=pl.DeviceIdType.MESH
            )

    for da in (1, -1):

        def beside():
            for dj in (1, -1):
                pl.when(inside(j + dj))(lambda: here(device(da, dj)))
            here(device(da, 0))

        pl.when(leaves[da])(beside)
    pl.when(inside(j - 1 + 2 * half))(lambda: here(sibling_far))
    here(sibling)

    raws = (raw_c, raw_s, raw_u)
    given = (conductance, source, initial)
    mine = pl.ds(pl.multiple_of(512 * half, 512), 512)
    theirs = pl.ds(pl.multiple_of(512 - 512 * half, 512), 512)
    held = pl.ds(3 * half, 3)
    locals_ = [pltpu.make_async_copy(counts, owners, local_sem.at[3])]
    for number in range(3):
        locals_.append(
            pltpu.make_async_copy(
                given[number].at[pl.ds(0, 3), :, mine], raws[number].at[held], local_sem.at[number]
            )
        )
    for copy in locals_:
        copy.start()

    around_x = 1 + (a > 0).astype(jnp.int32) + (a < 15).astype(jnp.int32)
    around_y = 1 + (j > 0).astype(jnp.int32) + (j < 7).astype(jnp.int32)
    pl.semaphore_wait(barrier, around_x * around_y - 1)

    swaps = [
        hand(
            [(given[number].at[s, :, theirs], raws[number].at[3 * half + s]) for s in range(3)],
            raws[number].at[held],
        )
        for number in range(3)
    ]
    locals_[0].wait()
    split = owners[me - half]
    own = jnp.where(half == 0, split, 4 - split)
    for s in range(4):
        out_held[s] = jnp.where(s < own, jnp.ones((32, 1024), F32), 0.0)
    places = [jnp.where(p < split, p, jnp.clip(3 + p - split, 0, 5)) for p in range(4)]

    def bring(number, ref):
        locals_[1 + number].wait()
        swaps[number]()
        raw = raws[number]

        def step(t):
            rows = pl.ds(pl.multiple_of(8 * t, 8), 8)
            out = []
            for q in range(4):
                four = [raw[places[p], rows, 128 * q : 128 * q + 128] for p in range(4)]
                for i, value in enumerate(transposed(four)):
                    out.append((ref, at(pl.multiple_of((4 + 4 * q + i) * RF + 8 + 8 * t, 8), 8), value))
            return out

        loop(0, 4, 4, step, group=1)

    ROWS = (RF, R1)
    OWN = ((4, 16, 8, 32), (8, 8, 8, 16))

    def near(first, count, side, depth):
        return first - 1 + depth if side < 0 else first + count - depth

    def far(first, count, side, depth):
        return first + count - 1 + depth if side < 0 else first - depth

    own2 = R2 + 2 * R2 + 8

    def there2(da, dj):
        return R2 + R2 * (2 - dj) + 8 * (1 - da)

    def pieces(strips, corners, block, da, dj, pick):
        out = []
        if block is not None:
            out.append((block, own2 if pick is near else there2(da, dj), 8, 1))
        if da == 0:
            for ref, level, depths in strips:
                plane, planes, row, rows = OWN[level]
                for d in depths:
                    out.append((ref, pick(plane, planes, dj, d) * ROWS[level] + row, rows, 1))
        elif dj == 0:
            for ref, level, depths in strips:
                plane, planes, row, rows = OWN[level]
                for d in depths:
                    out.append(
                        (ref, plane * ROWS[level] + pick(row, rows, da, d), planes, ROWS[level])
                    )
        else:
            for ref, level, depth, low, count in corners:
                plane, planes, row, rows = OWN[level]
                ends = [pick(row, rows, da, d) for d in (low, low + count - 1)]
                out.append((ref, pick(plane, planes, dj, depth) * ROWS[level] + min(ends), count, 1))
        return out

    def slab(ref, first, count, stride):
        return (pl.ds(first, count, stride=stride) if stride > 1 else pl.ds(first, count)), slice(None)

    spare = list(post)

    def filler(ref, firsts, messages):
        def without(*gaps):
            for n in gaps:
                ref[pl.ds(firsts[n], messages[n][0]), :] = jnp.ones((messages[n][0], LANES), F32)

        return without

    def exchange(strips, corners, block=None, where=FULL):
        out, got = spare.pop(0), spare.pop(0)
        arrivals, filled = [], []
        offset = 0
        for step_x in (1, -1, 0):
            copies, messages, group_row = [], [], offset
            for da, dj in FULL:
                if da != step_x:
                    continue
                first_row = offset
                for ref, first, count, stride in pieces(strips, corners, block, da, dj, near):
                    out[pl.ds(offset, count), :] = ref[slab(ref, first, count, stride)]
                    offset += count
                offset += -offset % 8
                rows = pl.ds(first_row, offset - first_row)
                copies.append((out.at[rows], got.at[rows], device(da, dj), dj))
                messages.append((rows.size, da, dj))
                filled.append((first_row, da, dj))
            firsts = [first for first, da, dj in filled if da == step_x]
            arrivals.append(start(copies, got, group_row, messages, filler(got, firsts, messages)))
        assert out.shape == (offset, LANES)

        def land():
            for arrived in arrivals:
                arrived()
            for offset, da, dj in filled:
                for ref, first, count, stride in pieces(strips, corners, block, da, dj, far):
                    ref[slab(ref, first, count, stride)] = got[pl.ds(offset, count), :]
                    offset += count

        return land

    def fine_corner(ref, depth):
        return [(ref, 0, d, 1, depth - d) for d in range(1, depth)]

    bring(0, cf)
    bring(1, sf)
    land_c = exchange(
        ((cf, 0, (1, 2, 3)), (sf, 0, (1, 2))), fine_corner(cf, 3) + fine_corner(sf, 2)
    )
    bring(2, uf)
    land_u = exchange(((uf, 0, (1, 2, 3)),), fine_corner(uf, 3))

    def coarse_c(i):
        total = pair_rows(cf, (4 + 2 * i) * RF + 8, 16, RF)
        return [(c1, at(pl.multiple_of((8 + i) * R1 + 8, 8), 16), pair_lanes(total, 1))]

    loop(0, 8, 8, coarse_c)

    def packed(ref):
        lanes = lane_ids(8) % 4
        total = jnp.zeros((8, LANES), F32)
        for i in range(4):
            value = pair_lanes(pair_rows(ref, (8 + 2 * i) * R1 + 8, 8, R1), 2)
            total = total + jnp.where(lanes == i, value, 0.0)
        return total

    def blocks2(ref, where):
        arrivals = []
        for step_x in (1, -1, 0):
            places_ = [(da, dj) for da, dj in where if da == step_x]
            copies = [
                (ref.at[pl.ds(own2, 8)], ref.at[pl.ds(there2(da, dj), 8)], device(da, dj), dj)
                for da, dj in places_
            ]
            firsts = [there2(da, dj) for da, dj in places_]
            messages = [(8, da, dj) for da, dj in places_]
            arrivals.append(start(copies, ref, 0, messages, filler(ref, firsts, messages)))

        def arrived():
            for part in arrivals:
                part()

        return arrived

    c2[pl.ds(own2, 8), :] = packed(c1)
    land_c1 = exchange(
        ((c1, 1, (1, 2, 3, 4, 5, 6)),), [(c1, 1, d, 1, 6 - d) for d in range(1, 6)], c2
    )

    land_c()
    far_c2 = blocks2(c2, FAR)

    def edges(ref, first, side, count, rows, plane, row, low_y, high_y, low_x, high_x):
        for outside, there, here in (
            (low_y, plane - 1, plane), (high_y, plane + count, plane + count - 1)
        ):
            slab_there = at(there * rows + first, side)
            ref[slab_there] = jnp.where(outside, ref[at(here * rows + first, side)], ref[slab_there])
        lines = 24
        for outside, there, here in ((low_x, row[0] - 1, row[0]), (high_x, row[1] + 1, row[1])):
            slab_there = slab(ref, there, lines, rows)
            ref[slab_there] = jnp.where(outside, ref[slab(ref, here, lines, rows)], ref[slab_there])

    def cut(faces, first, side, count, rows, plane, row, low_y, high_y, low_x, high_x):
        for n, outside, here in ((0, low_y, plane), (1, high_y, plane + count - 1)):
            where = (n,) + at(here * rows + first, side)
            faces[where] = jnp.where(outside, 0.0, faces[where])
        for n, outside, here in ((2, low_x, row[0]), (3, high_x, row[1])):
            where = (n,) + slab(faces, here, 24, rows)
            faces[where] = jnp.where(outside, 0.0, faces[where])

    ends = (j == 0, j == 7, a == 0, a == 15)
    edges(cf, 4, 40, 16, RF, 4, (8, 39), *ends)
    fine_faces = [fine.at[n] for n in range(6)]

    def fine_coeffs(p):
        base = p * RF + 4
        centre, besides = around(cf, base, 40, RF, 1)
        z = lane_ids(40)
        inside = (None, None, None, None, z != 0, z != 127)
        faces, total, quarter = coefficients(centre, besides, inside)
        out = [(fine, (n,) + at(base, 40), faces[n]) for n in range(6)]
        out.append((gf, at(base, 40), 2.0 * quarter))
        out.append((df, at(base, 40), 1.25 * total))
        return out

    loop(2, 22, 4, fine_coeffs, group=1)
    cut(fine, 4, 40, 16, RF, 4, (8, 39), *ends)
    land_u()

    def sweep(src, dst, faces, right, low, high, width, rows, start, count, twist):
        def step(p):
            base = p * rows + start
            centre, besides = around(src, base, count, rows, twist)
            value = 0.2 * centre + right[pl.ds(base, count), :] + weighted(faces, base, count, besides)
            return [(dst, at(base, count), value)]

        loop(low, high, width, step, group=5)

    def leftover(src, dst, faces, right, diag, low, high, width, rows, start, count, twist):
        def step(p):
            base = p * rows + start
            centre, besides = around(src, base, count, rows, twist)
            value = diag[pl.ds(base, count), :] * (
                right[pl.ds(base, count), :] + weighted(faces, base, count, besides) - 0.8 * centre
            )
            return [(dst, at(base, count), value)]

        loop(low, high, width, step, group=4)

    def first_sweep(p):
        base = p * RF + 4
        centre, besides = around(uf, base, 40, RF, 1)
        right = gf[pl.ds(base, 40), :] * sf[pl.ds(base, 40), :]
        value = 0.2 * centre + right + weighted(fine_faces, base, 40, besides)
        return [(u1, at(base, 40), value), (gf, at(base, 40), right)]

    loop(2, 22, 10, first_sweep, group=5)
    sweep(u1, u2, fine_faces, gf, 3, 21, 9, RF, 4, 40, 1)
    leftover(u2, u1, fine_faces, gf, df, 4, 20, 8, RF, 8, 32, 1)

    def coarse_f(i):
        total = pair_rows(u1, (4 + 2 * i) * RF + 8, 16, RF)
        return [(f1, at(pl.multiple_of((8 + i) * R1 + 8, 8), 16), pair_lanes(total, 1))]

    loop(0, 8, 8, coarse_f)
    land_f = exchange(((f1, 1, (1, 2)),), [(f1, 1, 1, 1, 1)])
    land_rest = exchange(
        ((f1, 1, (3, 4, 5)), (u2, 0, (1, 2, 3))),
        [(f1, 1, 1, 2, 3), (f1, 1, 2, 1, 3), (f1, 1, 3, 1, 2), (f1, 1, 4, 1, 1)] + fine_corner(u2, 3),
    )

    drain(but=6)
    land_c1()
    edges(c1, 0, 32, 8, R1, 8, (8, 23), *ends)
    mid_faces = [mid.at[n] for n in range(6)]

    def mid_coeffs(p):
        base = p * R1
        centre, besides = around(c1, base, 32, R1, 2)
        z = lane_ids(32)
        inside = (None, None, None, None, z >= 2, z < 126)
        faces, total, quarter = coefficients(centre, besides, inside)
        out = [(mid, (n,) + at(base, 32), faces[n]) for n in range(6)]
        out.append((w1, at(base, 32), 8.0 * quarter))
        out.append((d1, at(base, 32), 0.3125 * total))
        return out

    loop(6, 18, 3, mid_coeffs, group=1)
    cut(mid, 0, 32, 8, R1, 8, (8, 23), *ends)

    def guess(p):
        base = p * R1
        return [(g1, at(base, 32), w1[pl.ds(base, 32), :] * f1[pl.ds(base, 32), :])]

    land_f()
    loop(6, 18, 12, guess)
    sweep(g1, e1, mid_faces, g1, 7, 17, 10, R1, 4, 24, 2)
    leftover(e1, r1, mid_faces, g1, d1, 8, 16, 8, R1, 8, 16, 2)
    f2[pl.ds(own2, 8), :] = packed(r1)
    sixth = blocks2(f2, FAR + FULL)

    loop(3, 6, 3, mid_coeffs, group=1)
    loop(18, 21, 3, mid_coeffs, group=1)
    cut(mid, 0, 32, 8, R1, 8, (8, 23), *ends)
    far_c2()

    def around2(ref):
        lanes = lane_ids(5 * R2) % 4
        centre = ref[R2 : 6 * R2, :]
        return centre, (
            jnp.where(lanes == 0, turn(ref[0 : 5 * R2, :], -3), turn(centre, 1)),
            jnp.where(lanes == 3, turn(ref[2 * R2 : 7 * R2, :], 3), turn(centre, -1)),
            ref[pl.ds(zero + (R2 - 1), 5 * R2), :],
            ref[pl.ds(zero + (R2 + 1), 5 * R2), :],
            turn(centre, 4),
            turn(centre, -4),
        )

    rows2, lanes2 = row_ids(5 * R2), lane_ids(5 * R2)
    x = rows2 % R2 + (8 * a - 8)
    y = 4 * (rows2 // R2) + lanes2 % 4 + (4 * j - 8)
    inside2 = (y != 0, y != 31, x != 0, x != 127, lanes2 >= 4, lanes2 < 124)
    centre, besides = around2(c2)
    faces, total, quarter = coefficients(centre, besides, inside2)
    for n in range(6):
        deep[n] = faces[n]
    deep[6] = 32.0 * quarter

    drain(but=3)
    land_rest()
    loop(3, 21, 9, guess)
    sweep(g1, e1, mid_faces, g1, 4, 20, 8, R1, 4, 24, 2)

    sixth()
    g2[...] = deep[6] * f2[R2 : 6 * R2, :]
    e2[R2 : 6 * R2, :] = g2[...]
    for src, dst in ((e2, e2b), (e2b, e2), (e2, e2b)):
        centre, besides = around2(src)
        parts = [deep[n] * besides[n] for n in range(6)]
        dst[R2 : 6 * R2, :] = (
            (0.2 * centre + g2[...]) + (parts[0] + parts[1]) + (parts[2] + parts[3]) + (parts[4] + parts[5])
        )

    def spread(ref, first, count, rows, value):
        slabs = [slab(ref, first + offset, count, 2) for offset in (0, 1, rows, rows + 1)]
        return [(ref, where, ref[where] + value) for where in slabs]

    lanes16 = lane_ids(16) % 4
    hops = ((1, 2), (-1, 2), (1, -2), (-1, -2))
    added = []
    for number in range(8):
        block, i = (number + 6) // 4, (number + 6) % 4
        value = jnp.where(lanes16 == i, e2b[pl.ds(zero + (R2 + R2 * block + 4), 16), :], 0.0)
        value = value + turn(value, hops[i][0])
        value = value + turn(value, hops[i][1])
        added += spread(e1, (4 + 2 * number) * R1, 16, R1, value)
        if number % 4 == 3:
            for ref, where, total in added:
                ref[where] = total
            added = []

    sweep(e1, e1b, mid_faces, g1, 5, 19, 14, R1, 4, 24, 2)
    sweep(e1b, e1, mid_faces, g1, 6, 18, 12, R1, 4, 24, 2)

    def grown(i):
        return spread(u2, 2 * i * RF, 24, RF, e1[pl.ds((i + 6) * R1 + 4, 24), :])

    loop(0, 12, 6, grown, group=3)
    sweep(u2, u1, fine_faces, gf, 2, 22, 10, RF, 4, 40, 1)

    def give(ref, stage, other, quads):
        def step(t):
            rows = pl.ds(pl.multiple_of(8 * t, 8), 8)
            out = []
            for q in quads:
                four = [
                    ref[pl.ds(pl.multiple_of((4 + 4 * q + i) * RF + 8 + 8 * t, 8), 8), :]
                    for i in range(4)
                ]
                for p, value in enumerate(transposed(four)):
                    out.append((stage, (p, rows, slice(128 * q, 128 * q + 128)), value))
            return out

        loop(0, 4, 4, step)
        lanes = pl.ds(128 * quads[0], 128 * len(quads))
        return [(stage.at[pl.ds(1 - half, 3), :, lanes], other.at[:, :, lanes])], other.at[:, :, lanes]

    def keep(stage, out):
        for s in range(4):
            out[s, :, mine] = stage[jnp.clip(s + half * split, 0, 3)]

    def take(other, out):
        for s in range(4):
            out[s, :, theirs] = other[jnp.clip(s + half * (split - 1), 0, 2)]

    last = []
    sweep(u1, u2, fine_faces, gf, 3, 12, 9, RF, 4, 40, 1)
    last.append(hand(*give(u2, stage_f, other_f, (0, 1))))
    sweep(u1, u2, fine_faces, gf, 12, 21, 9, RF, 4, 40, 1)
    last.append(hand(*give(u2, stage_f, other_f, (2, 3))))
    leftover(u2, u1, fine_faces, gf, df, 4, 12, 8, RF, 8, 32, 1)
    last.append(hand(*give(u1, stage_r, other_r, (0, 1))))
    leftover(u2, u1, fine_faces, gf, df, 12, 20, 8, RF, 8, 32, 1)
    last.append(hand(*give(u1, stage_r, other_r, (2, 3))))
    keep(stage_f, out_field)
    last[0]()
    last[1]()
    take(other_f, out_field)
    keep(stage_r, out_resid)
    last[2]()
    last[3]()
    take(other_r, out_resid)
    drain()


def vmem(*shape):
    return pltpu.VMEM(shape, F32)


def body(source, conductance, initial, box_counts):
    fine_field = vmem(PF * RF, LANES)
    mid_field = vmem(P1 * R1, LANES)
    deep_field = vmem(7 * R2, LANES)
    scratch = [pltpu.SMEM(box_counts.shape, jnp.int32)] + [vmem(6, 32, 512)] * 3
    scratch += [fine_field] * 5 + [vmem(6, PF * RF, LANES)] + [fine_field] * 2
    scratch += [mid_field] * 4 + [vmem(6, P1 * R1, LANES)] + [mid_field] * 4
    scratch += [deep_field] * 4 + [vmem(7, 5 * R2, LANES), vmem(5 * R2, LANES)]
    scratch += [vmem(4, 32, 512)] * 2 + [vmem(3, 32, 512)] * 2
    for big, middle, small in ((160, 80, 8), (96, 48, 8), (104, 56, 24), (32, 16, 8), (144, 72, 16)):
        scratch += [vmem(2 * big + 2 * middle + 4 * small, LANES)] * 2
    scratch += [pltpu.SemaphoreType.DMA((4,))] + [pltpu.SemaphoreType.DMA((ROUNDS,))] * 2
    hbm = pl.BlockSpec(memory_space=pltpu.HBM)
    shape = jax.ShapeDtypeStruct(source.shape, source.dtype)
    field, resid, held = pl.pallas_call(
        kernel,
        out_shape=(shape,) * 3,
        in_specs=[hbm] * 4,
        out_specs=(pl.BlockSpec(memory_space=pltpu.VMEM),) * 3,
        scratch_shapes=scratch,
        compiler_params=pltpu.CompilerParams(
            collective_id=0, has_side_effects=True, vmem_limit_bytes=40 * 2**20
        ),
        cost_estimate=pl.CostEstimate(flops=3 * 10**7, bytes_accessed=3 * 10**6, transcendentals=0),
    )(*[pltpu.with_memory_space_constraint(x, pltpu.HBM) for x in (box_counts, source, conductance, initial)])
    return field * held, resid * held


def solution(mesh):
    return jax.shard_map(
        body,
        mesh=mesh,
        in_specs=(P("box", None, None), P("box", None, None), P("box", None, None), P()),
        out_specs=(P("box", None, None), P("box", None, None)),
        check_vma=False,
    )
```

```python
import functools

import jax
import jax.numpy as jnp
from jax import lax
from jax.experimental import pallas as pl
from jax.experimental.pallas import tpu as pltpu
from jax.sharding import PartitionSpec as P


RF, PF = 48, 24
R1, P1 = 32, 24
R2 = 24
LANES = 128
FULL = (1, 1), (1, -1), (1, 0), (-1, 1), (-1, -1), (-1, 0), (0, 1), (0, -1)
FAR = (1, 2), (1, -2), (-1, 2), (-1, -2), (0, 2), (0, -2)
F32 = jnp.float32
ROUNDS = 3 + 3 * (5 + 2) + 4


def lane_ids(rows):
    return lax.broadcasted_iota(jnp.int32, (rows, LANES), 1)


def row_ids(rows):
    return lax.broadcasted_iota(jnp.int32, (rows, LANES), 0)


def turn(value, steps):
    return pltpu.roll(value, steps % LANES, 1)


def transposed(four):
    lanes = lane_ids(four[0].shape[0])
    low = lanes < 64
    even = (lanes // 32) % 2 == 0
    a, b, c, d = four
    e = jnp.where(low, a, turn(c, 64))
    f = jnp.where(low, b, turn(d, 64))
    g = jnp.where(low, turn(a, 64), c)
    h = jnp.where(low, turn(b, 64), d)
    return (
        jnp.where(even, e, turn(f, 32)),
        jnp.where(even, turn(e, -32), f),
        jnp.where(even, g, turn(h, 32)),
        jnp.where(even, turn(g, -32), h),
    )


def coefficients(c, besides, inside):
    around_ = [
        beside if within is None else jnp.where(within, beside, c)
        for beside, within in zip(besides, inside)
    ]
    total = 3.0 * c + 0.5 * (
        (around_[0] + around_[1]) + (around_[2] + around_[3]) + (around_[4] + around_[5])
    )
    quarter = 0.4 / total
    faces = [
        (c + beside) * quarter if within is None else jnp.where(within, (c + beside) * quarter, 0.0)
        for beside, within in zip(besides, inside)
    ]
    return faces, total, quarter


def around(ref, base, count, rows, twist):
    centre = ref[pl.ds(base, count), :]
    return centre, (
        ref[pl.ds(base - rows, count), :],
        ref[pl.ds(base + rows, count), :],
        ref[pl.ds(base - 1, count), :],
        ref[pl.ds(base + 1, count), :],
        turn(centre, twist),
        turn(centre, -twist),
    )


def weighted(faces, base, count, besides):
    parts = [faces[n][pl.ds(base, count), :] * besides[n] for n in range(6)]
    return (parts[0] + parts[1]) + (parts[2] + parts[3]) + (parts[4] + parts[5])


def planes_loop(low, high, width, body, group=None, base=0):
    assert (high - low) % width == 0
    group = group or width

    def step(index, carry):
        first = base + low + index * width
        stores = []
        for m in range(width):
            stores += body(first + m)
            if (m + 1) % group == 0 or m == width - 1:
                for ref, index_, value in stores:
                    ref[index_] = value
                stores = []
        return carry

    if high - low == width:
        step(0, 0)
    else:
        lax.fori_loop(0, (high - low) // width, step, 0)


def at(base, count):
    return pl.ds(base, count), slice(None)


def pair_rows(ref, base, count, rows):
    got = [
        ref[pl.ds(base + offset, count, stride=2), :] for offset in (0, 1, rows, rows + 1)
    ]
    return (got[0] + got[1]) + (got[2] + got[3])


def pair_lanes(value, width):
    first = (lane_ids(value.shape[0]) // width) % 2 == 0
    return 0.125 * (value + jnp.where(first, turn(value, -width), turn(value, width)))


def kernel(
    counts, source, conductance, initial, out_field, out_resid, out_held,
    owners, raw_c, raw_u, raw_s, cf, uf, sf, u1, u2, fine, gf, df,
    c1, f1, e1, e1b, mid, w1, g1, d1, r1, c2, f2, e2, e2b, deep, g2,
    stage_f, stage_r, other_f, other_r, *rest,
):
    post, local_sem, send_sem, recv_sem = rest[:-3], rest[-3], rest[-2], rest[-1]
    me = lax.axis_index("box")
    a, j = me // 8, me % 8
    half = me % 2
    sibling = me + 1 - 2 * half
    zero = me // 1024
    loop = functools.partial(planes_loop, base=zero)
    across = {da: ((a + da + 16) % 16) * 8 for da in (-1, 0, 1)}
    along = {dj: (j + dj + 8) % 8 for dj in (-2, -1, 0, 1, 2)}

    sibling_far = across[0] + (j - 1 + 2 * half + 8) % 8

    def device(da, dj):
        return across[da] + along[dj]

    numbers = iter(range(ROUNDS))
    leaving = []

    def describe(src, dst, number, target):
        return pltpu.make_async_remote_copy(
            src_ref=src, dst_ref=dst, send_sem=send_sem.at[number], recv_sem=recv_sem.at[number],
            device_id=(target,), device_id_type=pl.DeviceIdType.MESH,
        )

    leaves = {1: a < 15, -1: a > 0}
    comes = {1: a > 0, -1: a < 15}

    def inside(column):
        return jnp.logical_and(column >= 0, column < 8)

    def sized(messages, whole, sign, act):
        sizes = {}
        for column in range(8):
            rows = sum(rows for rows, da, dj in messages if 0 <= column + sign * dj < 8)
            sizes.setdefault(rows, []).append(column)
        for rows, columns in sizes.items():
            if len(columns) == 8:
                act(rows)
            else:
                there = functools.reduce(jnp.logical_or, [j == column for column in columns])
                pl.when(there)(functools.partial(act, rows))

    def start(copies, ref, first_row, messages, without):
        number = next(numbers)
        step_x = messages[0][1]

        def some(rows):
            part = ref.at[pl.ds(first_row, rows)]
            return describe(part, part, number, sibling)

        def go():
            for src, dst, target, dj in copies:
                begin = describe(src, dst, number, target).start
                if dj == 0:
                    begin()
                else:
                    pl.when(inside(j + dj))(begin)

        def gone():
            sized(messages, ref, 1, lambda rows: some(rows).wait_send())

        def come():
            sized(messages, ref, -1, lambda rows: some(rows).wait_recv())
            for dj in sorted({dj for rows, da, dj in messages}):
                if dj != 0:
                    gaps = [n for n, item in enumerate(messages) if item[2] == dj]
                    pl.when(jnp.logical_not(inside(j - dj)))(functools.partial(without, *gaps))

        if step_x == 0:
            go()
            leaving.append(gone)
            return come
        pl.when(leaves[step_x])(go)
        leaving.append(lambda: pl.when(leaves[step_x])(gone))

        def arrived():
            pl.when(comes[step_x])(come)
            pl.when(jnp.logical_not(comes[step_x]))(functools.partial(without, *range(len(messages))))

        return arrived

    def hand(copies, whole):
        number = next(numbers)
        for src, dst in copies:
            describe(src, dst, number, sibling).start()
        everything = describe(whole, whole, number, sibling)
        leaving.append(everything.wait_send)
        return everything.wait_recv

    def drain(but=0):
        while len(leaving) > but:
            leaving.pop(0)()

    barrier = pltpu.get_barrier_semaphore()

    def here(*targets):
        for target in targets:
            pl.semaphore_signal(
                barrier, inc=1, device_id=(target,), device_id_type=pl.DeviceIdType.MESH
            )

    for da in (1, -1):

        def beside():
            for dj in (1, -1):
                pl.when(inside(j + dj))(lambda: here(device(da, dj)))
            here(device(da, 0))

        pl.when(leaves[da])(beside)
    pl.when(inside(j - 1 + 2 * half))(lambda: here(sibling_far))
    here(sibling)

    raws = (raw_c, raw_s, raw_u)
    given = (conductance, source, initial)
    mine = pl.ds(pl.multiple_of(512 * half, 512), 512)
    theirs = pl.ds(pl.multiple_of(512 - 512 * half, 512), 512)
    held = pl.ds(3 * half, 3)
    locals_ = [pltpu.make_async_copy(counts, owners, local_sem.at[3])]
    for number in range(3):
        locals_.append(
            pltpu.make_async_copy(
                given[number].at[pl.ds(0, 3), :, mine], raws[number].at[held], local_sem.at[number]
            )
        )
    for copy in locals_:
        copy.start()

    around_x = 1 + (a > 0).astype(jnp.int32) + (a < 15).astype(jnp.int32)
    around_y = 1 + (j > 0).astype(jnp.int32) + (j < 7).astype(jnp.int32)
    pl.semaphore_wait(barrier, around_x * around_y - 1)

    swaps = [
        hand(
            [(given[number].at[s, :, theirs], raws[number].at[3 * half + s]) for s in range(3)],
            raws[number].at[held],
        )
        for number in range(3)
    ]
    locals_[0].wait()
    split = owners[me - half]
    own = jnp.where(half == 0, split, 4 - split)
    for s in range(4):
        out_held[s] = jnp.where(s < own, jnp.ones((32, 1024), F32), 0.0)
    places = [jnp.where(p < split, p, jnp.clip(3 + p - split, 0, 5)) for p in range(4)]

    def bring(number, ref):
        locals_[1 + number].wait()
        swaps[number]()
        raw = raws[number]

        def step(t):
            rows = pl.ds(pl.multiple_of(8 * t, 8), 8)
            out = []
            for q in range(4):
                four = [raw[places[p], rows, 128 * q : 128 * q + 128] for p in range(4)]
                for i, value in enumerate(transposed(four)):
                    out.append((ref, at(pl.multiple_of((4 + 4 * q + i) * RF + 8 + 8 * t, 8), 8), value))
            return out

        loop(0, 4, 4, step, group=1)

    ROWS = (RF, R1)
    OWN = ((4, 16, 8, 32), (8, 8, 8, 16))

    def near(first, count, side, depth):
        return first - 1 + depth if side < 0 else first + count - depth

    def far(first, count, side, depth):
        return first + count - 1 + depth if side < 0 else first - depth

    own2 = R2 + 2 * R2 + 8

    def there2(da, dj):
        return R2 + R2 * (2 - dj) + 8 * (1 - da)

    def pieces(strips, corners, block, da, dj, pick):
        out = []
        if block is not None:
            out.append((block, own2 if pick is near else there2(da, dj), 8, 1))
        if da == 0:
            for ref, level, depths in strips:
                plane, planes, row, rows = OWN[level]
                for d in depths:
                    out.append((ref, pick(plane, planes, dj, d) * ROWS[level] + row, rows, 1))
        elif dj == 0:
            for ref, level, depths in strips:
                plane, planes, row, rows = OWN[level]
                for d in depths:
                    out.append(
                        (ref, plane * ROWS[level] + pick(row, rows, da, d), planes, ROWS[level])
                    )
        else:
            for ref, level, depth, low, count in corners:
                plane, planes, row, rows = OWN[level]
                ends = [pick(row, rows, da, d) for d in (low, low + count - 1)]
                out.append((ref, pick(plane, planes, dj, depth) * ROWS[level] + min(ends), count, 1))
        return out

    def slab(ref, first, count, stride):
        return (pl.ds(first, count, stride=stride) if stride > 1 else pl.ds(first, count)), slice(None)

    spare = list(post)

    def filler(ref, firsts, messages):
        def without(*gaps):
            for n in gaps:
                ref[pl.ds(firsts[n], messages[n][0]), :] = jnp.ones((messages[n][0], LANES), F32)

        return without

    def exchange(strips, corners, block=None, where=FULL):
        out, got = spare.pop(0), spare.pop(0)
        arrivals, filled = [], []
        offset = 0
        for step_x in (1, -1, 0):
            copies, messages, group_row = [], [], offset
            for da, dj in FULL:
                if da != step_x:
                    continue
                first_row = offset
                for ref, first, count, stride in pieces(strips, corners, block, da, dj, near):
                    out[pl.ds(offset, count), :] = ref[slab(ref, first, count, stride)]
                    offset += count
                offset += -offset % 8
                rows = pl.ds(first_row, offset - first_row)
                copies.append((out.at[rows], got.at[rows], device(da, dj), dj))
                messages.append((rows.size, da, dj))
                filled.append((first_row, da, dj))
            firsts = [first for first, da, dj in filled if da == step_x]
            arrivals.append(start(copies, got, group_row, messages, filler(got, firsts, messages)))
        assert out.shape == (offset, LANES)

        def land():
            for arrived in arrivals:
                arrived()
            for offset, da, dj in filled:
                for ref, first, count, stride in pieces(strips, corners, block, da, dj, far):
                    ref[slab(ref, first, count, stride)] = got[pl.ds(offset, count), :]
                    offset += count

        return land

    def fine_corner(ref, depth):
        return [(ref, 0, d, 1, depth - d) for d in range(1, depth)]

    bring(0, cf)
    bring(1, sf)
    land_c = exchange(
        ((cf, 0, (1, 2, 3)), (sf, 0, (1, 2))), fine_corner(cf, 3) + fine_corner(sf, 2)
    )
    bring(2, uf)
    land_u = exchange(((uf, 0, (1, 2, 3)),), fine_corner(uf, 3))

    def coarse_c(i):
        total = pair_rows(cf, (4 + 2 * i) * RF + 8, 16, RF)
        return [(c1, at(pl.multiple_of((8 + i) * R1 + 8, 8), 16), pair_lanes(total, 1))]

    loop(0, 8, 8, coarse_c)

    def packed(ref):
        lanes = lane_ids(8) % 4
        total = jnp.zeros((8, LANES), F32)
        for i in range(4):
            value = pair_lanes(pair_rows(ref, (8 + 2 * i) * R1 + 8, 8, R1), 2)
            total = total + jnp.where(lanes == i, value, 0.0)
        return total

    def blocks2(ref, where):
        arrivals = []
        for step_x in (1, -1, 0):
            places_ = [(da, dj) for da, dj in where if da == step_x]
            copies = [
                (ref.at[pl.ds(own2, 8)], ref.at[pl.ds(there2(da, dj), 8)], device(da, dj), dj)
                for da, dj in places_
            ]
            firsts = [there2(da, dj) for da, dj in places_]
            messages = [(8, da, dj) for da, dj in places_]
            arrivals.append(start(copies, ref, 0, messages, filler(ref, firsts, messages)))

        def arrived():
            for part in arrivals:
                part()

        return arrived

    c2[pl.ds(own2, 8), :] = packed(c1)
    land_c1 = exchange(
        ((c1, 1, (1, 2, 3, 4, 5, 6)),), [(c1, 1, d, 1, 6 - d) for d in range(1, 6)], c2
    )

    land_c()
    far_c2 = blocks2(c2, FAR)

    def edges(ref, first, side, count, rows, plane, row, low_y, high_y, low_x, high_x):
        for outside, there, here in (
            (low_y, plane - 1, plane), (high_y, plane + count, plane + count - 1)
        ):
            slab_there = at(there * rows + first, side)
            ref[slab_there] = jnp.where(outside, ref[at(here * rows + first, side)], ref[slab_there])
        lines = 24
        for outside, there, here in ((low_x, row[0] - 1, row[0]), (high_x, row[1] + 1, row[1])):
            slab_there = slab(ref, there, lines, rows)
            ref[slab_there] = jnp.where(outside, ref[slab(ref, here, lines, rows)], ref[slab_there])

    def cut(faces, first, side, count, rows, plane, row, low_y, high_y, low_x, high_x):
        for n, outside, here in ((0, low_y, plane), (1, high_y, plane + count - 1)):
            where = (n,) + at(here * rows + first, side)
            faces[where] = jnp.where(outside, 0.0, faces[where])
        for n, outside, here in ((2, low_x, row[0]), (3, high_x, row[1])):
            where = (n,) + slab(faces, here, 24, rows)
            faces[where] = jnp.where(outside, 0.0, faces[where])

    ends = (j == 0, j == 7, a == 0, a == 15)
    edges(cf, 4, 40, 16, RF, 4, (8, 39), *ends)
    fine_faces = [fine.at[n] for n in range(6)]

    def fine_coeffs(p):
        base = p * RF + 4
        centre, besides = around(cf, base, 40, RF, 1)
        z = lane_ids(40)
        inside = (None, None, None, None, z != 0, z != 127)
        faces, total, quarter = coefficients(centre, besides, inside)
        out = [(fine, (n,) + at(base, 40), faces[n]) for n in range(6)]
        out.append((gf, at(base, 40), 2.0 * quarter))
        out.append((df, at(base, 40), 1.25 * total))
        return out

    loop(2, 22, 4, fine_coeffs, group=1)
    cut(fine, 4, 40, 16, RF, 4, (8, 39), *ends)
    land_u()

    def sweep(src, dst, faces, right, low, high, width, rows, start, count, twist):
        def step(p):
            base = p * rows + start
            centre, besides = around(src, base, count, rows, twist)
            value = 0.2 * centre + right[pl.ds(base, count), :] + weighted(faces, base, count, besides)
            return [(dst, at(base, count), value)]

        loop(low, high, width, step, group=5)

    def leftover(src, dst, faces, right, diag, low, high, width, rows, start, count, twist):
        def step(p):
            base = p * rows + start
            centre, besides = around(src, base, count, rows, twist)
            value = diag[pl.ds(base, count), :] * (
                right[pl.ds(base, count), :] + weighted(faces, base, count, besides) - 0.8 * centre
            )
            return [(dst, at(base, count), value)]

        loop(low, high, width, step, group=4)

    def first_sweep(p):
        base = p * RF + 4
        centre, besides = around(uf, base, 40, RF, 1)
        right = gf[pl.ds(base, 40), :] * sf[pl.ds(base, 40), :]
        value = 0.2 * centre + right + weighted(fine_faces, base, 40, besides)
        return [(u1, at(base, 40), value), (gf, at(base, 40), right)]

    loop(2, 22, 10, first_sweep, group=5)
    sweep(u1, u2, fine_faces, gf, 3, 21, 9, RF, 4, 40, 1)
    leftover(u2, u1, fine_faces, gf, df, 4, 20, 8, RF, 8, 32, 1)

    def coarse_f(i):
        total = pair_rows(u1, (4 + 2 * i) * RF + 8, 16, RF)
        return [(f1, at(pl.multiple_of((8 + i) * R1 + 8, 8), 16), pair_lanes(total, 1))]

    loop(0, 8, 8, coarse_f)
    land_f = exchange(((f1, 1, (1, 2)),), [(f1, 1, 1, 1, 1)])
    land_rest = exchange(
        ((f1, 1, (3, 4, 5)), (u2, 0, (1, 2, 3))),
        [(f1, 1, 1, 2, 3), (f1, 1, 2, 1, 3), (f1, 1, 3, 1, 2), (f1, 1, 4, 1, 1)] + fine_corner(u2, 3),
    )

    drain(but=6)
    land_c1()
    edges(c1, 0, 32, 8, R1, 8, (8, 23), *ends)
    mid_faces = [mid.at[n] for n in range(6)]

    def mid_coeffs(p):
        base = p * R1
        centre, besides = around(c1, base, 32, R1, 2)
        z = lane_ids(32)
        inside = (None, None, None, None, z >= 2, z < 126)
        faces, total, quarter = coefficients(centre, besides, inside)
        out = [(mid, (n,) + at(base, 32), faces[n]) for n in range(6)]
        out.append((w1, at(base, 32), 8.0 * quarter))
        out.append((d1, at(base, 32), 0.3125 * total))
        return out

    loop(6, 18, 3, mid_coeffs, group=1)
    cut(mid, 0, 32, 8, R1, 8, (8, 23), *ends)

    def guess(p):
        base = p * R1
        return [(g1, at(base, 32), w1[pl.ds(base, 32), :] * f1[pl.ds(base, 32), :])]

    land_f()
    loop(6, 18, 12, guess)
    sweep(g1, e1, mid_faces, g1, 7, 17, 10, R1, 4, 24, 2)
    leftover(e1, r1, mid_faces, g1, d1, 8, 16, 8, R1, 8, 16, 2)
    f2[pl.ds(own2, 8), :] = packed(r1)
    sixth = blocks2(f2, FAR + FULL)

    loop(3, 6, 3, mid_coeffs, group=1)
    loop(18, 21, 3, mid_coeffs, group=1)
    cut(mid, 0, 32, 8, R1, 8, (8, 23), *ends)
    far_c2()

    def around2(ref):
        lanes = lane_ids(5 * R2) % 4
        centre = ref[R2 : 6 * R2, :]
        return centre, (
            jnp.where(lanes == 0, turn(ref[0 : 5 * R2, :], -3), turn(centre, 1)),
            jnp.where(lanes == 3, turn(ref[2 * R2 : 7 * R2, :], 3), turn(centre, -1)),
            ref[pl.ds(zero + (R2 - 1), 5 * R2), :],
            ref[pl.ds(zero + (R2 + 1), 5 * R2), :],
            turn(centre, 4),
            turn(centre, -4),
        )

    rows2, lanes2 = row_ids(5 * R2), lane_ids(5 * R2)
    x = rows2 % R2 + (8 * a - 8)
    y = 4 * (rows2 // R2) + lanes2 % 4 + (4 * j - 8)
    inside2 = (y != 0, y != 31, x != 0, x != 127, lanes2 >= 4, lanes2 < 124)
    centre, besides = around2(c2)
    faces, total, quarter = coefficients(centre, besides, inside2)
    for n in range(6):
        deep[n] = faces[n]
    deep[6] = 32.0 * quarter

    drain(but=3)
    land_rest()
    loop(3, 21, 9, guess)
    sweep(g1, e1, mid_faces, g1, 4, 20, 8, R1, 4, 24, 2)

    sixth()
    g2[...] = deep[6] * f2[R2 : 6 * R2, :]
    e2[R2 : 6 * R2, :] = g2[...]
    for src, dst in ((e2, e2b), (e2b, e2), (e2, e2b)):
        centre, besides = around2(src)
        parts = [deep[n] * besides[n] for n in range(6)]
        dst[R2 : 6 * R2, :] = (
            (0.2 * centre + g2[...]) + (parts[0] + parts[1]) + (parts[2] + parts[3]) + (parts[4] + parts[5])
        )

    def spread(ref, first, count, rows, value):
        slabs = [slab(ref, first + offset, count, 2) for offset in (0, 1, rows, rows + 1)]
        return [(ref, where, ref[where] + value) for where in slabs]

    lanes16 = lane_ids(16) % 4
    hops = ((1, 2), (-1, 2), (1, -2), (-1, -2))
    added = []
    for number in range(8):
        block, i = (number + 6) // 4, (number + 6) % 4
        value = jnp.where(lanes16 == i, e2b[pl.ds(zero + (R2 + R2 * block + 4), 16), :], 0.0)
        value = value + turn(value, hops[i][0])
        value = value + turn(value, hops[i][1])
        added += spread(e1, (4 + 2 * number) * R1, 16, R1, value)
        if number % 4 == 3:
            for ref, where, total in added:
                ref[where] = total
            added = []

    sweep(e1, e1b, mid_faces, g1, 5, 19, 14, R1, 4, 24, 2)
    sweep(e1b, e1, mid_faces, g1, 6, 18, 12, R1, 4, 24, 2)

    def grown(i):
        return spread(u2, 2 * i * RF, 24, RF, e1[pl.ds((i + 6) * R1 + 4, 24), :])

    loop(0, 12, 6, grown, group=3)
    sweep(u2, u1, fine_faces, gf, 2, 22, 10, RF, 4, 40, 1)

    def give(ref, stage, other, quads):
        def step(t):
            rows = pl.ds(pl.multiple_of(8 * t, 8), 8)
            out = []
            for q in quads:
                four = [
                    ref[pl.ds(pl.multiple_of((4 + 4 * q + i) * RF + 8 + 8 * t, 8), 8), :]
                    for i in range(4)
                ]
                for p, value in enumerate(transposed(four)):
                    out.append((stage, (p, rows, slice(128 * q, 128 * q + 128)), value))
            return out

        loop(0, 4, 4, step)
        lanes = pl.ds(128 * quads[0], 128 * len(quads))
        return [(stage.at[pl.ds(1 - half, 3), :, lanes], other.at[:, :, lanes])], other.at[:, :, lanes]

    def keep(stage, out):
        for s in range(4):
            out[s, :, mine] = stage[jnp.clip(s + half * split, 0, 3)]

    def take(other, out):
        for s in range(4):
            out[s, :, theirs] = other[jnp.clip(s + half * (split - 1), 0, 2)]

    last = []
    sweep(u1, u2, fine_faces, gf, 3, 12, 9, RF, 4, 40, 1)
    last.append(hand(*give(u2, stage_f, other_f, (0, 1))))
    sweep(u1, u2, fine_faces, gf, 12, 21, 9, RF, 4, 40, 1)
    last.append(hand(*give(u2, stage_f, other_f, (2, 3))))
    leftover(u2, u1, fine_faces, gf, df, 4, 12, 8, RF, 8, 32, 1)
    last.append(hand(*give(u1, stage_r, other_r, (0, 1))))
    leftover(u2, u1, fine_faces, gf, df, 12, 20, 8, RF, 8, 32, 1)
    last.append(hand(*give(u1, stage_r, other_r, (2, 3))))
    keep(stage_f, out_field)
    last[0]()
    last[1]()
    take(other_f, out_field)
    keep(stage_r, out_resid)
    last[2]()
    last[3]()
    take(other_r, out_resid)
    drain()


def vmem(*shape):
    return pltpu.VMEM(shape, F32)


def body(source, conductance, initial, box_counts):
    fine_field = vmem((PF + 1) * RF, LANES)
    mid_field = vmem((P1 + 1) * R1, LANES)
    deep_field = vmem(7 * R2, LANES)
    scratch = [pltpu.SMEM(box_counts.shape, jnp.int32)] + [vmem(6, 32, 512)] * 3
    scratch += [fine_field] * 5 + [vmem(6, (PF + 1) * RF, LANES)] + [fine_field] * 2
    scratch += [mid_field] * 4 + [vmem(6, (P1 + 1) * R1, LANES)] + [mid_field] * 4
    scratch += [deep_field] * 4 + [vmem(7, 5 * R2, LANES), vmem(5 * R2, LANES)]
    scratch += [vmem(4, 32, 512)] * 2 + [vmem(3, 32, 512)] * 2
    for big, middle, small in ((160, 80, 8), (96, 48, 8), (104, 56, 24), (32, 16, 8), (144, 72, 16)):
        scratch += [vmem(2 * big + 2 * middle + 4 * small, LANES)] * 2
    scratch += [pltpu.SemaphoreType.DMA((4,))] + [pltpu.SemaphoreType.DMA((ROUNDS,))] * 2
    hbm = pl.BlockSpec(memory_space=pltpu.HBM)
    shape = jax.ShapeDtypeStruct(source.shape, source.dtype)
    field, resid, held = pl.pallas_call(
        kernel,
        out_shape=(shape,) * 3,
        in_specs=[hbm] * 4,
        out_specs=(pl.BlockSpec(memory_space=pltpu.VMEM),) * 3,
        scratch_shapes=scratch,
        compiler_params=pltpu.CompilerParams(
            collective_id=0, has_side_effects=True, vmem_limit_bytes=40 * 2**20
        ),
        cost_estimate=pl.CostEstimate(flops=3 * 10**7, bytes_accessed=3 * 10**6, transcendentals=0),
    )(*[pltpu.with_memory_space_constraint(x, pltpu.HBM) for x in (box_counts, source, conductance, initial)])
    return field * held, resid * held


def solution(mesh):
    return jax.shard_map(
        body,
        mesh=mesh,
        in_specs=(P("box", None, None), P("box", None, None), P("box", None, None), P()),
        out_specs=(P("box", None, None), P("box", None, None)),
        check_vma=False,
    )
```
